32 devices in a mesh: dp: 4 (over y, x), ctx: 8 (over z, core).
Axes of the slice: x: 2, y: 2, z: 4, core: 2. Of those that a mesh axis runs over, the one named last changes fastest.
Arguments:
- tokens: bfloat16 [4, 1024, 768], P('dp', 'ctx'), may hold values from -6 to 6
- pair_of_rank: int32 [8], replicated, may hold values from 0 to 7, each once
- first_gain: bfloat16 [768], P('dp'), may hold values from 0.25 to 1.75
- first_shift: bfloat16 [768], P('dp'), may hold values from -1.75 to 1.75
- w_input: bfloat16 [768, 2304], P('dp'), may hold values from -0.3125 to 0.3125
- query_bias: bfloat16 [768], P('dp'), may hold values from -1.75 to 1.75
- value_bias: bfloat16 [768], P('dp'), may hold values from -1.75 to 1.75
- w_output: bfloat16 [768, 768], P('dp'), may hold values from -1.25 to 1.25
- output_bias: bfloat16 [768], P('dp'), may hold values from -1.75 to 1.75
- second_gain: bfloat16 [768], P('dp'), may hold values from 0.25 to 1.75
- second_shift: bfloat16 [768], P('dp'), may hold values from -1.75 to 1.75
- w_expand: bfloat16 [768, 3072], P('dp'), may hold values from -0.21875 to 0.21875
- expand_bias: bfloat16 [3072], P('dp'), may hold values from -1.75 to 1.75
- w_contract: bfloat16 [3072, 768], P('dp'), may hold values from -0.109375 to 0.109375
- contract_bias: bfloat16 [768], P('dp'), may hold values from -3.5 to 3.5
- cotangent: bfloat16 [4, 1024, 768], P('dp', 'ctx'), may hold values from -6 to 6
Outputs:
- out: bfloat16 [4, 1024, 768], P('dp', 'ctx')
- grad_tokens: float32 [4, 1024, 768], P('dp', 'ctx')
- grad_first_gain: float32 [768], P('dp')
- grad_first_shift: float32 [768], P('dp')
- grad_input: float32 [768, 2304], P('dp')
- grad_query_bias: float32 [768], P('dp')
- grad_value_bias: float32 [768], P('dp')
- grad_output: float32 [768, 768], P('dp')
- grad_output_bias: float32 [768], P('dp')
- grad_second_gain: float32 [768], P('dp')
- grad_second_shift: float32 [768], P('dp')
- grad_expand: float32 [768, 3072], P('dp')
- grad_expand_bias: float32 [3072], P('dp')
- grad_contract: float32 [3072, 768], P('dp')
- grad_contract_bias: float32 [768], P('dp')
The draws below stay inside these ranges and needn't reach their ends.
Inputs may be any that keep to these rules, and one draw needn't show every extreme that they name: Context rank r holds the blocks pair_of_rank[r] and 15 - pair_of_rank[r] of every sequence, each of 64 positions; every value occurs once.
All inputs are finite; a program needn't handle non-finite values.
Results may differ from the reference program's by a relative error of at most 0.024.
Values may be sent and summed in bfloat16 or wider, within the bound.
No kernel may reach another device: no remote copies, remote signals or barrier semaphores. Data moves between devices by JAX's collectives and lax.ppermute only.
A program may use at most 256 MiB of HBM per device.

```python
import math
import jax
import jax.numpy as jnp
from jax import lax

D = 768
HEADS = 12
HEAD_DIM = 64
FF = 3072
BLK = 64
SEQS = 4
LENGTH = 1024
N_CTX = 8


def steps_of(stream_key, extent, cuts, smallest, top_value):
    def one(dim, parts):
        draws = jax.random.uniform(jax.random.fold_in(jax.random.fold_in(stream_key, 6), dim), (parts,), jnp.float32, smallest / len(cuts), top_value / len(cuts))
        return jnp.repeat(jnp.exp(draws), extent[dim] // parts).reshape((-1,) + (1,) * (len(extent) - dim - 1))

    level = one(*cuts[0])
    for cut in cuts[1:]:
        level = level * one(*cut)
    return level


def noise(key, dims, deviation, limit, shards=(), held_as=jnp.bfloat16):
    drawn = deviation * jax.random.normal(key, dims, jnp.float32)
    if shards:
        drawn = drawn * steps_of(key, dims, shards, -0.22, 0.18)
    return jnp.clip(drawn, -limit, limit).astype(held_as)


def setup_inputs(seed: int = 0) -> dict:
    seeds = jax.random.split(jax.random.key(seed), 17)
    tokens = noise(seeds[0], (SEQS, LENGTH, D), 1.0, 6.0, ((0, 4), (1, 8)))
    pair_of_rank = jax.random.permutation(seeds[1], N_CTX).astype(jnp.int32)
    first_gain = jnp.clip(1.0 + 0.15 * jax.random.normal(seeds[2], (D,), jnp.float32), 0.25, 1.75).astype(jnp.bfloat16)
    first_shift = noise(seeds[3], (D,), 0.3, 1.75, ((0, 4),))
    w_input = noise(seeds[4], (D, 3 * D), (D // 2) ** -0.5, 0.3125, ((0, 4),))
    query_bias = noise(seeds[5], (D,), 0.3, 1.75, ((0, 4),))
    value_bias = noise(seeds[6], (D,), 0.3, 1.75, ((0, 4),))
    w_output = noise(seeds[7], (D, D), (D // 32) ** -0.5, 1.25, ((0, 4),))
    output_bias = noise(seeds[8], (D,), 0.3, 1.75, ((0, 4),))
    second_gain = jnp.clip(1.0 + 0.15 * jax.random.normal(seeds[9], (D,), jnp.float32), 0.25, 1.75).astype(jnp.bfloat16)
    second_shift = noise(seeds[10], (D,), 0.3, 1.75, ((0, 4),))
    w_expand = noise(seeds[11], (D, FF), D ** -0.5, 0.21875, ((0, 4),))
    expand_bias = noise(seeds[12], (FF,), 0.3, 1.75, ((0, 4),))
    w_contract = noise(seeds[13], (FF, D), FF ** -0.5, 0.109375, ((0, 4),))
    contract_bias = noise(seeds[14], (D,), 0.6, 3.5, ((0, 4),))
    cotangent = noise(seeds[15], (SEQS, LENGTH, D), 1.0, 6.0, ((0, 4), (1, 8)))
    return {"tokens": tokens, "pair_of_rank": pair_of_rank, "first_gain": first_gain, "first_shift": first_shift, "w_input": w_input, "query_bias": query_bias, "value_bias": value_bias, "w_output": w_output, "output_bias": output_bias, "second_gain": second_gain, "second_shift": second_shift, "w_expand": w_expand, "expand_bias": expand_bias, "w_contract": w_contract, "contract_bias": contract_bias, "cotangent": cotangent}


NEG_BIG = -1e+30
NORM_EPS = 1e-05
GELU_SCALE = 0.7978845608028654
GELU_CUBIC = 0.044715

@jax.custom_vjp
def low(v):
    return lax.optimization_barrier(v.astype(jnp.bfloat16)).astype(jnp.float32)

@jax.custom_vjp
def low_back(v):
    return v

def low_keep(v):
    return (low(v), None)

def low_pass(kept, grad):
    return (grad,)

def back_keep(v):
    return (v, None)

def back_low(kept, grad):
    return (low(grad),)
low.defvjp(low_keep, low_pass)
low_back.defvjp(back_keep, back_low)

def gelu_tanh(values):
    return 0.5 * values * (1.0 + jnp.tanh(GELU_SCALE * (values + GELU_CUBIC * values * values * values)))

def layer_norm(values, gain_row, shift_row):
    centre = values - lax.optimization_barrier(jnp.mean(values, axis=-1, keepdims=True))
    spread = lax.optimization_barrier(jnp.mean(centre * centre, axis=-1, keepdims=True))
    return centre * lax.rsqrt(spread + NORM_EPS) * gain_row + shift_row

def product(left_side, right_side):
    return jnp.dot(left_side, right_side, precision=lax.Precision.HIGHEST, preferred_element_type=jnp.float32)

def attention(query_rows, key_rows, value_rows, places):
    seq_rows = query_rows.shape[0]
    block_rows = math.gcd(seq_rows, 512)
    key_heads = key_rows.reshape(seq_rows, HEADS, HEAD_DIM)
    value_heads = value_rows.reshape(seq_rows, HEADS, HEAD_DIM)
    query_blocks = query_rows.reshape(seq_rows // block_rows, block_rows, HEADS, HEAD_DIM)
    place_blocks = places.reshape(seq_rows // block_rows, block_rows)

    @jax.checkpoint
    def one_block(inputs):
        block_query, block_places = inputs
        scores = jnp.einsum('qhd,khd->hqk', block_query, key_heads, precision=lax.Precision.HIGHEST) * HEAD_DIM ** (-0.5)
        scores = low_back(scores)
        visible = places[None, None, :] <= block_places[None, :, None]
        weights = low(jax.nn.softmax(jnp.where(visible, scores, NEG_BIG), axis=-1))
        return jnp.einsum('hqk,khd->qhd', weights, value_heads, precision=lax.Precision.HIGHEST)
    attended = lax.map(one_block, (query_blocks, place_blocks))
    return attended.reshape(seq_rows, HEADS * HEAD_DIM)

def block_forward(params, token_rows, places):
    first_gain, first_shift, w_input, query_bias, value_bias, w_output, output_bias, second_gain, second_shift, w_expand, expand_bias, w_contract, contract_bias = params
    model_width = token_rows.shape[1]
    normed = low(layer_norm(token_rows, first_gain, first_shift))
    mixed_rows = product(normed, w_input)
    query_rows = low_back(low(mixed_rows[:, :model_width] + query_bias))
    key_rows = low_back(low(mixed_rows[:, model_width:2 * model_width]))
    value_rows = low_back(low(mixed_rows[:, 2 * model_width:] + value_bias))
    attended = low_back(low(attention(query_rows, key_rows, value_rows, places)))
    middle = token_rows + low_back(product(attended, w_output) + output_bias)
    normed_two = low(layer_norm(middle, second_gain, second_shift))
    hidden = low_back(product(normed_two, w_expand) + expand_bias)
    active = low(gelu_tanh(hidden))
    return middle + low_back(product(active, w_contract) + contract_bias)

def add_pair(left_sum, right_sum):
    return left_sum + right_sum

def reference(tokens, pair_of_rank, first_gain, first_shift, w_input, query_bias, value_bias, w_output, output_bias, second_gain, second_shift, w_expand, expand_bias, w_contract, contract_bias, cotangent):
    seq_rows = tokens.shape[1]
    row_index = jnp.arange(seq_rows, dtype=jnp.int32)
    owner_pair = jnp.take(pair_of_rank, row_index // (2 * BLK)).astype(jnp.int32)
    block_index = jnp.where(row_index // BLK % 2 == 0, owner_pair, 2 * N_CTX - 1 - owner_pair)
    places = (block_index * BLK + row_index % BLK).astype(jnp.int32)
    params = tuple((weight_arg.astype(jnp.float32) for weight_arg in (first_gain, first_shift, w_input, query_bias, value_bias, w_output, output_bias, second_gain, second_shift, w_expand, expand_bias, w_contract, contract_bias)))

    def one_sequence(totals, inputs):
        sequence, seq_cotangent = inputs

        def forward(weight_set, rows_in):
            return block_forward(weight_set, rows_in, places)
        result, pullback = jax.vjp(forward, params, sequence.astype(jnp.float32))
        grad_params, grad_rows = pullback(seq_cotangent.astype(jnp.float32))
        totals = jax.tree.map(add_pair, totals, grad_params)
        return (totals, (result.astype(jnp.bfloat16), grad_rows))
    zero_grads = jax.tree.map(jnp.zeros_like, params)
    totals, (outputs, grad_tokens) = lax.scan(one_sequence, zero_grads, (tokens, cotangent))
    return (outputs, grad_tokens, totals[0], totals[1], totals[2], totals[3], totals[4], totals[5], totals[6], totals[7], totals[8], totals[9], totals[10], totals[11], totals[12])
```

```python
import math

import jax
import jax.numpy as jnp
from jax import lax
from jax.experimental import pallas as pl
from jax.experimental.pallas import tpu as pltpu
from jax.sharding import PartitionSpec as P

HEADS = 12
HEAD_DIM = 64


NEG_BIG = -1e30
NORM_EPS = 1e-05
GELU_SCALE = 0.7978845608028654
GELU_CUBIC = 0.044715


def gelu_tanh(values):
    return (
        0.5
        * values
        * (1.0 + jnp.tanh(GELU_SCALE * (values + GELU_CUBIC * values * values * values)))
    )


def layer_norm(values, gain_row, shift_row):
    centre = values - jnp.mean(values, axis=-1, keepdims=True)
    spread = jnp.mean(centre * centre, axis=-1, keepdims=True)
    return centre * lax.rsqrt(spread + NORM_EPS) * gain_row + shift_row


def lookup_pair(pair_table, positions):
    ranks_all = jnp.arange(pair_table.shape[0], dtype=jnp.int32)
    return jnp.sum(jnp.where(positions[..., None] == ranks_all, pair_table, 0), axis=-1)


def group_count(blocks, sub_rows):
    chosen_count = 1
    for candidate in range(1, blocks + 1):
        if blocks % candidate == 0 and candidate * sub_rows <= max(512, sub_rows):
            chosen_count = candidate
    return chosen_count


def slot_mask(slot_ids, wanted, rank_count):
    return (slot_ids == wanted).reshape((-1,) + (1,) * (rank_count - 1))


def slot_add(values, slot_ids):
    early_sum = jnp.sum(jnp.where(slot_mask(slot_ids, 0, values.ndim), values, 0.0), axis=0)
    late_sum = jnp.sum(jnp.where(slot_mask(slot_ids, 1, values.ndim), values, 0.0), axis=0)
    return jnp.stack([early_sum, late_sum])


def slot_max(values, slot_ids):
    early_max = jnp.max(jnp.where(slot_mask(slot_ids, 0, values.ndim), values, NEG_BIG), axis=0)
    late_max = jnp.max(jnp.where(slot_mask(slot_ids, 1, values.ndim), values, NEG_BIG), axis=0)
    return jnp.stack([early_max, late_max])


def slot_pick(per_slot, slot_ids):
    return jnp.where(slot_mask(slot_ids, 0, per_slot.ndim), per_slot[0][None], per_slot[1][None])


def query_tiles(blocks, chosen):
    target = chosen.shape + blocks.shape[2:]
    chosen_view = chosen.reshape((-1,) + (1,) * (blocks.ndim - 2))
    late_part = jnp.broadcast_to(blocks[1], target)
    picked = jnp.where(chosen_view, blocks[0], blocks[1])
    return jnp.concatenate([late_part, picked], axis=0)


def key_tiles(blocks, chosen):
    target = chosen.shape + blocks.shape[2:]
    chosen_view = chosen.reshape((-1,) + (1,) * (blocks.ndim - 2))
    early_part = jnp.broadcast_to(blocks[0], target)
    picked = jnp.where(chosen_view, blocks[0], blocks[1])
    return jnp.concatenate([early_part, picked], axis=0)


def tile_slots(chosen):
    late_slot = jnp.where(chosen, 0, 1).astype(jnp.int32)
    query_slot = jnp.concatenate([jnp.ones_like(late_slot), late_slot])
    key_slot = jnp.concatenate([jnp.zeros_like(late_slot), late_slot])
    return (query_slot, key_slot)


def tile_mask(is_own, query_places, key_places):
    visible = key_places[:, None, :] <= query_places[:, :, None]
    visible = jnp.logical_or(visible, jnp.logical_not(is_own)[:, None, None])
    return jnp.concatenate([jnp.ones_like(visible), visible], axis=0)


def tile_scores(tile_query, tile_key, score_scale):
    return (
        jnp.einsum("tqhd,tkhd->thqk", tile_query, tile_key, preferred_element_type=jnp.float32)
        * score_scale
    )


def tile_probs(tile_query, tile_key, tile_visible, row_lse, score_scale):
    scores = tile_scores(tile_query, tile_key, score_scale)
    return jnp.where(tile_visible[:, None], jnp.exp(scores - row_lse[..., None]), 0.0)


def tile_dscore(probs, tile_dout, tile_value, row_delta):
    grad_probs = jnp.einsum(
        "tqhd,tkhd->thqk", tile_dout, tile_value, preferred_element_type=jnp.float32
    )
    return (probs * (grad_probs - row_delta[..., None])).astype(jnp.bfloat16)


def stats_update(running, tile_query, tile_key, query_slot, tile_visible, score_scale):
    run_peak, run_total = running
    visible = tile_visible[:, None]
    masked = jnp.where(visible, tile_scores(tile_query, tile_key, score_scale), NEG_BIG)
    new_peak = jnp.maximum(run_peak, slot_max(jnp.max(masked, axis=-1), query_slot))
    weights = jnp.where(visible, jnp.exp(masked - slot_pick(new_peak, query_slot)[..., None]), 0.0)
    run_total = run_total * jnp.exp(run_peak - new_peak) + slot_add(
        jnp.sum(weights, axis=-1), query_slot
    )
    return (new_peak, run_total)


def values_update(
    running, tile_query, tile_key, tile_value, query_slot, tile_visible, row_lse, score_scale
):
    probs = tile_probs(tile_query, tile_key, tile_visible, row_lse, score_scale)
    part_out = jnp.einsum(
        "thqk,tkhd->tqhd",
        probs.astype(jnp.bfloat16),
        tile_value,
        preferred_element_type=jnp.float32,
    )
    return running + slot_add(part_out, query_slot)


def sweep_piece(carried, pieces, block_rows, my_rank, pair_table, update):
    piece_rows = pieces[0].shape[1]
    sub_rows = math.gcd(piece_rows, block_rows)
    unit_count = piece_rows // sub_rows
    group_size = group_count(unit_count, sub_rows)

    def group_step(loop_index, running):
        offset = loop_index * (group_size * sub_rows)
        slices = tuple(
            (
                lax.dynamic_slice_in_dim(member, offset, group_size * sub_rows, 1).reshape(
                    (2, group_size, sub_rows) + member.shape[2:]
                )
                for member in pieces
            )
        )
        places = offset + jnp.arange(group_size * sub_rows, dtype=jnp.int32).reshape(
            group_size, sub_rows
        )
        far_ranks = places[:, 0] // block_rows
        far_pair = lookup_pair(pair_table, far_ranks)
        return update(running, slices, far_pair, far_ranks == my_rank, places % block_rows, offset)

    return lax.fori_loop(0, unit_count // group_size, group_step, carried)


def per_device(
    tokens,
    pair_of_rank,
    first_gain,
    first_shift,
    w_input,
    query_bias,
    value_bias,
    w_output,
    output_bias,
    second_gain,
    second_shift,
    w_expand,
    expand_bias,
    w_contract,
    contract_bias,
    cotangent,
):
    gathered = (
        lax.all_gather(first_gain, "dp", axis=0, tiled=True),
        lax.all_gather(first_shift, "dp", axis=0, tiled=True),
        lax.all_gather(w_input, "dp", axis=0, tiled=True),
        lax.all_gather(query_bias, "dp", axis=0, tiled=True),
        lax.all_gather(value_bias, "dp", axis=0, tiled=True),
        lax.all_gather(w_output, "dp", axis=0, tiled=True),
        lax.all_gather(output_bias, "dp", axis=0, tiled=True),
        lax.all_gather(second_gain, "dp", axis=0, tiled=True),
        lax.all_gather(second_shift, "dp", axis=0, tiled=True),
        lax.all_gather(w_expand, "dp", axis=0, tiled=True),
        lax.all_gather(expand_bias, "dp", axis=0, tiled=True),
        lax.all_gather(w_contract, "dp", axis=0, tiled=True),
        lax.all_gather(contract_bias, "dp", axis=0, tiled=True),
    )
    (
        full_first_gain,
        full_first_shift,
        full_input,
        full_query_bias,
        full_value_bias,
        full_output,
        full_output_bias,
        full_second_gain,
        full_second_shift,
        full_expand,
        full_expand_bias,
        full_contract,
        full_contract_bias,
    ) = gathered
    model_width = tokens.shape[2]
    block_rows = tokens.shape[1] // 2
    score_scale = HEAD_DIM ** (-0.5)
    slot_view = (2, block_rows, model_width)
    head_view = (2, block_rows, HEADS, HEAD_DIM)
    my_rank = lax.axis_index("ctx")
    my_pair = lookup_pair(pair_of_rank, my_rank)
    own_places = jnp.arange(block_rows, dtype=jnp.int32)[None, :]
    diag_mask = (own_places <= own_places.reshape(-1, 1))[None]
    zero_slot = jnp.zeros((1,), jnp.int32)

    def split_heads(member):
        return member.reshape(member.shape[:3] + (HEADS, HEAD_DIM))

    token_rows = tokens[0].astype(jnp.float32)
    normed_full, first_pullback = jax.vjp(
        layer_norm,
        token_rows,
        full_first_gain.astype(jnp.float32),
        full_first_shift.astype(jnp.float32),
    )
    normed = normed_full.astype(jnp.bfloat16)
    mixed_rows = jnp.dot(normed, full_input, preferred_element_type=jnp.float32)
    query_rows = (mixed_rows[:, :model_width] + full_query_bias.astype(jnp.float32)).astype(
        jnp.bfloat16
    )
    key_rows = mixed_rows[:, model_width : 2 * model_width].astype(jnp.bfloat16)
    value_rows = (mixed_rows[:, 2 * model_width :] + full_value_bias.astype(jnp.float32)).astype(
        jnp.bfloat16
    )
    own_query = query_rows.reshape(head_view)
    own_key = key_rows.reshape(head_view)
    own_value = value_rows.reshape(head_view)
    diag_query = own_query[0][None]
    diag_key = own_key[0][None]
    diag_value = own_value[0][None]
    key_slots = key_rows.reshape(slot_view)
    value_slots = value_rows.reshape(slot_view)
    query_slots = query_rows.reshape(slot_view)

    def stats_group(running, slices, far_pair, is_own, far_places, first_row):
        chosen = far_pair < my_pair
        query_slot, key_slot = tile_slots(chosen)
        return stats_update(
            running,
            query_tiles(own_query[:, None], chosen),
            key_tiles(split_heads(slices[0]), chosen),
            query_slot,
            tile_mask(is_own, own_places, far_places),
            score_scale,
        )

    stats_start = (
        jnp.full((2, HEADS, block_rows), NEG_BIG, jnp.float32),
        jnp.zeros((2, HEADS, block_rows), jnp.float32),
    )
    stats_start = stats_update(stats_start, diag_query, diag_key, zero_slot, diag_mask, score_scale)
    run_peak, run_total = sweep_piece(
        stats_start,
        (lax.all_gather(key_slots, "ctx", axis=1, tiled=True),),
        block_rows,
        my_rank,
        pair_of_rank,
        stats_group,
    )
    row_lse = run_peak + jnp.log(run_total)

    def values_group(running, slices, far_pair, is_own, far_places, first_row):
        chosen = far_pair < my_pair
        query_slot, key_slot = tile_slots(chosen)
        return values_update(
            running,
            query_tiles(own_query[:, None], chosen),
            key_tiles(split_heads(slices[0]), chosen),
            key_tiles(split_heads(slices[1]), chosen),
            query_slot,
            tile_mask(is_own, own_places, far_places),
            slot_pick(row_lse, query_slot),
            score_scale,
        )

    values_start = values_update(
        jnp.zeros(head_view, jnp.float32),
        diag_query,
        diag_key,
        diag_value,
        zero_slot,
        diag_mask,
        row_lse[0][None],
        score_scale,
    )
    attended = sweep_piece(
        values_start,
        (
            lax.all_gather(key_slots, "ctx", axis=1, tiled=True),
            lax.all_gather(value_slots, "ctx", axis=1, tiled=True),
        ),
        block_rows,
        my_rank,
        pair_of_rank,
        values_group,
    )
    attended_low = attended.reshape(2 * block_rows, model_width).astype(jnp.bfloat16)
    middle = (
        token_rows
        + jnp.dot(attended_low, full_output, preferred_element_type=jnp.float32)
        + full_output_bias.astype(jnp.float32)
    )
    normed_full_two, second_pullback = jax.vjp(
        layer_norm,
        middle,
        full_second_gain.astype(jnp.float32),
        full_second_shift.astype(jnp.float32),
    )
    normed_two = normed_full_two.astype(jnp.bfloat16)
    hidden = jnp.dot(
        normed_two, full_expand, preferred_element_type=jnp.float32
    ) + full_expand_bias.astype(jnp.float32)
    active_full, gelu_pullback = jax.vjp(gelu_tanh, hidden)
    active_low = active_full.astype(jnp.bfloat16)
    result = (
        middle
        + jnp.dot(active_low, full_contract, preferred_element_type=jnp.float32)
        + full_contract_bias.astype(jnp.float32)
    )
    block_out = result.astype(jnp.bfloat16)[None]
    back_input, back_output, back_expand, back_contract = (
        lax.all_gather(w_input, "dp", axis=0, tiled=True),
        lax.all_gather(w_output, "dp", axis=0, tiled=True),
        lax.all_gather(w_expand, "dp", axis=0, tiled=True),
        lax.all_gather(w_contract, "dp", axis=0, tiled=True),
    )
    grad_out_low = cotangent[0]
    grad_out = grad_out_low.astype(jnp.float32)
    grad_contract = jnp.einsum(
        "rf,rd->fd", active_low, grad_out_low, preferred_element_type=jnp.float32
    )
    grad_contract_bias = jnp.sum(grad_out, axis=0)
    grad_active = jnp.einsum(
        "rd,fd->rf", grad_out_low, back_contract, preferred_element_type=jnp.float32
    )
    grad_hidden = gelu_pullback(grad_active)[0].astype(jnp.bfloat16)
    grad_expand = jnp.einsum(
        "rd,rf->df", normed_two, grad_hidden, preferred_element_type=jnp.float32
    )
    grad_expand_bias = jnp.sum(grad_hidden.astype(jnp.float32), axis=0)
    grad_normed_two = jnp.einsum(
        "rf,df->rd", grad_hidden, back_expand, preferred_element_type=jnp.float32
    )
    grad_middle_part, grad_second_gain, grad_second_shift = second_pullback(grad_normed_two)
    grad_middle = grad_out + grad_middle_part
    grad_branch = grad_middle.astype(jnp.bfloat16)
    grad_output = jnp.einsum(
        "rd,re->de", attended_low, grad_branch, preferred_element_type=jnp.float32
    )
    grad_output_bias = jnp.sum(grad_branch.astype(jnp.float32), axis=0)
    grad_attended = jnp.einsum(
        "re,de->rd", grad_branch, back_output, preferred_element_type=jnp.float32
    ).astype(jnp.bfloat16)
    own_dout = grad_attended.reshape(head_view)
    dout_slots = grad_attended.reshape(slot_view)
    delta_rows = jnp.sum(own_dout.astype(jnp.float32) * attended, axis=-1)
    row_delta = jnp.transpose(delta_rows, (0, 2, 1))
    lse_rows = jnp.transpose(row_lse, (0, 2, 1))
    far_lse, far_delta = (
        lax.all_gather(lse_rows, "ctx", axis=1, tiled=True),
        lax.all_gather(delta_rows, "ctx", axis=1, tiled=True),
    )
    diag_probs = tile_probs(diag_query, diag_key, diag_mask, row_lse[0][None], score_scale)
    diag_dscore = tile_dscore(diag_probs, own_dout[0][None], diag_value, row_delta[0][None])
    query_start = slot_add(
        jnp.einsum("thqk,tkhd->tqhd", diag_dscore, diag_key, preferred_element_type=jnp.float32)
        * score_scale,
        zero_slot,
    )
    key_start = slot_add(
        jnp.einsum("thqk,tqhd->tkhd", diag_dscore, diag_query, preferred_element_type=jnp.float32)
        * score_scale,
        zero_slot,
    )
    value_start = slot_add(
        jnp.einsum(
            "thqk,tqhd->tkhd",
            diag_probs.astype(jnp.bfloat16),
            own_dout[0][None],
            preferred_element_type=jnp.float32,
        ),
        zero_slot,
    )

    def query_grad_group(running, slices, far_pair, is_own, far_places, first_row):
        chosen = far_pair < my_pair
        query_slot, key_slot = tile_slots(chosen)
        tile_key = key_tiles(split_heads(slices[0]), chosen)
        tile_value = key_tiles(split_heads(slices[1]), chosen)
        probs = tile_probs(
            query_tiles(own_query[:, None], chosen),
            tile_key,
            tile_mask(is_own, own_places, far_places),
            slot_pick(row_lse, query_slot),
            score_scale,
        )
        dscore = tile_dscore(
            probs,
            query_tiles(own_dout[:, None], chosen),
            tile_value,
            slot_pick(row_delta, query_slot),
        )
        part_grad = (
            jnp.einsum("thqk,tkhd->tqhd", dscore, tile_key, preferred_element_type=jnp.float32)
            * score_scale
        )
        return running + slot_add(part_grad, query_slot)

    def key_grad_group(running, slices, far_pair, is_own, far_places, first_row):
        chosen = my_pair < far_pair
        query_slot, key_slot = tile_slots(chosen)
        group_size = far_places.shape[0]
        sub_rows = far_places.shape[1]
        tile_query = query_tiles(split_heads(slices[0]), chosen)
        tile_dout = query_tiles(split_heads(slices[1]), chosen)
        lse_part = lax.dynamic_slice_in_dim(far_lse, first_row, group_size * sub_rows, 1).reshape(
            2, group_size, sub_rows, HEADS
        )
        delta_part = lax.dynamic_slice_in_dim(
            far_delta, first_row, group_size * sub_rows, 1
        ).reshape(2, group_size, sub_rows, HEADS)
        tile_lse = jnp.transpose(query_tiles(lse_part, chosen), (0, 2, 1))
        tile_delta = jnp.transpose(query_tiles(delta_part, chosen), (0, 2, 1))
        tile_key = key_tiles(own_key[:, None], chosen)
        tile_value = key_tiles(own_value[:, None], chosen)
        probs = tile_probs(
            tile_query, tile_key, tile_mask(is_own, far_places, own_places), tile_lse, score_scale
        )
        dscore = tile_dscore(probs, tile_dout, tile_value, tile_delta)
        key_part = (
            jnp.einsum("thqk,tqhd->tkhd", dscore, tile_query, preferred_element_type=jnp.float32)
            * score_scale
        )
        value_part = jnp.einsum(
            "thqk,tqhd->tkhd",
            probs.astype(jnp.bfloat16),
            tile_dout,
            preferred_element_type=jnp.float32,
        )
        return (
            running[0] + slot_add(key_part, key_slot),
            running[1] + slot_add(value_part, key_slot),
        )

    grad_query_sum = sweep_piece(
        query_start,
        (
            lax.all_gather(key_slots, "ctx", axis=1, tiled=True),
            lax.all_gather(value_slots, "ctx", axis=1, tiled=True),
        ),
        block_rows,
        my_rank,
        pair_of_rank,
        query_grad_group,
    )
    grad_key_sum, grad_value_sum = sweep_piece(
        (key_start, value_start),
        (
            lax.all_gather(query_slots, "ctx", axis=1, tiled=True),
            lax.all_gather(dout_slots, "ctx", axis=1, tiled=True),
        ),
        block_rows,
        my_rank,
        pair_of_rank,
        key_grad_group,
    )
    flat_rows = 2 * block_rows
    grad_query_low = grad_query_sum.reshape(flat_rows, model_width).astype(jnp.bfloat16)
    grad_key_low = grad_key_sum.reshape(flat_rows, model_width).astype(jnp.bfloat16)
    grad_value_low = grad_value_sum.reshape(flat_rows, model_width).astype(jnp.bfloat16)
    grad_mixed = jnp.concatenate([grad_query_low, grad_key_low, grad_value_low], axis=1)
    grad_input = jnp.einsum("rd,re->de", normed, grad_mixed, preferred_element_type=jnp.float32)
    grad_query_bias = jnp.sum(grad_query_low.astype(jnp.float32), axis=0)
    grad_value_bias = jnp.sum(grad_value_low.astype(jnp.float32), axis=0)
    grad_normed = jnp.einsum(
        "re,de->rd", grad_mixed, back_input, preferred_element_type=jnp.float32
    )
    grad_token_part, grad_first_gain, grad_first_shift = first_pullback(grad_normed)
    grad_tokens = (grad_middle + grad_token_part)[None]
    grad_local = (
        grad_first_gain,
        grad_first_shift,
        grad_input,
        grad_query_bias,
        grad_value_bias,
        grad_output,
        grad_output_bias,
        grad_second_gain,
        grad_second_shift,
        grad_expand,
        grad_expand_bias,
        grad_contract,
        grad_contract_bias,
    )
    grad_owned = (
        lax.psum_scatter(
            grad_local[0].astype(jnp.bfloat16), "dp", scatter_dimension=0, tiled=True
        ).astype(jnp.float32),
        lax.psum_scatter(
            grad_local[1].astype(jnp.bfloat16), "dp", scatter_dimension=0, tiled=True
        ).astype(jnp.float32),
        lax.psum_scatter(
            grad_local[2].astype(jnp.bfloat16), "dp", scatter_dimension=0, tiled=True
        ).astype(jnp.float32),
        lax.psum_scatter(
            grad_local[3].astype(jnp.bfloat16), "dp", scatter_dimension=0, tiled=True
        ).astype(jnp.float32),
        lax.psum_scatter(
            grad_local[4].astype(jnp.bfloat16), "dp", scatter_dimension=0, tiled=True
        ).astype(jnp.float32),
        lax.psum_scatter(
            grad_local[5].astype(jnp.bfloat16), "dp", scatter_dimension=0, tiled=True
        ).astype(jnp.float32),
        lax.psum_scatter(
            grad_local[6].astype(jnp.bfloat16), "dp", scatter_dimension=0, tiled=True
        ).astype(jnp.float32),
        lax.psum_scatter(
            grad_local[7].astype(jnp.bfloat16), "dp", scatter_dimension=0, tiled=True
        ).astype(jnp.float32),
        lax.psum_scatter(
            grad_local[8].astype(jnp.bfloat16), "dp", scatter_dimension=0, tiled=True
        ).astype(jnp.float32),
        lax.psum_scatter(
            grad_local[9].astype(jnp.bfloat16), "dp", scatter_dimension=0, tiled=True
        ).astype(jnp.float32),
        lax.psum_scatter(
            grad_local[10].astype(jnp.bfloat16), "dp", scatter_dimension=0, tiled=True
        ).astype(jnp.float32),
        lax.psum_scatter(
            grad_local[11].astype(jnp.bfloat16), "dp", scatter_dimension=0, tiled=True
        ).astype(jnp.float32),
        lax.psum_scatter(
            grad_local[12].astype(jnp.bfloat16), "dp", scatter_dimension=0, tiled=True
        ).astype(jnp.float32),
    )
    grad_final = tuple(
        lax.psum(
            (
                grad_owned[0],
                grad_owned[1],
                grad_owned[2],
                grad_owned[3],
                grad_owned[4],
                grad_owned[5],
                grad_owned[6],
                grad_owned[7],
                grad_owned[8],
                grad_owned[9],
                grad_owned[10],
                grad_owned[11],
                grad_owned[12],
            ),
            "ctx",
        )
    )
    return (block_out, grad_tokens) + tuple(grad_final)


VMEM_BYTES = 40 * 1024 * 1024


def mm(left, right):
    return lax.dot_general(
        left, right, (((1,), (0,)), ((), ())), preferred_element_type=jnp.float32
    )


def mm_nt(left, right):
    return lax.dot_general(
        left, right, (((1,), (1,)), ((), ())), preferred_element_type=jnp.float32
    )


def mm_tn(left, right):
    return lax.dot_general(
        left, right, (((0,), (0,)), ((), ())), preferred_element_type=jnp.float32
    )


def aligned(index, size):
    return pl.ds(pl.multiple_of(index * size, size), size)


def norm_stats(values):
    centre = values - jnp.mean(values, axis=-1, keepdims=True)
    spread = jnp.mean(centre * centre, axis=-1, keepdims=True)
    scale = lax.rsqrt(spread + NORM_EPS)
    return centre * scale, scale


def norm_back(grad_normed, gain_row, xhat, scale):
    weighted = grad_normed * gain_row
    return scale * (
        weighted
        - jnp.mean(weighted, axis=-1, keepdims=True)
        - xhat * jnp.mean(weighted * xhat, axis=-1, keepdims=True)
    )


def column_sums(values):
    return jnp.sum(values, axis=0, keepdims=True)


def shape_of(dims, dtype):
    return jax.ShapeDtypeStruct(dims, dtype)


def local_call(kernel, name, outs, args, scalars=0, scratch=(), flops=0):
    moved = sum(math.prod(a.shape) * a.dtype.itemsize for a in tuple(args) + tuple(outs))
    return pl.pallas_call(
        kernel,
        out_shape=tuple(outs),
        in_specs=[pl.BlockSpec(memory_space=pltpu.SMEM)] * scalars
        + [pl.BlockSpec(memory_space=pltpu.VMEM)] * (len(args) - scalars),
        out_specs=tuple(pl.BlockSpec(memory_space=pltpu.VMEM) for _ in outs),
        scratch_shapes=list(scratch),
        compiler_params=pltpu.CompilerParams(vmem_limit_bytes=VMEM_BYTES),
        cost_estimate=pl.CostEstimate(flops=flops, bytes_accessed=moved, transcendentals=0),
        name=name,
    )(*args)


def place_of_block(pair_ref, info_ref, ranks, step, half, other_core):
    core = jnp.bitwise_xor(info_ref[2], other_core)
    rank = 2 * jnp.bitwise_xor(info_ref[1], step) + core
    pair = pair_ref[rank]
    return pair if half == 0 else 2 * ranks - 1 - pair


def fill_mask(bias_ref, pair_ref, info_ref, ranks, parts, block):
    rows = 2 * parts * block
    lanes = lax.broadcasted_iota(jnp.int32, (1, rows), 1)
    query_place = lanes % block
    for step in range(parts):
        for half in range(2):
            place = place_of_block(pair_ref, info_ref, ranks, step, half, 0)
            query_place = query_place + jnp.where(
                lanes // block == 2 * step + half, place * block, 0
            )
    ahead = lax.broadcasted_iota(jnp.int32, (block, rows), 0) - query_place
    for other in range(2):
        for step in range(parts):
            for half in range(2):
                place = place_of_block(pair_ref, info_ref, ranks, step, half, other)
                start = other * rows + (2 * step + half) * block
                bias_ref[start : start + block, :] = jnp.where(
                    ahead <= -place * block, 0.0, NEG_BIG
                )


def head_parallel(ranks, chips, seq_parts):
    parts = chips
    hw = HEADS // chips * HEAD_DIM

    def core_swap(member):
        return lax.ppermute(member, "ctx", [(i, i ^ 1) for i in range(ranks)])

    def chip_swap(member, step):
        return lax.ppermute(
            member, "ctx", [(i, 2 * ((i // 2) ^ step) + i % 2) for i in range(ranks)]
        )

    def seq_swap(member, step):
        return lax.ppermute(member, "dp", [(i, i ^ step) for i in range(seq_parts)])

    def per_device_heads(
        tokens,
        pair_of_rank,
        first_gain,
        first_shift,
        w_input,
        query_bias,
        value_bias,
        w_output,
        output_bias,
        second_gain,
        second_shift,
        w_expand,
        expand_bias,
        w_contract,
        contract_bias,
        cotangent,
    ):
        bf, f32 = jnp.bfloat16, jnp.float32
        rows, width = tokens.shape[1:]
        block = rows // 2
        own_width = width // seq_parts
        ff = expand_bias.shape[0]
        total = parts * rows
        half_width = width // 2
        half_ff = ff // 2
        sub = own_width // parts
        half_own = own_width // 2
        small_rows = 16
        others = range(1, parts)
        seq_id = lax.axis_index("dp")
        rank = lax.axis_index("ctx")
        chip = rank // 2
        core = rank % 2
        info = jnp.stack([seq_id, chip, core]).astype(jnp.int32)

        own_tokens = tokens[0]
        token_parts = [own_tokens] + [chip_swap(own_tokens, k) for k in others]
        small_own = jnp.stack(
            [
                first_gain,
                first_shift,
                query_bias,
                value_bias,
                output_bias,
                second_gain,
                second_shift,
                contract_bias,
            ]
        )
        small_own = jnp.pad(small_own, ((0, small_rows - 8), (0, 3 * hw - own_width)))
        w_heads = jnp.concatenate(
            [
                lax.dynamic_slice(w_input, (0, base * width + chip * hw), (own_width, hw))
                for base in range(3)
            ],
            axis=1,
        )
        packed = jnp.concatenate([w_heads, small_own], axis=0)
        packed_parts = [packed] + [seq_swap(packed, j) for j in others]
        out_parts = [w_output] + [seq_swap(w_output, j) for j in others]
        expand_own = [
            lax.dynamic_slice(w_expand, (0, jnp.bitwise_xor(seq_id, j) * ff), (own_width, ff))
            for j in range(seq_parts)
        ]
        expand_parts = [expand_own[0]] + [seq_swap(expand_own[j], j) for j in others]
        own_cot = cotangent[0]
        cot_parts = [own_cot] + [seq_swap(own_cot, j) for j in others]

        def qkv_kernel(info_ref, *refs):
            toks, packs = refs[:parts], refs[parts : 2 * parts]
            q_ref, kv_ref, normed_ref, w_ref, vec_ref, vec_scr = refs[2 * parts :]
            for j in range(parts):
                place = jnp.bitwise_xor(info_ref[0], j)
                w_ref[aligned(place, own_width), :] = packs[j][0:own_width, :]
                vec_scr[place] = packs[j][own_width : own_width + small_rows, 0:own_width].astype(
                    f32
                )
            vectors = jnp.concatenate([vec_scr[j] for j in range(parts)], axis=1)
            vec_ref[...] = vectors
            chosen = vec_scr[info_ref[1]]
            for k in range(parts):
                xhat, _ = norm_stats(toks[k][...].astype(f32))
                normed_ref[k * rows : (k + 1) * rows, :] = (
                    xhat * vectors[0:1] + vectors[1:2]
                ).astype(bf)
            mixed = mm(normed_ref[...], w_ref[...])
            q_ref[...] = (mixed[:, 0:hw] + chosen[2:3]).astype(bf)
            kv_ref[:, 0:hw] = mixed[:, hw : 2 * hw].astype(bf)
            kv_ref[:, hw : 2 * hw] = (mixed[:, 2 * hw :] + chosen[3:4]).astype(bf)

        query, own_kv, normed, w_heads_full, vectors = local_call(
            qkv_kernel,
            "project",
            [
                shape_of((total, hw), bf),
                shape_of((total, 2 * hw), bf),
                shape_of((total, width), bf),
                shape_of((width, 3 * hw), bf),
                shape_of((small_rows, width), f32),
            ],
            [info] + token_parts + packed_parts,
            scalars=1,
            scratch=[pltpu.VMEM((parts, small_rows, own_width), f32)],
            flops=2 * total * width * 3 * hw,
        )
        far_kv = core_swap(own_kv)

        head_count = hw // HEAD_DIM
        scale = HEAD_DIM ** (-0.5)

        def head_columns(ref, base, head):
            start = base + head * HEAD_DIM
            return ref[:, start : start + HEAD_DIM]

        def attend_kernel(info_ref, pair_ref, q_ref, kv_ref, far_ref, *refs):
            outs = refs[:parts]
            flat_ref, lse_ref, bias_ref = refs[parts:]
            fill_mask(bias_ref, pair_ref, info_ref, ranks, parts, block)
            columns = []
            for head in range(head_count):
                keys = jnp.concatenate(
                    [head_columns(kv_ref, 0, head), head_columns(far_ref, 0, head)], axis=0
                )
                values = jnp.concatenate(
                    [head_columns(kv_ref, hw, head), head_columns(far_ref, hw, head)], axis=0
                )
                scores = mm_nt(keys, head_columns(q_ref, 0, head)) * scale + bias_ref[...]
                peak = jnp.max(scores, axis=0, keepdims=True)
                weights = jnp.exp(scores - peak)
                mass = jnp.sum(weights, axis=0, keepdims=True)
                lse_ref[head : head + 1, :] = peak + jnp.log(mass)
                mixed = mm_tn(values, weights.astype(bf)) / mass
                flat_ref[head * HEAD_DIM : (head + 1) * HEAD_DIM, :] = mixed
            attended = flat_ref[...].T.astype(bf)
            for k in range(parts):
                outs[k][...] = attended[k * rows : (k + 1) * rows]

        attend_out = local_call(
            attend_kernel,
            "attend",
            [shape_of((rows, hw), bf)] * parts
            + [shape_of((hw, total), f32), shape_of((8, total), f32)],
            [info, pair_of_rank, query, own_kv, far_kv],
            scalars=2,
            scratch=[pltpu.VMEM((2 * total, total), f32)],
            flops=2 * 2 * head_count * 2 * total * total * HEAD_DIM,
        )
        flat_attended, row_lse = attend_out[parts:]
        att_parts = [attend_out[0]] + [chip_swap(attend_out[k], k) for k in others]

        def middle_kernel(info_ref, tok_ref, vec_ref, *refs):
            atts, outs = refs[:parts], refs[parts : 2 * parts]
            mid_ref, normed_ref, w_scr = refs[2 * parts :]
            for j in range(parts):
                w_scr[jnp.bitwise_xor(info_ref[0], j)] = outs[j][...]
            middle = tok_ref[...].astype(f32) + vec_ref[4:5]
            for k in range(parts):
                middle = middle + mm(atts[k][...], w_scr[jnp.bitwise_xor(info_ref[1], k)])
            mid_ref[...] = middle
            xhat, _ = norm_stats(middle)
            normed_ref[...] = (xhat * vec_ref[5:6] + vec_ref[6:7]).astype(bf)

        middle, own_normed_two = local_call(
            middle_kernel,
            "middle",
            [shape_of((rows, width), f32), shape_of((rows, width), bf)],
            [info, own_tokens, vectors] + att_parts + out_parts,
            scalars=1,
            scratch=[pltpu.VMEM((parts, own_width, width), bf)],
            flops=2 * rows * width * width,
        )
        n2_parts = [own_normed_two] + [seq_swap(own_normed_two, j) for j in others]

        def ffn_kernel(info_ref, bias_ref, wc_ref, *refs):
            n2s = refs[:parts]
            wes = refs[parts : 2 * parts]
            cots = refs[2 * parts : 3 * parts]
            gns = refs[3 * parts : 4 * parts]
            active_ref, gh_ref, n2_ref, cot_ref, w_scr = refs[4 * parts :]
            for j in range(parts):
                w_scr[aligned(jnp.bitwise_xor(info_ref[0], j), own_width), :] = wes[j][...]
                n2_ref[j * rows : (j + 1) * rows, :] = n2s[j][...]
                cot_ref[j * rows : (j + 1) * rows, :] = cots[j][...]
            hidden = mm(n2_ref[...], w_scr[...]) + bias_ref[...].astype(f32)
            square = hidden * hidden
            curve = jnp.tanh(GELU_SCALE * hidden * (1.0 + GELU_CUBIC * square))
            active_ref[...] = (0.5 * hidden * (1.0 + curve)).astype(bf)
            slope = 0.5 * (1.0 + curve) + 0.5 * hidden * (1.0 - curve * curve) * GELU_SCALE * (
                1.0 + 3.0 * GELU_CUBIC * square
            )
            gh_ref[...] = (mm_nt(cot_ref[...], wc_ref[...]) * slope).astype(bf)
            grad = mm_nt(gh_ref[...], w_scr[...]).astype(bf)
            for j in range(parts):
                gns[j][...] = grad[j * rows : (j + 1) * rows]

        ffn_out = local_call(
            ffn_kernel,
            "feed",
            [shape_of((rows, width), bf)] * parts
            + [
                shape_of((total, ff), bf),
                shape_of((total, ff), bf),
                shape_of((total, width), bf),
                shape_of((total, width), bf),
            ],
            [info, expand_bias.reshape(1, ff), w_contract] + n2_parts + expand_parts + cot_parts,
            scalars=1,
            scratch=[pltpu.VMEM((width, ff), bf)],
            flops=3 * 2 * total * width * ff,
        )
        active, grad_hidden, n2_all, cot_all = ffn_out[parts:]
        gn_parts = [ffn_out[0]] + [seq_swap(ffn_out[j], j) for j in others]

        def ffn_weights_kernel(info_ref, active_ref, gh_ref, n2_ref, cot_ref, wc_ref, *refs):
            results = refs[:parts]
            keep_ref, send_ref, bias_ref, scr = refs[parts:]
            result = mm(active_ref[...], wc_ref[...]).astype(bf)
            for j in range(parts):
                results[j][...] = result[j * rows : (j + 1) * rows]
            bias_ref[...] = column_sums(gh_ref[...].astype(f32))
            core_id = info_ref[2]
            for flip, out_ref in ((0, keep_ref), (1, send_ref)):
                half = jnp.bitwise_xor(core_id, flip)
                scr[...] = mm_tn(active_ref[...], cot_ref[:, aligned(half, half_width)]).astype(bf)
                for part in range(parts):
                    span = ff // parts
                    out_ref[part, 0:span, :] = scr[part * span : (part + 1) * span, :]
            for flip, out_ref in ((0, keep_ref), (1, send_ref)):
                half = jnp.bitwise_xor(core_id, flip)
                scr[...] = mm_tn(n2_ref[...], gh_ref[:, aligned(half, half_ff)]).astype(bf)
                for part in range(parts):
                    for j in range(seq_parts):
                        at = ff // parts + j * sub
                        row = j * own_width + part * sub
                        out_ref[part, at : at + sub, :] = scr[row : row + sub, :]

        span = ff // parts + own_width
        fw_out = local_call(
            ffn_weights_kernel,
            "feed_weights",
            [shape_of((rows, width), bf)] * parts
            + [
                shape_of((parts, span, half_width), bf),
                shape_of((parts, span, half_width), bf),
                shape_of((1, ff), f32),
            ],
            [info, active, grad_hidden, n2_all, cot_all, w_contract],
            scalars=1,
            scratch=[pltpu.VMEM((width, half_width), bf)],
            flops=3 * 2 * total * width * ff,
        )
        ffn_keep, ffn_send, grad_expand_row = fw_out[parts:]
        res_parts = [fw_out[0]] + [seq_swap(fw_out[j], j) for j in others]
        ffn_far = core_swap(ffn_send)

        def pick_kernel(info_ref, keep_ref, far_ref, *outs):
            for k in range(parts):
                at = jnp.bitwise_xor(info_ref[1], k)
                outs[k][...] = (keep_ref[at].astype(f32) + far_ref[at].astype(f32)).astype(bf)

        ffn_chunks = local_call(
            pick_kernel,
            "feed_chunks",
            [shape_of((span, half_width), bf)] * parts,
            [info, ffn_keep, ffn_far],
            scalars=1,
        )
        ffn_parts = [ffn_chunks[0]] + [chip_swap(ffn_chunks[k], k) for k in others]

        def back_kernel(info_ref, mid_ref, vec_ref, cot_ref, *refs):
            gns, outs = refs[:parts], refs[parts : 2 * parts]
            douts = refs[2 * parts : 3 * parts]
            gmid_ref, branch_ref, sums_ref, w_scr = refs[3 * parts :]
            for j in range(parts):
                w_scr[jnp.bitwise_xor(info_ref[0], j)] = outs[j][...]
            grad = gns[0][...].astype(f32)
            for j in others:
                grad = grad + gns[j][...].astype(f32)
            xhat, spread = norm_stats(mid_ref[...])
            cot = cot_ref[...].astype(f32)
            grad_middle = cot + norm_back(grad, vec_ref[5:6], xhat, spread)
            gmid_ref[...] = grad_middle
            branch = grad_middle.astype(bf)
            branch_ref[...] = branch
            for k in range(parts):
                douts[k][...] = mm_nt(branch, w_scr[jnp.bitwise_xor(info_ref[1], k)]).astype(bf)
            sums_ref[0:1, :] = column_sums(branch.astype(f32))
            sums_ref[1:2, :] = column_sums(grad * xhat)
            sums_ref[2:3, :] = column_sums(grad)
            sums_ref[3:4, :] = column_sums(cot)

        back_out = local_call(
            back_kernel,
            "middle_back",
            [shape_of((rows, hw), bf)] * parts
            + [
                shape_of((rows, width), f32),
                shape_of((rows, width), bf),
                shape_of((8, width), f32),
            ],
            [info, middle, vectors, own_cot] + gn_parts + out_parts,
            scalars=1,
            scratch=[pltpu.VMEM((parts, own_width, width), bf)],
            flops=2 * rows * width * width,
        )
        grad_middle, grad_branch, late_sums = back_out[parts:]
        dout_parts = [back_out[0]] + [chip_swap(back_out[k], k) for k in others]

        def out_weights_kernel(info_ref, branch_ref, *refs):
            atts = refs[:parts]
            keep_ref, send_ref = refs[parts:]
            for flip, out_ref in ((0, keep_ref), (1, send_ref)):
                half = jnp.bitwise_xor(info_ref[2], flip)
                piece = branch_ref[:, aligned(half, half_width)]
                for k in range(parts):
                    out_ref[jnp.bitwise_xor(info_ref[1], k)] = mm_tn(atts[k][...], piece).astype(bf)

        out_keep, out_send = local_call(
            out_weights_kernel,
            "output_weights",
            [shape_of((parts, hw, half_width), bf)] * 2,
            [info, grad_branch] + att_parts,
            scalars=1,
            flops=2 * rows * width * width,
        )
        out_far = core_swap(out_send)

        def attend_back_kernel(info_ref, pair_ref, q_ref, kv_ref, far_ref, flat_ref, lse_ref, *refs):
            douts = refs[:parts]
            dq_ref, own_ref, send_ref, bias_ref, dout_ref = refs[parts:]
            fill_mask(bias_ref, pair_ref, info_ref, ranks, parts, block)
            for k in range(parts):
                dout_ref[k * rows : (k + 1) * rows, :] = douts[k][...].astype(f32)
            flat_dout = dout_ref[...].T
            for head in range(head_count):
                at = slice(head * HEAD_DIM, (head + 1) * HEAD_DIM)
                keys = jnp.concatenate(
                    [head_columns(kv_ref, 0, head), head_columns(far_ref, 0, head)], axis=0
                )
                values = jnp.concatenate(
                    [head_columns(kv_ref, hw, head), head_columns(far_ref, hw, head)], axis=0
                )
                queries = head_columns(q_ref, 0, head)
                dout = dout_ref[:, at].astype(bf)
                dout_turned = flat_dout[at, :]
                delta = column_sums(dout_turned * flat_ref[at, :])
                scores = mm_nt(keys, queries) * scale + bias_ref[...]
                probs = jnp.exp(scores - lse_ref[head : head + 1, :])
                grad_value = mm(probs.astype(bf), dout)
                grad_weights = mm(values, dout_turned.astype(bf))
                grad_scores = (probs * (grad_weights - delta)).astype(bf)
                grad_key = mm(grad_scores, queries) * scale
                dq_ref[at, :] = mm_tn(keys, grad_scores) * scale
                vat = slice(hw + head * HEAD_DIM, hw + (head + 1) * HEAD_DIM)
                own_ref[:, at] = grad_key[0:total]
                own_ref[:, vat] = grad_value[0:total]
                send_ref[:, at] = grad_key[total:].astype(bf)
                send_ref[:, vat] = grad_value[total:].astype(bf)

        flat_dq, dkv_own, dkv_send = local_call(
            attend_back_kernel,
            "attend_back",
            [
                shape_of((hw, total), f32),
                shape_of((total, 2 * hw), f32),
                shape_of((total, 2 * hw), bf),
            ],
            [info, pair_of_rank, query, own_kv, far_kv, flat_attended, row_lse] + dout_parts,
            scalars=2,
            scratch=[pltpu.VMEM((2 * total, total), f32), pltpu.VMEM((total, hw), f32)],
            flops=5 * 2 * head_count * 2 * total * total * HEAD_DIM,
        )
        dkv_far = core_swap(dkv_send)

        def normed_back_kernel(dq_ref, own_ref, far_ref, w_ref, *refs):
            toks = refs[:parts]
            chunks = refs[parts : 2 * parts]
            mixed_ref, sums_ref, bias_ref = refs[2 * parts :]
            mixed_ref[:, 0:hw] = dq_ref[...].T.astype(bf)
            mixed_ref[:, hw:] = (own_ref[...] + far_ref[...].astype(f32)).astype(bf)
            shift_sum = jnp.zeros((1, width), f32)
            gain_sum = jnp.zeros((1, width), f32)
            for k in range(parts):
                grad = mm_nt(mixed_ref[k * rows : (k + 1) * rows, :], w_ref[...])
                chunks[k][...] = grad.astype(bf)
                xhat, _ = norm_stats(toks[k][...].astype(f32))
                shift_sum = shift_sum + column_sums(grad)
                gain_sum = gain_sum + column_sums(grad * xhat)
            sums_ref[0:1, :] = gain_sum
            sums_ref[1:2, :] = shift_sum
            bias_ref[0:1, :] = column_sums(mixed_ref[...].astype(f32))

        nb_out = local_call(
            normed_back_kernel,
            "normed_back",
            [shape_of((rows, width), bf)] * parts
            + [
                shape_of((total, 3 * hw), bf),
                shape_of((8, width), f32),
                shape_of((8, 3 * hw), f32),
            ],
            [flat_dq, dkv_own, dkv_far, w_heads_full] + token_parts,
            flops=2 * total * width * 3 * hw,
        )
        grad_mixed, first_sums, mixed_sums = nb_out[parts:]
        gt_parts = [nb_out[0]] + [chip_swap(nb_out[k], k) for k in others]

        tall = half_own + small_rows

        def input_weights_kernel(
            info_ref, normed_ref, mixed_ref, first_ref, bias_ref, late_ref, row_ref, *refs
        ):
            keep_ref, send_ref, grad_scr, small_scr = refs
            grad_scr[...] = mm_tn(normed_ref[...], mixed_ref[...])
            core_id, chip_id, seq = info_ref[2], info_ref[1], info_ref[0]
            small_scr[...] = jnp.zeros_like(small_scr)
            for j in range(seq_parts):
                at = slice(j * own_width, (j + 1) * own_width)
                small_scr[j, 0:2, 0:own_width] = first_ref[0:2, at]
                small_scr[j, 4:8, 0:own_width] = late_ref[0:4, at]
            small_scr[chip_id, 2:3, 0:hw] = bias_ref[0:1, 0:hw]
            small_scr[chip_id, 3:4, 0:hw] = bias_ref[0:1, 2 * hw : 3 * hw]
            for j in range(ff // own_width):
                small_scr[seq, 8 + j : 9 + j, 0:own_width] = row_ref[
                    :, j * own_width : (j + 1) * own_width
                ]
            for flip, out_ref in ((0, keep_ref), (1, send_ref)):
                half = jnp.bitwise_xor(core_id, flip)
                for j in range(seq_parts):
                    start = pl.multiple_of(j * own_width + half * half_own, 16)
                    out_ref[j, 0:half_own, :] = grad_scr[pl.ds(start, half_own), :].astype(bf)
                    out_ref[j, half_own:tall, :] = small_scr[j].astype(bf)

        in_keep, in_send = local_call(
            input_weights_kernel,
            "input_weights",
            [shape_of((seq_parts, tall, 3 * hw), bf)] * 2,
            [info, normed, grad_mixed, first_sums, mixed_sums, late_sums, grad_expand_row],
            scalars=1,
            scratch=[
                pltpu.VMEM((width, 3 * hw), f32),
                pltpu.VMEM((seq_parts, small_rows, 3 * hw), f32),
            ],
            flops=2 * total * width * 3 * hw,
        )
        in_far = core_swap(in_send)

        def owner_kernel(info_ref, keep_ref, far_ref, *refs):
            ffns = refs[:parts]
            con_ref = refs[parts]
            outs = refs[parts + 1 :]
            whole = ffns[0][...].astype(f32)
            for k in others:
                whole = whole + ffns[k][...].astype(f32)
            con_ref[...] = whole.astype(bf)
            for j in range(seq_parts):
                to = jnp.bitwise_xor(info_ref[0], j)
                start = pl.multiple_of(ff // parts + to * sub, 16)
                outs[j][0:sub, :] = con_ref[pl.ds(start, sub), :]
                outs[j][sub:, :] = (
                    keep_ref[to].astype(f32) + far_ref[to].astype(f32)
                ).astype(bf)

        ow_out = local_call(
            owner_kernel,
            "owners",
            [shape_of((span, half_width), bf)]
            + [shape_of((sub + own_width, half_width), bf)] * seq_parts,
            [info, out_keep, out_far] + ffn_parts,
            scalars=1,
        )
        ffn_whole = ow_out[0]
        ow_parts = [ow_out[1]] + [seq_swap(ow_out[1 + j], j) for j in others]

        gather_rows = span + sub

        def share_kernel(info_ref, whole_ref, *refs):
            owned = refs[:seq_parts]
            outs = refs[seq_parts : seq_parts + parts]
            (scr,) = refs[seq_parts + parts :]
            rows_out = owned[0][sub:, :].astype(f32)
            for j in others:
                rows_out = rows_out + owned[j][sub:, :].astype(f32)
            scr[...] = rows_out.astype(bf)
            for k in range(parts):
                out_ref = outs[k]
                out_ref[0 : ff // parts, :] = whole_ref[0 : ff // parts, :]
                for j in range(seq_parts):
                    start = pl.multiple_of(
                        ff // parts + jnp.bitwise_xor(info_ref[0], j) * sub, 16
                    )
                    out_ref[pl.ds(start, sub), :] = owned[j][0:sub, :]
                to = pl.multiple_of(jnp.bitwise_xor(info_ref[1], k) * sub, 16)
                out_ref[span:, :] = scr[pl.ds(to, sub), :]

        sh_out = local_call(
            share_kernel,
            "shares",
            [shape_of((gather_rows, half_width), bf)] * parts,
            [info, ffn_whole] + ow_parts,
            scalars=1,
            scratch=[pltpu.VMEM((own_width, half_width), bf)],
        )
        sh_parts = [sh_out[0]] + [chip_swap(sh_out[k], k) for k in others]
        sh_far = [core_swap(member) for member in sh_parts]

        def ffn_final_kernel(info_ref, *refs):
            own, far = refs[:parts], refs[parts : 2 * parts]
            con_ref, exp_ref = refs[2 * parts :]
            for flip, members in ((0, own), (1, far)):
                half = jnp.bitwise_xor(info_ref[2], flip)
                lanes = aligned(half, half_width)
                for k in range(parts):
                    at = jnp.bitwise_xor(info_ref[1], k)
                    con_ref[aligned(at, ff // parts), lanes] = members[k][
                        0 : ff // parts, :
                    ].astype(f32)
                    for j in range(seq_parts):
                        start = ff // parts + j * sub
                        cols = pl.ds(pl.multiple_of(j * ff + half * half_ff, 128), half_ff)
                        exp_ref[aligned(at, sub), cols] = members[k][
                            start : start + sub, :
                        ].astype(f32)

        grad_contract, grad_expand = local_call(
            ffn_final_kernel,
            "feed_final",
            [shape_of((ff, width), f32), shape_of((own_width, seq_parts * ff), f32)],
            [info] + sh_parts + sh_far,
            scalars=1,
        )

        def in_pick_kernel(info_ref, keep_ref, far_ref, *outs):
            for j in range(seq_parts):
                at = jnp.bitwise_xor(info_ref[0], j)
                outs[j][...] = (keep_ref[at].astype(f32) + far_ref[at].astype(f32)).astype(bf)

        in_chunks = local_call(
            in_pick_kernel,
            "input_chunks",
            [shape_of((tall, 3 * hw), bf)] * seq_parts,
            [info, in_keep, in_far],
            scalars=1,
        )
        in_parts = [in_chunks[0]] + [seq_swap(in_chunks[j], j) for j in others]

        def in_sum_kernel(*refs):
            owned, shared = refs[:seq_parts], refs[seq_parts : seq_parts + parts]
            (out_ref,) = refs[seq_parts + parts :]
            whole = owned[0][...].astype(f32)
            for j in others:
                whole = whole + owned[j][...].astype(f32)
            out_ref[0:tall, :] = whole.astype(bf)
            rows_out = shared[0][span:, :].astype(f32)
            for k in others:
                rows_out = rows_out + shared[k][span:, :].astype(f32)
            out_ref[tall:, 0:half_width] = rows_out.astype(bf)
            out_ref[tall:, half_width:] = jnp.zeros((sub, 3 * hw - half_width), bf)

        (in_whole,) = local_call(
            in_sum_kernel,
            "input_sum",
            [shape_of((tall + sub, 3 * hw), bf)],
            in_parts + sh_parts,
        )
        last_parts = [in_whole] + [chip_swap(in_whole, k) for k in others]
        last_far = [core_swap(member) for member in last_parts]

        def last_kernel(info_ref, *refs):
            own, far = refs[:parts], refs[parts : 2 * parts]
            gin_ref, gout_ref, small_ref, scr = refs[2 * parts :]
            for flip, members in ((0, own), (1, far)):
                half = jnp.bitwise_xor(info_ref[2], flip)
                for k in range(parts):
                    at = jnp.bitwise_xor(info_ref[1], k)
                    scr[at, aligned(half, half_own), :] = members[k][0:half_own, :].astype(f32)
                    gout_ref[aligned(at, sub), aligned(half, half_width)] = members[k][
                        tall:, 0:half_width
                    ].astype(f32)
            for at in range(parts):
                for base in range(3):
                    start = base * width + at * hw
                    gin_ref[:, start : start + hw] = scr[at, :, base * hw : (base + 1) * hw]
            small = own[0][half_own:tall, 0:own_width].astype(f32)
            for k in others:
                small = small + own[k][half_own:tall, 0:own_width].astype(f32)
            small_ref[...] = small

        grad_input, grad_output, small_sums = local_call(
            last_kernel,
            "weights_final",
            [
                shape_of((own_width, 3 * width), f32),
                shape_of((own_width, width), f32),
                shape_of((small_rows, own_width), f32),
            ],
            [info] + last_parts + last_far,
            scalars=1,
            scratch=[pltpu.VMEM((parts, own_width, 3 * hw), f32)],
        )

        def out_kernel(mid_ref, vec_ref, *refs):
            result = mid_ref[...] + vec_ref[7:8]
            for j in range(seq_parts):
                result = result + refs[j][...].astype(f32)
            refs[seq_parts][0] = result.astype(bf)

        (block_out,) = local_call(
            out_kernel,
            "result",
            [shape_of((1, rows, width), bf)],
            [middle, vectors] + res_parts,
        )

        def tokens_kernel(tok_ref, vec_ref, gmid_ref, *refs):
            grad = refs[0][...].astype(f32)
            for k in others:
                grad = grad + refs[k][...].astype(f32)
            xhat, spread = norm_stats(tok_ref[...].astype(f32))
            refs[parts][0] = gmid_ref[...] + norm_back(grad, vec_ref[0:1], xhat, spread)

        (grad_tokens,) = local_call(
            tokens_kernel,
            "tokens_back",
            [shape_of((1, rows, width), f32)],
            [own_tokens, vectors, grad_middle] + gt_parts,
        )
        small_of = [small_sums[i] for i in range(8)]
        grad_expand_bias = small_sums[8 : 8 + ff // own_width].reshape(ff)
        return (
            block_out,
            grad_tokens,
            small_of[0],
            small_of[1],
            grad_input,
            small_of[2],
            small_of[3],
            grad_output,
            small_of[4],
            small_of[5],
            small_of[6],
            grad_expand,
            grad_expand_bias,
            grad_contract,
            small_of[7],
        )

    return per_device_heads


def solution(mesh):
    ranks = mesh.shape["ctx"]
    chips = ranks // 2
    if chips == mesh.shape["dp"] and HEADS % chips == 0 and chips & (chips - 1) == 0:
        body = head_parallel(ranks, chips, mesh.shape["dp"])
    else:
        body = per_device
    return jax.shard_map(
        body,
        mesh=mesh,
        in_specs=(
            P("dp", "ctx", None),
            P(),
            P("dp"),
            P("dp"),
            P("dp", None),
            P("dp"),
            P("dp"),
            P("dp", None),
            P("dp"),
            P("dp"),
            P("dp"),
            P("dp", None),
            P("dp"),
            P("dp", None),
            P("dp"),
            P("dp", "ctx", None),
        ),
        out_specs=(
            P("dp", "ctx", None),
            P("dp", "ctx", None),
            P("dp"),
            P("dp"),
            P("dp", None),
            P("dp"),
            P("dp"),
            P("dp", None),
            P("dp"),
            P("dp"),
            P("dp"),
            P("dp", None),
            P("dp"),
            P("dp", None),
            P("dp"),
        ),
        check_vma=False,
    )
```

```python
import math

import jax
import jax.numpy as jnp
from jax import lax
from jax.experimental import pallas as pl
from jax.experimental.pallas import tpu as pltpu
from jax.sharding import PartitionSpec as P

HEADS = 12
HEAD_DIM = 64


NEG_BIG = -1e30
NORM_EPS = 1e-05
GELU_SCALE = 0.7978845608028654
GELU_CUBIC = 0.044715


def gelu_tanh(values):
    return (
        0.5
        * values
        * (1.0 + jnp.tanh(GELU_SCALE * (values + GELU_CUBIC * values * values * values)))
    )


def layer_norm(values, gain_row, shift_row):
    centre = values - jnp.mean(values, axis=-1, keepdims=True)
    spread = jnp.mean(centre * centre, axis=-1, keepdims=True)
    return centre * lax.rsqrt(spread + NORM_EPS) * gain_row + shift_row


def lookup_pair(pair_table, positions):
    ranks_all = jnp.arange(pair_table.shape[0], dtype=jnp.int32)
    return jnp.sum(jnp.where(positions[..., None] == ranks_all, pair_table, 0), axis=-1)


def group_count(blocks, sub_rows):
    chosen_count = 1
    for candidate in range(1, blocks + 1):
        if blocks % candidate == 0 and candidate * sub_rows <= max(512, sub_rows):
            chosen_count = candidate
    return chosen_count


def slot_mask(slot_ids, wanted, rank_count):
    return (slot_ids == wanted).reshape((-1,) + (1,) * (rank_count - 1))


def slot_add(values, slot_ids):
    early_sum = jnp.sum(jnp.where(slot_mask(slot_ids, 0, values.ndim), values, 0.0), axis=0)
    late_sum = jnp.sum(jnp.where(slot_mask(slot_ids, 1, values.ndim), values, 0.0), axis=0)
    return jnp.stack([early_sum, late_sum])


def slot_max(values, slot_ids):
    early_max = jnp.max(jnp.where(slot_mask(slot_ids, 0, values.ndim), values, NEG_BIG), axis=0)
    late_max = jnp.max(jnp.where(slot_mask(slot_ids, 1, values.ndim), values, NEG_BIG), axis=0)
    return jnp.stack([early_max, late_max])


def slot_pick(per_slot, slot_ids):
    return jnp.where(slot_mask(slot_ids, 0, per_slot.ndim), per_slot[0][None], per_slot[1][None])


def query_tiles(blocks, chosen):
    target = chosen.shape + blocks.shape[2:]
    chosen_view = chosen.reshape((-1,) + (1,) * (blocks.ndim - 2))
    late_part = jnp.broadcast_to(blocks[1], target)
    picked = jnp.where(chosen_view, blocks[0], blocks[1])
    return jnp.concatenate([late_part, picked], axis=0)


def key_tiles(blocks, chosen):
    target = chosen.shape + blocks.shape[2:]
    chosen_view = chosen.reshape((-1,) + (1,) * (blocks.ndim - 2))
    early_part = jnp.broadcast_to(blocks[0], target)
    picked = jnp.where(chosen_view, blocks[0], blocks[1])
    return jnp.concatenate([early_part, picked], axis=0)


def tile_slots(chosen):
    late_slot = jnp.where(chosen, 0, 1).astype(jnp.int32)
    query_slot = jnp.concatenate([jnp.ones_like(late_slot), late_slot])
    key_slot = jnp.concatenate([jnp.zeros_like(late_slot), late_slot])
    return (query_slot, key_slot)


def tile_mask(is_own, query_places, key_places):
    visible = key_places[:, None, :] <= query_places[:, :, None]
    visible = jnp.logical_or(visible, jnp.logical_not(is_own)[:, None, None])
    return jnp.concatenate([jnp.ones_like(visible), visible], axis=0)


def tile_scores(tile_query, tile_key, score_scale):
    return (
        jnp.einsum("tqhd,tkhd->thqk", tile_query, tile_key, preferred_element_type=jnp.float32)
        * score_scale
    )


def tile_probs(tile_query, tile_key, tile_visible, row_lse, score_scale):
    scores = tile_scores(tile_query, tile_key, score_scale)
    return jnp.where(tile_visible[:, None], jnp.exp(scores - row_lse[..., None]), 0.0)


def tile_dscore(probs, tile_dout, tile_value, row_delta):
    grad_probs = jnp.einsum(
        "tqhd,tkhd->thqk", tile_dout, tile_value, preferred_element_type=jnp.float32
    )
    return (probs * (grad_probs - row_delta[..., None])).astype(jnp.bfloat16)


def stats_update(running, tile_query, tile_key, query_slot, tile_visible, score_scale):
    run_peak, run_total = running
    visible = tile_visible[:, None]
    masked = jnp.where(visible, tile_scores(tile_query, tile_key, score_scale), NEG_BIG)
    new_peak = jnp.maximum(run_peak, slot_max(jnp.max(masked, axis=-1), query_slot))
    weights = jnp.where(visible, jnp.exp(masked - slot_pick(new_peak, query_slot)[..., None]), 0.0)
    run_total = run_total * jnp.exp(run_peak - new_peak) + slot_add(
        jnp.sum(weights, axis=-1), query_slot
    )
    return (new_peak, run_total)


def values_update(
    running, tile_query, tile_key, tile_value, query_slot, tile_visible, row_lse, score_scale
):
    probs = tile_probs(tile_query, tile_key, tile_visible, row_lse, score_scale)
    part_out = jnp.einsum(
        "thqk,tkhd->tqhd",
        probs.astype(jnp.bfloat16),
        tile_value,
        preferred_element_type=jnp.float32,
    )
    return running + slot_add(part_out, query_slot)


def sweep_piece(carried, pieces, block_rows, my_rank, pair_table, update):
    piece_rows = pieces[0].shape[1]
    sub_rows = math.gcd(piece_rows, block_rows)
    unit_count = piece_rows // sub_rows
    group_size = group_count(unit_count, sub_rows)

    def group_step(loop_index, running):
        offset = loop_index * (group_size * sub_rows)
        slices = tuple(
            (
                lax.dynamic_slice_in_dim(member, offset, group_size * sub_rows, 1).reshape(
                    (2, group_size, sub_rows) + member.shape[2:]
                )
                for member in pieces
            )
        )
        places = offset + jnp.arange(group_size * sub_rows, dtype=jnp.int32).reshape(
            group_size, sub_rows
        )
        far_ranks = places[:, 0] // block_rows
        far_pair = lookup_pair(pair_table, far_ranks)
        return update(running, slices, far_pair, far_ranks == my_rank, places % block_rows, offset)

    return lax.fori_loop(0, unit_count // group_size, group_step, carried)


def per_device(
    tokens,
    pair_of_rank,
    first_gain,
    first_shift,
    w_input,
    query_bias,
    value_bias,
    w_output,
    output_bias,
    second_gain,
    second_shift,
    w_expand,
    expand_bias,
    w_contract,
    contract_bias,
    cotangent,
):
    gathered = (
        lax.all_gather(first_gain, "dp", axis=0, tiled=True),
        lax.all_gather(first_shift, "dp", axis=0, tiled=True),
        lax.all_gather(w_input, "dp", axis=0, tiled=True),
        lax.all_gather(query_bias, "dp", axis=0, tiled=True),
        lax.all_gather(value_bias, "dp", axis=0, tiled=True),
        lax.all_gather(w_output, "dp", axis=0, tiled=True),
        lax.all_gather(output_bias, "dp", axis=0, tiled=True),
        lax.all_gather(second_gain, "dp", axis=0, tiled=True),
        lax.all_gather(second_shift, "dp", axis=0, tiled=True),
        lax.all_gather(w_expand, "dp", axis=0, tiled=True),
        lax.all_gather(expand_bias, "dp", axis=0, tiled=True),
        lax.all_gather(w_contract, "dp", axis=0, tiled=True),
        lax.all_gather(contract_bias, "dp", axis=0, tiled=True),
    )
    (
        full_first_gain,
        full_first_shift,
        full_input,
        full_query_bias,
        full_value_bias,
        full_output,
        full_output_bias,
        full_second_gain,
        full_second_shift,
        full_expand,
        full_expand_bias,
        full_contract,
        full_contract_bias,
    ) = gathered
    model_width = tokens.shape[2]
    block_rows = tokens.shape[1] // 2
    score_scale = HEAD_DIM ** (-0.5)
    slot_view = (2, block_rows, model_width)
    head_view = (2, block_rows, HEADS, HEAD_DIM)
    my_rank = lax.axis_index("ctx")
    my_pair = lookup_pair(pair_of_rank, my_rank)
    own_places = jnp.arange(block_rows, dtype=jnp.int32)[None, :]
    diag_mask = (own_places <= own_places.reshape(-1, 1))[None]
    zero_slot = jnp.zeros((1,), jnp.int32)

    def split_heads(member):
        return member.reshape(member.shape[:3] + (HEADS, HEAD_DIM))

    token_rows = tokens[0].astype(jnp.float32)
    normed_full, first_pullback = jax.vjp(
        layer_norm,
        token_rows,
        full_first_gain.astype(jnp.float32),
        full_first_shift.astype(jnp.float32),
    )
    normed = normed_full.astype(jnp.bfloat16)
    mixed_rows = jnp.dot(normed, full_input, preferred_element_type=jnp.float32)
    query_rows = (mixed_rows[:, :model_width] + full_query_bias.astype(jnp.float32)).astype(
        jnp.bfloat16
    )
    key_rows = mixed_rows[:, model_width : 2 * model_width].astype(jnp.bfloat16)
    value_rows = (mixed_rows[:, 2 * model_width :] + full_value_bias.astype(jnp.float32)).astype(
        jnp.bfloat16
    )
    own_query = query_rows.reshape(head_view)
    own_key = key_rows.reshape(head_view)
    own_value = value_rows.reshape(head_view)
    diag_query = own_query[0][None]
    diag_key = own_key[0][None]
    diag_value = own_value[0][None]
    key_slots = key_rows.reshape(slot_view)
    value_slots = value_rows.reshape(slot_view)
    query_slots = query_rows.reshape(slot_view)

    def stats_group(running, slices, far_pair, is_own, far_places, first_row):
        chosen = far_pair < my_pair
        query_slot, key_slot = tile_slots(chosen)
        return stats_update(
            running,
            query_tiles(own_query[:, None], chosen),
            key_tiles(split_heads(slices[0]), chosen),
            query_slot,
            tile_mask(is_own, own_places, far_places),
            score_scale,
        )

    stats_start = (
        jnp.full((2, HEADS, block_rows), NEG_BIG, jnp.float32),
        jnp.zeros((2, HEADS, block_rows), jnp.float32),
    )
    stats_start = stats_update(stats_start, diag_query, diag_key, zero_slot, diag_mask, score_scale)
    run_peak, run_total = sweep_piece(
        stats_start,
        (lax.all_gather(key_slots, "ctx", axis=1, tiled=True),),
        block_rows,
        my_rank,
        pair_of_rank,
        stats_group,
    )
    row_lse = run_peak + jnp.log(run_total)

    def values_group(running, slices, far_pair, is_own, far_places, first_row):
        chosen = far_pair < my_pair
        query_slot, key_slot = tile_slots(chosen)
        return values_update(
            running,
            query_tiles(own_query[:, None], chosen),
            key_tiles(split_heads(slices[0]), chosen),
            key_tiles(split_heads(slices[1]), chosen),
            query_slot,
            tile_mask(is_own, own_places, far_places),
            slot_pick(row_lse, query_slot),
            score_scale,
        )

    values_start = values_update(
        jnp.zeros(head_view, jnp.float32),
        diag_query,
        diag_key,
        diag_value,
        zero_slot,
        diag_mask,
        row_lse[0][None],
        score_scale,
    )
    attended = sweep_piece(
        values_start,
        (
            lax.all_gather(key_slots, "ctx", axis=1, tiled=True),
            lax.all_gather(value_slots, "ctx", axis=1, tiled=True),
        ),
        block_rows,
        my_rank,
        pair_of_rank,
        values_group,
    )
    attended_low = attended.reshape(2 * block_rows, model_width).astype(jnp.bfloat16)
    middle = (
        token_rows
        + jnp.dot(attended_low, full_output, preferred_element_type=jnp.float32)
        + full_output_bias.astype(jnp.float32)
    )
    normed_full_two, second_pullback = jax.vjp(
        layer_norm,
        middle,
        full_second_gain.astype(jnp.float32),
        full_second_shift.astype(jnp.float32),
    )
    normed_two = normed_full_two.astype(jnp.bfloat16)
    hidden = jnp.dot(
        normed_two, full_expand, preferred_element_type=jnp.float32
    ) + full_expand_bias.astype(jnp.float32)
    active_full, gelu_pullback = jax.vjp(gelu_tanh, hidden)
    active_low = active_full.astype(jnp.bfloat16)
    result = (
        middle
        + jnp.dot(active_low, full_contract, preferred_element_type=jnp.float32)
        + full_contract_bias.astype(jnp.float32)
    )
    block_out = result.astype(jnp.bfloat16)[None]
    back_input, back_output, back_expand, back_contract = (
        lax.all_gather(w_input, "dp", axis=0, tiled=True),
        lax.all_gather(w_output, "dp", axis=0, tiled=True),
        lax.all_gather(w_expand, "dp", axis=0, tiled=True),
        lax.all_gather(w_contract, "dp", axis=0, tiled=True),
    )
    grad_out_low = cotangent[0]
    grad_out = grad_out_low.astype(jnp.float32)
    grad_contract = jnp.einsum(
        "rf,rd->fd", active_low, grad_out_low, preferred_element_type=jnp.float32
    )
    grad_contract_bias = jnp.sum(grad_out, axis=0)
    grad_active = jnp.einsum(
        "rd,fd->rf", grad_out_low, back_contract, preferred_element_type=jnp.float32
    )
    grad_hidden = gelu_pullback(grad_active)[0].astype(jnp.bfloat16)
    grad_expand = jnp.einsum(
        "rd,rf->df", normed_two, grad_hidden, preferred_element_type=jnp.float32
    )
    grad_expand_bias = jnp.sum(grad_hidden.astype(jnp.float32), axis=0)
    grad_normed_two = jnp.einsum(
        "rf,df->rd", grad_hidden, back_expand, preferred_element_type=jnp.float32
    )
    grad_middle_part, grad_second_gain, grad_second_shift = second_pullback(grad_normed_two)
    grad_middle = grad_out + grad_middle_part
    grad_branch = grad_middle.astype(jnp.bfloat16)
    grad_output = jnp.einsum(
        "rd,re->de", attended_low, grad_branch, preferred_element_type=jnp.float32
    )
    grad_output_bias = jnp.sum(grad_branch.astype(jnp.float32), axis=0)
    grad_attended = jnp.einsum(
        "re,de->rd", grad_branch, back_output, preferred_element_type=jnp.float32
    ).astype(jnp.bfloat16)
    own_dout = grad_attended.reshape(head_view)
    dout_slots = grad_attended.reshape(slot_view)
    delta_rows = jnp.sum(own_dout.astype(jnp.float32) * attended, axis=-1)
    row_delta = jnp.transpose(delta_rows, (0, 2, 1))
    lse_rows = jnp.transpose(row_lse, (0, 2, 1))
    far_lse, far_delta = (
        lax.all_gather(lse_rows, "ctx", axis=1, tiled=True),
        lax.all_gather(delta_rows, "ctx", axis=1, tiled=True),
    )
    diag_probs = tile_probs(diag_query, diag_key, diag_mask, row_lse[0][None], score_scale)
    diag_dscore = tile_dscore(diag_probs, own_dout[0][None], diag_value, row_delta[0][None])
    query_start = slot_add(
        jnp.einsum("thqk,tkhd->tqhd", diag_dscore, diag_key, preferred_element_type=jnp.float32)
        * score_scale,
        zero_slot,
    )
    key_start = slot_add(
        jnp.einsum("thqk,tqhd->tkhd", diag_dscore, diag_query, preferred_element_type=jnp.float32)
        * score_scale,
        zero_slot,
    )
    value_start = slot_add(
        jnp.einsum(
            "thqk,tqhd->tkhd",
            diag_probs.astype(jnp.bfloat16),
            own_dout[0][None],
            preferred_element_type=jnp.float32,
        ),
        zero_slot,
    )

    def query_grad_group(running, slices, far_pair, is_own, far_places, first_row):
        chosen = far_pair < my_pair
        query_slot, key_slot = tile_slots(chosen)
        tile_key = key_tiles(split_heads(slices[0]), chosen)
        tile_value = key_tiles(split_heads(slices[1]), chosen)
        probs = tile_probs(
            query_tiles(own_query[:, None], chosen),
            tile_key,
            tile_mask(is_own, own_places, far_places),
            slot_pick(row_lse, query_slot),
            score_scale,
        )
        dscore = tile_dscore(
            probs,
            query_tiles(own_dout[:, None], chosen),
            tile_value,
            slot_pick(row_delta, query_slot),
        )
        part_grad = (
            jnp.einsum("thqk,tkhd->tqhd", dscore, tile_key, preferred_element_type=jnp.float32)
            * score_scale
        )
        return running + slot_add(part_grad, query_slot)

    def key_grad_group(running, slices, far_pair, is_own, far_places, first_row):
        chosen = my_pair < far_pair
        query_slot, key_slot = tile_slots(chosen)
        group_size = far_places.shape[0]
        sub_rows = far_places.shape[1]
        tile_query = query_tiles(split_heads(slices[0]), chosen)
        tile_dout = query_tiles(split_heads(slices[1]), chosen)
        lse_part = lax.dynamic_slice_in_dim(far_lse, first_row, group_size * sub_rows, 1).reshape(
            2, group_size, sub_rows, HEADS
        )
        delta_part = lax.dynamic_slice_in_dim(
            far_delta, first_row, group_size * sub_rows, 1
        ).reshape(2, group_size, sub_rows, HEADS)
        tile_lse = jnp.transpose(query_tiles(lse_part, chosen), (0, 2, 1))
        tile_delta = jnp.transpose(query_tiles(delta_part, chosen), (0, 2, 1))
        tile_key = key_tiles(own_key[:, None], chosen)
        tile_value = key_tiles(own_value[:, None], chosen)
        probs = tile_probs(
            tile_query, tile_key, tile_mask(is_own, far_places, own_places), tile_lse, score_scale
        )
        dscore = tile_dscore(probs, tile_dout, tile_value, tile_delta)
        key_part = (
            jnp.einsum("thqk,tqhd->tkhd", dscore, tile_query, preferred_element_type=jnp.float32)
            * score_scale
        )
        value_part = jnp.einsum(
            "thqk,tqhd->tkhd",
            probs.astype(jnp.bfloat16),
            tile_dout,
            preferred_element_type=jnp.float32,
        )
        return (
            running[0] + slot_add(key_part, key_slot),
            running[1] + slot_add(value_part, key_slot),
        )

    grad_query_sum = sweep_piece(
        query_start,
        (
            lax.all_gather(key_slots, "ctx", axis=1, tiled=True),
            lax.all_gather(value_slots, "ctx", axis=1, tiled=True),
        ),
        block_rows,
        my_rank,
        pair_of_rank,
        query_grad_group,
    )
    grad_key_sum, grad_value_sum = sweep_piece(
        (key_start, value_start),
        (
            lax.all_gather(query_slots, "ctx", axis=1, tiled=True),
            lax.all_gather(dout_slots, "ctx", axis=1, tiled=True),
        ),
        block_rows,
        my_rank,
        pair_of_rank,
        key_grad_group,
    )
    flat_rows = 2 * block_rows
    grad_query_low = grad_query_sum.reshape(flat_rows, model_width).astype(jnp.bfloat16)
    grad_key_low = grad_key_sum.reshape(flat_rows, model_width).astype(jnp.bfloat16)
    grad_value_low = grad_value_sum.reshape(flat_rows, model_width).astype(jnp.bfloat16)
    grad_mixed = jnp.concatenate([grad_query_low, grad_key_low, grad_value_low], axis=1)
    grad_input = jnp.einsum("rd,re->de", normed, grad_mixed, preferred_element_type=jnp.float32)
    grad_query_bias = jnp.sum(grad_query_low.astype(jnp.float32), axis=0)
    grad_value_bias = jnp.sum(grad_value_low.astype(jnp.float32), axis=0)
    grad_normed = jnp.einsum(
        "re,de->rd", grad_mixed, back_input, preferred_element_type=jnp.float32
    )
    grad_token_part, grad_first_gain, grad_first_shift = first_pullback(grad_normed)
    grad_tokens = (grad_middle + grad_token_part)[None]
    grad_local = (
        grad_first_gain,
        grad_first_shift,
        grad_input,
        grad_query_bias,
        grad_value_bias,
        grad_output,
        grad_output_bias,
        grad_second_gain,
        grad_second_shift,
        grad_expand,
        grad_expand_bias,
        grad_contract,
        grad_contract_bias,
    )
    grad_owned = (
        lax.psum_scatter(
            grad_local[0].astype(jnp.bfloat16), "dp", scatter_dimension=0, tiled=True
        ).astype(jnp.float32),
        lax.psum_scatter(
            grad_local[1].astype(jnp.bfloat16), "dp", scatter_dimension=0, tiled=True
        ).astype(jnp.float32),
        lax.psum_scatter(
            grad_local[2].astype(jnp.bfloat16), "dp", scatter_dimension=0, tiled=True
        ).astype(jnp.float32),
        lax.psum_scatter(
            grad_local[3].astype(jnp.bfloat16), "dp", scatter_dimension=0, tiled=True
        ).astype(jnp.float32),
        lax.psum_scatter(
            grad_local[4].astype(jnp.bfloat16), "dp", scatter_dimension=0, tiled=True
        ).astype(jnp.float32),
        lax.psum_scatter(
            grad_local[5].astype(jnp.bfloat16), "dp", scatter_dimension=0, tiled=True
        ).astype(jnp.float32),
        lax.psum_scatter(
            grad_local[6].astype(jnp.bfloat16), "dp", scatter_dimension=0, tiled=True
        ).astype(jnp.float32),
        lax.psum_scatter(
            grad_local[7].astype(jnp.bfloat16), "dp", scatter_dimension=0, tiled=True
        ).astype(jnp.float32),
        lax.psum_scatter(
            grad_local[8].astype(jnp.bfloat16), "dp", scatter_dimension=0, tiled=True
        ).astype(jnp.float32),
        lax.psum_scatter(
            grad_local[9].astype(jnp.bfloat16), "dp", scatter_dimension=0, tiled=True
        ).astype(jnp.float32),
        lax.psum_scatter(
            grad_local[10].astype(jnp.bfloat16), "dp", scatter_dimension=0, tiled=True
        ).astype(jnp.float32),
        lax.psum_scatter(
            grad_local[11].astype(jnp.bfloat16), "dp", scatter_dimension=0, tiled=True
        ).astype(jnp.float32),
        lax.psum_scatter(
            grad_local[12].astype(jnp.bfloat16), "dp", scatter_dimension=0, tiled=True
        ).astype(jnp.float32),
    )
    grad_final = tuple(
        lax.psum(
            (
                grad_owned[0],
                grad_owned[1],
                grad_owned[2],
                grad_owned[3],
                grad_owned[4],
                grad_owned[5],
                grad_owned[6],
                grad_owned[7],
                grad_owned[8],
                grad_owned[9],
                grad_owned[10],
                grad_owned[11],
                grad_owned[12],
            ),
            "ctx",
        )
    )
    return (block_out, grad_tokens) + tuple(grad_final)


VMEM_BYTES = 28 * 1024 * 1024


def mm(left, right):
    return lax.dot_general(
        left, right, (((1,), (0,)), ((), ())), preferred_element_type=jnp.float32
    )


def mm_nt(left, right):
    return lax.dot_general(
        left, right, (((1,), (1,)), ((), ())), preferred_element_type=jnp.float32
    )


def mm_tn(left, right):
    return lax.dot_general(
        left, right, (((0,), (0,)), ((), ())), preferred_element_type=jnp.float32
    )


def aligned(index, size):
    return pl.ds(pl.multiple_of(index * size, size), size)


def norm_stats(values):
    centre = values - jnp.mean(values, axis=-1, keepdims=True)
    spread = jnp.mean(centre * centre, axis=-1, keepdims=True)
    scale = lax.rsqrt(spread + NORM_EPS)
    return centre * scale, scale


def norm_back(grad_normed, gain_row, xhat, scale):
    weighted = grad_normed * gain_row
    return scale * (
        weighted
        - jnp.mean(weighted, axis=-1, keepdims=True)
        - xhat * jnp.mean(weighted * xhat, axis=-1, keepdims=True)
    )


def column_sums(values):
    return jnp.sum(values, axis=0, keepdims=True)


def shape_of(dims, dtype):
    return jax.ShapeDtypeStruct(dims, dtype)


def local_call(
    kernel, name, outs, args, scalars=0, scratch=(), flops=0, after=(), space=pltpu.VMEM, grant=VMEM_BYTES
):
    moved = sum(math.prod(a.shape) * a.dtype.itemsize for a in tuple(args) + tuple(outs))

    def ordered(*refs):
        kernel(*refs[: len(args)], *refs[len(args) + len(after) :])

    return pl.pallas_call(
        ordered,
        out_shape=tuple(outs),
        in_specs=[pl.BlockSpec(memory_space=pltpu.SMEM)] * scalars
        + [pl.BlockSpec(memory_space=space)] * (len(args) - scalars)
        + [pl.BlockSpec(memory_space=pl.ANY)] * len(after),
        out_specs=tuple(pl.BlockSpec(memory_space=pltpu.VMEM) for _ in outs),
        scratch_shapes=list(scratch),
        compiler_params=pltpu.CompilerParams(vmem_limit_bytes=grant),
        cost_estimate=pl.CostEstimate(flops=flops, bytes_accessed=moved, transcendentals=0),
        name=name,
    )(*args, *after)


def place_of_block(pair_ref, info_ref, ranks, step, half, other_core):
    core = jnp.bitwise_xor(info_ref[2], other_core)
    rank = 2 * jnp.bitwise_xor(info_ref[1], step) + core
    pair = pair_ref[rank]
    return pair if half == 0 else 2 * ranks - 1 - pair


def fill_mask(bias_ref, pair_ref, info_ref, ranks, parts, block):
    rows = 2 * parts * block
    lanes = lax.broadcasted_iota(jnp.int32, (1, rows), 1)
    query_place = lanes % block
    for step in range(parts):
        for half in range(2):
            place = place_of_block(pair_ref, info_ref, ranks, step, half, 0)
            query_place = query_place + jnp.where(
                lanes // block == 2 * step + half, place * block, 0
            )
    ahead = lax.broadcasted_iota(jnp.int32, (block, rows), 0) - query_place
    for other in range(2):
        for step in range(parts):
            for half in range(2):
                place = place_of_block(pair_ref, info_ref, ranks, step, half, other)
                start = other * rows + (2 * step + half) * block
                bias_ref[start : start + block, :] = jnp.where(
                    ahead <= -place * block, 0.0, NEG_BIG
                )


def head_parallel(ranks, chips, seq_parts):
    parts = chips
    hw = HEADS // chips * HEAD_DIM

    def core_swap(member):
        return lax.ppermute(member, "ctx", [(i, i ^ 1) for i in range(ranks)])

    def chip_swap(member, step):
        return lax.ppermute(
            member, "ctx", [(i, 2 * ((i // 2) ^ step) + i % 2) for i in range(ranks)]
        )

    def seq_swap(member, step):
        return lax.ppermute(member, "dp", [(i, i ^ step) for i in range(seq_parts)])

    def per_device_heads(
        tokens,
        pair_of_rank,
        first_gain,
        first_shift,
        w_input,
        query_bias,
        value_bias,
        w_output,
        output_bias,
        second_gain,
        second_shift,
        w_expand,
        expand_bias,
        w_contract,
        contract_bias,
        cotangent,
    ):
        bf, f32 = jnp.bfloat16, jnp.float32
        rows, width = tokens.shape[1:]
        block = rows // 2
        own_width = width // seq_parts
        ff = expand_bias.shape[0]
        total = parts * rows
        half_width = width // 2
        half_ff = ff // 2
        sub = own_width // parts
        half_own = own_width // 2
        small_rows = 16
        others = range(1, parts)
        seq_id = lax.axis_index("dp")
        rank = lax.axis_index("ctx")
        chip = rank // 2
        core = rank % 2
        info = jnp.stack([seq_id, chip, core]).astype(jnp.int32)

        own_tokens = tokens[0]
        token_parts = [own_tokens] + [chip_swap(own_tokens, k) for k in others]
        def pack_kernel(info_ref, w_ref, *refs):
            vecs, (packed_ref, w_scr), scrs, (sems,) = (
                refs[:8],
                refs[8:10],
                refs[10:18],
                refs[18:],
            )
            copies = [
                pltpu.make_async_copy(src, dst, sems.at[i])
                for i, (src, dst) in enumerate(zip((w_ref, *vecs), (w_scr, *scrs)))
            ]
            for copy in copies:
                copy.start()
            for copy in copies:
                copy.wait()
            for at in range(chips):

                @pl.when(info_ref[1] == at)
                def _():
                    for base in range(3):
                        start = base * width + at * hw
                        packed_ref[0:own_width, base * hw : (base + 1) * hw] = w_scr[
                            :, start : start + hw
                        ]

            small = jnp.concatenate(
                [v[...].astype(f32).reshape(1, own_width) for v in scrs], axis=0
            )
            small = jnp.concatenate([small, jnp.zeros_like(small)], axis=0)
            packed_ref[own_width:, 0:own_width] = small.astype(bf)
            packed_ref[own_width:, own_width:] = jnp.zeros((small_rows, 3 * hw - own_width), bf)

        small_args = (
            first_gain,
            first_shift,
            query_bias,
            value_bias,
            output_bias,
            second_gain,
            second_shift,
            contract_bias,
        )
        (packed,) = local_call(
            pack_kernel,
            "pack",
            [shape_of((own_width + small_rows, 3 * hw), bf)],
            [info, w_input] + list(small_args),
            scalars=1,
            scratch=[pltpu.VMEM((own_width, 3 * width), bf)]
            + [pltpu.VMEM((own_width,), bf)] * 8
            + [pltpu.SemaphoreType.DMA((9,))],
            space=pltpu.HBM,
            grant=60 * 1024 * 1024,
        )
        packed_parts = [packed] + [seq_swap(packed, j) for j in others]
        own_cot = cotangent[0]
        out_parts = [w_output] + [seq_swap(w_output, j) for j in others]

        def pack_more_kernel(info_ref, we_ref, cot_ref, *refs):
            for j in others:
                refs[j - 1][0:own_width, :] = we_ref[
                    :, aligned(jnp.bitwise_xor(info_ref[0], j), ff)
                ]
                refs[j - 1][own_width:, :] = cot_ref[...]

        more = local_call(
            pack_more_kernel,
            "pack_more",
            [shape_of((own_width + rows, width), bf)] * (seq_parts - 1),
            [info, w_expand, own_cot],
            scalars=1,
            after=[packed],
        )
        more_parts = [seq_swap(more[j - 1], j) for j in others]

        def qkv_kernel(info_ref, *refs):
            toks, packs = refs[:parts], refs[parts : 2 * parts]
            q_ref, kv_ref, normed_ref, w_ref, vec_ref, vec_scr = refs[2 * parts :]
            for j in range(parts):
                place = jnp.bitwise_xor(info_ref[0], j)
                w_ref[aligned(place, own_width), :] = packs[j][0:own_width, :]
                vec_scr[place] = packs[j][own_width : own_width + small_rows, 0:own_width].astype(
                    f32
                )
            vectors = jnp.concatenate([vec_scr[j] for j in range(parts)], axis=1)
            vec_ref[...] = vectors
            chosen = vec_scr[info_ref[1]]
            for k in range(parts):
                xhat, _ = norm_stats(toks[k][...].astype(f32))
                normed_ref[k * rows : (k + 1) * rows, :] = (
                    xhat * vectors[0:1] + vectors[1:2]
                ).astype(bf)
            mixed = mm(normed_ref[...], w_ref[...])
            q_ref[...] = (mixed[:, 0:hw] + chosen[2:3]).astype(bf)
            kv_ref[:, 0:hw] = mixed[:, hw : 2 * hw].astype(bf)
            kv_ref[:, hw : 2 * hw] = (mixed[:, 2 * hw :] + chosen[3:4]).astype(bf)

        query, own_kv, normed, w_heads_full, vectors = local_call(
            qkv_kernel,
            "project",
            [
                shape_of((total, hw), bf),
                shape_of((total, 2 * hw), bf),
                shape_of((total, width), bf),
                shape_of((width, 3 * hw), bf),
                shape_of((small_rows, width), f32),
            ],
            [info] + token_parts + packed_parts,
            scalars=1,
            after=out_parts[1:],
            scratch=[pltpu.VMEM((parts, small_rows, own_width), f32)],
            flops=2 * total * width * 3 * hw,
        )
        far_kv = core_swap(own_kv)

        head_count = hw // HEAD_DIM
        scale = HEAD_DIM ** (-0.5)

        def head_columns(ref, base, head):
            start = base + head * HEAD_DIM
            return ref[:, start : start + HEAD_DIM]

        def attend_kernel(info_ref, pair_ref, q_ref, kv_ref, far_ref, *refs):
            outs = refs[:parts]
            flat_ref, lse_ref, bias_ref = refs[parts:]
            fill_mask(bias_ref, pair_ref, info_ref, ranks, parts, block)
            columns = []
            for head in range(head_count):
                keys = jnp.concatenate(
                    [head_columns(kv_ref, 0, head), head_columns(far_ref, 0, head)], axis=0
                )
                values = jnp.concatenate(
                    [head_columns(kv_ref, hw, head), head_columns(far_ref, hw, head)], axis=0
                )
                scores = mm_nt(keys, head_columns(q_ref, 0, head)) * scale + bias_ref[...]
                peak = jnp.max(scores, axis=0, keepdims=True)
                weights = jnp.exp(scores - peak)
                mass = jnp.sum(weights, axis=0, keepdims=True)
                lse_ref[head : head + 1, :] = peak + jnp.log(mass)
                mixed = mm_tn(values, weights.astype(bf)) / mass
                flat_ref[head * HEAD_DIM : (head + 1) * HEAD_DIM, :] = mixed
            attended = flat_ref[...].T.astype(bf)
            for k in range(parts):
                outs[k][...] = attended[k * rows : (k + 1) * rows]

        attend_out = local_call(
            attend_kernel,
            "attend",
            [shape_of((rows, hw), bf)] * parts
            + [shape_of((hw, total), f32), shape_of((8, total), f32)],
            [info, pair_of_rank, query, own_kv, far_kv],
            scalars=2,
            scratch=[pltpu.VMEM((2 * total, total), f32)],
            flops=2 * 2 * head_count * 2 * total * total * HEAD_DIM,
        )
        flat_attended, row_lse = attend_out[parts:]
        att_parts = [attend_out[0]] + [chip_swap(attend_out[k], k) for k in others]

        def middle_kernel(info_ref, tok_ref, vec_ref, *refs):
            atts, outs = refs[:parts], refs[parts : 2 * parts]
            mid_ref, normed_ref, w_ref = refs[2 * parts :]
            for j in range(parts):
                w_ref[jnp.bitwise_xor(info_ref[0], j)] = outs[j][...]
            middle = tok_ref[...].astype(f32) + vec_ref[4:5]
            for k in range(parts):
                middle = middle + mm(atts[k][...], w_ref[jnp.bitwise_xor(info_ref[1], k)])
            mid_ref[...] = middle
            xhat, _ = norm_stats(middle)
            normed_ref[...] = (xhat * vec_ref[5:6] + vec_ref[6:7]).astype(bf)

        middle, own_normed_two, out_full = local_call(
            middle_kernel,
            "middle",
            [
                shape_of((rows, width), f32),
                shape_of((rows, width), bf),
                shape_of((parts, own_width, width), bf),
            ],
            [info, own_tokens, vectors] + att_parts + out_parts,
            scalars=1,
            flops=2 * rows * width * width,
        )
        n2_parts = [own_normed_two] + [seq_swap(own_normed_two, j) for j in others]

        span = ff // parts + own_width

        def ffn_kernel(info_ref, bias_ref, wc_ref, we_ref, own_cot_ref, *refs):
            n2s = refs[:parts]
            mores = refs[parts : 2 * parts - 1]
            gns = refs[2 * parts - 1 : 3 * parts - 1]
            result_ref, keep_ref, send_ref, sum_ref = refs[3 * parts - 1 : 3 * parts + 3]
            active_ref, gh_ref, n2_ref, cot_ref, w_scr, scr = refs[3 * parts + 3 :]
            w_scr[aligned(info_ref[0], own_width), :] = we_ref[:, aligned(info_ref[0], ff)]
            for j in range(seq_parts):
                at = slice(j * rows, (j + 1) * rows)
                n2_ref[at, :] = n2s[j][...]
                if j == 0:
                    cot_ref[at, :] = own_cot_ref[...]
                    continue
                place = jnp.bitwise_xor(info_ref[0], j)
                w_scr[aligned(place, own_width), :] = mores[j - 1][0:own_width, :]
                cot_ref[at, :] = mores[j - 1][own_width:, :]
            hidden = mm(n2_ref[...], w_scr[...]) + bias_ref[...].astype(f32).reshape(1, ff)
            square = hidden * hidden
            curve = jnp.tanh(GELU_SCALE * hidden * (1.0 + GELU_CUBIC * square))
            active_ref[...] = (0.5 * hidden * (1.0 + curve)).astype(bf)
            slope = 0.5 * (1.0 + curve) + 0.5 * hidden * (1.0 - curve * curve) * GELU_SCALE * (
                1.0 + 3.0 * GELU_CUBIC * square
            )
            grad_hidden = mm_nt(cot_ref[...], wc_ref[...]) * slope
            gh_ref[...] = grad_hidden.astype(bf)
            sum_ref[...] = column_sums(gh_ref[...].astype(f32))
            grad = mm_nt(gh_ref[...], w_scr[...]).astype(bf)
            for j in range(parts):
                gns[j][...] = grad[j * rows : (j + 1) * rows]
            result_ref[...] = mm(active_ref[...], wc_ref[...]).astype(bf)
            core_id = info_ref[2]
            for flip, out_ref in ((0, keep_ref), (1, send_ref)):
                half = jnp.bitwise_xor(core_id, flip)
                scr[...] = mm_tn(active_ref[...], cot_ref[:, aligned(half, half_width)]).astype(bf)
                for part in range(parts):
                    rows_to = ff // parts
                    out_ref[part, 0:rows_to, :] = scr[part * rows_to : (part + 1) * rows_to, :]
                scr[...] = mm_tn(n2_ref[...], gh_ref[:, aligned(half, half_ff)]).astype(bf)
                for part in range(parts):
                    for j in range(seq_parts):
                        at = ff // parts + j * sub
                        row = j * own_width + part * sub
                        out_ref[part, at : at + sub, :] = scr[row : row + sub, :]

        ffn_out = local_call(
            ffn_kernel,
            "feed",
            [shape_of((rows, width), bf)] * parts
            + [
                shape_of((total, width), bf),
                shape_of((parts, span, half_width), bf),
                shape_of((parts, span, half_width), bf),
                shape_of((1, ff), f32),
            ],
            [info, expand_bias, w_contract, w_expand, own_cot] + n2_parts + more_parts,
            scalars=1,
            scratch=[
                pltpu.VMEM((total, ff), bf),
                pltpu.VMEM((total, ff), bf),
                pltpu.VMEM((total, width), bf),
                pltpu.VMEM((total, width), bf),
                pltpu.VMEM((width, ff), bf),
                pltpu.VMEM((width, half_ff), bf),
            ],
            flops=6 * 2 * total * width * ff,
        )
        result, ffn_keep, ffn_send, grad_expand_row = ffn_out[parts:]
        gn_parts = [ffn_out[0]] + [seq_swap(ffn_out[j], j) for j in others]
        ffn_far = core_swap(ffn_send)

        def halve_kernel(info_ref, keep_ref, far_ref, own_ref, out_ref):
            for k in range(parts):
                at = jnp.bitwise_xor(info_ref[1], k)
                piece = keep_ref[at].astype(f32) + far_ref[at].astype(f32)
                if k % 2:
                    out_ref[k // 2] = piece.astype(bf)
                else:
                    own_ref[k // 2] = piece

        rs_own, rs_send = local_call(
            halve_kernel,
            "feed_halves",
            [
                shape_of((parts // 2, span, half_width), f32),
                shape_of((parts // 2, span, half_width), bf),
            ],
            [info, ffn_keep, ffn_far],
            scalars=1,
            after=gn_parts[1:],
        )
        rs_far = chip_swap(rs_send, 1)

        def back_kernel(info_ref, mid_ref, vec_ref, cot_ref, w_ref, *refs):
            gns = refs[:parts]
            douts = refs[parts : 2 * parts]
            gmid_ref, branch_ref, sums_ref = refs[2 * parts :]
            grad = gns[0][...].astype(f32)
            for j in others:
                grad = grad + gns[j][...].astype(f32)
            xhat, spread = norm_stats(mid_ref[...])
            cot = cot_ref[...].astype(f32)
            grad_middle = cot + norm_back(grad, vec_ref[5:6], xhat, spread)
            gmid_ref[...] = grad_middle
            branch = grad_middle.astype(bf)
            branch_ref[...] = branch
            for k in range(parts):
                douts[k][...] = mm_nt(branch, w_ref[jnp.bitwise_xor(info_ref[1], k)]).astype(bf)
            sums_ref[0:1, :] = column_sums(branch.astype(f32))
            sums_ref[1:2, :] = column_sums(grad * xhat)
            sums_ref[2:3, :] = column_sums(grad)
            sums_ref[3:4, :] = column_sums(cot)

        back_out = local_call(
            back_kernel,
            "middle_back",
            [shape_of((rows, hw), bf)] * parts
            + [
                shape_of((rows, width), f32),
                shape_of((rows, width), bf),
                shape_of((8, width), f32),
            ],
            [info, middle, vectors, own_cot, out_full] + gn_parts,
            scalars=1,
            after=[rs_send],
            flops=2 * rows * width * width,
        )
        grad_middle, grad_branch, late_sums = back_out[parts:]
        dout_parts = [back_out[0]] + [chip_swap(back_out[k], k) for k in others]

        def out_weights_kernel(info_ref, branch_ref, *refs):
            atts = refs[:parts]
            keep_ref, send_ref = refs[parts:]
            for flip, out_ref in ((0, keep_ref), (1, send_ref)):
                half = jnp.bitwise_xor(info_ref[2], flip)
                piece = branch_ref[:, aligned(half, half_width)]
                for k in range(parts):
                    out_ref[jnp.bitwise_xor(info_ref[1], k)] = mm_tn(atts[k][...], piece).astype(bf)

        out_keep, out_send = local_call(
            out_weights_kernel,
            "output_weights",
            [shape_of((parts, hw, half_width), bf)] * 2,
            [info, grad_branch] + att_parts,
            scalars=1,
            flops=2 * rows * width * width,
        )
        out_far = core_swap(out_send)

        fold = own_width // 2

        def out_chunks_kernel(info_ref, result_ref, keep_ref, far_ref, *outs):
            for j in range(seq_parts):
                to = jnp.bitwise_xor(info_ref[0], j)
                outs[j][0:rows, :] = result_ref[j * rows : (j + 1) * rows, :]
                whole = (keep_ref[to].astype(f32) + far_ref[to].astype(f32)).astype(bf)
                outs[j][rows:, 0:half_width] = whole[0:fold]
                outs[j][rows:, half_width:] = whole[fold:]

        out_chunks = local_call(
            out_chunks_kernel,
            "output_chunks",
            [shape_of((rows + fold, width), bf)] * seq_parts,
            [info, result, out_keep, out_far],
            scalars=1,
        )
        oc_parts = [out_chunks[0]] + [seq_swap(out_chunks[j], j) for j in others]

        def attend_back_kernel(info_ref, pair_ref, q_ref, kv_ref, far_ref, flat_ref, lse_ref, *refs):
            douts = refs[:parts]
            dq_ref, own_ref, send_ref, bias_ref, dout_ref = refs[parts:]
            fill_mask(bias_ref, pair_ref, info_ref, ranks, parts, block)
            for k in range(parts):
                dout_ref[k * rows : (k + 1) * rows, :] = douts[k][...].astype(f32)
            flat_dout = dout_ref[...].T
            for head in range(head_count):
                at = slice(head * HEAD_DIM, (head + 1) * HEAD_DIM)
                keys = jnp.concatenate(
                    [head_columns(kv_ref, 0, head), head_columns(far_ref, 0, head)], axis=0
                )
                values = jnp.concatenate(
                    [head_columns(kv_ref, hw, head), head_columns(far_ref, hw, head)], axis=0
                )
                queries = head_columns(q_ref, 0, head)
                dout = dout_ref[:, at].astype(bf)
                dout_turned = flat_dout[at, :]
                delta = column_sums(dout_turned * flat_ref[at, :])
                scores = mm_nt(keys, queries) * scale + bias_ref[...]
                probs = jnp.exp(scores - lse_ref[head : head + 1, :])
                grad_value = mm(probs.astype(bf), dout)
                grad_weights = mm(values, dout_turned.astype(bf))
                grad_scores = (probs * (grad_weights - delta)).astype(bf)
                grad_key = mm(grad_scores, queries) * scale
                dq_ref[at, :] = mm_tn(keys, grad_scores) * scale
                vat = slice(hw + head * HEAD_DIM, hw + (head + 1) * HEAD_DIM)
                own_ref[:, at] = grad_key[0:total]
                own_ref[:, vat] = grad_value[0:total]
                send_ref[:, at] = grad_key[total:].astype(bf)
                send_ref[:, vat] = grad_value[total:].astype(bf)

        flat_dq, dkv_own, dkv_send = local_call(
            attend_back_kernel,
            "attend_back",
            [
                shape_of((hw, total), f32),
                shape_of((total, 2 * hw), f32),
                shape_of((total, 2 * hw), bf),
            ],
            [info, pair_of_rank, query, own_kv, far_kv, flat_attended, row_lse] + dout_parts,
            scalars=2,
            after=[out_chunks[0]],
            scratch=[pltpu.VMEM((2 * total, total), f32), pltpu.VMEM((total, hw), f32)],
            flops=5 * 2 * head_count * 2 * total * total * HEAD_DIM,
        )
        dkv_far = core_swap(dkv_send)

        def quarter_kernel(own_ref, far_ref, keep_ref, send_ref):
            keep_ref[...] = own_ref[0] + far_ref[0].astype(f32)
            send_ref[...] = (own_ref[1] + far_ref[1].astype(f32)).astype(bf)

        rs_own_two, rs_send_two = local_call(
            quarter_kernel,
            "feed_quarters",
            [shape_of((span, half_width), f32), shape_of((span, half_width), bf)],
            [rs_own, rs_far],
            after=[dkv_send],
        )
        rs_far_two = chip_swap(rs_send_two, 2)

        def normed_back_kernel(dq_ref, own_ref, far_ref, w_ref, *refs):
            toks = refs[:parts]
            keep_ref, send_ref, mixed_ref, sums_ref, bias_ref = refs[parts:]
            mixed_ref[:, 0:hw] = dq_ref[...].T.astype(bf)
            mixed_ref[:, hw:] = (own_ref[...] + far_ref[...].astype(f32)).astype(bf)
            shift_sum = jnp.zeros((1, width), f32)
            gain_sum = jnp.zeros((1, width), f32)
            for k in range(parts):
                grad = mm_nt(mixed_ref[k * rows : (k + 1) * rows, :], w_ref[...])
                if k % 2:
                    send_ref[k // 2] = grad.astype(bf)
                else:
                    keep_ref[k // 2] = grad
                xhat, _ = norm_stats(toks[k][...].astype(f32))
                shift_sum = shift_sum + column_sums(grad)
                gain_sum = gain_sum + column_sums(grad * xhat)
            sums_ref[0:1, :] = gain_sum
            sums_ref[1:2, :] = shift_sum
            bias_ref[0:1, :] = column_sums(mixed_ref[...].astype(f32))

        nb_out = local_call(
            normed_back_kernel,
            "normed_back",
            [
                shape_of((parts // 2, rows, width), f32),
                shape_of((parts // 2, rows, width), bf),
                shape_of((total, 3 * hw), bf),
                shape_of((8, width), f32),
                shape_of((8, 3 * hw), f32),
            ],
            [flat_dq, dkv_own, dkv_far, w_heads_full] + token_parts,
            flops=2 * total * width * 3 * hw,
            after=[rs_send_two],
        )
        gt_keep, gt_send, grad_mixed, first_sums, mixed_sums = nb_out
        gt_far = chip_swap(gt_send, 1)

        tall = half_own + small_rows

        def input_weights_kernel(
            info_ref, normed_ref, mixed_ref, first_ref, bias_ref, late_ref, row_ref, *refs
        ):
            keep_ref, send_ref, grad_scr, small_scr = refs
            grad_scr[...] = mm_tn(normed_ref[...], mixed_ref[...])
            core_id, chip_id, seq = info_ref[2], info_ref[1], info_ref[0]
            small_scr[...] = jnp.zeros_like(small_scr)
            for j in range(seq_parts):
                at = slice(j * own_width, (j + 1) * own_width)
                small_scr[j, 0:2, 0:own_width] = first_ref[0:2, at]
                small_scr[j, 4:8, 0:own_width] = late_ref[0:4, at]
            small_scr[chip_id, 2:3, 0:hw] = bias_ref[0:1, 0:hw]
            small_scr[chip_id, 3:4, 0:hw] = bias_ref[0:1, 2 * hw : 3 * hw]
            for j in range(ff // own_width):
                small_scr[seq, 8 + j : 9 + j, 0:own_width] = row_ref[
                    :, j * own_width : (j + 1) * own_width
                ]
            for flip, out_ref in ((0, keep_ref), (1, send_ref)):
                half = jnp.bitwise_xor(core_id, flip)
                for j in range(seq_parts):
                    start = pl.multiple_of(j * own_width + half * half_own, 16)
                    out_ref[j, 0:half_own, :] = grad_scr[pl.ds(start, half_own), :].astype(bf)
                    out_ref[j, half_own:tall, :] = small_scr[j].astype(bf)

        in_keep, in_send = local_call(
            input_weights_kernel,
            "input_weights",
            [shape_of((seq_parts, tall, 3 * hw), bf)] * 2,
            [info, normed, grad_mixed, first_sums, mixed_sums, late_sums, grad_expand_row],
            scalars=1,
            scratch=[
                pltpu.VMEM((width, 3 * hw), f32),
                pltpu.VMEM((seq_parts, small_rows, 3 * hw), f32),
            ],
            flops=2 * total * width * 3 * hw,
        )
        in_far = core_swap(in_send)

        def out_sum_kernel(info_ref, mid_ref, vec_ref, *refs):
            owned = refs[:seq_parts]
            keep_ref, send_ref, block_ref, scr = refs[seq_parts:]
            result = mid_ref[...] + vec_ref[7:8]
            outs = jnp.zeros((fold, width), f32)
            for j in range(seq_parts):
                result = result + owned[j][0:rows, :].astype(f32)
                outs = outs + owned[j][rows:, :].astype(f32)
            block_ref[0] = result.astype(bf)
            scr[0:fold, :] = outs[:, 0:half_width]
            scr[fold:, :] = outs[:, half_width:]
            for k in range(parts):
                piece = scr[aligned(jnp.bitwise_xor(info_ref[1], k), sub), :]
                if k % 2:
                    send_ref[k // 2] = piece.astype(bf)
                else:
                    keep_ref[k // 2] = piece

        os_keep, os_send, block_out = local_call(
            out_sum_kernel,
            "output_sum",
            [
                shape_of((parts // 2, sub, half_width), f32),
                shape_of((parts // 2, sub, half_width), bf),
                shape_of((1, rows, width), bf),
            ],
            [info, middle, vectors] + oc_parts,
            scalars=1,
            scratch=[pltpu.VMEM((own_width, half_width), f32)],
            after=[in_send],
        )
        os_far = chip_swap(os_send, 1)

        def dp_pack_kernel(info_ref, own_ref, far_two_ref, keep_ref, far_ref, *refs):
            con_ref, scr = refs[seq_parts:]
            whole = own_ref[...] + far_two_ref[...].astype(f32)
            con_ref[...] = whole[0 : ff // parts].astype(bf)
            scr[...] = whole[ff // parts :]
            for j in range(seq_parts):
                at = jnp.bitwise_xor(info_ref[0], j)
                refs[j][0:tall, :] = (keep_ref[at].astype(f32) + far_ref[at].astype(f32)).astype(
                    bf
                )
                refs[j][tall:, 0:half_ff] = scr[aligned(at, sub), :].astype(bf)
                refs[j][tall:, half_ff:] = jnp.zeros((sub, 3 * hw - half_ff), bf)

        dp_out = local_call(
            dp_pack_kernel,
            "owners",
            [shape_of((tall + sub, 3 * hw), bf)] * seq_parts
            + [shape_of((ff // parts, half_width), bf)],
            [info, rs_own_two, rs_far_two, in_keep, in_far],
            scalars=1,
            scratch=[pltpu.VMEM((own_width, half_ff), f32)],
            after=[block_out],
        )
        dp_parts = [dp_out[0]] + [seq_swap(dp_out[j], j) for j in others]
        con_one = dp_out[seq_parts]
        con_two = chip_swap(con_one, 2)

        wide = tall + sub
        tail = own_width * half_ff // (3 * hw)
        over = own_width - tail

        def dp_sum_kernel(info_ref, gk_ref, gf_ref, ok_ref, of_ref, *refs):
            owned = refs[:seq_parts]
            last_ref, gown_ref, gsend_ref, scr = refs[seq_parts:]
            whole = owned[0][0:tall, :].astype(f32)
            for j in others:
                whole = whole + owned[j][0:tall, :].astype(f32)
            last_ref[0:tall, :] = whole.astype(bf)
            for j in range(seq_parts):
                place = jnp.bitwise_xor(info_ref[0], j)
                scr[aligned(place, sub), :] = owned[j][tall:, 0:half_ff]
            last_ref[tall : tall + tail, 0:half_ff] = scr[0:tail, :]
            last_ref[tall : tall + over, half_ff:] = scr[tail:, 0 : half_ff // 2]
            last_ref[tall + over : tall + tail, half_ff:] = scr[tail:, half_ff // 2 :]
            for k in range(2):
                at = slice(tall + tail + k * sub, tall + tail + (k + 1) * sub)
                last_ref[at, 0:half_width] = (ok_ref[k] + of_ref[k].astype(f32)).astype(bf)
                last_ref[at, half_width:] = jnp.zeros((sub, 3 * hw - half_width), bf)
            gown_ref[...] = gk_ref[0] + gf_ref[0].astype(f32)
            gsend_ref[...] = (gk_ref[1] + gf_ref[1].astype(f32)).astype(bf)

        last_one, gt_own, gt_send_two = local_call(
            dp_sum_kernel,
            "shares",
            [
                shape_of((tall + tail + 2 * sub, 3 * hw), bf),
                shape_of((rows, width), f32),
                shape_of((rows, width), bf),
            ],
            [info, gt_keep, gt_far, os_keep, os_far] + dp_parts,
            scalars=1,
            scratch=[pltpu.VMEM((own_width, half_ff), bf)],
            after=[con_two],
        )
        last_one_far = chip_swap(last_one, 2)
        gt_far_two = chip_swap(gt_send_two, 2)
        con_one_far = chip_swap(con_one, 1)
        con_two_far = chip_swap(con_two, 1)
        con_parts = [con_one, con_one_far, con_two, con_two_far]
        con_far = [core_swap(member) for member in con_parts]

        def contract_kernel(info_ref, *refs):
            con_ref = refs[2 * parts]
            for flip in range(2):
                lanes = aligned(jnp.bitwise_xor(info_ref[2], flip), half_width)
                for k in range(parts):
                    at = jnp.bitwise_xor(info_ref[1], k)
                    con_ref[aligned(at, ff // parts), lanes] = refs[flip * parts + k][...].astype(
                        f32
                    )

        (grad_contract,) = local_call(
            contract_kernel,
            "contract_final",
            [shape_of((ff, width), f32)],
            [info] + con_parts + con_far,
            scalars=1,
        )

        def last_pair_kernel(own_ref, far_ref, out_ref):
            for slot, (first, second) in enumerate(((own_ref, far_ref), (far_ref, own_ref))):
                out_ref[slot, 0 : tall + tail, :] = first[0 : tall + tail, :]
                outs = first[tall + tail : wide + tail, :].astype(f32)
                outs = outs + second[wide + tail :, :].astype(f32)
                out_ref[slot, tall + tail :, :] = outs.astype(bf)

        (last_two,) = local_call(
            last_pair_kernel,
            "input_pair",
            [shape_of((2, wide + tail, 3 * hw), bf)],
            [last_one, last_one_far],
            after=[gt_far_two, con_one_far, con_two_far],
        )
        last_two_far = chip_swap(last_two, 1)
        core_two = core_swap(last_two)
        core_two_far = core_swap(last_two_far)

        def tokens_kernel(tok_ref, vec_ref, gmid_ref, own_ref, far_ref, out_ref):
            grad = own_ref[...] + far_ref[...].astype(f32)
            xhat, spread = norm_stats(tok_ref[...].astype(f32))
            out_ref[0] = gmid_ref[...] + norm_back(grad, vec_ref[0:1], xhat, spread)

        (grad_tokens,) = local_call(
            tokens_kernel,
            "tokens_back",
            [shape_of((1, rows, width), f32)],
            [own_tokens, vectors, grad_middle, gt_own, gt_far_two],
        )

        def last_kernel(info_ref, *refs):
            gin_ref, gout_ref, small_ref, exp_ref, scr = refs[4:]

            def member(far_core, k):
                return refs[2 * far_core + k % 2][k // 2]

            for flip in range(2):
                half = jnp.bitwise_xor(info_ref[2], flip)
                for k in range(parts):
                    at = jnp.bitwise_xor(info_ref[1], k)
                    piece = member(flip, k).astype(f32)
                    scr[at, aligned(half, half_own), :] = piece[0:half_own]
                    gout_ref[aligned(at, sub), aligned(half, half_width)] = piece[
                        tall + tail :, 0:half_width
                    ]
                    turned = jnp.concatenate(
                        [
                            piece[tall : tall + over, half_ff:],
                            piece[tall + over : tall + tail, half_ff:],
                        ],
                        axis=1,
                    )
                    turned = jnp.concatenate(
                        [piece[tall : tall + tail, 0:half_ff], turned], axis=0
                    )
                    for j in range(seq_parts):
                        cols = pl.ds(pl.multiple_of(j * ff + half * half_ff, 128), half_ff)
                        exp_ref[aligned(at, sub), cols] = turned[j * sub : (j + 1) * sub]
            for at in range(parts):
                for base in range(3):
                    start = base * width + at * hw
                    gin_ref[:, start : start + hw] = scr[at, :, base * hw : (base + 1) * hw]
            small = member(0, 0)[half_own:tall, 0:own_width].astype(f32)
            for k in others:
                small = small + member(0, k)[half_own:tall, 0:own_width].astype(f32)
            small_ref[...] = small

        grad_input, grad_output, small_sums, grad_expand = local_call(
            last_kernel,
            "weights_final",
            [
                shape_of((own_width, 3 * width), f32),
                shape_of((own_width, width), f32),
                shape_of((small_rows, own_width), f32),
                shape_of((own_width, seq_parts * ff), f32),
            ],
            [info, last_two, last_two_far, core_two, core_two_far],
            scalars=1,
            after=[grad_tokens, grad_contract],
            scratch=[pltpu.VMEM((parts, own_width, 3 * hw), f32)],
        )

        small_of = [small_sums[i] for i in range(8)]
        grad_expand_bias = small_sums[8 : 8 + ff // own_width].reshape(ff)
        return (
            block_out,
            grad_tokens,
            small_of[0],
            small_of[1],
            grad_input,
            small_of[2],
            small_of[3],
            grad_output,
            small_of[4],
            small_of[5],
            small_of[6],
            grad_expand,
            grad_expand_bias,
            grad_contract,
            small_of[7],
        )

    return per_device_heads


def solution(mesh):
    ranks = mesh.shape["ctx"]
    chips = ranks // 2
    if chips == mesh.shape["dp"] and HEADS % chips == 0 and chips & (chips - 1) == 0:
        body = head_parallel(ranks, chips, mesh.shape["dp"])
    else:
        body = per_device
    return jax.shard_map(
        body,
        mesh=mesh,
        in_specs=(
            P("dp", "ctx", None),
            P(),
            P("dp"),
            P("dp"),
            P("dp", None),
            P("dp"),
            P("dp"),
            P("dp", None),
            P("dp"),
            P("dp"),
            P("dp"),
            P("dp", None),
            P("dp"),
            P("dp", None),
            P("dp"),
            P("dp", "ctx", None),
        ),
        out_specs=(
            P("dp", "ctx", None),
            P("dp", "ctx", None),
            P("dp"),
            P("dp"),
            P("dp", None),
            P("dp"),
            P("dp"),
            P("dp", None),
            P("dp"),
            P("dp"),
            P("dp"),
            P("dp", None),
            P("dp"),
            P("dp", None),
            P("dp"),
        ),
        check_vma=False,
    )
```

```python
import math

import jax
import jax.numpy as jnp
from jax import lax
from jax.experimental import pallas as pl
from jax.experimental.pallas import tpu as pltpu
from jax.sharding import PartitionSpec as P

HEADS = 12
HEAD_DIM = 64


NEG_BIG = -1e30
NORM_EPS = 1e-05
GELU_SCALE = 0.7978845608028654
GELU_CUBIC = 0.044715


def gelu_tanh(values):
    return (
        0.5
        * values
        * (1.0 + jnp.tanh(GELU_SCALE * (values + GELU_CUBIC * values * values * values)))
    )


def layer_norm(values, gain_row, shift_row):
    centre = values - jnp.mean(values, axis=-1, keepdims=True)
    spread = jnp.mean(centre * centre, axis=-1, keepdims=True)
    return centre * lax.rsqrt(spread + NORM_EPS) * gain_row + shift_row


def lookup_pair(pair_table, positions):
    ranks_all = jnp.arange(pair_table.shape[0], dtype=jnp.int32)
    return jnp.sum(jnp.where(positions[..., None] == ranks_all, pair_table, 0), axis=-1)


def group_count(blocks, sub_rows):
    chosen_count = 1
    for candidate in range(1, blocks + 1):
        if blocks % candidate == 0 and candidate * sub_rows <= max(512, sub_rows):
            chosen_count = candidate
    return chosen_count


def slot_mask(slot_ids, wanted, rank_count):
    return (slot_ids == wanted).reshape((-1,) + (1,) * (rank_count - 1))


def slot_add(values, slot_ids):
    early_sum = jnp.sum(jnp.where(slot_mask(slot_ids, 0, values.ndim), values, 0.0), axis=0)
    late_sum = jnp.sum(jnp.where(slot_mask(slot_ids, 1, values.ndim), values, 0.0), axis=0)
    return jnp.stack([early_sum, late_sum])


def slot_max(values, slot_ids):
    early_max = jnp.max(jnp.where(slot_mask(slot_ids, 0, values.ndim), values, NEG_BIG), axis=0)
    late_max = jnp.max(jnp.where(slot_mask(slot_ids, 1, values.ndim), values, NEG_BIG), axis=0)
    return jnp.stack([early_max, late_max])


def slot_pick(per_slot, slot_ids):
    return jnp.where(slot_mask(slot_ids, 0, per_slot.ndim), per_slot[0][None], per_slot[1][None])


def query_tiles(blocks, chosen):
    target = chosen.shape + blocks.shape[2:]
    chosen_view = chosen.reshape((-1,) + (1,) * (blocks.ndim - 2))
    late_part = jnp.broadcast_to(blocks[1], target)
    picked = jnp.where(chosen_view, blocks[0], blocks[1])
    return jnp.concatenate([late_part, picked], axis=0)


def key_tiles(blocks, chosen):
    target = chosen.shape + blocks.shape[2:]
    chosen_view = chosen.reshape((-1,) + (1,) * (blocks.ndim - 2))
    early_part = jnp.broadcast_to(blocks[0], target)
    picked = jnp.where(chosen_view, blocks[0], blocks[1])
    return jnp.concatenate([early_part, picked], axis=0)


def tile_slots(chosen):
    late_slot = jnp.where(chosen, 0, 1).astype(jnp.int32)
    query_slot = jnp.concatenate([jnp.ones_like(late_slot), late_slot])
    key_slot = jnp.concatenate([jnp.zeros_like(late_slot), late_slot])
    return (query_slot, key_slot)


def tile_mask(is_own, query_places, key_places):
    visible = key_places[:, None, :] <= query_places[:, :, None]
    visible = jnp.logical_or(visible, jnp.logical_not(is_own)[:, None, None])
    return jnp.concatenate([jnp.ones_like(visible), visible], axis=0)


def tile_scores(tile_query, tile_key, score_scale):
    return (
        jnp.einsum("tqhd,tkhd->thqk", tile_query, tile_key, preferred_element_type=jnp.float32)
        * score_scale
    )


def tile_probs(tile_query, tile_key, tile_visible, row_lse, score_scale):
    scores = tile_scores(tile_query, tile_key, score_scale)
    return jnp.where(tile_visible[:, None], jnp.exp(scores - row_lse[..., None]), 0.0)


def tile_dscore(probs, tile_dout, tile_value, row_delta):
    grad_probs = jnp.einsum(
        "tqhd,tkhd->thqk", tile_dout, tile_value, preferred_element_type=jnp.float32
    )
    return (probs * (grad_probs - row_delta[..., None])).astype(jnp.bfloat16)


def stats_update(running, tile_query, tile_key, query_slot, tile_visible, score_scale):
    run_peak, run_total = running
    visible = tile_visible[:, None]
    masked = jnp.where(visible, tile_scores(tile_query, tile_key, score_scale), NEG_BIG)
    new_peak = jnp.maximum(run_peak, slot_max(jnp.max(masked, axis=-1), query_slot))
    weights = jnp.where(visible, jnp.exp(masked - slot_pick(new_peak, query_slot)[..., None]), 0.0)
    run_total = run_total * jnp.exp(run_peak - new_peak) + slot_add(
        jnp.sum(weights, axis=-1), query_slot
    )
    return (new_peak, run_total)


def values_update(
    running, tile_query, tile_key, tile_value, query_slot, tile_visible, row_lse, score_scale
):
    probs = tile_probs(tile_query, tile_key, tile_visible, row_lse, score_scale)
    part_out = jnp.einsum(
        "thqk,tkhd->tqhd",
        probs.astype(jnp.bfloat16),
        tile_value,
        preferred_element_type=jnp.float32,
    )
    return running + slot_add(part_out, query_slot)


def sweep_piece(carried, pieces, block_rows, my_rank, pair_table, update):
    piece_rows = pieces[0].shape[1]
    sub_rows = math.gcd(piece_rows, block_rows)
    unit_count = piece_rows // sub_rows
    group_size = group_count(unit_count, sub_rows)

    def group_step(loop_index, running):
        offset = loop_index * (group_size * sub_rows)
        slices = tuple(
            (
                lax.dynamic_slice_in_dim(member, offset, group_size * sub_rows, 1).reshape(
                    (2, group_size, sub_rows) + member.shape[2:]
                )
                for member in pieces
            )
        )
        places = offset + jnp.arange(group_size * sub_rows, dtype=jnp.int32).reshape(
            group_size, sub_rows
        )
        far_ranks = places[:, 0] // block_rows
        far_pair = lookup_pair(pair_table, far_ranks)
        return update(running, slices, far_pair, far_ranks == my_rank, places % block_rows, offset)

    return lax.fori_loop(0, unit_count // group_size, group_step, carried)


def per_device(
    tokens,
    pair_of_rank,
    first_gain,
    first_shift,
    w_input,
    query_bias,
    value_bias,
    w_output,
    output_bias,
    second_gain,
    second_shift,
    w_expand,
    expand_bias,
    w_contract,
    contract_bias,
    cotangent,
):
    gathered = (
        lax.all_gather(first_gain, "dp", axis=0, tiled=True),
        lax.all_gather(first_shift, "dp", axis=0, tiled=True),
        lax.all_gather(w_input, "dp", axis=0, tiled=True),
        lax.all_gather(query_bias, "dp", axis=0, tiled=True),
        lax.all_gather(value_bias, "dp", axis=0, tiled=True),
        lax.all_gather(w_output, "dp", axis=0, tiled=True),
        lax.all_gather(output_bias, "dp", axis=0, tiled=True),
        lax.all_gather(second_gain, "dp", axis=0, tiled=True),
        lax.all_gather(second_shift, "dp", axis=0, tiled=True),
        lax.all_gather(w_expand, "dp", axis=0, tiled=True),
        lax.all_gather(expand_bias, "dp", axis=0, tiled=True),
        lax.all_gather(w_contract, "dp", axis=0, tiled=True),
        lax.all_gather(contract_bias, "dp", axis=0, tiled=True),
    )
    (
        full_first_gain,
        full_first_shift,
        full_input,
        full_query_bias,
        full_value_bias,
        full_output,
        full_output_bias,
        full_second_gain,
        full_second_shift,
        full_expand,
        full_expand_bias,
        full_contract,
        full_contract_bias,
    ) = gathered
    model_width = tokens.shape[2]
    block_rows = tokens.shape[1] // 2
    score_scale = HEAD_DIM ** (-0.5)
    slot_view = (2, block_rows, model_width)
    head_view = (2, block_rows, HEADS, HEAD_DIM)
    my_rank = lax.axis_index("ctx")
    my_pair = lookup_pair(pair_of_rank, my_rank)
    own_places = jnp.arange(block_rows, dtype=jnp.int32)[None, :]
    diag_mask = (own_places <= own_places.reshape(-1, 1))[None]
    zero_slot = jnp.zeros((1,), jnp.int32)

    def split_heads(member):
        return member.reshape(member.shape[:3] + (HEADS, HEAD_DIM))

    token_rows = tokens[0].astype(jnp.float32)
    normed_full, first_pullback = jax.vjp(
        layer_norm,
        token_rows,
        full_first_gain.astype(jnp.float32),
        full_first_shift.astype(jnp.float32),
    )
    normed = normed_full.astype(jnp.bfloat16)
    mixed_rows = jnp.dot(normed, full_input, preferred_element_type=jnp.float32)
    query_rows = (mixed_rows[:, :model_width] + full_query_bias.astype(jnp.float32)).astype(
        jnp.bfloat16
    )
    key_rows = mixed_rows[:, model_width : 2 * model_width].astype(jnp.bfloat16)
    value_rows = (mixed_rows[:, 2 * model_width :] + full_value_bias.astype(jnp.float32)).astype(
        jnp.bfloat16
    )
    own_query = query_rows.reshape(head_view)
    own_key = key_rows.reshape(head_view)
    own_value = value_rows.reshape(head_view)
    diag_query = own_query[0][None]
    diag_key = own_key[0][None]
    diag_value = own_value[0][None]
    key_slots = key_rows.reshape(slot_view)
    value_slots = value_rows.reshape(slot_view)
    query_slots = query_rows.reshape(slot_view)

    def stats_group(running, slices, far_pair, is_own, far_places, first_row):
        chosen = far_pair < my_pair
        query_slot, key_slot = tile_slots(chosen)
        return stats_update(
            running,
            query_tiles(own_query[:, None], chosen),
            key_tiles(split_heads(slices[0]), chosen),
            query_slot,
            tile_mask(is_own, own_places, far_places),
            score_scale,
        )

    stats_start = (
        jnp.full((2, HEADS, block_rows), NEG_BIG, jnp.float32),
        jnp.zeros((2, HEADS, block_rows), jnp.float32),
    )
    stats_start = stats_update(stats_start, diag_query, diag_key, zero_slot, diag_mask, score_scale)
    run_peak, run_total = sweep_piece(
        stats_start,
        (lax.all_gather(key_slots, "ctx", axis=1, tiled=True),),
        block_rows,
        my_rank,
        pair_of_rank,
        stats_group,
    )
    row_lse = run_peak + jnp.log(run_total)

    def values_group(running, slices, far_pair, is_own, far_places, first_row):
        chosen = far_pair < my_pair
        query_slot, key_slot = tile_slots(chosen)
        return values_update(
            running,
            query_tiles(own_query[:, None], chosen),
            key_tiles(split_heads(slices[0]), chosen),
            key_tiles(split_heads(slices[1]), chosen),
            query_slot,
            tile_mask(is_own, own_places, far_places),
            slot_pick(row_lse, query_slot),
            score_scale,
        )

    values_start = values_update(
        jnp.zeros(head_view, jnp.float32),
        diag_query,
        diag_key,
        diag_value,
        zero_slot,
        diag_mask,
        row_lse[0][None],
        score_scale,
    )
    attended = sweep_piece(
        values_start,
        (
            lax.all_gather(key_slots, "ctx", axis=1, tiled=True),
            lax.all_gather(value_slots, "ctx", axis=1, tiled=True),
        ),
        block_rows,
        my_rank,
        pair_of_rank,
        values_group,
    )
    attended_low = attended.reshape(2 * block_rows, model_width).astype(jnp.bfloat16)
    middle = (
        token_rows
        + jnp.dot(attended_low, full_output, preferred_element_type=jnp.float32)
        + full_output_bias.astype(jnp.float32)
    )
    normed_full_two, second_pullback = jax.vjp(
        layer_norm,
        middle,
        full_second_gain.astype(jnp.float32),
        full_second_shift.astype(jnp.float32),
    )
    normed_two = normed_full_two.astype(jnp.bfloat16)
    hidden = jnp.dot(
        normed_two, full_expand, preferred_element_type=jnp.float32
    ) + full_expand_bias.astype(jnp.float32)
    active_full, gelu_pullback = jax.vjp(gelu_tanh, hidden)
    active_low = active_full.astype(jnp.bfloat16)
    result = (
        middle
        + jnp.dot(active_low, full_contract, preferred_element_type=jnp.float32)
        + full_contract_bias.astype(jnp.float32)
    )
    block_out = result.astype(jnp.bfloat16)[None]
    back_input, back_output, back_expand, back_contract = (
        lax.all_gather(w_input, "dp", axis=0, tiled=True),
        lax.all_gather(w_output, "dp", axis=0, tiled=True),
        lax.all_gather(w_expand, "dp", axis=0, tiled=True),
        lax.all_gather(w_contract, "dp", axis=0, tiled=True),
    )
    grad_out_low = cotangent[0]
    grad_out = grad_out_low.astype(jnp.float32)
    grad_contract = jnp.einsum(
        "rf,rd->fd", active_low, grad_out_low, preferred_element_type=jnp.float32
    )
    grad_contract_bias = jnp.sum(grad_out, axis=0)
    grad_active = jnp.einsum(
        "rd,fd->rf", grad_out_low, back_contract, preferred_element_type=jnp.float32
    )
    grad_hidden = gelu_pullback(grad_active)[0].astype(jnp.bfloat16)
    grad_expand = jnp.einsum(
        "rd,rf->df", normed_two, grad_hidden, preferred_element_type=jnp.float32
    )
    grad_expand_bias = jnp.sum(grad_hidden.astype(jnp.float32), axis=0)
    grad_normed_two = jnp.einsum(
        "rf,df->rd", grad_hidden, back_expand, preferred_element_type=jnp.float32
    )
    grad_middle_part, grad_second_gain, grad_second_shift = second_pullback(grad_normed_two)
    grad_middle = grad_out + grad_middle_part
    grad_branch = grad_middle.astype(jnp.bfloat16)
    grad_output = jnp.einsum(
        "rd,re->de", attended_low, grad_branch, preferred_element_type=jnp.float32
    )
    grad_output_bias = jnp.sum(grad_branch.astype(jnp.float32), axis=0)
    grad_attended = jnp.einsum(
        "re,de->rd", grad_branch, back_output, preferred_element_type=jnp.float32
    ).astype(jnp.bfloat16)
    own_dout = grad_attended.reshape(head_view)
    dout_slots = grad_attended.reshape(slot_view)
    delta_rows = jnp.sum(own_dout.astype(jnp.float32) * attended, axis=-1)
    row_delta = jnp.transpose(delta_rows, (0, 2, 1))
    lse_rows = jnp.transpose(row_lse, (0, 2, 1))
    far_lse, far_delta = (
        lax.all_gather(lse_rows, "ctx", axis=1, tiled=True),
        lax.all_gather(delta_rows, "ctx", axis=1, tiled=True),
    )
    diag_probs = tile_probs(diag_query, diag_key, diag_mask, row_lse[0][None], score_scale)
    diag_dscore = tile_dscore(diag_probs, own_dout[0][None], diag_value, row_delta[0][None])
    query_start = slot_add(
        jnp.einsum("thqk,tkhd->tqhd", diag_dscore, diag_key, preferred_element_type=jnp.float32)
        * score_scale,
        zero_slot,
    )
    key_start = slot_add(
        jnp.einsum("thqk,tqhd->tkhd", diag_dscore, diag_query, preferred_element_type=jnp.float32)
        * score_scale,
        zero_slot,
    )
    value_start = slot_add(
        jnp.einsum(
            "thqk,tqhd->tkhd",
            diag_probs.astype(jnp.bfloat16),
            own_dout[0][None],
            preferred_element_type=jnp.float32,
        ),
        zero_slot,
    )

    def query_grad_group(running, slices, far_pair, is_own, far_places, first_row):
        chosen = far_pair < my_pair
        query_slot, key_slot = tile_slots(chosen)
        tile_key = key_tiles(split_heads(slices[0]), chosen)
        tile_value = key_tiles(split_heads(slices[1]), chosen)
        probs = tile_probs(
            query_tiles(own_query[:, None], chosen),
            tile_key,
            tile_mask(is_own, own_places, far_places),
            slot_pick(row_lse, query_slot),
            score_scale,
        )
        dscore = tile_dscore(
            probs,
            query_tiles(own_dout[:, None], chosen),
            tile_value,
            slot_pick(row_delta, query_slot),
        )
        part_grad = (
            jnp.einsum("thqk,tkhd->tqhd", dscore, tile_key, preferred_element_type=jnp.float32)
            * score_scale
        )
        return running + slot_add(part_grad, query_slot)

    def key_grad_group(running, slices, far_pair, is_own, far_places, first_row):
        chosen = my_pair < far_pair
        query_slot, key_slot = tile_slots(chosen)
        group_size = far_places.shape[0]
        sub_rows = far_places.shape[1]
        tile_query = query_tiles(split_heads(slices[0]), chosen)
        tile_dout = query_tiles(split_heads(slices[1]), chosen)
        lse_part = lax.dynamic_slice_in_dim(far_lse, first_row, group_size * sub_rows, 1).reshape(
            2, group_size, sub_rows, HEADS
        )
        delta_part = lax.dynamic_slice_in_dim(
            far_delta, first_row, group_size * sub_rows, 1
        ).reshape(2, group_size, sub_rows, HEADS)
        tile_lse = jnp.transpose(query_tiles(lse_part, chosen), (0, 2, 1))
        tile_delta = jnp.transpose(query_tiles(delta_part, chosen), (0, 2, 1))
        tile_key = key_tiles(own_key[:, None], chosen)
        tile_value = key_tiles(own_value[:, None], chosen)
        probs = tile_probs(
            tile_query, tile_key, tile_mask(is_own, far_places, own_places), tile_lse, score_scale
        )
        dscore = tile_dscore(probs, tile_dout, tile_value, tile_delta)
        key_part = (
            jnp.einsum("thqk,tqhd->tkhd", dscore, tile_query, preferred_element_type=jnp.float32)
            * score_scale
        )
        value_part = jnp.einsum(
            "thqk,tqhd->tkhd",
            probs.astype(jnp.bfloat16),
            tile_dout,
            preferred_element_type=jnp.float32,
        )
        return (
            running[0] + slot_add(key_part, key_slot),
            running[1] + slot_add(value_part, key_slot),
        )

    grad_query_sum = sweep_piece(
        query_start,
        (
            lax.all_gather(key_slots, "ctx", axis=1, tiled=True),
            lax.all_gather(value_slots, "ctx", axis=1, tiled=True),
        ),
        block_rows,
        my_rank,
        pair_of_rank,
        query_grad_group,
    )
    grad_key_sum, grad_value_sum = sweep_piece(
        (key_start, value_start),
        (
            lax.all_gather(query_slots, "ctx", axis=1, tiled=True),
            lax.all_gather(dout_slots, "ctx", axis=1, tiled=True),
        ),
        block_rows,
        my_rank,
        pair_of_rank,
        key_grad_group,
    )
    flat_rows = 2 * block_rows
    grad_query_low = grad_query_sum.reshape(flat_rows, model_width).astype(jnp.bfloat16)
    grad_key_low = grad_key_sum.reshape(flat_rows, model_width).astype(jnp.bfloat16)
    grad_value_low = grad_value_sum.reshape(flat_rows, model_width).astype(jnp.bfloat16)
    grad_mixed = jnp.concatenate([grad_query_low, grad_key_low, grad_value_low], axis=1)
    grad_input = jnp.einsum("rd,re->de", normed, grad_mixed, preferred_element_type=jnp.float32)
    grad_query_bias = jnp.sum(grad_query_low.astype(jnp.float32), axis=0)
    grad_value_bias = jnp.sum(grad_value_low.astype(jnp.float32), axis=0)
    grad_normed = jnp.einsum(
        "re,de->rd", grad_mixed, back_input, preferred_element_type=jnp.float32
    )
    grad_token_part, grad_first_gain, grad_first_shift = first_pullback(grad_normed)
    grad_tokens = (grad_middle + grad_token_part)[None]
    grad_local = (
        grad_first_gain,
        grad_first_shift,
        grad_input,
        grad_query_bias,
        grad_value_bias,
        grad_output,
        grad_output_bias,
        grad_second_gain,
        grad_second_shift,
        grad_expand,
        grad_expand_bias,
        grad_contract,
        grad_contract_bias,
    )
    grad_owned = (
        lax.psum_scatter(
            grad_local[0].astype(jnp.bfloat16), "dp", scatter_dimension=0, tiled=True
        ).astype(jnp.float32),
        lax.psum_scatter(
            grad_local[1].astype(jnp.bfloat16), "dp", scatter_dimension=0, tiled=True
        ).astype(jnp.float32),
        lax.psum_scatter(
            grad_local[2].astype(jnp.bfloat16), "dp", scatter_dimension=0, tiled=True
        ).astype(jnp.float32),
        lax.psum_scatter(
            grad_local[3].astype(jnp.bfloat16), "dp", scatter_dimension=0, tiled=True
        ).astype(jnp.float32),
        lax.psum_scatter(
            grad_local[4].astype(jnp.bfloat16), "dp", scatter_dimension=0, tiled=True
        ).astype(jnp.float32),
        lax.psum_scatter(
            grad_local[5].astype(jnp.bfloat16), "dp", scatter_dimension=0, tiled=True
        ).astype(jnp.float32),
        lax.psum_scatter(
            grad_local[6].astype(jnp.bfloat16), "dp", scatter_dimension=0, tiled=True
        ).astype(jnp.float32),
        lax.psum_scatter(
            grad_local[7].astype(jnp.bfloat16), "dp", scatter_dimension=0, tiled=True
        ).astype(jnp.float32),
        lax.psum_scatter(
            grad_local[8].astype(jnp.bfloat16), "dp", scatter_dimension=0, tiled=True
        ).astype(jnp.float32),
        lax.psum_scatter(
            grad_local[9].astype(jnp.bfloat16), "dp", scatter_dimension=0, tiled=True
        ).astype(jnp.float32),
        lax.psum_scatter(
            grad_local[10].astype(jnp.bfloat16), "dp", scatter_dimension=0, tiled=True
        ).astype(jnp.float32),
        lax.psum_scatter(
            grad_local[11].astype(jnp.bfloat16), "dp", scatter_dimension=0, tiled=True
        ).astype(jnp.float32),
        lax.psum_scatter(
            grad_local[12].astype(jnp.bfloat16), "dp", scatter_dimension=0, tiled=True
        ).astype(jnp.float32),
    )
    grad_final = tuple(
        lax.psum(
            (
                grad_owned[0],
                grad_owned[1],
                grad_owned[2],
                grad_owned[3],
                grad_owned[4],
                grad_owned[5],
                grad_owned[6],
                grad_owned[7],
                grad_owned[8],
                grad_owned[9],
                grad_owned[10],
                grad_owned[11],
                grad_owned[12],
            ),
            "ctx",
        )
    )
    return (block_out, grad_tokens) + tuple(grad_final)


VMEM_BYTES = 16 * 1024 * 1024
VMEM_LARGE = 28 * 1024 * 1024


def mm(left, right):
    return lax.dot_general(
        left, right, (((1,), (0,)), ((), ())), preferred_element_type=jnp.float32
    )


def mm_nt(left, right):
    return lax.dot_general(
        left, right, (((1,), (1,)), ((), ())), preferred_element_type=jnp.float32
    )


def mm_tn(left, right):
    return lax.dot_general(
        left, right, (((0,), (0,)), ((), ())), preferred_element_type=jnp.float32
    )


def aligned(index, size):
    return pl.ds(pl.multiple_of(index * size, size), size)


def norm_stats(values):
    centre = values - jnp.mean(values, axis=-1, keepdims=True)
    spread = jnp.mean(centre * centre, axis=-1, keepdims=True)
    scale = lax.rsqrt(spread + NORM_EPS)
    return centre * scale, scale


def norm_back(grad_normed, gain_row, xhat, scale):
    weighted = grad_normed * gain_row
    return scale * (
        weighted
        - jnp.mean(weighted, axis=-1, keepdims=True)
        - xhat * jnp.mean(weighted * xhat, axis=-1, keepdims=True)
    )


def column_sums(values):
    return jnp.sum(values, axis=0, keepdims=True)


def shape_of(dims, dtype):
    return jax.ShapeDtypeStruct(dims, dtype)


def local_call(
    kernel, name, outs, args, scalars=0, scratch=(), flops=0, after=(), space=pltpu.VMEM, grant=VMEM_BYTES
):
    moved = sum(math.prod(a.shape) * a.dtype.itemsize for a in tuple(args) + tuple(outs))

    def ordered(*refs):
        kernel(*refs[: len(args)], *refs[len(args) + len(after) :])

    return pl.pallas_call(
        ordered,
        out_shape=tuple(outs),
        in_specs=[pl.BlockSpec(memory_space=pltpu.SMEM)] * scalars
        + [pl.BlockSpec(memory_space=space)] * (len(args) - scalars)
        + [pl.BlockSpec(memory_space=pl.ANY)] * len(after),
        out_specs=tuple(pl.BlockSpec(memory_space=pltpu.VMEM) for _ in outs),
        scratch_shapes=list(scratch),
        compiler_params=pltpu.CompilerParams(vmem_limit_bytes=grant),
        cost_estimate=pl.CostEstimate(flops=flops, bytes_accessed=moved, transcendentals=0),
        name=name,
    )(*args, *after)


def place_of_block(pair_ref, info_ref, ranks, step, half, other_core):
    core = jnp.bitwise_xor(info_ref[2], other_core)
    rank = 2 * jnp.bitwise_xor(info_ref[1], step) + core
    pair = pair_ref[rank]
    return pair if half == 0 else 2 * ranks - 1 - pair


def fill_mask(bias_ref, pair_ref, info_ref, ranks, parts, block):
    rows = 2 * parts * block
    lanes = lax.broadcasted_iota(jnp.int32, (1, rows), 1)
    query_place = lanes % block
    for step in range(parts):
        for half in range(2):
            place = place_of_block(pair_ref, info_ref, ranks, step, half, 0)
            query_place = query_place + jnp.where(
                lanes // block == 2 * step + half, place * block, 0
            )
    ahead = lax.broadcasted_iota(jnp.int32, (block, rows), 0) - query_place
    for other in range(2):
        for step in range(parts):
            for half in range(2):
                place = place_of_block(pair_ref, info_ref, ranks, step, half, other)
                start = other * rows + (2 * step + half) * block
                bias_ref[start : start + block, :] = jnp.where(
                    ahead <= -place * block, 0.0, NEG_BIG
                )


def head_parallel(ranks, chips, seq_parts):
    parts = chips
    hw = HEADS // chips * HEAD_DIM

    def core_swap(member):
        return lax.ppermute(member, "ctx", [(i, i ^ 1) for i in range(ranks)])

    def chip_swap(member, step):
        return lax.ppermute(
            member, "ctx", [(i, 2 * ((i // 2) ^ step) + i % 2) for i in range(ranks)]
        )

    def seq_swap(member, step):
        return lax.ppermute(member, "dp", [(i, i ^ step) for i in range(seq_parts)])

    def per_device_heads(
        tokens,
        pair_of_rank,
        first_gain,
        first_shift,
        w_input,
        query_bias,
        value_bias,
        w_output,
        output_bias,
        second_gain,
        second_shift,
        w_expand,
        expand_bias,
        w_contract,
        contract_bias,
        cotangent,
    ):
        bf, f32 = jnp.bfloat16, jnp.float32
        rows, width = tokens.shape[1:]
        block = rows // 2
        own_width = width // seq_parts
        ff = expand_bias.shape[0]
        total = parts * rows
        half_width = width // 2
        half_ff = ff // 2
        sub = own_width // parts
        half_own = own_width // 2
        small_rows = 16
        others = range(1, parts)
        seq_id = lax.axis_index("dp")
        rank = lax.axis_index("ctx")
        chip = rank // 2
        core = rank % 2
        info = jnp.stack([seq_id, chip, core]).astype(jnp.int32)

        side = width - 3 * hw
        pack_rows = 2 * half_own

        def pack_kernel(info_ref, tok_ref, w_ref, wo_ref, *refs):
            vecs = refs[:8]
            packed_ref, tokens_ref, w_scr, wo_scr = refs[8:12]
            scrs, sems = refs[12:20], refs[20]
            mine = pl.ds(pl.multiple_of(info_ref[2] * half_own, half_own), half_own)
            pairs = [(w_ref.at[mine], w_scr), (wo_ref.at[mine], wo_scr), (tok_ref, tokens_ref)]
            pairs += list(zip(vecs, scrs))
            copies = [
                pltpu.make_async_copy(src, dst, sems.at[i]) for i, (src, dst) in enumerate(pairs)
            ]
            for copy in copies:
                copy.start()
            for copy in copies:
                copy.wait()
            at_w = slice(half_own, 2 * half_own)
            for at in range(chips):

                @pl.when(info_ref[1] == at)
                def _():
                    for base in range(3):
                        start = base * width + at * hw
                        packed_ref[at_w, base * hw : (base + 1) * hw] = w_scr[
                            :, start : start + hw
                        ]

            packed_ref[0:half_own, :] = wo_scr[...]
            small = jnp.concatenate(
                [v[...].astype(f32).reshape(1, own_width) for v in scrs], axis=0
            )
            small = jnp.concatenate([small, jnp.zeros_like(small)], axis=0)
            packed_ref[half_own : half_own + small_rows, 3 * hw :] = small.astype(bf)
            packed_ref[half_own + small_rows :, 3 * hw :] = jnp.zeros(
                (half_own - small_rows, side), bf
            )

        small_args = (
            first_gain,
            first_shift,
            query_bias,
            value_bias,
            output_bias,
            second_gain,
            second_shift,
            contract_bias,
        )
        packed, own_tokens = local_call(
            pack_kernel,
            "pack",
            [shape_of((pack_rows, width), bf), shape_of((rows, width), bf)],
            [info, tokens[0], w_input, w_output] + list(small_args),
            scalars=1,
            scratch=[pltpu.VMEM((half_own, 3 * width), bf), pltpu.VMEM((half_own, width), bf)]
            + [pltpu.VMEM((own_width,), bf)] * 8
            + [pltpu.SemaphoreType.DMA((11,))],
            space=pltpu.HBM,
            grant=60 * 1024 * 1024,
        )
        token_parts = [own_tokens] + [chip_swap(own_tokens, k) for k in others]
        packed_near = [seq_swap(packed, j) for j in others]

        def stack_kernel(*refs):
            depth = refs[0].shape[0]
            for i, ref in enumerate(refs[:-1]):
                refs[-1][i * depth : (i + 1) * depth, :] = ref[...]

        (packed_all,) = local_call(
            stack_kernel,
            "pack_stack",
            [shape_of(((seq_parts - 1) * pack_rows, width), bf)],
            packed_near,
            after=token_parts[1:],
        )
        packed_far = core_swap(packed_all)
        own_cot = cotangent[0]

        def pack_more_kernel(info_ref, we_ref, cot_ref, *refs):
            for j in others:
                start = pl.multiple_of(info_ref[2] * half_own, half_own)
                refs[j - 1][0:half_own, :] = we_ref[
                    pl.ds(start, half_own), aligned(jnp.bitwise_xor(info_ref[0], j), ff)
                ]
                refs[j - 1][half_own:, :] = cot_ref[...]

        more = local_call(
            pack_more_kernel,
            "pack_more",
            [shape_of((half_own + rows, width), bf)] * (seq_parts - 1),
            [info, w_expand, own_cot],
            scalars=1,
            after=[packed],
        )
        more_parts = [seq_swap(more[j - 1], j) for j in others]

        def qkv_kernel(info_ref, w_own_ref, wo_own_ref, *refs):
            toks, own_pack, packs = refs[:parts], refs[parts], refs[parts + 1 : parts + 3]
            q_ref, kv_ref, normed_ref, w_ref, vec_ref, wo_ref, vec_scr = refs[parts + 3 :]
            for at in range(chips):

                @pl.when(info_ref[1] == at)
                def _():
                    for base in range(3):
                        start = base * width + at * hw
                        w_ref[aligned(info_ref[0], own_width), base * hw : (base + 1) * hw] = (
                            w_own_ref[:, start : start + hw]
                        )

            wo_ref[info_ref[0]] = wo_own_ref[...]
            at_small = slice(half_own, half_own + small_rows)
            vec_scr[info_ref[0]] = own_pack[at_small, 3 * hw :].astype(f32)
            for j in others:
                place = jnp.bitwise_xor(info_ref[0], j)
                base = (j - 1) * pack_rows
                vec_scr[place] = packs[0][
                    base + half_own : base + half_own + small_rows, 3 * hw :
                ].astype(f32)
                for flip in range(2):
                    member = packs[flip]
                    half = jnp.bitwise_xor(info_ref[2], flip)
                    down = pl.multiple_of(half * half_own, half_own)
                    wo_ref[place, pl.ds(down, half_own), :] = member[base : base + half_own, :]
                    start = pl.multiple_of(place * own_width + half * half_own, half_own)
                    w_ref[pl.ds(start, half_own), :] = member[
                        base + half_own : base + pack_rows, 0 : 3 * hw
                    ]
            vectors = jnp.concatenate([vec_scr[j] for j in range(parts)], axis=1)
            vec_ref[...] = vectors
            chosen = vec_scr[info_ref[1]]
            for k in range(parts):
                xhat, _ = norm_stats(toks[k][...].astype(f32))
                normed_ref[k * rows : (k + 1) * rows, :] = (
                    xhat * vectors[0:1] + vectors[1:2]
                ).astype(bf)
            mixed = mm(normed_ref[...], w_ref[...])
            q_ref[...] = (mixed[:, 0:hw] + chosen[2:3]).astype(bf)
            kv_ref[:, 0:hw] = mixed[:, hw : 2 * hw].astype(bf)
            kv_ref[:, hw : 2 * hw] = (mixed[:, 2 * hw :] + chosen[3:4]).astype(bf)

        query, own_kv, normed, w_heads_full, vectors, out_full = local_call(
            qkv_kernel,
            "project",
            [
                shape_of((total, hw), bf),
                shape_of((total, 2 * hw), bf),
                shape_of((total, width), bf),
                shape_of((width, 3 * hw), bf),
                shape_of((small_rows, width), f32),
                shape_of((parts, own_width, width), bf),
            ],
            [info, w_input, w_output] + token_parts + [packed, packed_all, packed_far],
            scalars=1,
            scratch=[pltpu.VMEM((parts, small_rows, own_width), f32)],
            flops=2 * total * width * 3 * hw,
        )
        far_kv = core_swap(own_kv)

        head_count = hw // HEAD_DIM
        scale = HEAD_DIM ** (-0.5)

        def head_columns(ref, base, head):
            start = base + head * HEAD_DIM
            return ref[:, start : start + HEAD_DIM]

        def attend_kernel(info_ref, pair_ref, q_ref, kv_ref, far_ref, *refs):
            outs = refs[:parts]
            flat_ref, lse_ref, bias_ref = refs[parts:]
            fill_mask(bias_ref, pair_ref, info_ref, ranks, parts, block)
            columns = []
            for head in range(head_count):
                keys = jnp.concatenate(
                    [head_columns(kv_ref, 0, head), head_columns(far_ref, 0, head)], axis=0
                )
                values = jnp.concatenate(
                    [head_columns(kv_ref, hw, head), head_columns(far_ref, hw, head)], axis=0
                )
                scores = mm_nt(keys, head_columns(q_ref, 0, head)) * scale + bias_ref[...]
                peak = jnp.max(scores, axis=0, keepdims=True)
                weights = jnp.exp(scores - peak)
                mass = jnp.sum(weights, axis=0, keepdims=True)
                lse_ref[head : head + 1, :] = peak + jnp.log(mass)
                mixed = mm_tn(values, weights.astype(bf)) / mass
                flat_ref[head * HEAD_DIM : (head + 1) * HEAD_DIM, :] = mixed
            attended = flat_ref[...].T.astype(bf)
            for k in range(parts):
                outs[k][...] = attended[k * rows : (k + 1) * rows]

        attend_out = local_call(
            attend_kernel,
            "attend",
            [shape_of((rows, hw), bf)] * parts
            + [shape_of((hw, total), f32), shape_of((8, total), f32)],
            [info, pair_of_rank, query, own_kv, far_kv],
            scalars=2,
            scratch=[pltpu.VMEM((2 * total, total), f32)],
            flops=2 * 2 * head_count * 2 * total * total * HEAD_DIM,
            grant=VMEM_LARGE,
        )
        flat_attended, row_lse = attend_out[parts:]
        att_parts = [attend_out[0]] + [chip_swap(attend_out[k], k) for k in others]

        def middle_kernel(info_ref, tok_ref, vec_ref, w_ref, *refs):
            atts = refs[:parts]
            mid_ref, normed_ref = refs[parts:]
            middle = tok_ref[...].astype(f32) + vec_ref[4:5]
            for k in range(parts):
                middle = middle + mm(atts[k][...], w_ref[jnp.bitwise_xor(info_ref[1], k)])
            mid_ref[...] = middle
            xhat, _ = norm_stats(middle)
            normed_ref[...] = (xhat * vec_ref[5:6] + vec_ref[6:7]).astype(bf)

        middle, own_normed_two = local_call(
            middle_kernel,
            "middle",
            [shape_of((rows, width), f32), shape_of((rows, width), bf)],
            [info, own_tokens, vectors, out_full] + att_parts,
            scalars=1,
            flops=2 * rows * width * width,
        )

        def expand_stack_kernel(*refs):
            for i, ref in enumerate(refs[:-1]):
                refs[-1][i * half_own : (i + 1) * half_own, :] = ref[0:half_own, :]

        (expand_all,) = local_call(
            expand_stack_kernel,
            "expand_stack",
            [shape_of(((seq_parts - 1) * half_own, ff), bf)],
            more_parts,
            after=[own_normed_two],
        )
        expand_far = core_swap(expand_all)
        n2_parts = [own_normed_two] + [seq_swap(own_normed_two, j) for j in others]

        span = ff // parts + own_width

        def ffn_kernel(info_ref, bias_ref, wc_ref, we_ref, own_cot_ref, far_we_ref, *refs):
            n2s = refs[:parts]
            mores = refs[parts : 2 * parts - 1]
            gns = refs[2 * parts - 1 : 3 * parts - 1]
            results = refs[3 * parts - 1 : 4 * parts - 1]
            keep_ref, send_ref, sum_ref = refs[4 * parts - 1 : 4 * parts + 2]
            active_ref, gh_ref, n2_ref, cot_ref, w_scr, scr = refs[4 * parts + 2 :]
            w_scr[aligned(info_ref[0], own_width), :] = we_ref[:, aligned(info_ref[0], ff)]
            for j in range(seq_parts):
                at = slice(j * rows, (j + 1) * rows)
                n2_ref[at, :] = n2s[j][...]
                if j == 0:
                    cot_ref[at, :] = own_cot_ref[...]
                    continue
                place = jnp.bitwise_xor(info_ref[0], j)
                for flip in range(2):
                    half = jnp.bitwise_xor(info_ref[2], flip)
                    start = pl.multiple_of(place * own_width + half * half_own, half_own)
                    w_scr[pl.ds(start, half_own), :] = (
                        far_we_ref[(j - 1) * half_own : j * half_own, :]
                        if flip
                        else mores[j - 1][0:half_own, :]
                    )
                cot_ref[at, :] = mores[j - 1][half_own:, :]
            hidden = mm(n2_ref[...], w_scr[...]) + bias_ref[...].astype(f32).reshape(1, ff)
            square = hidden * hidden
            curve = jnp.tanh(GELU_SCALE * hidden * (1.0 + GELU_CUBIC * square))
            active_ref[...] = (0.5 * hidden * (1.0 + curve)).astype(bf)
            slope = 0.5 * (1.0 + curve) + 0.5 * hidden * (1.0 - curve * curve) * GELU_SCALE * (
                1.0 + 3.0 * GELU_CUBIC * square
            )
            grad_hidden = mm_nt(cot_ref[...], wc_ref[...]) * slope
            gh_ref[...] = grad_hidden.astype(bf)
            sum_ref[...] = column_sums(gh_ref[...].astype(f32))
            grad = mm_nt(gh_ref[...], w_scr[...]).astype(bf)
            for j in range(parts):
                gns[j][...] = grad[j * rows : (j + 1) * rows]
            result = mm(active_ref[...], wc_ref[...]).astype(bf)
            for j in range(seq_parts):
                results[j][...] = result[j * rows : (j + 1) * rows]
            core_id = info_ref[2]
            for flip, out_ref in ((0, keep_ref), (1, send_ref)):
                half = jnp.bitwise_xor(core_id, flip)
                scr[...] = mm_tn(active_ref[...], cot_ref[:, aligned(half, half_width)]).astype(bf)
                for part in range(parts):
                    rows_to = ff // parts
                    out_ref[part, 0:rows_to, :] = scr[part * rows_to : (part + 1) * rows_to, :]
                scr[...] = mm_tn(n2_ref[...], gh_ref[:, aligned(half, half_ff)]).astype(bf)
                for part in range(parts):
                    for j in range(seq_parts):
                        at = ff // parts + j * sub
                        row = j * own_width + part * sub
                        out_ref[part, at : at + sub, :] = scr[row : row + sub, :]

        ffn_out = local_call(
            ffn_kernel,
            "feed",
            [shape_of((rows, width), bf)] * 2 * parts
            + [
                shape_of((parts, span, half_width), bf),
                shape_of((parts, span, half_width), bf),
                shape_of((1, ff), f32),
            ],
            [info, expand_bias, w_contract, w_expand, own_cot, expand_far] + n2_parts + more_parts,
            scalars=1,
            scratch=[
                pltpu.VMEM((total, ff), bf),
                pltpu.VMEM((total, ff), bf),
                pltpu.VMEM((total, width), bf),
                pltpu.VMEM((total, width), bf),
                pltpu.VMEM((width, ff), bf),
                pltpu.VMEM((width, half_ff), bf),
            ],
            flops=6 * 2 * total * width * ff,
            grant=VMEM_LARGE,
        )
        results = ffn_out[parts : 2 * parts]
        ffn_keep, ffn_send, grad_expand_row = ffn_out[2 * parts :]
        gn_parts = [ffn_out[0]] + [seq_swap(ffn_out[j], j) for j in others]
        ffn_far = core_swap(ffn_send)

        def halve_kernel(info_ref, keep_ref, far_ref, own_ref, out_ref):
            for k in range(parts):
                at = jnp.bitwise_xor(info_ref[1], k)
                piece = keep_ref[at].astype(f32) + far_ref[at].astype(f32)
                if k % 2:
                    out_ref[k // 2] = piece.astype(bf)
                else:
                    own_ref[k // 2] = piece

        rs_own, rs_send = local_call(
            halve_kernel,
            "feed_halves",
            [
                shape_of((parts // 2, span, half_width), f32),
                shape_of((parts // 2, span, half_width), bf),
            ],
            [info, ffn_keep, ffn_far],
            scalars=1,
        )
        rs_far = chip_swap(rs_send, 1)

        def back_kernel(info_ref, mid_ref, vec_ref, cot_ref, w_ref, *refs):
            gns = refs[:parts]
            douts = refs[parts : 2 * parts]
            gmid_ref, branch_ref, sums_ref = refs[2 * parts :]
            grad = gns[0][...].astype(f32)
            for j in others:
                grad = grad + gns[j][...].astype(f32)
            xhat, spread = norm_stats(mid_ref[...])
            cot = cot_ref[...].astype(f32)
            grad_middle = cot + norm_back(grad, vec_ref[5:6], xhat, spread)
            gmid_ref[...] = grad_middle
            branch = grad_middle.astype(bf)
            branch_ref[...] = branch
            for k in range(parts):
                douts[k][...] = mm_nt(branch, w_ref[jnp.bitwise_xor(info_ref[1], k)]).astype(bf)
            sums_ref[0:1, :] = column_sums(branch.astype(f32))
            sums_ref[1:2, :] = column_sums(grad * xhat)
            sums_ref[2:3, :] = column_sums(grad)
            sums_ref[3:4, :] = column_sums(cot)

        back_out = local_call(
            back_kernel,
            "middle_back",
            [shape_of((rows, hw), bf)] * parts
            + [
                shape_of((rows, width), f32),
                shape_of((rows, width), bf),
                shape_of((8, width), f32),
            ],
            [info, middle, vectors, own_cot, out_full] + gn_parts,
            scalars=1,
            after=[rs_send],
            flops=2 * rows * width * width,
        )
        grad_middle, grad_branch, late_sums = back_out[parts:]
        dout_parts = [back_out[0]] + [chip_swap(back_out[k], k) for k in others]

        def out_weights_kernel(info_ref, branch_ref, *refs):
            atts = refs[:parts]
            keep_ref, send_ref = refs[parts:]
            for flip, out_ref in ((0, keep_ref), (1, send_ref)):
                half = jnp.bitwise_xor(info_ref[2], flip)
                piece = branch_ref[:, aligned(half, half_width)]
                for k in range(parts):
                    out_ref[jnp.bitwise_xor(info_ref[1], k)] = mm_tn(atts[k][...], piece).astype(bf)

        out_keep, out_send = local_call(
            out_weights_kernel,
            "output_weights",
            [shape_of((parts, hw, half_width), bf)] * 2,
            [info, grad_branch] + att_parts,
            scalars=1,
            flops=2 * rows * width * width,
        )
        out_far = core_swap(out_send)

        def quarter_kernel(own_ref, far_ref, keep_ref, send_ref):
            keep_ref[...] = own_ref[0] + far_ref[0].astype(f32)
            send_ref[...] = (own_ref[1] + far_ref[1].astype(f32)).astype(bf)

        rs_own_two, rs_send_two = local_call(
            quarter_kernel,
            "feed_quarters",
            [shape_of((span, half_width), f32), shape_of((span, half_width), bf)],
            [rs_own, rs_far],
            after=[dout_parts[parts - 1]],
        )
        rs_far_two = chip_swap(rs_send_two, 2)

        def attend_back_kernel(info_ref, pair_ref, q_ref, kv_ref, far_ref, flat_ref, lse_ref, *refs):
            douts = refs[:parts]
            dq_ref, own_ref, send_ref, bias_ref, dout_ref = refs[parts:]
            fill_mask(bias_ref, pair_ref, info_ref, ranks, parts, block)
            for k in range(parts):
                dout_ref[k * rows : (k + 1) * rows, :] = douts[k][...].astype(f32)
            flat_dout = dout_ref[...].T
            for head in range(head_count):
                at = slice(head * HEAD_DIM, (head + 1) * HEAD_DIM)
                keys = jnp.concatenate(
                    [head_columns(kv_ref, 0, head), head_columns(far_ref, 0, head)], axis=0
                )
                values = jnp.concatenate(
                    [head_columns(kv_ref, hw, head), head_columns(far_ref, hw, head)], axis=0
                )
                queries = head_columns(q_ref, 0, head)
                dout = dout_ref[:, at].astype(bf)
                dout_turned = flat_dout[at, :]
                delta = column_sums(dout_turned * flat_ref[at, :])
                scores = mm_nt(keys, queries) * scale + bias_ref[...]
                probs = jnp.exp(scores - lse_ref[head : head + 1, :])
                grad_value = mm(probs.astype(bf), dout)
                grad_weights = mm(values, dout_turned.astype(bf))
                grad_scores = (probs * (grad_weights - delta)).astype(bf)
                grad_key = mm(grad_scores, queries) * scale
                dq_ref[at, :] = mm_tn(keys, grad_scores) * scale
                vat = slice(hw + head * HEAD_DIM, hw + (head + 1) * HEAD_DIM)
                own_ref[:, at] = grad_key[0:total]
                own_ref[:, vat] = grad_value[0:total]
                send_ref[:, at] = grad_key[total:].astype(bf)
                send_ref[:, vat] = grad_value[total:].astype(bf)

        flat_dq, dkv_own, dkv_send = local_call(
            attend_back_kernel,
            "attend_back",
            [
                shape_of((hw, total), f32),
                shape_of((total, 2 * hw), f32),
                shape_of((total, 2 * hw), bf),
            ],
            [info, pair_of_rank, query, own_kv, far_kv, flat_attended, row_lse] + dout_parts,
            scalars=2,
            after=[rs_send_two, out_send],
            scratch=[pltpu.VMEM((2 * total, total), f32), pltpu.VMEM((total, hw), f32)],
            flops=5 * 2 * head_count * 2 * total * total * HEAD_DIM,
            grant=VMEM_LARGE,
        )
        dkv_far = core_swap(dkv_send)

        def normed_back_kernel(dq_ref, own_ref, far_ref, w_ref, *refs):
            toks = refs[:parts]
            keep_ref, send_ref, mixed_ref, sums_ref, bias_ref = refs[parts:]
            mixed_ref[:, 0:hw] = dq_ref[...].T.astype(bf)
            mixed_ref[:, hw:] = (own_ref[...] + far_ref[...].astype(f32)).astype(bf)
            shift_sum = jnp.zeros((1, width), f32)
            gain_sum = jnp.zeros((1, width), f32)
            for k in range(parts):
                grad = mm_nt(mixed_ref[k * rows : (k + 1) * rows, :], w_ref[...])
                if k % 2:
                    send_ref[k // 2] = grad.astype(bf)
                else:
                    keep_ref[k // 2] = grad
                xhat, _ = norm_stats(toks[k][...].astype(f32))
                shift_sum = shift_sum + column_sums(grad)
                gain_sum = gain_sum + column_sums(grad * xhat)
            sums_ref[0:1, :] = gain_sum
            sums_ref[1:2, :] = shift_sum
            bias_ref[0:1, :] = column_sums(mixed_ref[...].astype(f32))

        nb_out = local_call(
            normed_back_kernel,
            "normed_back",
            [
                shape_of((parts // 2, rows, width), f32),
                shape_of((parts // 2, rows, width), bf),
                shape_of((total, 3 * hw), bf),
                shape_of((8, width), f32),
                shape_of((8, 3 * hw), f32),
            ],
            [flat_dq, dkv_own, dkv_far, w_heads_full] + token_parts,
            flops=2 * total * width * 3 * hw,
        )
        gt_keep, gt_send, grad_mixed, first_sums, mixed_sums = nb_out
        gt_far = chip_swap(gt_send, 1)


        def input_weights_kernel(
            info_ref, normed_ref, mixed_ref, first_ref, bias_ref, late_ref, row_ref, *refs
        ):
            keep_ref, send_ref, grad_scr, small_scr = refs
            grad_scr[...] = mm_tn(normed_ref[...], mixed_ref[...])
            core_id, chip_id, seq = info_ref[2], info_ref[1], info_ref[0]
            small_scr[...] = jnp.zeros_like(small_scr)
            for j in range(seq_parts):
                at = slice(j * own_width, (j + 1) * own_width)
                small_scr[j, 0:2, :] = first_ref[0:2, at]
                small_scr[j, 4:8, :] = late_ref[0:4, at]
            small_scr[chip_id, 2:3, :] = bias_ref[0:1, 0:hw]
            small_scr[chip_id, 3:4, :] = bias_ref[0:1, 2 * hw : 3 * hw]
            for j in range(ff // own_width):
                small_scr[seq, 8 + j : 9 + j, :] = row_ref[:, j * own_width : (j + 1) * own_width]
            for flip, out_ref in ((0, keep_ref), (1, send_ref)):
                half = jnp.bitwise_xor(core_id, flip)
                for j in range(seq_parts):
                    start = pl.multiple_of(j * own_width + half * half_own, 16)
                    out_ref[j, :, 0 : 3 * hw] = grad_scr[pl.ds(start, half_own), :].astype(bf)
                    out_ref[j, 0:small_rows, 3 * hw :] = small_scr[j].astype(bf)
                    out_ref[j, small_rows:, 3 * hw :] = jnp.zeros(
                        (half_own - small_rows, side), bf
                    )

        in_keep, in_send = local_call(
            input_weights_kernel,
            "input_weights",
            [shape_of((seq_parts, half_own, width), bf)] * 2,
            [info, normed, grad_mixed, first_sums, mixed_sums, late_sums, grad_expand_row],
            scalars=1,
            scratch=[
                pltpu.VMEM((width, 3 * hw), f32),
                pltpu.VMEM((seq_parts, small_rows, own_width), f32),
            ],
            flops=2 * total * width * 3 * hw,
        )
        in_far = core_swap(in_send)

        fold = own_width // 2
        rider = -(-sub // 32) * 16
        at_outs = slice(half_own, half_own + fold)

        def fold_in(value):
            down = value.shape[0] // 2
            return jnp.concatenate([value[0:down], value[down:]], axis=1)

        def fold_out(value):
            across = value.shape[1] // 2
            return jnp.concatenate([value[:, 0:across], value[:, across:]], axis=0)

        def dp_pack_kernel(
            info_ref, own_ref, far_two_ref, keep_ref, far_ref, ok_ref, of_ref, gk_ref, gf_ref, *refs
        ):
            con_ref, gown_ref, gsend_ref, scr = refs[seq_parts:]
            whole = own_ref[...] + far_two_ref[...].astype(f32)
            con_ref[...] = whole[0 : ff // parts].astype(bf)
            scr[...] = whole[ff // parts :]
            for j in range(seq_parts):
                at = jnp.bitwise_xor(info_ref[0], j)
                refs[j][0:half_own, :] = (
                    keep_ref[at].astype(f32) + far_ref[at].astype(f32)
                ).astype(bf)
                refs[j][at_outs, :] = fold_in(ok_ref[at].astype(f32) + of_ref[at].astype(f32)).astype(
                    bf
                )
                piece = fold_in(scr[aligned(at, sub), :])
                piece = jnp.concatenate(
                    [piece, jnp.zeros((rider - sub // 2, width), f32)], axis=0
                )
                refs[j][half_own + fold :, :] = piece.astype(bf)
            gown_ref[...] = gk_ref[0] + gf_ref[0].astype(f32)
            gsend_ref[...] = (gk_ref[1] + gf_ref[1].astype(f32)).astype(bf)

        dp_out = local_call(
            dp_pack_kernel,
            "owners",
            [shape_of((half_own + fold + rider, width), bf)] * seq_parts
            + [
                shape_of((ff // parts, half_width), bf),
                shape_of((rows, width), f32),
                shape_of((rows, width), bf),
            ],
            [info, rs_own_two, rs_far_two, in_keep, in_far, out_keep, out_far, gt_keep, gt_far],
            scalars=1,
            scratch=[pltpu.VMEM((own_width, half_ff), f32)],
        )
        dp_parts = [dp_out[0]] + [seq_swap(dp_out[j], j) for j in others]
        con_one, gt_own, gt_send_two = dp_out[seq_parts:]
        con_two = chip_swap(con_one, 2)
        gt_far_two = chip_swap(gt_send_two, 2)

        con_one_far = chip_swap(con_one, 1)
        con_two_far = chip_swap(con_two, 1)

        def dp_sum_kernel(info_ref, *refs):
            owned = refs[:seq_parts]
            last_ref, scr = refs[seq_parts:]
            whole = owned[0][0 : half_own + fold, :].astype(f32)
            for j in others:
                whole = whole + owned[j][0 : half_own + fold, :].astype(f32)
            last_ref[0 : half_own + fold, :] = whole.astype(bf)
            for j in range(seq_parts):
                place = jnp.bitwise_xor(info_ref[0], j)
                piece = owned[j][half_own + fold :, :].astype(f32)
                scr[aligned(place, sub), :] = fold_out(piece[0 : sub // 2])
            last_ref[half_own + fold :, :] = fold_in(scr[...]).astype(bf)

        (last_one,) = local_call(
            dp_sum_kernel,
            "shares",
            [shape_of((half_own + 2 * fold, width), bf)],
            [info] + dp_parts,
            scalars=1,
            scratch=[pltpu.VMEM((own_width, half_ff), f32)],
            after=[con_one_far, con_two_far, gt_far_two],
        )
        last_two = chip_swap(last_one, 2)
        last_one_far = chip_swap(last_one, 1)
        last_two_far = chip_swap(last_two, 1)
        last_parts = [last_one, last_one_far, last_two, last_two_far]
        last_far = [core_swap(member) for member in last_parts]
        con_parts = [con_one, con_one_far, con_two, con_two_far]
        con_far = [core_swap(member) for member in con_parts]

        def contract_kernel(info_ref, *refs):
            con_ref, done_ref = refs[2 * parts :]
            done_ref[...] = jnp.zeros_like(done_ref)
            for flip in range(2):
                lanes = aligned(jnp.bitwise_xor(info_ref[2], flip), half_width)
                for k in range(parts):
                    at = jnp.bitwise_xor(info_ref[1], k)
                    con_ref[aligned(at, ff // parts), lanes] = refs[flip * parts + k][...].astype(
                        f32
                    )

        grad_contract, contract_done = local_call(
            contract_kernel,
            "contract_final",
            [shape_of((ff, width), f32), shape_of((8, 128), f32)],
            [info] + con_parts + con_far,
            scalars=1,
        )

        res_parts = [results[0]] + [seq_swap(results[j], j) for j in others]

        def result_kernel(mid_ref, vec_ref, *refs):
            result = mid_ref[...] + vec_ref[7:8]
            for j in range(seq_parts):
                result = result + refs[j][...].astype(f32)
            refs[seq_parts][0] = result.astype(bf)

        (block_out,) = local_call(
            result_kernel,
            "result",
            [shape_of((1, rows, width), bf)],
            [middle, vectors] + res_parts,
            after=[last_one],
        )

        def tokens_kernel(tok_ref, vec_ref, gmid_ref, own_ref, far_ref, out_ref):
            grad = own_ref[...] + far_ref[...].astype(f32)
            xhat, spread = norm_stats(tok_ref[...].astype(f32))
            out_ref[0] = gmid_ref[...] + norm_back(grad, vec_ref[0:1], xhat, spread)

        (grad_tokens,) = local_call(
            tokens_kernel,
            "tokens_back",
            [shape_of((1, rows, width), f32)],
            [own_tokens, vectors, grad_middle, gt_own, gt_far_two],
        )

        def last_kernel(info_ref, *refs):
            gin_ref, gout_ref, exp_ref = refs[2 * parts : 2 * parts + 3]
            bias_ref, smalls, scr = refs[2 * parts + 3], refs[2 * parts + 4 : -1], refs[-1]
            for flip in range(2):
                half = jnp.bitwise_xor(info_ref[2], flip)
                outs = jnp.zeros((fold, width), f32)
                for k in range(parts):
                    at = jnp.bitwise_xor(info_ref[1], k)
                    piece = refs[flip * parts + k][...].astype(f32)
                    scr[at, aligned(half, half_own), :] = piece[0:half_own, 0 : 3 * hw]
                    outs = outs + piece[at_outs]
                    turned = fold_out(piece[half_own + fold :])
                    for j in range(seq_parts):
                        cols = pl.ds(pl.multiple_of(j * ff + half * half_ff, 128), half_ff)
                        exp_ref[aligned(at, sub), cols] = turned[j * sub : (j + 1) * sub]
                gout_ref[:, aligned(half, half_width)] = fold_out(outs)
            for at in range(parts):
                for base in range(3):
                    start = base * width + at * hw
                    gin_ref[:, start : start + hw] = scr[at, :, base * hw : (base + 1) * hw]
            small = refs[0][0:small_rows, 3 * hw :].astype(f32)
            for k in others:
                small = small + refs[k][0:small_rows, 3 * hw :].astype(f32)
            for i in range(8):
                smalls[i][...] = small[i : i + 1].reshape(own_width)
            bias_ref[...] = jnp.concatenate(
                [small[8 + i : 9 + i] for i in range(ff // own_width)], axis=1
            ).reshape(ff)

        last_out = local_call(
            last_kernel,
            "weights_final",
            [
                shape_of((own_width, 3 * width), f32),
                shape_of((own_width, width), f32),
                shape_of((own_width, seq_parts * ff), f32),
                shape_of((ff,), f32),
            ]
            + [shape_of((own_width,), f32)] * 8,
            [info] + last_parts + last_far,
            scalars=1,
            scratch=[pltpu.VMEM((parts, own_width, 3 * hw), f32)],
            after=[contract_done],
            grant=VMEM_LARGE,
        )
        grad_input, grad_output, grad_expand, grad_expand_bias = last_out[:4]
        small_of = last_out[4:]
        return (
            block_out,
            grad_tokens,
            small_of[0],
            small_of[1],
            grad_input,
            small_of[2],
            small_of[3],
            grad_output,
            small_of[4],
            small_of[5],
            small_of[6],
            grad_expand,
            grad_expand_bias,
            grad_contract,
            small_of[7],
        )

    return per_device_heads


def solution(mesh):
    ranks = mesh.shape["ctx"]
    chips = ranks // 2
    if chips == mesh.shape["dp"] and HEADS % chips == 0 and chips & (chips - 1) == 0:
        body = head_parallel(ranks, chips, mesh.shape["dp"])
    else:
        body = per_device
    return jax.shard_map(
        body,
        mesh=mesh,
        in_specs=(
            P("dp", "ctx", None),
            P(),
            P("dp"),
            P("dp"),
            P("dp", None),
            P("dp"),
            P("dp"),
            P("dp", None),
            P("dp"),
            P("dp"),
            P("dp"),
            P("dp", None),
            P("dp"),
            P("dp", None),
            P("dp"),
            P("dp", "ctx", None),
        ),
        out_specs=(
            P("dp", "ctx", None),
            P("dp", "ctx", None),
            P("dp"),
            P("dp"),
            P("dp", None),
            P("dp"),
            P("dp"),
            P("dp", None),
            P("dp"),
            P("dp"),
            P("dp"),
            P("dp", None),
            P("dp"),
            P("dp", None),
            P("dp"),
        ),
        check_vma=False,
    )
```

```python
import math

import jax
import jax.numpy as jnp
from jax import lax
from jax.experimental import pallas as pl
from jax.experimental.pallas import tpu as pltpu
from jax.sharding import PartitionSpec as P

HEADS = 12
HEAD_DIM = 64


NEG_BIG = -1e30
NORM_EPS = 1e-05
GELU_SCALE = 0.7978845608028654
GELU_CUBIC = 0.044715


def gelu_tanh(values):
    return (
        0.5
        * values
        * (1.0 + jnp.tanh(GELU_SCALE * (values + GELU_CUBIC * values * values * values)))
    )


def layer_norm(values, gain_row, shift_row):
    centre = values - jnp.mean(values, axis=-1, keepdims=True)
    spread = jnp.mean(centre * centre, axis=-1, keepdims=True)
    return centre * lax.rsqrt(spread + NORM_EPS) * gain_row + shift_row


def lookup_pair(pair_table, positions):
    ranks_all = jnp.arange(pair_table.shape[0], dtype=jnp.int32)
    return jnp.sum(jnp.where(positions[..., None] == ranks_all, pair_table, 0), axis=-1)


def group_count(blocks, sub_rows):
    chosen_count = 1
    for candidate in range(1, blocks + 1):
        if blocks % candidate == 0 and candidate * sub_rows <= max(512, sub_rows):
            chosen_count = candidate
    return chosen_count


def slot_mask(slot_ids, wanted, rank_count):
    return (slot_ids == wanted).reshape((-1,) + (1,) * (rank_count - 1))


def slot_add(values, slot_ids):
    early_sum = jnp.sum(jnp.where(slot_mask(slot_ids, 0, values.ndim), values, 0.0), axis=0)
    late_sum = jnp.sum(jnp.where(slot_mask(slot_ids, 1, values.ndim), values, 0.0), axis=0)
    return jnp.stack([early_sum, late_sum])


def slot_max(values, slot_ids):
    early_max = jnp.max(jnp.where(slot_mask(slot_ids, 0, values.ndim), values, NEG_BIG), axis=0)
    late_max = jnp.max(jnp.where(slot_mask(slot_ids, 1, values.ndim), values, NEG_BIG), axis=0)
    return jnp.stack([early_max, late_max])


def slot_pick(per_slot, slot_ids):
    return jnp.where(slot_mask(slot_ids, 0, per_slot.ndim), per_slot[0][None], per_slot[1][None])


def query_tiles(blocks, chosen):
    target = chosen.shape + blocks.shape[2:]
    chosen_view = chosen.reshape((-1,) + (1,) * (blocks.ndim - 2))
    late_part = jnp.broadcast_to(blocks[1], target)
    picked = jnp.where(chosen_view, blocks[0], blocks[1])
    return jnp.concatenate([late_part, picked], axis=0)


def key_tiles(blocks, chosen):
    target = chosen.shape + blocks.shape[2:]
    chosen_view = chosen.reshape((-1,) + (1,) * (blocks.ndim - 2))
    early_part = jnp.broadcast_to(blocks[0], target)
    picked = jnp.where(chosen_view, blocks[0], blocks[1])
    return jnp.concatenate([early_part, picked], axis=0)


def tile_slots(chosen):
    late_slot = jnp.where(chosen, 0, 1).astype(jnp.int32)
    query_slot = jnp.concatenate([jnp.ones_like(late_slot), late_slot])
    key_slot = jnp.concatenate([jnp.zeros_like(late_slot), late_slot])
    return (query_slot, key_slot)


def tile_mask(is_own, query_places, key_places):
    visible = key_places[:, None, :] <= query_places[:, :, None]
    visible = jnp.logical_or(visible, jnp.logical_not(is_own)[:, None, None])
    return jnp.concatenate([jnp.ones_like(visible), visible], axis=0)


def tile_scores(tile_query, tile_key, score_scale):
    return (
        jnp.einsum("tqhd,tkhd->thqk", tile_query, tile_key, preferred_element_type=jnp.float32)
        * score_scale
    )


def tile_probs(tile_query, tile_key, tile_visible, row_lse, score_scale):
    scores = tile_scores(tile_query, tile_key, score_scale)
    return jnp.where(tile_visible[:, None], jnp.exp(scores - row_lse[..., None]), 0.0)


def tile_dscore(probs, tile_dout, tile_value, row_delta):
    grad_probs = jnp.einsum(
        "tqhd,tkhd->thqk", tile_dout, tile_value, preferred_element_type=jnp.float32
    )
    return (probs * (grad_probs - row_delta[..., None])).astype(jnp.bfloat16)


def stats_update(running, tile_query, tile_key, query_slot, tile_visible, score_scale):
    run_peak, run_total = running
    visible = tile_visible[:, None]
    masked = jnp.where(visible, tile_scores(tile_query, tile_key, score_scale), NEG_BIG)
    new_peak = jnp.maximum(run_peak, slot_max(jnp.max(masked, axis=-1), query_slot))
    weights = jnp.where(visible, jnp.exp(masked - slot_pick(new_peak, query_slot)[..., None]), 0.0)
    run_total = run_total * jnp.exp(run_peak - new_peak) + slot_add(
        jnp.sum(weights, axis=-1), query_slot
    )
    return (new_peak, run_total)


def values_update(
    running, tile_query, tile_key, tile_value, query_slot, tile_visible, row_lse, score_scale
):
    probs = tile_probs(tile_query, tile_key, tile_visible, row_lse, score_scale)
    part_out = jnp.einsum(
        "thqk,tkhd->tqhd",
        probs.astype(jnp.bfloat16),
        tile_value,
        preferred_element_type=jnp.float32,
    )
    return running + slot_add(part_out, query_slot)


def sweep_piece(carried, pieces, block_rows, my_rank, pair_table, update):
    piece_rows = pieces[0].shape[1]
    sub_rows = math.gcd(piece_rows, block_rows)
    unit_count = piece_rows // sub_rows
    group_size = group_count(unit_count, sub_rows)

    def group_step(loop_index, running):
        offset = loop_index * (group_size * sub_rows)
        slices = tuple(
            (
                lax.dynamic_slice_in_dim(member, offset, group_size * sub_rows, 1).reshape(
                    (2, group_size, sub_rows) + member.shape[2:]
                )
                for member in pieces
            )
        )
        places = offset + jnp.arange(group_size * sub_rows, dtype=jnp.int32).reshape(
            group_size, sub_rows
        )
        far_ranks = places[:, 0] // block_rows
        far_pair = lookup_pair(pair_table, far_ranks)
        return update(running, slices, far_pair, far_ranks == my_rank, places % block_rows, offset)

    return lax.fori_loop(0, unit_count // group_size, group_step, carried)


def per_device(
    tokens,
    pair_of_rank,
    first_gain,
    first_shift,
    w_input,
    query_bias,
    value_bias,
    w_output,
    output_bias,
    second_gain,
    second_shift,
    w_expand,
    expand_bias,
    w_contract,
    contract_bias,
    cotangent,
):
    gathered = (
        lax.all_gather(first_gain, "dp", axis=0, tiled=True),
        lax.all_gather(first_shift, "dp", axis=0, tiled=True),
        lax.all_gather(w_input, "dp", axis=0, tiled=True),
        lax.all_gather(query_bias, "dp", axis=0, tiled=True),
        lax.all_gather(value_bias, "dp", axis=0, tiled=True),
        lax.all_gather(w_output, "dp", axis=0, tiled=True),
        lax.all_gather(output_bias, "dp", axis=0, tiled=True),
        lax.all_gather(second_gain, "dp", axis=0, tiled=True),
        lax.all_gather(second_shift, "dp", axis=0, tiled=True),
        lax.all_gather(w_expand, "dp", axis=0, tiled=True),
        lax.all_gather(expand_bias, "dp", axis=0, tiled=True),
        lax.all_gather(w_contract, "dp", axis=0, tiled=True),
        lax.all_gather(contract_bias, "dp", axis=0, tiled=True),
    )
    (
        full_first_gain,
        full_first_shift,
        full_input,
        full_query_bias,
        full_value_bias,
        full_output,
        full_output_bias,
        full_second_gain,
        full_second_shift,
        full_expand,
        full_expand_bias,
        full_contract,
        full_contract_bias,
    ) = gathered
    model_width = tokens.shape[2]
    block_rows = tokens.shape[1] // 2
    score_scale = HEAD_DIM ** (-0.5)
    slot_view = (2, block_rows, model_width)
    head_view = (2, block_rows, HEADS, HEAD_DIM)
    my_rank = lax.axis_index("ctx")
    my_pair = lookup_pair(pair_of_rank, my_rank)
    own_places = jnp.arange(block_rows, dtype=jnp.int32)[None, :]
    diag_mask = (own_places <= own_places.reshape(-1, 1))[None]
    zero_slot = jnp.zeros((1,), jnp.int32)

    def split_heads(member):
        return member.reshape(member.shape[:3] + (HEADS, HEAD_DIM))

    token_rows = tokens[0].astype(jnp.float32)
    normed_full, first_pullback = jax.vjp(
        layer_norm,
        token_rows,
        full_first_gain.astype(jnp.float32),
        full_first_shift.astype(jnp.float32),
    )
    normed = normed_full.astype(jnp.bfloat16)
    mixed_rows = jnp.dot(normed, full_input, preferred_element_type=jnp.float32)
    query_rows = (mixed_rows[:, :model_width] + full_query_bias.astype(jnp.float32)).astype(
        jnp.bfloat16
    )
    key_rows = mixed_rows[:, model_width : 2 * model_width].astype(jnp.bfloat16)
    value_rows = (mixed_rows[:, 2 * model_width :] + full_value_bias.astype(jnp.float32)).astype(
        jnp.bfloat16
    )
    own_query = query_rows.reshape(head_view)
    own_key = key_rows.reshape(head_view)
    own_value = value_rows.reshape(head_view)
    diag_query = own_query[0][None]
    diag_key = own_key[0][None]
    diag_value = own_value[0][None]
    key_slots = key_rows.reshape(slot_view)
    value_slots = value_rows.reshape(slot_view)
    query_slots = query_rows.reshape(slot_view)

    def stats_group(running, slices, far_pair, is_own, far_places, first_row):
        chosen = far_pair < my_pair
        query_slot, key_slot = tile_slots(chosen)
        return stats_update(
            running,
            query_tiles(own_query[:, None], chosen),
            key_tiles(split_heads(slices[0]), chosen),
            query_slot,
            tile_mask(is_own, own_places, far_places),
            score_scale,
        )

    stats_start = (
        jnp.full((2, HEADS, block_rows), NEG_BIG, jnp.float32),
        jnp.zeros((2, HEADS, block_rows), jnp.float32),
    )
    stats_start = stats_update(stats_start, diag_query, diag_key, zero_slot, diag_mask, score_scale)
    run_peak, run_total = sweep_piece(
        stats_start,
        (lax.all_gather(key_slots, "ctx", axis=1, tiled=True),),
        block_rows,
        my_rank,
        pair_of_rank,
        stats_group,
    )
    row_lse = run_peak + jnp.log(run_total)

    def values_group(running, slices, far_pair, is_own, far_places, first_row):
        chosen = far_pair < my_pair
        query_slot, key_slot = tile_slots(chosen)
        return values_update(
            running,
            query_tiles(own_query[:, None], chosen),
            key_tiles(split_heads(slices[0]), chosen),
            key_tiles(split_heads(slices[1]), chosen),
            query_slot,
            tile_mask(is_own, own_places, far_places),
            slot_pick(row_lse, query_slot),
            score_scale,
        )

    values_start = values_update(
        jnp.zeros(head_view, jnp.float32),
        diag_query,
        diag_key,
        diag_value,
        zero_slot,
        diag_mask,
        row_lse[0][None],
        score_scale,
    )
    attended = sweep_piece(
        values_start,
        (
            lax.all_gather(key_slots, "ctx", axis=1, tiled=True),
            lax.all_gather(value_slots, "ctx", axis=1, tiled=True),
        ),
        block_rows,
        my_rank,
        pair_of_rank,
        values_group,
    )
    attended_low = attended.reshape(2 * block_rows, model_width).astype(jnp.bfloat16)
    middle = (
        token_rows
        + jnp.dot(attended_low, full_output, preferred_element_type=jnp.float32)
        + full_output_bias.astype(jnp.float32)
    )
    normed_full_two, second_pullback = jax.vjp(
        layer_norm,
        middle,
        full_second_gain.astype(jnp.float32),
        full_second_shift.astype(jnp.float32),
    )
    normed_two = normed_full_two.astype(jnp.bfloat16)
    hidden = jnp.dot(
        normed_two, full_expand, preferred_element_type=jnp.float32
    ) + full_expand_bias.astype(jnp.float32)
    active_full, gelu_pullback = jax.vjp(gelu_tanh, hidden)
    active_low = active_full.astype(jnp.bfloat16)
    result = (
        middle
        + jnp.dot(active_low, full_contract, preferred_element_type=jnp.float32)
        + full_contract_bias.astype(jnp.float32)
    )
    block_out = result.astype(jnp.bfloat16)[None]
    back_input, back_output, back_expand, back_contract = (
        lax.all_gather(w_input, "dp", axis=0, tiled=True),
        lax.all_gather(w_output, "dp", axis=0, tiled=True),
        lax.all_gather(w_expand, "dp", axis=0, tiled=True),
        lax.all_gather(w_contract, "dp", axis=0, tiled=True),
    )
    grad_out_low = cotangent[0]
    grad_out = grad_out_low.astype(jnp.float32)
    grad_contract = jnp.einsum(
        "rf,rd->fd", active_low, grad_out_low, preferred_element_type=jnp.float32
    )
    grad_contract_bias = jnp.sum(grad_out, axis=0)
    grad_active = jnp.einsum(
        "rd,fd->rf", grad_out_low, back_contract, preferred_element_type=jnp.float32
    )
    grad_hidden = gelu_pullback(grad_active)[0].astype(jnp.bfloat16)
    grad_expand = jnp.einsum(
        "rd,rf->df", normed_two, grad_hidden, preferred_element_type=jnp.float32
    )
    grad_expand_bias = jnp.sum(grad_hidden.astype(jnp.float32), axis=0)
    grad_normed_two = jnp.einsum(
        "rf,df->rd", grad_hidden, back_expand, preferred_element_type=jnp.float32
    )
    grad_middle_part, grad_second_gain, grad_second_shift = second_pullback(grad_normed_two)
    grad_middle = grad_out + grad_middle_part
    grad_branch = grad_middle.astype(jnp.bfloat16)
    grad_output = jnp.einsum(
        "rd,re->de", attended_low, grad_branch, preferred_element_type=jnp.float32
    )
    grad_output_bias = jnp.sum(grad_branch.astype(jnp.float32), axis=0)
    grad_attended = jnp.einsum(
        "re,de->rd", grad_branch, back_output, preferred_element_type=jnp.float32
    ).astype(jnp.bfloat16)
    own_dout = grad_attended.reshape(head_view)
    dout_slots = grad_attended.reshape(slot_view)
    delta_rows = jnp.sum(own_dout.astype(jnp.float32) * attended, axis=-1)
    row_delta = jnp.transpose(delta_rows, (0, 2, 1))
    lse_rows = jnp.transpose(row_lse, (0, 2, 1))
    far_lse, far_delta = (
        lax.all_gather(lse_rows, "ctx", axis=1, tiled=True),
        lax.all_gather(delta_rows, "ctx", axis=1, tiled=True),
    )
    diag_probs = tile_probs(diag_query, diag_key, diag_mask, row_lse[0][None], score_scale)
    diag_dscore = tile_dscore(diag_probs, own_dout[0][None], diag_value, row_delta[0][None])
    query_start = slot_add(
        jnp.einsum("thqk,tkhd->tqhd", diag_dscore, diag_key, preferred_element_type=jnp.float32)
        * score_scale,
        zero_slot,
    )
    key_start = slot_add(
        jnp.einsum("thqk,tqhd->tkhd", diag_dscore, diag_query, preferred_element_type=jnp.float32)
        * score_scale,
        zero_slot,
    )
    value_start = slot_add(
        jnp.einsum(
            "thqk,tqhd->tkhd",
            diag_probs.astype(jnp.bfloat16),
            own_dout[0][None],
            preferred_element_type=jnp.float32,
        ),
        zero_slot,
    )

    def query_grad_group(running, slices, far_pair, is_own, far_places, first_row):
        chosen = far_pair < my_pair
        query_slot, key_slot = tile_slots(chosen)
        tile_key = key_tiles(split_heads(slices[0]), chosen)
        tile_value = key_tiles(split_heads(slices[1]), chosen)
        probs = tile_probs(
            query_tiles(own_query[:, None], chosen),
            tile_key,
            tile_mask(is_own, own_places, far_places),
            slot_pick(row_lse, query_slot),
            score_scale,
        )
        dscore = tile_dscore(
            probs,
            query_tiles(own_dout[:, None], chosen),
            tile_value,
            slot_pick(row_delta, query_slot),
        )
        part_grad = (
            jnp.einsum("thqk,tkhd->tqhd", dscore, tile_key, preferred_element_type=jnp.float32)
            * score_scale
        )
        return running + slot_add(part_grad, query_slot)

    def key_grad_group(running, slices, far_pair, is_own, far_places, first_row):
        chosen = my_pair < far_pair
        query_slot, key_slot = tile_slots(chosen)
        group_size = far_places.shape[0]
        sub_rows = far_places.shape[1]
        tile_query = query_tiles(split_heads(slices[0]), chosen)
        tile_dout = query_tiles(split_heads(slices[1]), chosen)
        lse_part = lax.dynamic_slice_in_dim(far_lse, first_row, group_size * sub_rows, 1).reshape(
            2, group_size, sub_rows, HEADS
        )
        delta_part = lax.dynamic_slice_in_dim(
            far_delta, first_row, group_size * sub_rows, 1
        ).reshape(2, group_size, sub_rows, HEADS)
        tile_lse = jnp.transpose(query_tiles(lse_part, chosen), (0, 2, 1))
        tile_delta = jnp.transpose(query_tiles(delta_part, chosen), (0, 2, 1))
        tile_key = key_tiles(own_key[:, None], chosen)
        tile_value = key_tiles(own_value[:, None], chosen)
        probs = tile_probs(
            tile_query, tile_key, tile_mask(is_own, far_places, own_places), tile_lse, score_scale
        )
        dscore = tile_dscore(probs, tile_dout, tile_value, tile_delta)
        key_part = (
            jnp.einsum("thqk,tqhd->tkhd", dscore, tile_query, preferred_element_type=jnp.float32)
            * score_scale
        )
        value_part = jnp.einsum(
            "thqk,tqhd->tkhd",
            probs.astype(jnp.bfloat16),
            tile_dout,
            preferred_element_type=jnp.float32,
        )
        return (
            running[0] + slot_add(key_part, key_slot),
            running[1] + slot_add(value_part, key_slot),
        )

    grad_query_sum = sweep_piece(
        query_start,
        (
            lax.all_gather(key_slots, "ctx", axis=1, tiled=True),
            lax.all_gather(value_slots, "ctx", axis=1, tiled=True),
        ),
        block_rows,
        my_rank,
        pair_of_rank,
        query_grad_group,
    )
    grad_key_sum, grad_value_sum = sweep_piece(
        (key_start, value_start),
        (
            lax.all_gather(query_slots, "ctx", axis=1, tiled=True),
            lax.all_gather(dout_slots, "ctx", axis=1, tiled=True),
        ),
        block_rows,
        my_rank,
        pair_of_rank,
        key_grad_group,
    )
    flat_rows = 2 * block_rows
    grad_query_low = grad_query_sum.reshape(flat_rows, model_width).astype(jnp.bfloat16)
    grad_key_low = grad_key_sum.reshape(flat_rows, model_width).astype(jnp.bfloat16)
    grad_value_low = grad_value_sum.reshape(flat_rows, model_width).astype(jnp.bfloat16)
    grad_mixed = jnp.concatenate([grad_query_low, grad_key_low, grad_value_low], axis=1)
    grad_input = jnp.einsum("rd,re->de", normed, grad_mixed, preferred_element_type=jnp.float32)
    grad_query_bias = jnp.sum(grad_query_low.astype(jnp.float32), axis=0)
    grad_value_bias = jnp.sum(grad_value_low.astype(jnp.float32), axis=0)
    grad_normed = jnp.einsum(
        "re,de->rd", grad_mixed, back_input, preferred_element_type=jnp.float32
    )
    grad_token_part, grad_first_gain, grad_first_shift = first_pullback(grad_normed)
    grad_tokens = (grad_middle + grad_token_part)[None]
    grad_local = (
        grad_first_gain,
        grad_first_shift,
        grad_input,
        grad_query_bias,
        grad_value_bias,
        grad_output,
        grad_output_bias,
        grad_second_gain,
        grad_second_shift,
        grad_expand,
        grad_expand_bias,
        grad_contract,
        grad_contract_bias,
    )
    grad_owned = (
        lax.psum_scatter(
            grad_local[0].astype(jnp.bfloat16), "dp", scatter_dimension=0, tiled=True
        ).astype(jnp.float32),
        lax.psum_scatter(
            grad_local[1].astype(jnp.bfloat16), "dp", scatter_dimension=0, tiled=True
        ).astype(jnp.float32),
        lax.psum_scatter(
            grad_local[2].astype(jnp.bfloat16), "dp", scatter_dimension=0, tiled=True
        ).astype(jnp.float32),
        lax.psum_scatter(
            grad_local[3].astype(jnp.bfloat16), "dp", scatter_dimension=0, tiled=True
        ).astype(jnp.float32),
        lax.psum_scatter(
            grad_local[4].astype(jnp.bfloat16), "dp", scatter_dimension=0, tiled=True
        ).astype(jnp.float32),
        lax.psum_scatter(
            grad_local[5].astype(jnp.bfloat16), "dp", scatter_dimension=0, tiled=True
        ).astype(jnp.float32),
        lax.psum_scatter(
            grad_local[6].astype(jnp.bfloat16), "dp", scatter_dimension=0, tiled=True
        ).astype(jnp.float32),
        lax.psum_scatter(
            grad_local[7].astype(jnp.bfloat16), "dp", scatter_dimension=0, tiled=True
        ).astype(jnp.float32),
        lax.psum_scatter(
            grad_local[8].astype(jnp.bfloat16), "dp", scatter_dimension=0, tiled=True
        ).astype(jnp.float32),
        lax.psum_scatter(
            grad_local[9].astype(jnp.bfloat16), "dp", scatter_dimension=0, tiled=True
        ).astype(jnp.float32),
        lax.psum_scatter(
            grad_local[10].astype(jnp.bfloat16), "dp", scatter_dimension=0, tiled=True
        ).astype(jnp.float32),
        lax.psum_scatter(
            grad_local[11].astype(jnp.bfloat16), "dp", scatter_dimension=0, tiled=True
        ).astype(jnp.float32),
        lax.psum_scatter(
            grad_local[12].astype(jnp.bfloat16), "dp", scatter_dimension=0, tiled=True
        ).astype(jnp.float32),
    )
    grad_final = tuple(
        lax.psum(
            (
                grad_owned[0],
                grad_owned[1],
                grad_owned[2],
                grad_owned[3],
                grad_owned[4],
                grad_owned[5],
                grad_owned[6],
                grad_owned[7],
                grad_owned[8],
                grad_owned[9],
                grad_owned[10],
                grad_owned[11],
                grad_owned[12],
            ),
            "ctx",
        )
    )
    return (block_out, grad_tokens) + tuple(grad_final)


VMEM_BYTES = 16 * 1024 * 1024
VMEM_LARGE = 28 * 1024 * 1024


def mm(left, right):
    return lax.dot_general(
        left, right, (((1,), (0,)), ((), ())), preferred_element_type=jnp.float32
    )


def mm_nt(left, right):
    return lax.dot_general(
        left, right, (((1,), (1,)), ((), ())), preferred_element_type=jnp.float32
    )


def mm_tn(left, right):
    return lax.dot_general(
        left, right, (((0,), (0,)), ((), ())), preferred_element_type=jnp.float32
    )


def aligned(index, size):
    return pl.ds(pl.multiple_of(index * size, size), size)


def norm_stats(values):
    centre = values - jnp.mean(values, axis=-1, keepdims=True)
    spread = jnp.mean(centre * centre, axis=-1, keepdims=True)
    scale = lax.rsqrt(spread + NORM_EPS)
    return centre * scale, scale


def norm_back(grad_normed, gain_row, xhat, scale):
    weighted = grad_normed * gain_row
    return scale * (
        weighted
        - jnp.mean(weighted, axis=-1, keepdims=True)
        - xhat * jnp.mean(weighted * xhat, axis=-1, keepdims=True)
    )


def column_sums(values):
    return jnp.sum(values, axis=0, keepdims=True)


def shape_of(dims, dtype):
    return jax.ShapeDtypeStruct(dims, dtype)


def local_call(
    kernel, name, outs, args, scalars=0, scratch=(), flops=0, after=(), space=pltpu.VMEM, grant=VMEM_BYTES
):
    moved = sum(math.prod(a.shape) * a.dtype.itemsize for a in tuple(args) + tuple(outs))

    def ordered(*refs):
        kernel(*refs[: len(args)], *refs[len(args) + len(after) :])

    return pl.pallas_call(
        ordered,
        out_shape=tuple(outs),
        in_specs=[pl.BlockSpec(memory_space=pltpu.SMEM)] * scalars
        + [pl.BlockSpec(memory_space=space)] * (len(args) - scalars)
        + [pl.BlockSpec(memory_space=pl.ANY)] * len(after),
        out_specs=tuple(pl.BlockSpec(memory_space=pltpu.VMEM) for _ in outs),
        scratch_shapes=list(scratch),
        compiler_params=pltpu.CompilerParams(vmem_limit_bytes=grant),
        cost_estimate=pl.CostEstimate(flops=flops, bytes_accessed=moved, transcendentals=0),
        name=name,
    )(*args, *after)


def place_of_block(pair_ref, info_ref, ranks, step, half, other_core):
    core = jnp.bitwise_xor(info_ref[2], other_core)
    rank = 2 * jnp.bitwise_xor(info_ref[1], step) + core
    pair = pair_ref[rank]
    return pair if half == 0 else 2 * ranks - 1 - pair


def fill_mask(bias_ref, pair_ref, info_ref, ranks, parts, block):
    rows = 2 * parts * block
    lanes = lax.broadcasted_iota(jnp.int32, (1, rows), 1)
    query_place = lanes % block
    for step in range(parts):
        for half in range(2):
            place = place_of_block(pair_ref, info_ref, ranks, step, half, 0)
            query_place = query_place + jnp.where(
                lanes // block == 2 * step + half, place * block, 0
            )
    ahead = lax.broadcasted_iota(jnp.int32, (block, rows), 0) - query_place
    for other in range(2):
        for step in range(parts):
            for half in range(2):
                place = place_of_block(pair_ref, info_ref, ranks, step, half, other)
                start = other * rows + (2 * step + half) * block
                bias_ref[start : start + block, :] = jnp.where(
                    ahead <= -place * block, 0.0, NEG_BIG
                )


def head_parallel(ranks, chips, seq_parts):
    parts = chips
    hw = HEADS // chips * HEAD_DIM

    def core_swap(member):
        return lax.ppermute(member, "ctx", [(i, i ^ 1) for i in range(ranks)])

    def chip_swap(member, step):
        return lax.ppermute(
            member, "ctx", [(i, 2 * ((i // 2) ^ step) + i % 2) for i in range(ranks)]
        )

    def seq_swap(member, step):
        return lax.ppermute(member, "dp", [(i, i ^ step) for i in range(seq_parts)])

    def per_device_heads(
        tokens,
        pair_of_rank,
        first_gain,
        first_shift,
        w_input,
        query_bias,
        value_bias,
        w_output,
        output_bias,
        second_gain,
        second_shift,
        w_expand,
        expand_bias,
        w_contract,
        contract_bias,
        cotangent,
    ):
        bf, f32 = jnp.bfloat16, jnp.float32
        rows, width = tokens.shape[1:]
        block = rows // 2
        own_width = width // seq_parts
        ff = expand_bias.shape[0]
        total = parts * rows
        half_width = width // 2
        half_ff = ff // 2
        sub = own_width // parts
        half_own = own_width // 2
        small_rows = 16
        others = range(1, parts)
        seq_id = lax.axis_index("dp")
        rank = lax.axis_index("ctx")
        chip = rank // 2
        core = rank % 2
        info = jnp.stack([seq_id, chip, core]).astype(jnp.int32)

        side = width - 3 * hw
        pack_rows = 2 * half_own

        def pack_kernel(info_ref, tok_ref, w_ref, wo_ref, *refs):
            vecs = refs[:8]
            packed_ref, tokens_ref, w_scr, wo_scr = refs[8:12]
            scrs, sems = refs[12:20], refs[20]
            mine = pl.ds(pl.multiple_of(info_ref[2] * half_own, half_own), half_own)
            pairs = [(w_ref.at[mine], w_scr), (wo_ref.at[mine], wo_scr), (tok_ref, tokens_ref)]
            pairs += list(zip(vecs, scrs))
            copies = [
                pltpu.make_async_copy(src, dst, sems.at[i]) for i, (src, dst) in enumerate(pairs)
            ]
            for copy in copies:
                copy.start()
            for copy in copies:
                copy.wait()
            at_w = slice(half_own, 2 * half_own)
            for at in range(chips):

                @pl.when(info_ref[1] == at)
                def _():
                    for base in range(3):
                        start = base * width + at * hw
                        packed_ref[at_w, base * hw : (base + 1) * hw] = w_scr[
                            :, start : start + hw
                        ]

            packed_ref[0:half_own, :] = wo_scr[...]
            small = jnp.concatenate(
                [v[...].astype(f32).reshape(1, own_width) for v in scrs], axis=0
            )
            small = jnp.concatenate([small, jnp.zeros_like(small)], axis=0)
            packed_ref[half_own : half_own + small_rows, 3 * hw :] = small.astype(bf)
            packed_ref[half_own + small_rows :, 3 * hw :] = jnp.zeros(
                (half_own - small_rows, side), bf
            )

        small_args = (
            first_gain,
            first_shift,
            query_bias,
            value_bias,
            output_bias,
            second_gain,
            second_shift,
            contract_bias,
        )
        packed, own_tokens = local_call(
            pack_kernel,
            "pack",
            [shape_of((pack_rows, width), bf), shape_of((rows, width), bf)],
            [info, tokens[0], w_input, w_output] + list(small_args),
            scalars=1,
            scratch=[pltpu.VMEM((half_own, 3 * width), bf), pltpu.VMEM((half_own, width), bf)]
            + [pltpu.VMEM((own_width,), bf)] * 8
            + [pltpu.SemaphoreType.DMA((11,))],
            space=pltpu.HBM,
            grant=60 * 1024 * 1024,
        )
        token_two = chip_swap(own_tokens, 2)
        token_parts = [own_tokens, chip_swap(own_tokens, 1), token_two, chip_swap(token_two, 1)]
        packed_near = [seq_swap(packed, j) for j in others]

        def stack_kernel(*refs):
            depth = refs[0].shape[0]
            for i, ref in enumerate(refs[:-1]):
                refs[-1][i * depth : (i + 1) * depth, :] = ref[...]

        (packed_all,) = local_call(
            stack_kernel,
            "pack_stack",
            [shape_of(((seq_parts - 1) * pack_rows, width), bf)],
            packed_near,
            after=token_parts[1:],
        )
        packed_far = core_swap(packed_all)
        own_cot = cotangent[0]

        def pack_more_kernel(info_ref, we_ref, cot_ref, *refs):
            for j in others:
                start = pl.multiple_of(info_ref[2] * half_own, half_own)
                refs[j - 1][0:half_own, :] = we_ref[
                    pl.ds(start, half_own), aligned(jnp.bitwise_xor(info_ref[0], j), ff)
                ]
                refs[j - 1][half_own:, :] = cot_ref[...]

        more = local_call(
            pack_more_kernel,
            "pack_more",
            [shape_of((half_own + rows, width), bf)] * (seq_parts - 1),
            [info, w_expand, own_cot],
            scalars=1,
            after=[packed],
        )
        more_parts = [seq_swap(more[j - 1], j) for j in others]

        def qkv_kernel(info_ref, w_own_ref, wo_own_ref, *refs):
            toks, own_pack, packs = refs[:parts], refs[parts], refs[parts + 1 : parts + 3]
            q_ref, kv_ref, normed_ref, w_ref, vec_ref, wo_ref, vec_scr = refs[parts + 3 :]
            for at in range(chips):

                @pl.when(info_ref[1] == at)
                def _():
                    for base in range(3):
                        start = base * width + at * hw
                        w_ref[aligned(info_ref[0], own_width), base * hw : (base + 1) * hw] = (
                            w_own_ref[:, start : start + hw]
                        )

            wo_ref[info_ref[0]] = wo_own_ref[...]
            at_small = slice(half_own, half_own + small_rows)
            vec_scr[info_ref[0]] = own_pack[at_small, 3 * hw :].astype(f32)
            for j in others:
                place = jnp.bitwise_xor(info_ref[0], j)
                base = (j - 1) * pack_rows
                vec_scr[place] = packs[0][
                    base + half_own : base + half_own + small_rows, 3 * hw :
                ].astype(f32)
                for flip in range(2):
                    member = packs[flip]
                    half = jnp.bitwise_xor(info_ref[2], flip)
                    down = pl.multiple_of(half * half_own, half_own)
                    wo_ref[place, pl.ds(down, half_own), :] = member[base : base + half_own, :]
                    start = pl.multiple_of(place * own_width + half * half_own, half_own)
                    w_ref[pl.ds(start, half_own), :] = member[
                        base + half_own : base + pack_rows, 0 : 3 * hw
                    ]
            vectors = jnp.concatenate([vec_scr[j] for j in range(parts)], axis=1)
            vec_ref[...] = vectors
            chosen = vec_scr[info_ref[1]]
            for k in range(parts):
                xhat, _ = norm_stats(toks[k][...].astype(f32))
                normed_ref[k * rows : (k + 1) * rows, :] = (
                    xhat * vectors[0:1] + vectors[1:2]
                ).astype(bf)
            mixed = mm(normed_ref[...], w_ref[...])
            q_ref[...] = (mixed[:, 0:hw] + chosen[2:3]).astype(bf)
            kv_ref[:, 0:hw] = mixed[:, hw : 2 * hw].astype(bf)
            kv_ref[:, hw : 2 * hw] = (mixed[:, 2 * hw :] + chosen[3:4]).astype(bf)

        query, own_kv, normed, w_heads_full, vectors, out_full = local_call(
            qkv_kernel,
            "project",
            [
                shape_of((total, hw), bf),
                shape_of((total, 2 * hw), bf),
                shape_of((total, width), bf),
                shape_of((width, 3 * hw), bf),
                shape_of((small_rows, width), f32),
                shape_of((parts, own_width, width), bf),
            ],
            [info, w_input, w_output] + token_parts + [packed, packed_all, packed_far],
            scalars=1,
            scratch=[pltpu.VMEM((parts, small_rows, own_width), f32)],
            flops=2 * total * width * 3 * hw,
        )
        far_kv = core_swap(own_kv)

        head_count = hw // HEAD_DIM
        scale = HEAD_DIM ** (-0.5)

        def head_columns(ref, base, head):
            start = base + head * HEAD_DIM
            return ref[:, start : start + HEAD_DIM]

        def attend_kernel(info_ref, pair_ref, q_ref, kv_ref, far_ref, *refs):
            outs = refs[:parts]
            flat_ref, lse_ref, bias_ref = refs[parts:]
            fill_mask(bias_ref, pair_ref, info_ref, ranks, parts, block)
            columns = []
            for head in range(head_count):
                keys = jnp.concatenate(
                    [head_columns(kv_ref, 0, head), head_columns(far_ref, 0, head)], axis=0
                )
                values = jnp.concatenate(
                    [head_columns(kv_ref, hw, head), head_columns(far_ref, hw, head)], axis=0
                )
                scores = mm_nt(keys, head_columns(q_ref, 0, head)) * scale + bias_ref[...]
                peak = jnp.max(scores, axis=0, keepdims=True)
                weights = jnp.exp(scores - peak)
                mass = jnp.sum(weights, axis=0, keepdims=True)
                lse_ref[head : head + 1, :] = peak + jnp.log(mass)
                mixed = mm_tn(values, weights.astype(bf)) / mass
                flat_ref[head * HEAD_DIM : (head + 1) * HEAD_DIM, :] = mixed
            attended = flat_ref[...].T.astype(bf)
            for k in range(parts):
                outs[k][...] = attended[k * rows : (k + 1) * rows]

        attend_out = local_call(
            attend_kernel,
            "attend",
            [shape_of((rows, hw), bf)] * parts
            + [shape_of((hw, total), f32), shape_of((8, total), f32)],
            [info, pair_of_rank, query, own_kv, far_kv],
            scalars=2,
            scratch=[pltpu.VMEM((2 * total, total), f32)],
            flops=2 * 2 * head_count * 2 * total * total * HEAD_DIM,
            grant=VMEM_LARGE,
        )
        flat_attended, row_lse = attend_out[parts:]
        att_parts = [attend_out[0]] + [chip_swap(attend_out[k], k) for k in others]

        def middle_kernel(info_ref, tok_ref, vec_ref, w_ref, *refs):
            atts = refs[:parts]
            mid_ref, normed_ref = refs[parts:]
            middle = tok_ref[...].astype(f32) + vec_ref[4:5]
            for k in range(parts):
                middle = middle + mm(atts[k][...], w_ref[jnp.bitwise_xor(info_ref[1], k)])
            mid_ref[...] = middle
            xhat, _ = norm_stats(middle)
            normed_ref[...] = (xhat * vec_ref[5:6] + vec_ref[6:7]).astype(bf)

        middle, own_normed_two = local_call(
            middle_kernel,
            "middle",
            [shape_of((rows, width), f32), shape_of((rows, width), bf)],
            [info, own_tokens, vectors, out_full] + att_parts,
            scalars=1,
            flops=2 * rows * width * width,
        )

        def expand_stack_kernel(*refs):
            for i, ref in enumerate(refs[:-1]):
                refs[-1][i * half_own : (i + 1) * half_own, :] = ref[0:half_own, :]

        (expand_all,) = local_call(
            expand_stack_kernel,
            "expand_stack",
            [shape_of(((seq_parts - 1) * half_own, ff), bf)],
            more_parts,
            after=[own_normed_two],
        )
        expand_far = core_swap(expand_all)
        n2_parts = [own_normed_two] + [seq_swap(own_normed_two, j) for j in others]

        span = ff // parts + own_width

        def ffn_kernel(info_ref, bias_ref, wc_ref, we_ref, own_cot_ref, far_we_ref, *refs):
            n2s = refs[:parts]
            mores = refs[parts : 2 * parts - 1]
            gns = refs[2 * parts - 1 : 3 * parts - 1]
            results = refs[3 * parts - 1 : 4 * parts - 1]
            keep_ref, send_ref, sum_ref = refs[4 * parts - 1 : 4 * parts + 2]
            active_ref, gh_ref, n2_ref, cot_ref, w_scr, scr = refs[4 * parts + 2 :]
            w_scr[aligned(info_ref[0], own_width), :] = we_ref[:, aligned(info_ref[0], ff)]
            for j in range(seq_parts):
                at = slice(j * rows, (j + 1) * rows)
                n2_ref[at, :] = n2s[j][...]
                if j == 0:
                    cot_ref[at, :] = own_cot_ref[...]
                    continue
                place = jnp.bitwise_xor(info_ref[0], j)
                for flip in range(2):
                    half = jnp.bitwise_xor(info_ref[2], flip)
                    start = pl.multiple_of(place * own_width + half * half_own, half_own)
                    w_scr[pl.ds(start, half_own), :] = (
                        far_we_ref[(j - 1) * half_own : j * half_own, :]
                        if flip
                        else mores[j - 1][0:half_own, :]
                    )
                cot_ref[at, :] = mores[j - 1][half_own:, :]
            hidden = mm(n2_ref[...], w_scr[...]) + bias_ref[...].astype(f32).reshape(1, ff)
            square = hidden * hidden
            curve = jnp.tanh(GELU_SCALE * hidden * (1.0 + GELU_CUBIC * square))
            active_ref[...] = (0.5 * hidden * (1.0 + curve)).astype(bf)
            slope = 0.5 * (1.0 + curve) + 0.5 * hidden * (1.0 - curve * curve) * GELU_SCALE * (
                1.0 + 3.0 * GELU_CUBIC * square
            )
            grad_hidden = mm_nt(cot_ref[...], wc_ref[...]) * slope
            gh_ref[...] = grad_hidden.astype(bf)
            sum_ref[...] = column_sums(gh_ref[...].astype(f32))
            grad = mm_nt(gh_ref[...], w_scr[...]).astype(bf)
            for j in range(parts):
                gns[j][...] = grad[j * rows : (j + 1) * rows]
            result = mm(active_ref[...], wc_ref[...]).astype(bf)
            for j in range(seq_parts):
                results[j][...] = result[j * rows : (j + 1) * rows]
            core_id = info_ref[2]
            for flip, out_ref in ((0, keep_ref), (1, send_ref)):
                half = jnp.bitwise_xor(core_id, flip)
                scr[...] = mm_tn(active_ref[...], cot_ref[:, aligned(half, half_width)]).astype(bf)
                for part in range(parts):
                    rows_to = ff // parts
                    out_ref[part, 0:rows_to, :] = scr[part * rows_to : (part + 1) * rows_to, :]
                scr[...] = mm_tn(n2_ref[...], gh_ref[:, aligned(half, half_ff)]).astype(bf)
                for part in range(parts):
                    for j in range(seq_parts):
                        at = ff // parts + j * sub
                        row = j * own_width + part * sub
                        out_ref[part, at : at + sub, :] = scr[row : row + sub, :]

        ffn_out = local_call(
            ffn_kernel,
            "feed",
            [shape_of((rows, width), bf)] * 2 * parts
            + [
                shape_of((parts, span, half_width), bf),
                shape_of((parts, span, half_width), bf),
                shape_of((1, ff), f32),
            ],
            [info, expand_bias, w_contract, w_expand, own_cot, expand_far] + n2_parts + more_parts,
            scalars=1,
            scratch=[
                pltpu.VMEM((total, ff), bf),
                pltpu.VMEM((total, ff), bf),
                pltpu.VMEM((total, width), bf),
                pltpu.VMEM((total, width), bf),
                pltpu.VMEM((width, ff), bf),
                pltpu.VMEM((width, half_ff), bf),
            ],
            flops=6 * 2 * total * width * ff,
            grant=VMEM_LARGE,
        )
        results = ffn_out[parts : 2 * parts]
        ffn_keep, ffn_send, grad_expand_row = ffn_out[2 * parts :]
        gn_parts = [ffn_out[0]] + [seq_swap(ffn_out[j], j) for j in others]
        ffn_far = core_swap(ffn_send)

        def halve_kernel(info_ref, keep_ref, far_ref, own_ref, out_ref):
            for k in range(parts):
                at = jnp.bitwise_xor(info_ref[1], k)
                piece = keep_ref[at].astype(f32) + far_ref[at].astype(f32)
                if k % 2:
                    out_ref[k // 2] = piece.astype(bf)
                else:
                    own_ref[k // 2] = piece

        rs_own, rs_send = local_call(
            halve_kernel,
            "feed_halves",
            [
                shape_of((parts // 2, span, half_width), f32),
                shape_of((parts // 2, span, half_width), bf),
            ],
            [info, ffn_keep, ffn_far],
            scalars=1,
        )
        rs_far = chip_swap(rs_send, 1)

        def back_kernel(info_ref, mid_ref, vec_ref, cot_ref, w_ref, *refs):
            gns = refs[:parts]
            douts = refs[parts : 2 * parts]
            gmid_ref, branch_ref, sums_ref = refs[2 * parts :]
            grad = gns[0][...].astype(f32)
            for j in others:
                grad = grad + gns[j][...].astype(f32)
            xhat, spread = norm_stats(mid_ref[...])
            cot = cot_ref[...].astype(f32)
            grad_middle = cot + norm_back(grad, vec_ref[5:6], xhat, spread)
            gmid_ref[...] = grad_middle
            branch = grad_middle.astype(bf)
            branch_ref[...] = branch
            for k in range(parts):
                douts[k][...] = mm_nt(branch, w_ref[jnp.bitwise_xor(info_ref[1], k)]).astype(bf)
            sums_ref[0:1, :] = column_sums(branch.astype(f32))
            sums_ref[1:2, :] = column_sums(grad * xhat)
            sums_ref[2:3, :] = column_sums(grad)
            sums_ref[3:4, :] = column_sums(cot)

        back_out = local_call(
            back_kernel,
            "middle_back",
            [shape_of((rows, hw), bf)] * parts
            + [
                shape_of((rows, width), f32),
                shape_of((rows, width), bf),
                shape_of((8, width), f32),
            ],
            [info, middle, vectors, own_cot, out_full] + gn_parts,
            scalars=1,
            after=[rs_send],
            flops=2 * rows * width * width,
        )
        grad_middle, grad_branch, late_sums = back_out[parts:]
        dout_parts = [back_out[0]] + [chip_swap(back_out[k], k) for k in others]

        def out_weights_kernel(info_ref, branch_ref, *refs):
            atts = refs[:parts]
            keep_ref, send_ref = refs[parts:]
            for flip, out_ref in ((0, keep_ref), (1, send_ref)):
                half = jnp.bitwise_xor(info_ref[2], flip)
                piece = branch_ref[:, aligned(half, half_width)]
                for k in range(parts):
                    out_ref[jnp.bitwise_xor(info_ref[1], k)] = mm_tn(atts[k][...], piece).astype(bf)

        out_keep, out_send = local_call(
            out_weights_kernel,
            "output_weights",
            [shape_of((parts, hw, half_width), bf)] * 2,
            [info, grad_branch] + att_parts,
            scalars=1,
            flops=2 * rows * width * width,
        )
        out_far = core_swap(out_send)

        def quarter_kernel(own_ref, far_ref, keep_ref, send_ref):
            keep_ref[...] = own_ref[0] + far_ref[0].astype(f32)
            send_ref[...] = (own_ref[1] + far_ref[1].astype(f32)).astype(bf)

        rs_own_two, rs_send_two = local_call(
            quarter_kernel,
            "feed_quarters",
            [shape_of((span, half_width), f32), shape_of((span, half_width), bf)],
            [rs_own, rs_far],
            after=[dout_parts[parts - 1]],
        )
        rs_far_two = chip_swap(rs_send_two, 2)

        def attend_back_kernel(info_ref, pair_ref, q_ref, kv_ref, far_ref, flat_ref, lse_ref, *refs):
            douts = refs[:parts]
            dq_ref, own_ref, send_ref, bias_ref, dout_ref = refs[parts:]
            fill_mask(bias_ref, pair_ref, info_ref, ranks, parts, block)
            for k in range(parts):
                dout_ref[k * rows : (k + 1) * rows, :] = douts[k][...].astype(f32)
            flat_dout = dout_ref[...].T
            for head in range(head_count):
                at = slice(head * HEAD_DIM, (head + 1) * HEAD_DIM)
                keys = jnp.concatenate(
                    [head_columns(kv_ref, 0, head), head_columns(far_ref, 0, head)], axis=0
                )
                values = jnp.concatenate(
                    [head_columns(kv_ref, hw, head), head_columns(far_ref, hw, head)], axis=0
                )
                queries = head_columns(q_ref, 0, head)
                dout = dout_ref[:, at].astype(bf)
                dout_turned = flat_dout[at, :]
                delta = column_sums(dout_turned * flat_ref[at, :])
                scores = mm_nt(keys, queries) * scale + bias_ref[...]
                probs = jnp.exp(scores - lse_ref[head : head + 1, :])
                grad_value = mm(probs.astype(bf), dout)
                grad_weights = mm(values, dout_turned.astype(bf))
                grad_scores = (probs * (grad_weights - delta)).astype(bf)
                grad_key = mm(grad_scores, queries) * scale
                dq_ref[at, :] = mm_tn(keys, grad_scores) * scale
                vat = slice(hw + head * HEAD_DIM, hw + (head + 1) * HEAD_DIM)
                own_ref[:, at] = grad_key[0:total]
                own_ref[:, vat] = grad_value[0:total]
                send_ref[:, at] = grad_key[total:].astype(bf)
                send_ref[:, vat] = grad_value[total:].astype(bf)

        flat_dq, dkv_own, dkv_send = local_call(
            attend_back_kernel,
            "attend_back",
            [
                shape_of((hw, total), f32),
                shape_of((total, 2 * hw), f32),
                shape_of((total, 2 * hw), bf),
            ],
            [info, pair_of_rank, query, own_kv, far_kv, flat_attended, row_lse] + dout_parts,
            scalars=2,
            after=[rs_send_two, out_send],
            scratch=[pltpu.VMEM((2 * total, total), f32), pltpu.VMEM((total, hw), f32)],
            flops=5 * 2 * head_count * 2 * total * total * HEAD_DIM,
            grant=VMEM_LARGE,
        )
        dkv_far = core_swap(dkv_send)

        def normed_back_kernel(dq_ref, own_ref, far_ref, w_ref, *refs):
            toks = refs[:parts]
            keep_ref, *send_refs, mixed_ref, sums_ref, bias_ref = refs[parts:]
            mixed_ref[:, 0:hw] = dq_ref[...].T.astype(bf)
            mixed_ref[:, hw:] = (own_ref[...] + far_ref[...].astype(f32)).astype(bf)
            shift_sum = jnp.zeros((1, width), f32)
            gain_sum = jnp.zeros((1, width), f32)
            for k in range(parts):
                grad = mm_nt(mixed_ref[k * rows : (k + 1) * rows, :], w_ref[...])
                if k % 2:
                    send_refs[k // 2][...] = grad.astype(bf)
                else:
                    keep_ref[k // 2] = grad
                xhat, _ = norm_stats(toks[k][...].astype(f32))
                shift_sum = shift_sum + column_sums(grad)
                gain_sum = gain_sum + column_sums(grad * xhat)
            sums_ref[0:1, :] = gain_sum
            sums_ref[1:2, :] = shift_sum
            bias_ref[0:1, :] = column_sums(mixed_ref[...].astype(f32))

        nb_out = local_call(
            normed_back_kernel,
            "normed_back",
            [
                shape_of((parts // 2, rows, width), f32),
                shape_of((rows, width), bf),
                shape_of((rows, width), bf),
                shape_of((total, 3 * hw), bf),
                shape_of((8, width), f32),
                shape_of((8, 3 * hw), f32),
            ],
            [flat_dq, dkv_own, dkv_far, w_heads_full] + token_parts,
            flops=2 * total * width * 3 * hw,
        )
        gt_keep, *gt_send, grad_mixed, first_sums, mixed_sums = nb_out
        gt_far = [chip_swap(member, 1) for member in gt_send]


        def input_weights_kernel(
            info_ref, normed_ref, mixed_ref, first_ref, bias_ref, late_ref, row_ref, *refs
        ):
            keep_ref, *send_refs, grad_scr, small_scr = refs
            grad_scr[...] = mm_tn(normed_ref[...], mixed_ref[...])
            core_id, chip_id, seq = info_ref[2], info_ref[1], info_ref[0]
            small_scr[...] = jnp.zeros_like(small_scr)
            for j in range(seq_parts):
                at = slice(j * own_width, (j + 1) * own_width)
                small_scr[j, 0:2, :] = first_ref[0:2, at]
                small_scr[j, 4:8, :] = late_ref[0:4, at]
            small_scr[chip_id, 2:3, :] = bias_ref[0:1, 0:hw]
            small_scr[chip_id, 3:4, :] = bias_ref[0:1, 2 * hw : 3 * hw]
            for j in range(ff // own_width):
                small_scr[seq, 8 + j : 9 + j, :] = row_ref[:, j * own_width : (j + 1) * own_width]
            for flip in range(2):
                half = jnp.bitwise_xor(core_id, flip)
                for j in range(seq_parts):
                    out_ref = send_refs[j] if flip else keep_ref.at[j]
                    start = pl.multiple_of(j * own_width + half * half_own, 16)
                    out_ref[:, 0 : 3 * hw] = grad_scr[pl.ds(start, half_own), :].astype(bf)
                    out_ref[0:small_rows, 3 * hw :] = small_scr[j].astype(bf)
                    out_ref[small_rows:, 3 * hw :] = jnp.zeros(
                        (half_own - small_rows, side), bf
                    )

        in_keep, *in_send = local_call(
            input_weights_kernel,
            "input_weights",
            [shape_of((seq_parts, half_own, width), bf)]
            + [shape_of((half_own, width), bf)] * seq_parts,
            [info, normed, grad_mixed, first_sums, mixed_sums, late_sums, grad_expand_row],
            scalars=1,
            scratch=[
                pltpu.VMEM((width, 3 * hw), f32),
                pltpu.VMEM((seq_parts, small_rows, own_width), f32),
            ],
            flops=2 * total * width * 3 * hw,
        )
        in_far = [core_swap(member) for member in in_send]

        fold = own_width // 2
        rider = -(-sub // 32) * 16
        at_outs = slice(half_own, half_own + fold)

        def fold_in(value):
            down = value.shape[0] // 2
            return jnp.concatenate([value[0:down], value[down:]], axis=1)

        def fold_out(value):
            across = value.shape[1] // 2
            return jnp.concatenate([value[:, 0:across], value[:, across:]], axis=0)

        res_parts = [results[0]] + [seq_swap(results[j], j) for j in others]

        def result_kernel(mid_ref, vec_ref, *refs):
            result = mid_ref[...] + vec_ref[7:8]
            for j in range(seq_parts):
                result = result + refs[j][...].astype(f32)
            refs[seq_parts][0] = result.astype(bf)
            refs[seq_parts + 1][...] = jnp.zeros((8, 128), f32)

        block_out, block_done = local_call(
            result_kernel,
            "result",
            [shape_of((1, rows, width), bf), shape_of((8, 128), f32)],
            [middle, vectors] + res_parts,
            after=[in_keep],
        )

        def dp_pack_kernel(
            info_ref, own_ref, far_two_ref, keep_ref, ok_ref, of_ref, *refs
        ):
            fars, refs = refs[:seq_parts], refs[seq_parts:]
            con_ref, scr, far_scr = refs[seq_parts:]
            for j in range(seq_parts):
                far_scr[j] = fars[j][...]
            whole = own_ref[...] + far_two_ref[...].astype(f32)
            con_ref[...] = whole[0 : ff // parts].astype(bf)
            scr[...] = whole[ff // parts :]
            for j in range(seq_parts):
                at = jnp.bitwise_xor(info_ref[0], j)
                refs[j][0:half_own, :] = (
                    keep_ref[at].astype(f32) + far_scr[at].astype(f32)
                ).astype(bf)
                refs[j][at_outs, :] = fold_in(ok_ref[at].astype(f32) + of_ref[at].astype(f32)).astype(
                    bf
                )
                piece = fold_in(scr[aligned(at, sub), :])
                piece = jnp.concatenate(
                    [piece, jnp.zeros((rider - sub // 2, width), f32)], axis=0
                )
                refs[j][half_own + fold :, :] = piece.astype(bf)
        dp_out = local_call(
            dp_pack_kernel,
            "owners",
            [shape_of((half_own + fold + rider, width), bf)] * seq_parts
            + [shape_of((ff // parts, half_width), bf)],
            [info, rs_own_two, rs_far_two, in_keep, out_keep, out_far] + in_far,
            scalars=1,
            scratch=[
                pltpu.VMEM((own_width, half_ff), f32),
                pltpu.VMEM((seq_parts, half_own, width), bf),
            ],
            after=[block_done],
        )
        dp_parts = [dp_out[0]] + [seq_swap(dp_out[j], j) for j in others]
        con_one = dp_out[seq_parts]

        def half_sum_kernel(keep_ref, first_ref, second_ref, own_ref, send_ref):
            own_ref[...] = keep_ref[0] + first_ref[...].astype(f32)
            send_ref[...] = (keep_ref[1] + second_ref[...].astype(f32)).astype(bf)

        gt_own, gt_send_two = local_call(
            half_sum_kernel,
            "tokens_halves",
            [shape_of((rows, width), f32), shape_of((rows, width), bf)],
            [gt_keep] + gt_far,
            after=[con_one],
        )
        con_two = chip_swap(con_one, 2)
        gt_far_two = chip_swap(gt_send_two, 2)

        con_one_far = chip_swap(con_one, 1)
        con_two_far = chip_swap(con_two, 1)

        con_parts = [con_one, con_one_far, con_two, con_two_far]
        con_far = [core_swap(member) for member in con_parts]

        def contract_kernel(info_ref, *refs):
            con_ref, done_ref = refs[2 * parts :]
            done_ref[...] = jnp.zeros_like(done_ref)
            for flip in range(2):
                lanes = aligned(jnp.bitwise_xor(info_ref[2], flip), half_width)
                for k in range(parts):
                    at = jnp.bitwise_xor(info_ref[1], k)
                    con_ref[aligned(at, ff // parts), lanes] = refs[flip * parts + k][...].astype(
                        f32
                    )

        grad_contract, contract_done = local_call(
            contract_kernel,
            "contract_final",
            [shape_of((ff, width), f32), shape_of((8, 128), f32)],
            [info] + con_parts + con_far,
            scalars=1,
        )

        def dp_sum_kernel(info_ref, *refs):
            owned = refs[:seq_parts]
            last_ref, scr = refs[seq_parts:]
            whole = owned[0][0 : half_own + fold, :].astype(f32)
            for j in others:
                whole = whole + owned[j][0 : half_own + fold, :].astype(f32)
            last_ref[0 : half_own + fold, :] = whole.astype(bf)
            for j in range(seq_parts):
                place = jnp.bitwise_xor(info_ref[0], j)
                piece = owned[j][half_own + fold :, :].astype(f32)
                scr[aligned(place, sub), :] = fold_out(piece[0 : sub // 2])
            last_ref[half_own + fold :, :] = fold_in(scr[...]).astype(bf)

        (last_one,) = local_call(
            dp_sum_kernel,
            "shares",
            [shape_of((half_own + 2 * fold, width), bf)],
            [info] + dp_parts,
            scalars=1,
            scratch=[pltpu.VMEM((own_width, half_ff), f32)],
            after=[con_one_far, con_two_far, gt_far_two],
        )
        last_two = chip_swap(last_one, 2)
        last_one_far = chip_swap(last_one, 1)
        def tokens_kernel(tok_ref, vec_ref, gmid_ref, own_ref, far_ref, out_ref, done_ref):
            done_ref[...] = jnp.zeros_like(done_ref)
            grad = own_ref[...] + far_ref[...].astype(f32)
            xhat, spread = norm_stats(tok_ref[...].astype(f32))
            out_ref[0] = gmid_ref[...] + norm_back(grad, vec_ref[0:1], xhat, spread)

        grad_tokens, tokens_done = local_call(
            tokens_kernel,
            "tokens_back",
            [shape_of((1, rows, width), f32), shape_of((8, 128), f32)],
            [own_tokens, vectors, grad_middle, gt_own, gt_far_two],
        )

        def pass_kernel(in_ref, out_ref):
            out_ref[...] = in_ref[...]

        (last_two_on,) = local_call(
            pass_kernel,
            "pass_on",
            [shape_of((half_own + 2 * fold, width), bf)],
            [last_two],
            after=[contract_done, tokens_done, last_one_far],
        )
        last_two_far = chip_swap(last_two_on, 1)
        last_parts = [last_one, last_one_far, last_two, last_two_far]
        last_far = [core_swap(member) for member in last_parts]

        def last_kernel(info_ref, *refs):
            gin_ref, gout_ref, exp_ref = refs[2 * parts : 2 * parts + 3]
            bias_ref, smalls, scr = refs[2 * parts + 3], refs[2 * parts + 4 : -1], refs[-1]
            for flip in range(2):
                half = jnp.bitwise_xor(info_ref[2], flip)
                outs = jnp.zeros((fold, width), f32)
                for k in range(parts):
                    at = jnp.bitwise_xor(info_ref[1], k)
                    piece = refs[flip * parts + k][...].astype(f32)
                    scr[at, aligned(half, half_own), :] = piece[0:half_own, 0 : 3 * hw]
                    outs = outs + piece[at_outs]
                    turned = fold_out(piece[half_own + fold :])
                    for j in range(seq_parts):
                        cols = pl.ds(pl.multiple_of(j * ff + half * half_ff, 128), half_ff)
                        exp_ref[aligned(at, sub), cols] = turned[j * sub : (j + 1) * sub]
                gout_ref[:, aligned(half, half_width)] = fold_out(outs)
            for at in range(parts):
                for base in range(3):
                    start = base * width + at * hw
                    gin_ref[:, start : start + hw] = scr[at, :, base * hw : (base + 1) * hw]
            small = refs[0][0:small_rows, 3 * hw :].astype(f32)
            for k in others:
                small = small + refs[k][0:small_rows, 3 * hw :].astype(f32)
            for i in range(8):
                smalls[i][...] = small[i : i + 1].reshape(own_width)
            bias_ref[...] = jnp.concatenate(
                [small[8 + i : 9 + i] for i in range(ff // own_width)], axis=1
            ).reshape(ff)

        last_out = local_call(
            last_kernel,
            "weights_final",
            [
                shape_of((own_width, 3 * width), f32),
                shape_of((own_width, width), f32),
                shape_of((own_width, seq_parts * ff), f32),
                shape_of((ff,), f32),
            ]
            + [shape_of((own_width,), f32)] * 8,
            [info] + last_parts + last_far,
            scalars=1,
            scratch=[pltpu.VMEM((parts, own_width, 3 * hw), f32)],
            grant=VMEM_LARGE,
        )
        grad_input, grad_output, grad_expand, grad_expand_bias = last_out[:4]
        small_of = last_out[4:]
        return (
            block_out,
            grad_tokens,
            small_of[0],
            small_of[1],
            grad_input,
            small_of[2],
            small_of[3],
            grad_output,
            small_of[4],
            small_of[5],
            small_of[6],
            grad_expand,
            grad_expand_bias,
            grad_contract,
            small_of[7],
        )

    return per_device_heads


def solution(mesh):
    ranks = mesh.shape["ctx"]
    chips = ranks // 2
    if chips == mesh.shape["dp"] and HEADS % chips == 0 and chips & (chips - 1) == 0:
        body = head_parallel(ranks, chips, mesh.shape["dp"])
    else:
        body = per_device
    return jax.shard_map(
        body,
        mesh=mesh,
        in_specs=(
            P("dp", "ctx", None),
            P(),
            P("dp"),
            P("dp"),
            P("dp", None),
            P("dp"),
            P("dp"),
            P("dp", None),
            P("dp"),
            P("dp"),
            P("dp"),
            P("dp", None),
            P("dp"),
            P("dp", None),
            P("dp"),
            P("dp", "ctx", None),
        ),
        out_specs=(
            P("dp", "ctx", None),
            P("dp", "ctx", None),
            P("dp"),
            P("dp"),
            P("dp", None),
            P("dp"),
            P("dp"),
            P("dp", None),
            P("dp"),
            P("dp"),
            P("dp"),
            P("dp", None),
            P("dp"),
            P("dp", None),
            P("dp"),
        ),
        check_vma=False,
    )
```

```python
import math

import jax
import jax.numpy as jnp
from jax import lax
from jax.experimental import pallas as pl
from jax.experimental.pallas import tpu as pltpu
from jax.sharding import PartitionSpec as P

HEADS = 12
HEAD_DIM = 64


NEG_BIG = -1e30
NORM_EPS = 1e-05
GELU_SCALE = 0.7978845608028654
GELU_CUBIC = 0.044715


def gelu_tanh(values):
    return (
        0.5
        * values
        * (1.0 + jnp.tanh(GELU_SCALE * (values + GELU_CUBIC * values * values * values)))
    )


def layer_norm(values, gain_row, shift_row):
    centre = values - jnp.mean(values, axis=-1, keepdims=True)
    spread = jnp.mean(centre * centre, axis=-1, keepdims=True)
    return centre * lax.rsqrt(spread + NORM_EPS) * gain_row + shift_row


def lookup_pair(pair_table, positions):
    ranks_all = jnp.arange(pair_table.shape[0], dtype=jnp.int32)
    return jnp.sum(jnp.where(positions[..., None] == ranks_all, pair_table, 0), axis=-1)


def group_count(blocks, sub_rows):
    chosen_count = 1
    for candidate in range(1, blocks + 1):
        if blocks % candidate == 0 and candidate * sub_rows <= max(512, sub_rows):
            chosen_count = candidate
    return chosen_count


def slot_mask(slot_ids, wanted, rank_count):
    return (slot_ids == wanted).reshape((-1,) + (1,) * (rank_count - 1))


def slot_add(values, slot_ids):
    early_sum = jnp.sum(jnp.where(slot_mask(slot_ids, 0, values.ndim), values, 0.0), axis=0)
    late_sum = jnp.sum(jnp.where(slot_mask(slot_ids, 1, values.ndim), values, 0.0), axis=0)
    return jnp.stack([early_sum, late_sum])


def slot_max(values, slot_ids):
    early_max = jnp.max(jnp.where(slot_mask(slot_ids, 0, values.ndim), values, NEG_BIG), axis=0)
    late_max = jnp.max(jnp.where(slot_mask(slot_ids, 1, values.ndim), values, NEG_BIG), axis=0)
    return jnp.stack([early_max, late_max])


def slot_pick(per_slot, slot_ids):
    return jnp.where(slot_mask(slot_ids, 0, per_slot.ndim), per_slot[0][None], per_slot[1][None])


def query_tiles(blocks, chosen):
    target = chosen.shape + blocks.shape[2:]
    chosen_view = chosen.reshape((-1,) + (1,) * (blocks.ndim - 2))
    late_part = jnp.broadcast_to(blocks[1], target)
    picked = jnp.where(chosen_view, blocks[0], blocks[1])
    return jnp.concatenate([late_part, picked], axis=0)


def key_tiles(blocks, chosen):
    target = chosen.shape + blocks.shape[2:]
    chosen_view = chosen.reshape((-1,) + (1,) * (blocks.ndim - 2))
    early_part = jnp.broadcast_to(blocks[0], target)
    picked = jnp.where(chosen_view, blocks[0], blocks[1])
    return jnp.concatenate([early_part, picked], axis=0)


def tile_slots(chosen):
    late_slot = jnp.where(chosen, 0, 1).astype(jnp.int32)
    query_slot = jnp.concatenate([jnp.ones_like(late_slot), late_slot])
    key_slot = jnp.concatenate([jnp.zeros_like(late_slot), late_slot])
    return (query_slot, key_slot)


def tile_mask(is_own, query_places, key_places):
    visible = key_places[:, None, :] <= query_places[:, :, None]
    visible = jnp.logical_or(visible, jnp.logical_not(is_own)[:, None, None])
    return jnp.concatenate([jnp.ones_like(visible), visible], axis=0)


def tile_scores(tile_query, tile_key, score_scale):
    return (
        jnp.einsum("tqhd,tkhd->thqk", tile_query, tile_key, preferred_element_type=jnp.float32)
        * score_scale
    )


def tile_probs(tile_query, tile_key, tile_visible, row_lse, score_scale):
    scores = tile_scores(tile_query, tile_key, score_scale)
    return jnp.where(tile_visible[:, None], jnp.exp(scores - row_lse[..., None]), 0.0)


def tile_dscore(probs, tile_dout, tile_value, row_delta):
    grad_probs = jnp.einsum(
        "tqhd,tkhd->thqk", tile_dout, tile_value, preferred_element_type=jnp.float32
    )
    return (probs * (grad_probs - row_delta[..., None])).astype(jnp.bfloat16)


def stats_update(running, tile_query, tile_key, query_slot, tile_visible, score_scale):
    run_peak, run_total = running
    visible = tile_visible[:, None]
    masked = jnp.where(visible, tile_scores(tile_query, tile_key, score_scale), NEG_BIG)
    new_peak = jnp.maximum(run_peak, slot_max(jnp.max(masked, axis=-1), query_slot))
    weights = jnp.where(visible, jnp.exp(masked - slot_pick(new_peak, query_slot)[..., None]), 0.0)
    run_total = run_total * jnp.exp(run_peak - new_peak) + slot_add(
        jnp.sum(weights, axis=-1), query_slot
    )
    return (new_peak, run_total)


def values_update(
    running, tile_query, tile_key, tile_value, query_slot, tile_visible, row_lse, score_scale
):
    probs = tile_probs(tile_query, tile_key, tile_visible, row_lse, score_scale)
    part_out = jnp.einsum(
        "thqk,tkhd->tqhd",
        probs.astype(jnp.bfloat16),
        tile_value,
        preferred_element_type=jnp.float32,
    )
    return running + slot_add(part_out, query_slot)


def sweep_piece(carried, pieces, block_rows, my_rank, pair_table, update):
    piece_rows = pieces[0].shape[1]
    sub_rows = math.gcd(piece_rows, block_rows)
    unit_count = piece_rows // sub_rows
    group_size = group_count(unit_count, sub_rows)

    def group_step(loop_index, running):
        offset = loop_index * (group_size * sub_rows)
        slices = tuple(
            (
                lax.dynamic_slice_in_dim(member, offset, group_size * sub_rows, 1).reshape(
                    (2, group_size, sub_rows) + member.shape[2:]
                )
                for member in pieces
            )
        )
        places = offset + jnp.arange(group_size * sub_rows, dtype=jnp.int32).reshape(
            group_size, sub_rows
        )
        far_ranks = places[:, 0] // block_rows
        far_pair = lookup_pair(pair_table, far_ranks)
        return update(running, slices, far_pair, far_ranks == my_rank, places % block_rows, offset)

    return lax.fori_loop(0, unit_count // group_size, group_step, carried)


def per_device(
    tokens,
    pair_of_rank,
    first_gain,
    first_shift,
    w_input,
    query_bias,
    value_bias,
    w_output,
    output_bias,
    second_gain,
    second_shift,
    w_expand,
    expand_bias,
    w_contract,
    contract_bias,
    cotangent,
):
    gathered = (
        lax.all_gather(first_gain, "dp", axis=0, tiled=True),
        lax.all_gather(first_shift, "dp", axis=0, tiled=True),
        lax.all_gather(w_input, "dp", axis=0, tiled=True),
        lax.all_gather(query_bias, "dp", axis=0, tiled=True),
        lax.all_gather(value_bias, "dp", axis=0, tiled=True),
        lax.all_gather(w_output, "dp", axis=0, tiled=True),
        lax.all_gather(output_bias, "dp", axis=0, tiled=True),
        lax.all_gather(second_gain, "dp", axis=0, tiled=True),
        lax.all_gather(second_shift, "dp", axis=0, tiled=True),
        lax.all_gather(w_expand, "dp", axis=0, tiled=True),
        lax.all_gather(expand_bias, "dp", axis=0, tiled=True),
        lax.all_gather(w_contract, "dp", axis=0, tiled=True),
        lax.all_gather(contract_bias, "dp", axis=0, tiled=True),
    )
    (
        full_first_gain,
        full_first_shift,
        full_input,
        full_query_bias,
        full_value_bias,
        full_output,
        full_output_bias,
        full_second_gain,
        full_second_shift,
        full_expand,
        full_expand_bias,
        full_contract,
        full_contract_bias,
    ) = gathered
    model_width = tokens.shape[2]
    block_rows = tokens.shape[1] // 2
    score_scale = HEAD_DIM ** (-0.5)
    slot_view = (2, block_rows, model_width)
    head_view = (2, block_rows, HEADS, HEAD_DIM)
    my_rank = lax.axis_index("ctx")
    my_pair = lookup_pair(pair_of_rank, my_rank)
    own_places = jnp.arange(block_rows, dtype=jnp.int32)[None, :]
    diag_mask = (own_places <= own_places.reshape(-1, 1))[None]
    zero_slot = jnp.zeros((1,), jnp.int32)

    def split_heads(member):
        return member.reshape(member.shape[:3] + (HEADS, HEAD_DIM))

    token_rows = tokens[0].astype(jnp.float32)
    normed_full, first_pullback = jax.vjp(
        layer_norm,
        token_rows,
        full_first_gain.astype(jnp.float32),
        full_first_shift.astype(jnp.float32),
    )
    normed = normed_full.astype(jnp.bfloat16)
    mixed_rows = jnp.dot(normed, full_input, preferred_element_type=jnp.float32)
    query_rows = (mixed_rows[:, :model_width] + full_query_bias.astype(jnp.float32)).astype(
        jnp.bfloat16
    )
    key_rows = mixed_rows[:, model_width : 2 * model_width].astype(jnp.bfloat16)
    value_rows = (mixed_rows[:, 2 * model_width :] + full_value_bias.astype(jnp.float32)).astype(
        jnp.bfloat16
    )
    own_query = query_rows.reshape(head_view)
    own_key = key_rows.reshape(head_view)
    own_value = value_rows.reshape(head_view)
    diag_query = own_query[0][None]
    diag_key = own_key[0][None]
    diag_value = own_value[0][None]
    key_slots = key_rows.reshape(slot_view)
    value_slots = value_rows.reshape(slot_view)
    query_slots = query_rows.reshape(slot_view)

    def stats_group(running, slices, far_pair, is_own, far_places, first_row):
        chosen = far_pair < my_pair
        query_slot, key_slot = tile_slots(chosen)
        return stats_update(
            running,
            query_tiles(own_query[:, None], chosen),
            key_tiles(split_heads(slices[0]), chosen),
            query_slot,
            tile_mask(is_own, own_places, far_places),
            score_scale,
        )

    stats_start = (
        jnp.full((2, HEADS, block_rows), NEG_BIG, jnp.float32),
        jnp.zeros((2, HEADS, block_rows), jnp.float32),
    )
    stats_start = stats_update(stats_start, diag_query, diag_key, zero_slot, diag_mask, score_scale)
    run_peak, run_total = sweep_piece(
        stats_start,
        (lax.all_gather(key_slots, "ctx", axis=1, tiled=True),),
        block_rows,
        my_rank,
        pair_of_rank,
        stats_group,
    )
    row_lse = run_peak + jnp.log(run_total)

    def values_group(running, slices, far_pair, is_own, far_places, first_row):
        chosen = far_pair < my_pair
        query_slot, key_slot = tile_slots(chosen)
        return values_update(
            running,
            query_tiles(own_query[:, None], chosen),
            key_tiles(split_heads(slices[0]), chosen),
            key_tiles(split_heads(slices[1]), chosen),
            query_slot,
            tile_mask(is_own, own_places, far_places),
            slot_pick(row_lse, query_slot),
            score_scale,
        )

    values_start = values_update(
        jnp.zeros(head_view, jnp.float32),
        diag_query,
        diag_key,
        diag_value,
        zero_slot,
        diag_mask,
        row_lse[0][None],
        score_scale,
    )
    attended = sweep_piece(
        values_start,
        (
            lax.all_gather(key_slots, "ctx", axis=1, tiled=True),
            lax.all_gather(value_slots, "ctx", axis=1, tiled=True),
        ),
        block_rows,
        my_rank,
        pair_of_rank,
        values_group,
    )
    attended_low = attended.reshape(2 * block_rows, model_width).astype(jnp.bfloat16)
    middle = (
        token_rows
        + jnp.dot(attended_low, full_output, preferred_element_type=jnp.float32)
        + full_output_bias.astype(jnp.float32)
    )
    normed_full_two, second_pullback = jax.vjp(
        layer_norm,
        middle,
        full_second_gain.astype(jnp.float32),
        full_second_shift.astype(jnp.float32),
    )
    normed_two = normed_full_two.astype(jnp.bfloat16)
    hidden = jnp.dot(
        normed_two, full_expand, preferred_element_type=jnp.float32
    ) + full_expand_bias.astype(jnp.float32)
    active_full, gelu_pullback = jax.vjp(gelu_tanh, hidden)
    active_low = active_full.astype(jnp.bfloat16)
    result = (
        middle
        + jnp.dot(active_low, full_contract, preferred_element_type=jnp.float32)
        + full_contract_bias.astype(jnp.float32)
    )
    block_out = result.astype(jnp.bfloat16)[None]
    back_input, back_output, back_expand, back_contract = (
        lax.all_gather(w_input, "dp", axis=0, tiled=True),
        lax.all_gather(w_output, "dp", axis=0, tiled=True),
        lax.all_gather(w_expand, "dp", axis=0, tiled=True),
        lax.all_gather(w_contract, "dp", axis=0, tiled=True),
    )
    grad_out_low = cotangent[0]
    grad_out = grad_out_low.astype(jnp.float32)
    grad_contract = jnp.einsum(
        "rf,rd->fd", active_low, grad_out_low, preferred_element_type=jnp.float32
    )
    grad_contract_bias = jnp.sum(grad_out, axis=0)
    grad_active = jnp.einsum(
        "rd,fd->rf", grad_out_low, back_contract, preferred_element_type=jnp.float32
    )
    grad_hidden = gelu_pullback(grad_active)[0].astype(jnp.bfloat16)
    grad_expand = jnp.einsum(
        "rd,rf->df", normed_two, grad_hidden, preferred_element_type=jnp.float32
    )
    grad_expand_bias = jnp.sum(grad_hidden.astype(jnp.float32), axis=0)
    grad_normed_two = jnp.einsum(
        "rf,df->rd", grad_hidden, back_expand, preferred_element_type=jnp.float32
    )
    grad_middle_part, grad_second_gain, grad_second_shift = second_pullback(grad_normed_two)
    grad_middle = grad_out + grad_middle_part
    grad_branch = grad_middle.astype(jnp.bfloat16)
    grad_output = jnp.einsum(
        "rd,re->de", attended_low, grad_branch, preferred_element_type=jnp.float32
    )
    grad_output_bias = jnp.sum(grad_branch.astype(jnp.float32), axis=0)
    grad_attended = jnp.einsum(
        "re,de->rd", grad_branch, back_output, preferred_element_type=jnp.float32
    ).astype(jnp.bfloat16)
    own_dout = grad_attended.reshape(head_view)
    dout_slots = grad_attended.reshape(slot_view)
    delta_rows = jnp.sum(own_dout.astype(jnp.float32) * attended, axis=-1)
    row_delta = jnp.transpose(delta_rows, (0, 2, 1))
    lse_rows = jnp.transpose(row_lse, (0, 2, 1))
    far_lse, far_delta = (
        lax.all_gather(lse_rows, "ctx", axis=1, tiled=True),
        lax.all_gather(delta_rows, "ctx", axis=1, tiled=True),
    )
    diag_probs = tile_probs(diag_query, diag_key, diag_mask, row_lse[0][None], score_scale)
    diag_dscore = tile_dscore(diag_probs, own_dout[0][None], diag_value, row_delta[0][None])
    query_start = slot_add(
        jnp.einsum("thqk,tkhd->tqhd", diag_dscore, diag_key, preferred_element_type=jnp.float32)
        * score_scale,
        zero_slot,
    )
    key_start = slot_add(
        jnp.einsum("thqk,tqhd->tkhd", diag_dscore, diag_query, preferred_element_type=jnp.float32)
        * score_scale,
        zero_slot,
    )
    value_start = slot_add(
        jnp.einsum(
            "thqk,tqhd->tkhd",
            diag_probs.astype(jnp.bfloat16),
            own_dout[0][None],
            preferred_element_type=jnp.float32,
        ),
        zero_slot,
    )

    def query_grad_group(running, slices, far_pair, is_own, far_places, first_row):
        chosen = far_pair < my_pair
        query_slot, key_slot = tile_slots(chosen)
        tile_key = key_tiles(split_heads(slices[0]), chosen)
        tile_value = key_tiles(split_heads(slices[1]), chosen)
        probs = tile_probs(
            query_tiles(own_query[:, None], chosen),
            tile_key,
            tile_mask(is_own, own_places, far_places),
            slot_pick(row_lse, query_slot),
            score_scale,
        )
        dscore = tile_dscore(
            probs,
            query_tiles(own_dout[:, None], chosen),
            tile_value,
            slot_pick(row_delta, query_slot),
        )
        part_grad = (
            jnp.einsum("thqk,tkhd->tqhd", dscore, tile_key, preferred_element_type=jnp.float32)
            * score_scale
        )
        return running + slot_add(part_grad, query_slot)

    def key_grad_group(running, slices, far_pair, is_own, far_places, first_row):
        chosen = my_pair < far_pair
        query_slot, key_slot = tile_slots(chosen)
        group_size = far_places.shape[0]
        sub_rows = far_places.shape[1]
        tile_query = query_tiles(split_heads(slices[0]), chosen)
        tile_dout = query_tiles(split_heads(slices[1]), chosen)
        lse_part = lax.dynamic_slice_in_dim(far_lse, first_row, group_size * sub_rows, 1).reshape(
            2, group_size, sub_rows, HEADS
        )
        delta_part = lax.dynamic_slice_in_dim(
            far_delta, first_row, group_size * sub_rows, 1
        ).reshape(2, group_size, sub_rows, HEADS)
        tile_lse = jnp.transpose(query_tiles(lse_part, chosen), (0, 2, 1))
        tile_delta = jnp.transpose(query_tiles(delta_part, chosen), (0, 2, 1))
        tile_key = key_tiles(own_key[:, None], chosen)
        tile_value = key_tiles(own_value[:, None], chosen)
        probs = tile_probs(
            tile_query, tile_key, tile_mask(is_own, far_places, own_places), tile_lse, score_scale
        )
        dscore = tile_dscore(probs, tile_dout, tile_value, tile_delta)
        key_part = (
            jnp.einsum("thqk,tqhd->tkhd", dscore, tile_query, preferred_element_type=jnp.float32)
            * score_scale
        )
        value_part = jnp.einsum(
            "thqk,tqhd->tkhd",
            probs.astype(jnp.bfloat16),
            tile_dout,
            preferred_element_type=jnp.float32,
        )
        return (
            running[0] + slot_add(key_part, key_slot),
            running[1] + slot_add(value_part, key_slot),
        )

    grad_query_sum = sweep_piece(
        query_start,
        (
            lax.all_gather(key_slots, "ctx", axis=1, tiled=True),
            lax.all_gather(value_slots, "ctx", axis=1, tiled=True),
        ),
        block_rows,
        my_rank,
        pair_of_rank,
        query_grad_group,
    )
    grad_key_sum, grad_value_sum = sweep_piece(
        (key_start, value_start),
        (
            lax.all_gather(query_slots, "ctx", axis=1, tiled=True),
            lax.all_gather(dout_slots, "ctx", axis=1, tiled=True),
        ),
        block_rows,
        my_rank,
        pair_of_rank,
        key_grad_group,
    )
    flat_rows = 2 * block_rows
    grad_query_low = grad_query_sum.reshape(flat_rows, model_width).astype(jnp.bfloat16)
    grad_key_low = grad_key_sum.reshape(flat_rows, model_width).astype(jnp.bfloat16)
    grad_value_low = grad_value_sum.reshape(flat_rows, model_width).astype(jnp.bfloat16)
    grad_mixed = jnp.concatenate([grad_query_low, grad_key_low, grad_value_low], axis=1)
    grad_input = jnp.einsum("rd,re->de", normed, grad_mixed, preferred_element_type=jnp.float32)
    grad_query_bias = jnp.sum(grad_query_low.astype(jnp.float32), axis=0)
    grad_value_bias = jnp.sum(grad_value_low.astype(jnp.float32), axis=0)
    grad_normed = jnp.einsum(
        "re,de->rd", grad_mixed, back_input, preferred_element_type=jnp.float32
    )
    grad_token_part, grad_first_gain, grad_first_shift = first_pullback(grad_normed)
    grad_tokens = (grad_middle + grad_token_part)[None]
    grad_local = (
        grad_first_gain,
        grad_first_shift,
        grad_input,
        grad_query_bias,
        grad_value_bias,
        grad_output,
        grad_output_bias,
        grad_second_gain,
        grad_second_shift,
        grad_expand,
        grad_expand_bias,
        grad_contract,
        grad_contract_bias,
    )
    grad_owned = (
        lax.psum_scatter(
            grad_local[0].astype(jnp.bfloat16), "dp", scatter_dimension=0, tiled=True
        ).astype(jnp.float32),
        lax.psum_scatter(
            grad_local[1].astype(jnp.bfloat16), "dp", scatter_dimension=0, tiled=True
        ).astype(jnp.float32),
        lax.psum_scatter(
            grad_local[2].astype(jnp.bfloat16), "dp", scatter_dimension=0, tiled=True
        ).astype(jnp.float32),
        lax.psum_scatter(
            grad_local[3].astype(jnp.bfloat16), "dp", scatter_dimension=0, tiled=True
        ).astype(jnp.float32),
        lax.psum_scatter(
            grad_local[4].astype(jnp.bfloat16), "dp", scatter_dimension=0, tiled=True
        ).astype(jnp.float32),
        lax.psum_scatter(
            grad_local[5].astype(jnp.bfloat16), "dp", scatter_dimension=0, tiled=True
        ).astype(jnp.float32),
        lax.psum_scatter(
            grad_local[6].astype(jnp.bfloat16), "dp", scatter_dimension=0, tiled=True
        ).astype(jnp.float32),
        lax.psum_scatter(
            grad_local[7].astype(jnp.bfloat16), "dp", scatter_dimension=0, tiled=True
        ).astype(jnp.float32),
        lax.psum_scatter(
            grad_local[8].astype(jnp.bfloat16), "dp", scatter_dimension=0, tiled=True
        ).astype(jnp.float32),
        lax.psum_scatter(
            grad_local[9].astype(jnp.bfloat16), "dp", scatter_dimension=0, tiled=True
        ).astype(jnp.float32),
        lax.psum_scatter(
            grad_local[10].astype(jnp.bfloat16), "dp", scatter_dimension=0, tiled=True
        ).astype(jnp.float32),
        lax.psum_scatter(
            grad_local[11].astype(jnp.bfloat16), "dp", scatter_dimension=0, tiled=True
        ).astype(jnp.float32),
        lax.psum_scatter(
            grad_local[12].astype(jnp.bfloat16), "dp", scatter_dimension=0, tiled=True
        ).astype(jnp.float32),
    )
    grad_final = tuple(
        lax.psum(
            (
                grad_owned[0],
                grad_owned[1],
                grad_owned[2],
                grad_owned[3],
                grad_owned[4],
                grad_owned[5],
                grad_owned[6],
                grad_owned[7],
                grad_owned[8],
                grad_owned[9],
                grad_owned[10],
                grad_owned[11],
                grad_owned[12],
            ),
            "ctx",
        )
    )
    return (block_out, grad_tokens) + tuple(grad_final)


VMEM_BYTES = 16 * 1024 * 1024
VMEM_LARGE = 28 * 1024 * 1024


def mm(left, right):
    return lax.dot_general(
        left, right, (((1,), (0,)), ((), ())), preferred_element_type=jnp.float32
    )


def mm_nt(left, right):
    return lax.dot_general(
        left, right, (((1,), (1,)), ((), ())), preferred_element_type=jnp.float32
    )


def mm_tn(left, right):
    return lax.dot_general(
        left, right, (((0,), (0,)), ((), ())), preferred_element_type=jnp.float32
    )


def aligned(index, size):
    return pl.ds(pl.multiple_of(index * size, size), size)


def norm_stats(values):
    centre = values - jnp.mean(values, axis=-1, keepdims=True)
    spread = jnp.mean(centre * centre, axis=-1, keepdims=True)
    scale = lax.rsqrt(spread + NORM_EPS)
    return centre * scale, scale


def norm_back(grad_normed, gain_row, xhat, scale):
    weighted = grad_normed * gain_row
    return scale * (
        weighted
        - jnp.mean(weighted, axis=-1, keepdims=True)
        - xhat * jnp.mean(weighted * xhat, axis=-1, keepdims=True)
    )


def column_sums(values):
    return jnp.sum(values, axis=0, keepdims=True)


def shape_of(dims, dtype):
    return jax.ShapeDtypeStruct(dims, dtype)


def local_call(
    kernel, name, outs, args, scalars=0, scratch=(), flops=0, after=(), space=pltpu.VMEM, grant=VMEM_BYTES
):
    moved = sum(math.prod(a.shape) * a.dtype.itemsize for a in tuple(args) + tuple(outs))

    def ordered(*refs):
        kernel(*refs[: len(args)], *refs[len(args) + len(after) :])

    return pl.pallas_call(
        ordered,
        out_shape=tuple(outs),
        in_specs=[pl.BlockSpec(memory_space=pltpu.SMEM)] * scalars
        + [pl.BlockSpec(memory_space=space)] * (len(args) - scalars)
        + [pl.BlockSpec(memory_space=pl.ANY)] * len(after),
        out_specs=tuple(pl.BlockSpec(memory_space=pltpu.VMEM) for _ in outs),
        scratch_shapes=list(scratch),
        compiler_params=pltpu.CompilerParams(vmem_limit_bytes=grant),
        cost_estimate=pl.CostEstimate(
            flops=flops, bytes_accessed=moved if flops else 0, transcendentals=0
        ),
        name=name,
    )(*args, *after)


def place_of_block(pair_ref, info_ref, ranks, step, half, other_core):
    core = jnp.bitwise_xor(info_ref[2], other_core)
    rank = 2 * jnp.bitwise_xor(info_ref[1], step) + core
    pair = pair_ref[rank]
    return pair if half == 0 else 2 * ranks - 1 - pair


def fill_mask(bias_ref, pair_ref, info_ref, ranks, parts, block):
    rows = 2 * parts * block
    lanes = lax.broadcasted_iota(jnp.int32, (1, rows), 1)
    query_place = lanes % block
    for step in range(parts):
        for half in range(2):
            place = place_of_block(pair_ref, info_ref, ranks, step, half, 0)
            query_place = query_place + jnp.where(
                lanes // block == 2 * step + half, place * block, 0
            )
    ahead = lax.broadcasted_iota(jnp.int32, (block, rows), 0) - query_place
    for other in range(2):
        for step in range(parts):
            for half in range(2):
                place = place_of_block(pair_ref, info_ref, ranks, step, half, other)
                start = other * rows + (2 * step + half) * block
                bias_ref[start : start + block, :] = jnp.where(
                    ahead <= -place * block, 0.0, NEG_BIG
                )


def head_parallel(ranks, chips, seq_parts):
    parts = chips
    hw = HEADS // chips * HEAD_DIM

    def core_swap(member):
        return lax.ppermute(member, "ctx", [(i, i ^ 1) for i in range(ranks)])

    def chip_swap(member, step):
        return lax.ppermute(
            member, "ctx", [(i, 2 * ((i // 2) ^ step) + i % 2) for i in range(ranks)]
        )

    def seq_swap(member, step):
        return lax.ppermute(member, "dp", [(i, i ^ step) for i in range(seq_parts)])

    def per_device_heads(
        tokens,
        pair_of_rank,
        first_gain,
        first_shift,
        w_input,
        query_bias,
        value_bias,
        w_output,
        output_bias,
        second_gain,
        second_shift,
        w_expand,
        expand_bias,
        w_contract,
        contract_bias,
        cotangent,
    ):
        bf, f32 = jnp.bfloat16, jnp.float32
        rows, width = tokens.shape[1:]
        block = rows // 2
        own_width = width // seq_parts
        ff = expand_bias.shape[0]
        total = parts * rows
        half_width = width // 2
        half_ff = ff // 2
        sub = own_width // parts
        half_own = own_width // 2
        small_rows = 16
        others = range(1, parts)
        seq_id = lax.axis_index("dp")
        rank = lax.axis_index("ctx")
        chip = rank // 2
        core = rank % 2
        info = jnp.stack([seq_id, chip, core]).astype(jnp.int32)

        side = width - 3 * hw
        pack_rows = 2 * half_own

        def pack_kernel(info_ref, tok_ref, w_ref, wo_ref, *refs):
            vecs = refs[:8]
            packed_ref, tokens_ref, w_scr, wo_scr = refs[8:12]
            scrs, sems = refs[12:20], refs[20]
            mine = pl.ds(pl.multiple_of(info_ref[2] * half_own, half_own), half_own)
            pairs = [(w_ref.at[mine], w_scr), (wo_ref.at[mine], wo_scr), (tok_ref, tokens_ref)]
            pairs += list(zip(vecs, scrs))
            copies = [
                pltpu.make_async_copy(src, dst, sems.at[i]) for i, (src, dst) in enumerate(pairs)
            ]
            for copy in copies:
                copy.start()
            for copy in copies:
                copy.wait()
            at_w = slice(half_own, 2 * half_own)
            for at in range(chips):

                @pl.when(info_ref[1] == at)
                def _():
                    for base in range(3):
                        start = base * width + at * hw
                        packed_ref[at_w, base * hw : (base + 1) * hw] = w_scr[
                            :, start : start + hw
                        ]

            packed_ref[0:half_own, :] = wo_scr[...]
            small = jnp.concatenate(
                [v[...].astype(f32).reshape(1, own_width) for v in scrs], axis=0
            )
            small = jnp.concatenate([small, jnp.zeros_like(small)], axis=0)
            packed_ref[half_own : half_own + small_rows, 3 * hw :] = small.astype(bf)
            packed_ref[half_own + small_rows :, 3 * hw :] = jnp.zeros(
                (half_own - small_rows, side), bf
            )

        small_args = (
            first_gain,
            first_shift,
            query_bias,
            value_bias,
            output_bias,
            second_gain,
            second_shift,
            contract_bias,
        )
        packed, own_tokens = local_call(
            pack_kernel,
            "pack",
            [shape_of((pack_rows, width), bf), shape_of((rows, width), bf)],
            [info, tokens[0], w_input, w_output] + list(small_args),
            scalars=1,
            scratch=[pltpu.VMEM((half_own, 3 * width), bf), pltpu.VMEM((half_own, width), bf)]
            + [pltpu.VMEM((own_width,), bf)] * 8
            + [pltpu.SemaphoreType.DMA((11,))],
            space=pltpu.HBM,
            grant=60 * 1024 * 1024,
        )
        token_two = chip_swap(own_tokens, 2)
        token_parts = [own_tokens, chip_swap(own_tokens, 1), token_two, chip_swap(token_two, 1)]
        packed_near = [seq_swap(packed, j) for j in others]

        def stack_kernel(*refs):
            depth = refs[0].shape[0]
            for i, ref in enumerate(refs[:-1]):
                refs[-1][i * depth : (i + 1) * depth, :] = ref[...]

        (packed_all,) = local_call(
            stack_kernel,
            "pack_stack",
            [shape_of(((seq_parts - 1) * pack_rows, width), bf)],
            packed_near,
            after=token_parts[1:],
        )
        packed_far = core_swap(packed_all)
        own_cot = cotangent[0]

        def pack_more_kernel(info_ref, we_ref, cot_ref, *refs):
            for j in others:
                start = pl.multiple_of(info_ref[2] * half_own, half_own)
                refs[j - 1][0:half_own, :] = we_ref[
                    pl.ds(start, half_own), aligned(jnp.bitwise_xor(info_ref[0], j), ff)
                ]
                refs[j - 1][half_own:, :] = cot_ref[...]

        more = local_call(
            pack_more_kernel,
            "pack_more",
            [shape_of((half_own + rows, width), bf)] * (seq_parts - 1),
            [info, w_expand, own_cot],
            scalars=1,
            after=[packed],
        )
        more_parts = [seq_swap(more[j - 1], j) for j in others]

        def qkv_kernel(info_ref, w_own_ref, wo_own_ref, *refs):
            toks, own_pack, packs = refs[:parts], refs[parts], refs[parts + 1 : parts + 3]
            q_ref, kv_ref, normed_ref, w_ref, vec_ref, wo_ref, vec_scr = refs[parts + 3 :]
            for at in range(chips):

                @pl.when(info_ref[1] == at)
                def _():
                    for base in range(3):
                        start = base * width + at * hw
                        w_ref[aligned(info_ref[0], own_width), base * hw : (base + 1) * hw] = (
                            w_own_ref[:, start : start + hw]
                        )

            wo_ref[info_ref[0]] = wo_own_ref[...]
            at_small = slice(half_own, half_own + small_rows)
            vec_scr[info_ref[0]] = own_pack[at_small, 3 * hw :].astype(f32)
            for j in others:
                place = jnp.bitwise_xor(info_ref[0], j)
                base = (j - 1) * pack_rows
                vec_scr[place] = packs[0][
                    base + half_own : base + half_own + small_rows, 3 * hw :
                ].astype(f32)
                for flip in range(2):
                    member = packs[flip]
                    half = jnp.bitwise_xor(info_ref[2], flip)
                    down = pl.multiple_of(half * half_own, half_own)
                    wo_ref[place, pl.ds(down, half_own), :] = member[base : base + half_own, :]
                    start = pl.multiple_of(place * own_width + half * half_own, half_own)
                    w_ref[pl.ds(start, half_own), :] = member[
                        base + half_own : base + pack_rows, 0 : 3 * hw
                    ]
            vectors = jnp.concatenate([vec_scr[j] for j in range(parts)], axis=1)
            vec_ref[...] = vectors
            chosen = vec_scr[info_ref[1]]
            for k in range(parts):
                xhat, _ = norm_stats(toks[k][...].astype(f32))
                normed_ref[k * rows : (k + 1) * rows, :] = (
                    xhat * vectors[0:1] + vectors[1:2]
                ).astype(bf)
            mixed = mm(normed_ref[...], w_ref[...])
            q_ref[...] = (mixed[:, 0:hw] + chosen[2:3]).astype(bf)
            kv_ref[:, 0:hw] = mixed[:, hw : 2 * hw].astype(bf)
            kv_ref[:, hw : 2 * hw] = (mixed[:, 2 * hw :] + chosen[3:4]).astype(bf)

        query, own_kv, normed, w_heads_full, vectors, out_full = local_call(
            qkv_kernel,
            "project",
            [
                shape_of((total, hw), bf),
                shape_of((total, 2 * hw), bf),
                shape_of((total, width), bf),
                shape_of((width, 3 * hw), bf),
                shape_of((small_rows, width), f32),
                shape_of((parts, own_width, width), bf),
            ],
            [info, w_input, w_output] + token_parts + [packed, packed_all, packed_far],
            scalars=1,
            scratch=[pltpu.VMEM((parts, small_rows, own_width), f32)],
            flops=2 * total * width * 3 * hw,
        )
        far_kv = core_swap(own_kv)

        head_count = hw // HEAD_DIM
        scale = HEAD_DIM ** (-0.5)

        def head_columns(ref, base, head):
            start = base + head * HEAD_DIM
            return ref[:, start : start + HEAD_DIM]

        def attend_kernel(info_ref, pair_ref, q_ref, kv_ref, far_ref, *refs):
            outs = refs[:parts]
            flat_ref, lse_ref, bias_ref = refs[parts:]
            fill_mask(bias_ref, pair_ref, info_ref, ranks, parts, block)
            columns = []
            for head in range(head_count):
                keys = jnp.concatenate(
                    [head_columns(kv_ref, 0, head), head_columns(far_ref, 0, head)], axis=0
                )
                values = jnp.concatenate(
                    [head_columns(kv_ref, hw, head), head_columns(far_ref, hw, head)], axis=0
                )
                scores = mm_nt(keys, head_columns(q_ref, 0, head)) * scale + bias_ref[...]
                peak = jnp.max(scores, axis=0, keepdims=True)
                weights = jnp.exp(scores - peak)
                mass = jnp.sum(weights, axis=0, keepdims=True)
                lse_ref[head : head + 1, :] = peak + jnp.log(mass)
                mixed = mm_tn(values, weights.astype(bf)) / mass
                flat_ref[head * HEAD_DIM : (head + 1) * HEAD_DIM, :] = mixed
            attended = flat_ref[...].T.astype(bf)
            for k in range(parts):
                outs[k][...] = attended[k * rows : (k + 1) * rows]

        attend_out = local_call(
            attend_kernel,
            "attend",
            [shape_of((rows, hw), bf)] * parts
            + [shape_of((hw, total), f32), shape_of((8, total), f32)],
            [info, pair_of_rank, query, own_kv, far_kv],
            scalars=2,
            scratch=[pltpu.VMEM((2 * total, total), f32)],
            flops=2 * 2 * head_count * 2 * total * total * HEAD_DIM,
            grant=VMEM_LARGE,
        )
        flat_attended, row_lse = attend_out[parts:]
        att_parts = [attend_out[0]] + [chip_swap(attend_out[k], k) for k in others]

        def middle_kernel(info_ref, tok_ref, vec_ref, w_ref, *refs):
            atts = refs[:parts]
            mid_ref, normed_ref = refs[parts:]
            middle = tok_ref[...].astype(f32) + vec_ref[4:5]
            for k in range(parts):
                middle = middle + mm(atts[k][...], w_ref[jnp.bitwise_xor(info_ref[1], k)])
            mid_ref[...] = middle
            xhat, _ = norm_stats(middle)
            normed_ref[...] = (xhat * vec_ref[5:6] + vec_ref[6:7]).astype(bf)

        middle, own_normed_two = local_call(
            middle_kernel,
            "middle",
            [shape_of((rows, width), f32), shape_of((rows, width), bf)],
            [info, own_tokens, vectors, out_full] + att_parts,
            scalars=1,
            flops=2 * rows * width * width,
        )

        def expand_stack_kernel(*refs):
            for i, ref in enumerate(refs[:-1]):
                refs[-1][i * half_own : (i + 1) * half_own, :] = ref[0:half_own, :]

        (expand_all,) = local_call(
            expand_stack_kernel,
            "expand_stack",
            [shape_of(((seq_parts - 1) * half_own, ff), bf)],
            more_parts,
            after=[own_normed_two],
        )
        expand_far = core_swap(expand_all)
        n2_parts = [own_normed_two] + [seq_swap(own_normed_two, j) for j in others]

        span = ff // parts + own_width

        def ffn_kernel(info_ref, bias_ref, wc_ref, we_ref, own_cot_ref, far_we_ref, *refs):
            n2s = refs[:parts]
            mores = refs[parts : 2 * parts - 1]
            gns = refs[2 * parts - 1 : 3 * parts - 1]
            results = refs[3 * parts - 1 : 4 * parts - 1]
            keep_ref, send_ref, sum_ref = refs[4 * parts - 1 : 4 * parts + 2]
            active_ref, gh_ref, n2_ref, cot_ref, w_scr, scr = refs[4 * parts + 2 :]
            w_scr[aligned(info_ref[0], own_width), :] = we_ref[:, aligned(info_ref[0], ff)]
            for j in range(seq_parts):
                at = slice(j * rows, (j + 1) * rows)
                n2_ref[at, :] = n2s[j][...]
                if j == 0:
                    cot_ref[at, :] = own_cot_ref[...]
                    continue
                place = jnp.bitwise_xor(info_ref[0], j)
                for flip in range(2):
                    half = jnp.bitwise_xor(info_ref[2], flip)
                    start = pl.multiple_of(place * own_width + half * half_own, half_own)
                    w_scr[pl.ds(start, half_own), :] = (
                        far_we_ref[(j - 1) * half_own : j * half_own, :]
                        if flip
                        else mores[j - 1][0:half_own, :]
                    )
                cot_ref[at, :] = mores[j - 1][half_own:, :]
            hidden = mm(n2_ref[...], w_scr[...]) + bias_ref[...].astype(f32).reshape(1, ff)
            square = hidden * hidden
            curve = jnp.tanh(GELU_SCALE * hidden * (1.0 + GELU_CUBIC * square))
            active_ref[...] = (0.5 * hidden * (1.0 + curve)).astype(bf)
            slope = 0.5 * (1.0 + curve) + 0.5 * hidden * (1.0 - curve * curve) * GELU_SCALE * (
                1.0 + 3.0 * GELU_CUBIC * square
            )
            grad_hidden = mm_nt(cot_ref[...], wc_ref[...]) * slope
            gh_ref[...] = grad_hidden.astype(bf)
            sum_ref[...] = column_sums(gh_ref[...].astype(f32))
            grad = mm_nt(gh_ref[...], w_scr[...]).astype(bf)
            for j in range(parts):
                gns[j][...] = grad[j * rows : (j + 1) * rows]
            result = mm(active_ref[...], wc_ref[...]).astype(bf)
            for j in range(seq_parts):
                results[j][...] = result[j * rows : (j + 1) * rows]
            core_id = info_ref[2]
            for flip, out_ref in ((0, keep_ref), (1, send_ref)):
                half = jnp.bitwise_xor(core_id, flip)
                scr[...] = mm_tn(active_ref[...], cot_ref[:, aligned(half, half_width)]).astype(bf)
                for part in range(parts):
                    rows_to = ff // parts
                    out_ref[part, 0:rows_to, :] = scr[part * rows_to : (part + 1) * rows_to, :]
                scr[...] = mm_tn(n2_ref[...], gh_ref[:, aligned(half, half_ff)]).astype(bf)
                for part in range(parts):
                    for j in range(seq_parts):
                        at = ff // parts + j * sub
                        row = j * own_width + part * sub
                        out_ref[part, at : at + sub, :] = scr[row : row + sub, :]

        ffn_out = local_call(
            ffn_kernel,
            "feed",
            [shape_of((rows, width), bf)] * 2 * parts
            + [
                shape_of((parts, span, half_width), bf),
                shape_of((parts, span, half_width), bf),
                shape_of((1, ff), f32),
            ],
            [info, expand_bias, w_contract, w_expand, own_cot, expand_far] + n2_parts + more_parts,
            scalars=1,
            scratch=[
                pltpu.VMEM((total, ff), bf),
                pltpu.VMEM((total, ff), bf),
                pltpu.VMEM((total, width), bf),
                pltpu.VMEM((total, width), bf),
                pltpu.VMEM((width, ff), bf),
                pltpu.VMEM((width, half_ff), bf),
            ],
            flops=6 * 2 * total * width * ff,
            grant=VMEM_LARGE,
        )
        results = ffn_out[parts : 2 * parts]
        ffn_keep, ffn_send, grad_expand_row = ffn_out[2 * parts :]
        gn_parts = [ffn_out[0]] + [seq_swap(ffn_out[j], j) for j in others]
        ffn_far = core_swap(ffn_send)

        def halve_kernel(info_ref, keep_ref, far_ref, own_ref, out_ref):
            for k in range(parts):
                at = jnp.bitwise_xor(info_ref[1], k)
                piece = keep_ref[at].astype(f32) + far_ref[at].astype(f32)
                if k % 2:
                    out_ref[k // 2] = piece.astype(bf)
                else:
                    own_ref[k // 2] = piece

        rs_own, rs_send = local_call(
            halve_kernel,
            "feed_halves",
            [
                shape_of((parts // 2, span, half_width), f32),
                shape_of((parts // 2, span, half_width), bf),
            ],
            [info, ffn_keep, ffn_far],
            scalars=1,
        )
        rs_far = chip_swap(rs_send, 1)

        def back_kernel(info_ref, mid_ref, vec_ref, cot_ref, w_ref, *refs):
            gns = refs[:parts]
            douts = refs[parts : 2 * parts]
            gmid_ref, branch_ref, sums_ref = refs[2 * parts :]
            grad = gns[0][...].astype(f32)
            for j in others:
                grad = grad + gns[j][...].astype(f32)
            xhat, spread = norm_stats(mid_ref[...])
            cot = cot_ref[...].astype(f32)
            grad_middle = cot + norm_back(grad, vec_ref[5:6], xhat, spread)
            gmid_ref[...] = grad_middle
            branch = grad_middle.astype(bf)
            branch_ref[...] = branch
            for k in range(parts):
                douts[k][...] = mm_nt(branch, w_ref[jnp.bitwise_xor(info_ref[1], k)]).astype(bf)
            sums_ref[0:1, :] = column_sums(branch.astype(f32))
            sums_ref[1:2, :] = column_sums(grad * xhat)
            sums_ref[2:3, :] = column_sums(grad)
            sums_ref[3:4, :] = column_sums(cot)

        back_out = local_call(
            back_kernel,
            "middle_back",
            [shape_of((rows, hw), bf)] * parts
            + [
                shape_of((rows, width), f32),
                shape_of((rows, width), bf),
                shape_of((8, width), f32),
            ],
            [info, middle, vectors, own_cot, out_full] + gn_parts,
            scalars=1,
            after=[rs_send],
            flops=2 * rows * width * width,
        )
        grad_middle, grad_branch, late_sums = back_out[parts:]
        dout_parts = [back_out[0]] + [chip_swap(back_out[k], k) for k in others]

        def out_weights_kernel(info_ref, branch_ref, *refs):
            atts = refs[:parts]
            keep_ref, send_ref = refs[parts:]
            for flip, out_ref in ((0, keep_ref), (1, send_ref)):
                half = jnp.bitwise_xor(info_ref[2], flip)
                piece = branch_ref[:, aligned(half, half_width)]
                for k in range(parts):
                    out_ref[jnp.bitwise_xor(info_ref[1], k)] = mm_tn(atts[k][...], piece).astype(bf)

        out_keep, out_send = local_call(
            out_weights_kernel,
            "output_weights",
            [shape_of((parts, hw, half_width), bf)] * 2,
            [info, grad_branch] + att_parts,
            scalars=1,
            flops=2 * rows * width * width,
        )
        out_far = core_swap(out_send)

        fold = own_width // 2
        rider = -(-sub // 32) * 16
        pair_rows = fold // 2
        at_outs = slice(half_own, half_own + pair_rows)

        def fold_in(value):
            down = value.shape[0] // 2
            return jnp.concatenate([value[0:down], value[down:]], axis=1)

        def fold_out(value):
            across = value.shape[1] // 2
            return jnp.concatenate([value[:, 0:across], value[:, across:]], axis=0)

        def out_halves_kernel(info_ref, keep_ref, far_ref, own_ref, send_ref, scr):
            mine = info_ref[1] % 2
            for to in range(seq_parts):
                whole = fold_in(keep_ref[to].astype(f32) + far_ref[to].astype(f32))
                scr[0] = whole[0:pair_rows]
                scr[1] = whole[pair_rows:]
                own_ref[to] = scr[mine]
                send_ref[to] = scr[1 - mine].astype(bf)

        oh_own, oh_send = local_call(
            out_halves_kernel,
            "output_halves",
            [
                shape_of((seq_parts, pair_rows, width), f32),
                shape_of((seq_parts, pair_rows, width), bf),
            ],
            [info, out_keep, out_far],
            scalars=1,
            scratch=[pltpu.VMEM((2, pair_rows, width), f32)],
        )
        oh_far = chip_swap(oh_send, 1)

        def quarter_kernel(own_ref, far_ref, keep_ref, send_ref):
            keep_ref[...] = own_ref[0] + far_ref[0].astype(f32)
            send_ref[...] = (own_ref[1] + far_ref[1].astype(f32)).astype(bf)

        rs_own_two, rs_send_two = local_call(
            quarter_kernel,
            "feed_quarters",
            [shape_of((span, half_width), f32), shape_of((span, half_width), bf)],
            [rs_own, rs_far],
            after=[dout_parts[parts - 1]],
        )
        rs_far_two = chip_swap(rs_send_two, 2)

        def attend_back_kernel(info_ref, pair_ref, q_ref, kv_ref, far_ref, flat_ref, lse_ref, *refs):
            douts = refs[:parts]
            dq_ref, own_ref, send_ref, bias_ref, dout_ref = refs[parts:]
            fill_mask(bias_ref, pair_ref, info_ref, ranks, parts, block)
            for k in range(parts):
                dout_ref[k * rows : (k + 1) * rows, :] = douts[k][...].astype(f32)
            flat_dout = dout_ref[...].T
            for head in range(head_count):
                at = slice(head * HEAD_DIM, (head + 1) * HEAD_DIM)
                keys = jnp.concatenate(
                    [head_columns(kv_ref, 0, head), head_columns(far_ref, 0, head)], axis=0
                )
                values = jnp.concatenate(
                    [head_columns(kv_ref, hw, head), head_columns(far_ref, hw, head)], axis=0
                )
                queries = head_columns(q_ref, 0, head)
                dout = dout_ref[:, at].astype(bf)
                dout_turned = flat_dout[at, :]
                delta = column_sums(dout_turned * flat_ref[at, :])
                scores = mm_nt(keys, queries) * scale + bias_ref[...]
                probs = jnp.exp(scores - lse_ref[head : head + 1, :])
                grad_value = mm(probs.astype(bf), dout)
                grad_weights = mm(values, dout_turned.astype(bf))
                grad_scores = (probs * (grad_weights - delta)).astype(bf)
                grad_key = mm(grad_scores, queries) * scale
                dq_ref[at, :] = mm_tn(keys, grad_scores) * scale
                vat = slice(hw + head * HEAD_DIM, hw + (head + 1) * HEAD_DIM)
                own_ref[:, at] = grad_key[0:total]
                own_ref[:, vat] = grad_value[0:total]
                send_ref[:, at] = grad_key[total:].astype(bf)
                send_ref[:, vat] = grad_value[total:].astype(bf)

        flat_dq, dkv_own, dkv_send = local_call(
            attend_back_kernel,
            "attend_back",
            [
                shape_of((hw, total), f32),
                shape_of((total, 2 * hw), f32),
                shape_of((total, 2 * hw), bf),
            ],
            [info, pair_of_rank, query, own_kv, far_kv, flat_attended, row_lse] + dout_parts,
            scalars=2,
            after=[rs_send_two, out_send],
            scratch=[pltpu.VMEM((2 * total, total), f32), pltpu.VMEM((total, hw), f32)],
            flops=8 * 5 * 2 * head_count * 2 * total * total * HEAD_DIM,
            grant=VMEM_LARGE,
        )
        dkv_far = core_swap(dkv_send)

        def normed_back_kernel(dq_ref, own_ref, far_ref, w_ref, *refs):
            toks = refs[:parts]
            keep_ref, *send_refs, mixed_ref, sums_ref, bias_ref = refs[parts:]
            mixed_ref[:, 0:hw] = dq_ref[...].T.astype(bf)
            mixed_ref[:, hw:] = (own_ref[...] + far_ref[...].astype(f32)).astype(bf)
            shift_sum = jnp.zeros((1, width), f32)
            gain_sum = jnp.zeros((1, width), f32)
            for k in range(parts):
                grad = mm_nt(mixed_ref[k * rows : (k + 1) * rows, :], w_ref[...])
                if k % 2:
                    send_refs[k // 2][...] = grad.astype(bf)
                else:
                    keep_ref[k // 2] = grad
                xhat, _ = norm_stats(toks[k][...].astype(f32))
                shift_sum = shift_sum + column_sums(grad)
                gain_sum = gain_sum + column_sums(grad * xhat)
            sums_ref[0:1, :] = gain_sum
            sums_ref[1:2, :] = shift_sum
            bias_ref[0:1, :] = column_sums(mixed_ref[...].astype(f32))

        nb_out = local_call(
            normed_back_kernel,
            "normed_back",
            [
                shape_of((parts // 2, rows, width), f32),
                shape_of((rows, width), bf),
                shape_of((rows, width), bf),
                shape_of((total, 3 * hw), bf),
                shape_of((8, width), f32),
                shape_of((8, 3 * hw), f32),
            ],
            [flat_dq, dkv_own, dkv_far, w_heads_full] + token_parts,
            flops=0,
        )
        gt_keep, *gt_send, grad_mixed, first_sums, mixed_sums = nb_out
        gt_far = [chip_swap(member, 1) for member in gt_send]


        def input_weights_kernel(
            info_ref, normed_ref, mixed_ref, first_ref, bias_ref, late_ref, row_ref, *refs
        ):
            keep_ref, *send_refs, grad_scr, small_scr = refs
            grad_scr[...] = mm_tn(normed_ref[...], mixed_ref[...])
            core_id, chip_id, seq = info_ref[2], info_ref[1], info_ref[0]
            small_scr[...] = jnp.zeros_like(small_scr)
            for j in range(seq_parts):
                at = slice(j * own_width, (j + 1) * own_width)
                small_scr[j, 0:2, :] = first_ref[0:2, at]
                small_scr[j, 4:8, :] = late_ref[0:4, at]
            small_scr[chip_id, 2:3, :] = bias_ref[0:1, 0:hw]
            small_scr[chip_id, 3:4, :] = bias_ref[0:1, 2 * hw : 3 * hw]
            for j in range(ff // own_width):
                small_scr[seq, 8 + j : 9 + j, :] = row_ref[:, j * own_width : (j + 1) * own_width]
            for flip in range(2):
                half = jnp.bitwise_xor(core_id, flip)
                for j in range(seq_parts):
                    out_ref = send_refs[j] if flip else keep_ref.at[j]
                    start = pl.multiple_of(j * own_width + half * half_own, 16)
                    out_ref[:, 0 : 3 * hw] = grad_scr[pl.ds(start, half_own), :].astype(bf)
                    out_ref[0:small_rows, 3 * hw :] = small_scr[j].astype(bf)
                    out_ref[small_rows:, 3 * hw :] = jnp.zeros(
                        (half_own - small_rows, side), bf
                    )

        in_keep, *in_send = local_call(
            input_weights_kernel,
            "input_weights",
            [shape_of((seq_parts, half_own, width), bf)]
            + [shape_of((half_own, width), bf)] * seq_parts,
            [info, normed, grad_mixed, first_sums, mixed_sums, late_sums, grad_expand_row],
            scalars=1,
            scratch=[
                pltpu.VMEM((width, 3 * hw), f32),
                pltpu.VMEM((seq_parts, small_rows, own_width), f32),
            ],
            flops=0,
        )
        in_far = [core_swap(member) for member in in_send]

        res_parts = [results[0]] + [seq_swap(results[j], j) for j in others]

        def result_kernel(mid_ref, vec_ref, *refs):
            result = mid_ref[...] + vec_ref[7:8]
            for j in range(seq_parts):
                result = result + refs[j][...].astype(f32)
            refs[seq_parts][0] = result.astype(bf)
            refs[seq_parts + 1][...] = jnp.zeros((8, 128), f32)

        block_out, block_done = local_call(
            result_kernel,
            "result",
            [shape_of((1, rows, width), bf), shape_of((8, 128), f32)],
            [middle, vectors] + res_parts,
            after=[in_keep],
        )

        def dp_pack_kernel(
            info_ref, own_ref, far_two_ref, keep_ref, ok_ref, of_ref, *refs
        ):
            fars, refs = refs[:seq_parts], refs[seq_parts:]
            con_ref, scr, far_scr = refs[seq_parts:]
            for j in range(seq_parts):
                far_scr[j] = fars[j][...]
            whole = own_ref[...] + far_two_ref[...].astype(f32)
            con_ref[...] = whole[0 : ff // parts].astype(bf)
            scr[...] = whole[ff // parts :]
            for j in range(seq_parts):
                at = jnp.bitwise_xor(info_ref[0], j)
                refs[j][0:half_own, :] = (
                    keep_ref[at].astype(f32) + far_scr[at].astype(f32)
                ).astype(bf)
                refs[j][at_outs, :] = (ok_ref[at] + of_ref[at].astype(f32)).astype(bf)
                piece = fold_in(scr[aligned(at, sub), :])
                piece = jnp.concatenate(
                    [piece, jnp.zeros((rider - sub // 2, width), f32)], axis=0
                )
                refs[j][half_own + pair_rows :, :] = piece.astype(bf)
        dp_out = local_call(
            dp_pack_kernel,
            "owners",
            [shape_of((half_own + pair_rows + rider, width), bf)] * seq_parts
            + [shape_of((ff // parts, half_width), bf)],
            [info, rs_own_two, rs_far_two, in_keep, oh_own, oh_far] + in_far,
            scalars=1,
            scratch=[
                pltpu.VMEM((own_width, half_ff), f32),
                pltpu.VMEM((seq_parts, half_own, width), bf),
            ],
            after=[block_done],
        )
        dp_parts = [dp_out[0]] + [seq_swap(dp_out[j], j) for j in others]
        con_one = dp_out[seq_parts]

        def half_sum_kernel(keep_ref, first_ref, second_ref, own_ref, send_ref):
            own_ref[...] = keep_ref[0] + first_ref[...].astype(f32)
            send_ref[...] = (keep_ref[1] + second_ref[...].astype(f32)).astype(bf)

        gt_own, gt_send_two = local_call(
            half_sum_kernel,
            "tokens_halves",
            [shape_of((rows, width), f32), shape_of((rows, width), bf)],
            [gt_keep] + gt_far,
            after=[con_one],
        )
        con_two = chip_swap(con_one, 2)
        gt_far_two = chip_swap(gt_send_two, 2)

        con_one_far = chip_swap(con_one, 1)
        con_two_far = chip_swap(con_two, 1)

        con_parts = [con_one, con_one_far, con_two, con_two_far]
        con_far = [core_swap(member) for member in con_parts]

        def contract_kernel(info_ref, *refs):
            con_ref, done_ref = refs[2 * parts :]
            done_ref[...] = jnp.zeros_like(done_ref)
            for flip in range(2):
                lanes = aligned(jnp.bitwise_xor(info_ref[2], flip), half_width)
                for k in range(parts):
                    at = jnp.bitwise_xor(info_ref[1], k)
                    con_ref[aligned(at, ff // parts), lanes] = refs[flip * parts + k][...].astype(
                        f32
                    )

        grad_contract, contract_done = local_call(
            contract_kernel,
            "contract_final",
            [shape_of((ff, width), f32), shape_of((8, 128), f32)],
            [info] + con_parts + con_far,
            scalars=1,
        )

        def dp_sum_kernel(info_ref, *refs):
            owned = refs[:seq_parts]
            last_ref, scr = refs[seq_parts:]
            top = half_own + pair_rows
            whole = owned[0][0:top, :].astype(f32)
            for j in others:
                whole = whole + owned[j][0:top, :].astype(f32)
            last_ref[0:top, :] = whole.astype(bf)
            for j in range(seq_parts):
                place = jnp.bitwise_xor(info_ref[0], j)
                piece = owned[j][top:, :].astype(f32)
                scr[aligned(place, sub), :] = fold_out(piece[0 : sub // 2])
            last_ref[top:, :] = fold_in(scr[...]).astype(bf)

        (last_one,) = local_call(
            dp_sum_kernel,
            "shares",
            [shape_of((half_own + pair_rows + fold, width), bf)],
            [info] + dp_parts,
            scalars=1,
            scratch=[pltpu.VMEM((own_width, half_ff), f32)],
            after=[con_one_far, con_two_far, gt_far_two],
        )
        last_two = chip_swap(last_one, 2)
        last_one_far = chip_swap(last_one, 1)
        def tokens_kernel(tok_ref, vec_ref, gmid_ref, own_ref, far_ref, out_ref, done_ref):
            done_ref[...] = jnp.zeros_like(done_ref)
            grad = own_ref[...] + far_ref[...].astype(f32)
            xhat, spread = norm_stats(tok_ref[...].astype(f32))
            out_ref[0] = gmid_ref[...] + norm_back(grad, vec_ref[0:1], xhat, spread)

        grad_tokens, tokens_done = local_call(
            tokens_kernel,
            "tokens_back",
            [shape_of((1, rows, width), f32), shape_of((8, 128), f32)],
            [own_tokens, vectors, grad_middle, gt_own, gt_far_two],
        )

        def pass_kernel(in_ref, out_ref):
            out_ref[...] = in_ref[...]

        (last_two_on,) = local_call(
            pass_kernel,
            "pass_on",
            [shape_of((half_own + pair_rows + fold, width), bf)],
            [last_two],
            after=[contract_done, tokens_done, last_one_far],
        )
        last_two_far = chip_swap(last_two_on, 1)
        last_parts = [last_one, last_one_far, last_two, last_two_far]
        last_far = [core_swap(member) for member in last_parts]

        def last_kernel(info_ref, *refs):
            gin_ref, gout_ref, exp_ref = refs[2 * parts : 2 * parts + 3]
            bias_ref, smalls, scr, out_scr = refs[2 * parts + 3], refs[2 * parts + 4 : -2], *refs[-2:]
            for flip in range(2):
                half = jnp.bitwise_xor(info_ref[2], flip)
                outs = [jnp.zeros((pair_rows, width), f32)] * 2
                for k in range(parts):
                    at = jnp.bitwise_xor(info_ref[1], k)
                    piece = refs[flip * parts + k][...].astype(f32)
                    scr[at, aligned(half, half_own), :] = piece[0:half_own, 0 : 3 * hw]
                    outs[k % 2] = outs[k % 2] + piece[at_outs]
                    turned = fold_out(piece[half_own + pair_rows :])
                    for j in range(seq_parts):
                        cols = pl.ds(pl.multiple_of(j * ff + half * half_ff, 128), half_ff)
                        exp_ref[aligned(at, sub), cols] = turned[j * sub : (j + 1) * sub]
                mine = info_ref[1] % 2
                out_scr[mine] = outs[0]
                out_scr[1 - mine] = outs[1]
                gout_ref[:, aligned(half, half_width)] = fold_out(
                    jnp.concatenate([out_scr[0], out_scr[1]], axis=0)
                )
            for at in range(parts):
                for base in range(3):
                    start = base * width + at * hw
                    gin_ref[:, start : start + hw] = scr[at, :, base * hw : (base + 1) * hw]
            small = refs[0][0:small_rows, 3 * hw :].astype(f32)
            for k in others:
                small = small + refs[k][0:small_rows, 3 * hw :].astype(f32)
            for i in range(8):
                smalls[i][...] = small[i : i + 1].reshape(own_width)
            bias_ref[...] = jnp.concatenate(
                [small[8 + i : 9 + i] for i in range(ff // own_width)], axis=1
            ).reshape(ff)

        last_out = local_call(
            last_kernel,
            "weights_final",
            [
                shape_of((own_width, 3 * width), f32),
                shape_of((own_width, width), f32),
                shape_of((own_width, seq_parts * ff), f32),
                shape_of((ff,), f32),
            ]
            + [shape_of((own_width,), f32)] * 8,
            [info] + last_parts + last_far,
            scalars=1,
            scratch=[
                pltpu.VMEM((parts, own_width, 3 * hw), f32),
                pltpu.VMEM((2, pair_rows, width), f32),
            ],
            grant=VMEM_LARGE,
        )
        grad_input, grad_output, grad_expand, grad_expand_bias = last_out[:4]
        small_of = last_out[4:]
        return (
            block_out,
            grad_tokens,
            small_of[0],
            small_of[1],
            grad_input,
            small_of[2],
            small_of[3],
            grad_output,
            small_of[4],
            small_of[5],
            small_of[6],
            grad_expand,
            grad_expand_bias,
            grad_contract,
            small_of[7],
        )

    return per_device_heads


def solution(mesh):
    ranks = mesh.shape["ctx"]
    chips = ranks // 2
    if chips == mesh.shape["dp"] and HEADS % chips == 0 and chips & (chips - 1) == 0:
        body = head_parallel(ranks, chips, mesh.shape["dp"])
    else:
        body = per_device
    return jax.shard_map(
        body,
        mesh=mesh,
        in_specs=(
            P("dp", "ctx", None),
            P(),
            P("dp"),
            P("dp"),
            P("dp", None),
            P("dp"),
            P("dp"),
            P("dp", None),
            P("dp"),
            P("dp"),
            P("dp"),
            P("dp", None),
            P("dp"),
            P("dp", None),
            P("dp"),
            P("dp", "ctx", None),
        ),
        out_specs=(
            P("dp", "ctx", None),
            P("dp", "ctx", None),
            P("dp"),
            P("dp"),
            P("dp", None),
            P("dp"),
            P("dp"),
            P("dp", None),
            P("dp"),
            P("dp"),
            P("dp"),
            P("dp", None),
            P("dp"),
            P("dp", None),
            P("dp"),
        ),
        check_vma=False,
    )
```

```python
import math

import jax
import jax.numpy as jnp
from jax import lax
from jax.experimental import pallas as pl
from jax.experimental.pallas import tpu as pltpu
from jax.sharding import PartitionSpec as P

HEADS = 12
HEAD_DIM = 64


NEG_BIG = -1e30
NORM_EPS = 1e-05
GELU_SCALE = 0.7978845608028654
GELU_CUBIC = 0.044715


def gelu_tanh(values):
    return (
        0.5
        * values
        * (1.0 + jnp.tanh(GELU_SCALE * (values + GELU_CUBIC * values * values * values)))
    )


def layer_norm(values, gain_row, shift_row):
    centre = values - jnp.mean(values, axis=-1, keepdims=True)
    spread = jnp.mean(centre * centre, axis=-1, keepdims=True)
    return centre * lax.rsqrt(spread + NORM_EPS) * gain_row + shift_row


def lookup_pair(pair_table, positions):
    ranks_all = jnp.arange(pair_table.shape[0], dtype=jnp.int32)
    return jnp.sum(jnp.where(positions[..., None] == ranks_all, pair_table, 0), axis=-1)


def group_count(blocks, sub_rows):
    chosen_count = 1
    for candidate in range(1, blocks + 1):
        if blocks % candidate == 0 and candidate * sub_rows <= max(512, sub_rows):
            chosen_count = candidate
    return chosen_count


def slot_mask(slot_ids, wanted, rank_count):
    return (slot_ids == wanted).reshape((-1,) + (1,) * (rank_count - 1))


def slot_add(values, slot_ids):
    early_sum = jnp.sum(jnp.where(slot_mask(slot_ids, 0, values.ndim), values, 0.0), axis=0)
    late_sum = jnp.sum(jnp.where(slot_mask(slot_ids, 1, values.ndim), values, 0.0), axis=0)
    return jnp.stack([early_sum, late_sum])


def slot_max(values, slot_ids):
    early_max = jnp.max(jnp.where(slot_mask(slot_ids, 0, values.ndim), values, NEG_BIG), axis=0)
    late_max = jnp.max(jnp.where(slot_mask(slot_ids, 1, values.ndim), values, NEG_BIG), axis=0)
    return jnp.stack([early_max, late_max])


def slot_pick(per_slot, slot_ids):
    return jnp.where(slot_mask(slot_ids, 0, per_slot.ndim), per_slot[0][None], per_slot[1][None])


def query_tiles(blocks, chosen):
    target = chosen.shape + blocks.shape[2:]
    chosen_view = chosen.reshape((-1,) + (1,) * (blocks.ndim - 2))
    late_part = jnp.broadcast_to(blocks[1], target)
    picked = jnp.where(chosen_view, blocks[0], blocks[1])
    return jnp.concatenate([late_part, picked], axis=0)


def key_tiles(blocks, chosen):
    target = chosen.shape + blocks.shape[2:]
    chosen_view = chosen.reshape((-1,) + (1,) * (blocks.ndim - 2))
    early_part = jnp.broadcast_to(blocks[0], target)
    picked = jnp.where(chosen_view, blocks[0], blocks[1])
    return jnp.concatenate([early_part, picked], axis=0)


def tile_slots(chosen):
    late_slot = jnp.where(chosen, 0, 1).astype(jnp.int32)
    query_slot = jnp.concatenate([jnp.ones_like(late_slot), late_slot])
    key_slot = jnp.concatenate([jnp.zeros_like(late_slot), late_slot])
    return (query_slot, key_slot)


def tile_mask(is_own, query_places, key_places):
    visible = key_places[:, None, :] <= query_places[:, :, None]
    visible = jnp.logical_or(visible, jnp.logical_not(is_own)[:, None, None])
    return jnp.concatenate([jnp.ones_like(visible), visible], axis=0)


def tile_scores(tile_query, tile_key, score_scale):
    return (
        jnp.einsum("tqhd,tkhd->thqk", tile_query, tile_key, preferred_element_type=jnp.float32)
        * score_scale
    )


def tile_probs(tile_query, tile_key, tile_visible, row_lse, score_scale):
    scores = tile_scores(tile_query, tile_key, score_scale)
    return jnp.where(tile_visible[:, None], jnp.exp(scores - row_lse[..., None]), 0.0)


def tile_dscore(probs, tile_dout, tile_value, row_delta):
    grad_probs = jnp.einsum(
        "tqhd,tkhd->thqk", tile_dout, tile_value, preferred_element_type=jnp.float32
    )
    return (probs * (grad_probs - row_delta[..., None])).astype(jnp.bfloat16)


def stats_update(running, tile_query, tile_key, query_slot, tile_visible, score_scale):
    run_peak, run_total = running
    visible = tile_visible[:, None]
    masked = jnp.where(visible, tile_scores(tile_query, tile_key, score_scale), NEG_BIG)
    new_peak = jnp.maximum(run_peak, slot_max(jnp.max(masked, axis=-1), query_slot))
    weights = jnp.where(visible, jnp.exp(masked - slot_pick(new_peak, query_slot)[..., None]), 0.0)
    run_total = run_total * jnp.exp(run_peak - new_peak) + slot_add(
        jnp.sum(weights, axis=-1), query_slot
    )
    return (new_peak, run_total)


def values_update(
    running, tile_query, tile_key, tile_value, query_slot, tile_visible, row_lse, score_scale
):
    probs = tile_probs(tile_query, tile_key, tile_visible, row_lse, score_scale)
    part_out = jnp.einsum(
        "thqk,tkhd->tqhd",
        probs.astype(jnp.bfloat16),
        tile_value,
        preferred_element_type=jnp.float32,
    )
    return running + slot_add(part_out, query_slot)


def sweep_piece(carried, pieces, block_rows, my_rank, pair_table, update):
    piece_rows = pieces[0].shape[1]
    sub_rows = math.gcd(piece_rows, block_rows)
    unit_count = piece_rows // sub_rows
    group_size = group_count(unit_count, sub_rows)

    def group_step(loop_index, running):
        offset = loop_index * (group_size * sub_rows)
        slices = tuple(
            (
                lax.dynamic_slice_in_dim(member, offset, group_size * sub_rows, 1).reshape(
                    (2, group_size, sub_rows) + member.shape[2:]
                )
                for member in pieces
            )
        )
        places = offset + jnp.arange(group_size * sub_rows, dtype=jnp.int32).reshape(
            group_size, sub_rows
        )
        far_ranks = places[:, 0] // block_rows
        far_pair = lookup_pair(pair_table, far_ranks)
        return update(running, slices, far_pair, far_ranks == my_rank, places % block_rows, offset)

    return lax.fori_loop(0, unit_count // group_size, group_step, carried)


def per_device(
    tokens,
    pair_of_rank,
    first_gain,
    first_shift,
    w_input,
    query_bias,
    value_bias,
    w_output,
    output_bias,
    second_gain,
    second_shift,
    w_expand,
    expand_bias,
    w_contract,
    contract_bias,
    cotangent,
):
    gathered = (
        lax.all_gather(first_gain, "dp", axis=0, tiled=True),
        lax.all_gather(first_shift, "dp", axis=0, tiled=True),
        lax.all_gather(w_input, "dp", axis=0, tiled=True),
        lax.all_gather(query_bias, "dp", axis=0, tiled=True),
        lax.all_gather(value_bias, "dp", axis=0, tiled=True),
        lax.all_gather(w_output, "dp", axis=0, tiled=True),
        lax.all_gather(output_bias, "dp", axis=0, tiled=True),
        lax.all_gather(second_gain, "dp", axis=0, tiled=True),
        lax.all_gather(second_shift, "dp", axis=0, tiled=True),
        lax.all_gather(w_expand, "dp", axis=0, tiled=True),
        lax.all_gather(expand_bias, "dp", axis=0, tiled=True),
        lax.all_gather(w_contract, "dp", axis=0, tiled=True),
        lax.all_gather(contract_bias, "dp", axis=0, tiled=True),
    )
    (
        full_first_gain,
        full_first_shift,
        full_input,
        full_query_bias,
        full_value_bias,
        full_output,
        full_output_bias,
        full_second_gain,
        full_second_shift,
        full_expand,
        full_expand_bias,
        full_contract,
        full_contract_bias,
    ) = gathered
    model_width = tokens.shape[2]
    block_rows = tokens.shape[1] // 2
    score_scale = HEAD_DIM ** (-0.5)
    slot_view = (2, block_rows, model_width)
    head_view = (2, block_rows, HEADS, HEAD_DIM)
    my_rank = lax.axis_index("ctx")
    my_pair = lookup_pair(pair_of_rank, my_rank)
    own_places = jnp.arange(block_rows, dtype=jnp.int32)[None, :]
    diag_mask = (own_places <= own_places.reshape(-1, 1))[None]
    zero_slot = jnp.zeros((1,), jnp.int32)

    def split_heads(member):
        return member.reshape(member.shape[:3] + (HEADS, HEAD_DIM))

    token_rows = tokens[0].astype(jnp.float32)
    normed_full, first_pullback = jax.vjp(
        layer_norm,
        token_rows,
        full_first_gain.astype(jnp.float32),
        full_first_shift.astype(jnp.float32),
    )
    normed = normed_full.astype(jnp.bfloat16)
    mixed_rows = jnp.dot(normed, full_input, preferred_element_type=jnp.float32)
    query_rows = (mixed_rows[:, :model_width] + full_query_bias.astype(jnp.float32)).astype(
        jnp.bfloat16
    )
    key_rows = mixed_rows[:, model_width : 2 * model_width].astype(jnp.bfloat16)
    value_rows = (mixed_rows[:, 2 * model_width :] + full_value_bias.astype(jnp.float32)).astype(
        jnp.bfloat16
    )
    own_query = query_rows.reshape(head_view)
    own_key = key_rows.reshape(head_view)
    own_value = value_rows.reshape(head_view)
    diag_query = own_query[0][None]
    diag_key = own_key[0][None]
    diag_value = own_value[0][None]
    key_slots = key_rows.reshape(slot_view)
    value_slots = value_rows.reshape(slot_view)
    query_slots = query_rows.reshape(slot_view)

    def stats_group(running, slices, far_pair, is_own, far_places, first_row):
        chosen = far_pair < my_pair
        query_slot, key_slot = tile_slots(chosen)
        return stats_update(
            running,
            query_tiles(own_query[:, None], chosen),
            key_tiles(split_heads(slices[0]), chosen),
            query_slot,
            tile_mask(is_own, own_places, far_places),
            score_scale,
        )

    stats_start = (
        jnp.full((2, HEADS, block_rows), NEG_BIG, jnp.float32),
        jnp.zeros((2, HEADS, block_rows), jnp.float32),
    )
    stats_start = stats_update(stats_start, diag_query, diag_key, zero_slot, diag_mask, score_scale)
    run_peak, run_total = sweep_piece(
        stats_start,
        (lax.all_gather(key_slots, "ctx", axis=1, tiled=True),),
        block_rows,
        my_rank,
        pair_of_rank,
        stats_group,
    )
    row_lse = run_peak + jnp.log(run_total)

    def values_group(running, slices, far_pair, is_own, far_places, first_row):
        chosen = far_pair < my_pair
        query_slot, key_slot = tile_slots(chosen)
        return values_update(
            running,
            query_tiles(own_query[:, None], chosen),
            key_tiles(split_heads(slices[0]), chosen),
            key_tiles(split_heads(slices[1]), chosen),
            query_slot,
            tile_mask(is_own, own_places, far_places),
            slot_pick(row_lse, query_slot),
            score_scale,
        )

    values_start = values_update(
        jnp.zeros(head_view, jnp.float32),
        diag_query,
        diag_key,
        diag_value,
        zero_slot,
        diag_mask,
        row_lse[0][None],
        score_scale,
    )
    attended = sweep_piece(
        values_start,
        (
            lax.all_gather(key_slots, "ctx", axis=1, tiled=True),
            lax.all_gather(value_slots, "ctx", axis=1, tiled=True),
        ),
        block_rows,
        my_rank,
        pair_of_rank,
        values_group,
    )
    attended_low = attended.reshape(2 * block_rows, model_width).astype(jnp.bfloat16)
    middle = (
        token_rows
        + jnp.dot(attended_low, full_output, preferred_element_type=jnp.float32)
        + full_output_bias.astype(jnp.float32)
    )
    normed_full_two, second_pullback = jax.vjp(
        layer_norm,
        middle,
        full_second_gain.astype(jnp.float32),
        full_second_shift.astype(jnp.float32),
    )
    normed_two = normed_full_two.astype(jnp.bfloat16)
    hidden = jnp.dot(
        normed_two, full_expand, preferred_element_type=jnp.float32
    ) + full_expand_bias.astype(jnp.float32)
    active_full, gelu_pullback = jax.vjp(gelu_tanh, hidden)
    active_low = active_full.astype(jnp.bfloat16)
    result = (
        middle
        + jnp.dot(active_low, full_contract, preferred_element_type=jnp.float32)
        + full_contract_bias.astype(jnp.float32)
    )
    block_out = result.astype(jnp.bfloat16)[None]
    back_input, back_output, back_expand, back_contract = (
        lax.all_gather(w_input, "dp", axis=0, tiled=True),
        lax.all_gather(w_output, "dp", axis=0, tiled=True),
        lax.all_gather(w_expand, "dp", axis=0, tiled=True),
        lax.all_gather(w_contract, "dp", axis=0, tiled=True),
    )
    grad_out_low = cotangent[0]
    grad_out = grad_out_low.astype(jnp.float32)
    grad_contract = jnp.einsum(
        "rf,rd->fd", active_low, grad_out_low, preferred_element_type=jnp.float32
    )
    grad_contract_bias = jnp.sum(grad_out, axis=0)
    grad_active = jnp.einsum(
        "rd,fd->rf", grad_out_low, back_contract, preferred_element_type=jnp.float32
    )
    grad_hidden = gelu_pullback(grad_active)[0].astype(jnp.bfloat16)
    grad_expand = jnp.einsum(
        "rd,rf->df", normed_two, grad_hidden, preferred_element_type=jnp.float32
    )
    grad_expand_bias = jnp.sum(grad_hidden.astype(jnp.float32), axis=0)
    grad_normed_two = jnp.einsum(
        "rf,df->rd", grad_hidden, back_expand, preferred_element_type=jnp.float32
    )
    grad_middle_part, grad_second_gain, grad_second_shift = second_pullback(grad_normed_two)
    grad_middle = grad_out + grad_middle_part
    grad_branch = grad_middle.astype(jnp.bfloat16)
    grad_output = jnp.einsum(
        "rd,re->de", attended_low, grad_branch, preferred_element_type=jnp.float32
    )
    grad_output_bias = jnp.sum(grad_branch.astype(jnp.float32), axis=0)
    grad_attended = jnp.einsum(
        "re,de->rd", grad_branch, back_output, preferred_element_type=jnp.float32
    ).astype(jnp.bfloat16)
    own_dout = grad_attended.reshape(head_view)
    dout_slots = grad_attended.reshape(slot_view)
    delta_rows = jnp.sum(own_dout.astype(jnp.float32) * attended, axis=-1)
    row_delta = jnp.transpose(delta_rows, (0, 2, 1))
    lse_rows = jnp.transpose(row_lse, (0, 2, 1))
    far_lse, far_delta = (
        lax.all_gather(lse_rows, "ctx", axis=1, tiled=True),
        lax.all_gather(delta_rows, "ctx", axis=1, tiled=True),
    )
    diag_probs = tile_probs(diag_query, diag_key, diag_mask, row_lse[0][None], score_scale)
    diag_dscore = tile_dscore(diag_probs, own_dout[0][None], diag_value, row_delta[0][None])
    query_start = slot_add(
        jnp.einsum("thqk,tkhd->tqhd", diag_dscore, diag_key, preferred_element_type=jnp.float32)
        * score_scale,
        zero_slot,
    )
    key_start = slot_add(
        jnp.einsum("thqk,tqhd->tkhd", diag_dscore, diag_query, preferred_element_type=jnp.float32)
        * score_scale,
        zero_slot,
    )
    value_start = slot_add(
        jnp.einsum(
            "thqk,tqhd->tkhd",
            diag_probs.astype(jnp.bfloat16),
            own_dout[0][None],
            preferred_element_type=jnp.float32,
        ),
        zero_slot,
    )

    def query_grad_group(running, slices, far_pair, is_own, far_places, first_row):
        chosen = far_pair < my_pair
        query_slot, key_slot = tile_slots(chosen)
        tile_key = key_tiles(split_heads(slices[0]), chosen)
        tile_value = key_tiles(split_heads(slices[1]), chosen)
        probs = tile_probs(
            query_tiles(own_query[:, None], chosen),
            tile_key,
            tile_mask(is_own, own_places, far_places),
            slot_pick(row_lse, query_slot),
            score_scale,
        )
        dscore = tile_dscore(
            probs,
            query_tiles(own_dout[:, None], chosen),
            tile_value,
            slot_pick(row_delta, query_slot),
        )
        part_grad = (
            jnp.einsum("thqk,tkhd->tqhd", dscore, tile_key, preferred_element_type=jnp.float32)
            * score_scale
        )
        return running + slot_add(part_grad, query_slot)

    def key_grad_group(running, slices, far_pair, is_own, far_places, first_row):
        chosen = my_pair < far_pair
        query_slot, key_slot = tile_slots(chosen)
        group_size = far_places.shape[0]
        sub_rows = far_places.shape[1]
        tile_query = query_tiles(split_heads(slices[0]), chosen)
        tile_dout = query_tiles(split_heads(slices[1]), chosen)
        lse_part = lax.dynamic_slice_in_dim(far_lse, first_row, group_size * sub_rows, 1).reshape(
            2, group_size, sub_rows, HEADS
        )
        delta_part = lax.dynamic_slice_in_dim(
            far_delta, first_row, group_size * sub_rows, 1
        ).reshape(2, group_size, sub_rows, HEADS)
        tile_lse = jnp.transpose(query_tiles(lse_part, chosen), (0, 2, 1))
        tile_delta = jnp.transpose(query_tiles(delta_part, chosen), (0, 2, 1))
        tile_key = key_tiles(own_key[:, None], chosen)
        tile_value = key_tiles(own_value[:, None], chosen)
        probs = tile_probs(
            tile_query, tile_key, tile_mask(is_own, far_places, own_places), tile_lse, score_scale
        )
        dscore = tile_dscore(probs, tile_dout, tile_value, tile_delta)
        key_part = (
            jnp.einsum("thqk,tqhd->tkhd", dscore, tile_query, preferred_element_type=jnp.float32)
            * score_scale
        )
        value_part = jnp.einsum(
            "thqk,tqhd->tkhd",
            probs.astype(jnp.bfloat16),
            tile_dout,
            preferred_element_type=jnp.float32,
        )
        return (
            running[0] + slot_add(key_part, key_slot),
            running[1] + slot_add(value_part, key_slot),
        )

    grad_query_sum = sweep_piece(
        query_start,
        (
            lax.all_gather(key_slots, "ctx", axis=1, tiled=True),
            lax.all_gather(value_slots, "ctx", axis=1, tiled=True),
        ),
        block_rows,
        my_rank,
        pair_of_rank,
        query_grad_group,
    )
    grad_key_sum, grad_value_sum = sweep_piece(
        (key_start, value_start),
        (
            lax.all_gather(query_slots, "ctx", axis=1, tiled=True),
            lax.all_gather(dout_slots, "ctx", axis=1, tiled=True),
        ),
        block_rows,
        my_rank,
        pair_of_rank,
        key_grad_group,
    )
    flat_rows = 2 * block_rows
    grad_query_low = grad_query_sum.reshape(flat_rows, model_width).astype(jnp.bfloat16)
    grad_key_low = grad_key_sum.reshape(flat_rows, model_width).astype(jnp.bfloat16)
    grad_value_low = grad_value_sum.reshape(flat_rows, model_width).astype(jnp.bfloat16)
    grad_mixed = jnp.concatenate([grad_query_low, grad_key_low, grad_value_low], axis=1)
    grad_input = jnp.einsum("rd,re->de", normed, grad_mixed, preferred_element_type=jnp.float32)
    grad_query_bias = jnp.sum(grad_query_low.astype(jnp.float32), axis=0)
    grad_value_bias = jnp.sum(grad_value_low.astype(jnp.float32), axis=0)
    grad_normed = jnp.einsum(
        "re,de->rd", grad_mixed, back_input, preferred_element_type=jnp.float32
    )
    grad_token_part, grad_first_gain, grad_first_shift = first_pullback(grad_normed)
    grad_tokens = (grad_middle + grad_token_part)[None]
    grad_local = (
        grad_first_gain,
        grad_first_shift,
        grad_input,
        grad_query_bias,
        grad_value_bias,
        grad_output,
        grad_output_bias,
        grad_second_gain,
        grad_second_shift,
        grad_expand,
        grad_expand_bias,
        grad_contract,
        grad_contract_bias,
    )
    grad_owned = (
        lax.psum_scatter(
            grad_local[0].astype(jnp.bfloat16), "dp", scatter_dimension=0, tiled=True
        ).astype(jnp.float32),
        lax.psum_scatter(
            grad_local[1].astype(jnp.bfloat16), "dp", scatter_dimension=0, tiled=True
        ).astype(jnp.float32),
        lax.psum_scatter(
            grad_local[2].astype(jnp.bfloat16), "dp", scatter_dimension=0, tiled=True
        ).astype(jnp.float32),
        lax.psum_scatter(
            grad_local[3].astype(jnp.bfloat16), "dp", scatter_dimension=0, tiled=True
        ).astype(jnp.float32),
        lax.psum_scatter(
            grad_local[4].astype(jnp.bfloat16), "dp", scatter_dimension=0, tiled=True
        ).astype(jnp.float32),
        lax.psum_scatter(
            grad_local[5].astype(jnp.bfloat16), "dp", scatter_dimension=0, tiled=True
        ).astype(jnp.float32),
        lax.psum_scatter(
            grad_local[6].astype(jnp.bfloat16), "dp", scatter_dimension=0, tiled=True
        ).astype(jnp.float32),
        lax.psum_scatter(
            grad_local[7].astype(jnp.bfloat16), "dp", scatter_dimension=0, tiled=True
        ).astype(jnp.float32),
        lax.psum_scatter(
            grad_local[8].astype(jnp.bfloat16), "dp", scatter_dimension=0, tiled=True
        ).astype(jnp.float32),
        lax.psum_scatter(
            grad_local[9].astype(jnp.bfloat16), "dp", scatter_dimension=0, tiled=True
        ).astype(jnp.float32),
        lax.psum_scatter(
            grad_local[10].astype(jnp.bfloat16), "dp", scatter_dimension=0, tiled=True
        ).astype(jnp.float32),
        lax.psum_scatter(
            grad_local[11].astype(jnp.bfloat16), "dp", scatter_dimension=0, tiled=True
        ).astype(jnp.float32),
        lax.psum_scatter(
            grad_local[12].astype(jnp.bfloat16), "dp", scatter_dimension=0, tiled=True
        ).astype(jnp.float32),
    )
    grad_final = tuple(
        lax.psum(
            (
                grad_owned[0],
                grad_owned[1],
                grad_owned[2],
                grad_owned[3],
                grad_owned[4],
                grad_owned[5],
                grad_owned[6],
                grad_owned[7],
                grad_owned[8],
                grad_owned[9],
                grad_owned[10],
                grad_owned[11],
                grad_owned[12],
            ),
            "ctx",
        )
    )
    return (block_out, grad_tokens) + tuple(grad_final)


VMEM_BYTES = 16 * 1024 * 1024
VMEM_LARGE = 28 * 1024 * 1024


def mm(left, right):
    return lax.dot_general(
        left, right, (((1,), (0,)), ((), ())), preferred_element_type=jnp.float32
    )


def mm_nt(left, right):
    return lax.dot_general(
        left, right, (((1,), (1,)), ((), ())), preferred_element_type=jnp.float32
    )


def mm_tn(left, right):
    return lax.dot_general(
        left, right, (((0,), (0,)), ((), ())), preferred_element_type=jnp.float32
    )


def aligned(index, size):
    return pl.ds(pl.multiple_of(index * size, size), size)


def norm_stats(values):
    centre = values - jnp.mean(values, axis=-1, keepdims=True)
    spread = jnp.mean(centre * centre, axis=-1, keepdims=True)
    scale = lax.rsqrt(spread + NORM_EPS)
    return centre * scale, scale


def norm_back(grad_normed, gain_row, xhat, scale):
    weighted = grad_normed * gain_row
    return scale * (
        weighted
        - jnp.mean(weighted, axis=-1, keepdims=True)
        - xhat * jnp.mean(weighted * xhat, axis=-1, keepdims=True)
    )


def column_sums(values):
    return jnp.sum(values, axis=0, keepdims=True)


def shape_of(dims, dtype):
    return jax.ShapeDtypeStruct(dims, dtype)


def local_call(
    kernel, name, outs, args, scalars=0, scratch=(), flops=0, after=(), space=pltpu.VMEM, grant=VMEM_BYTES
):
    moved = sum(math.prod(a.shape) * a.dtype.itemsize for a in tuple(args) + tuple(outs))

    def ordered(*refs):
        kernel(*refs[: len(args)], *refs[len(args) + len(after) :])

    return pl.pallas_call(
        ordered,
        out_shape=tuple(outs),
        in_specs=[pl.BlockSpec(memory_space=pltpu.SMEM)] * scalars
        + [pl.BlockSpec(memory_space=space)] * (len(args) - scalars)
        + [pl.BlockSpec(memory_space=pl.ANY)] * len(after),
        out_specs=tuple(pl.BlockSpec(memory_space=pltpu.VMEM) for _ in outs),
        scratch_shapes=list(scratch),
        compiler_params=pltpu.CompilerParams(vmem_limit_bytes=grant),
        cost_estimate=pl.CostEstimate(
            flops=flops, bytes_accessed=moved if flops else 0, transcendentals=0
        ),
        name=name,
    )(*args, *after)


def place_of_block(pair_ref, info_ref, ranks, step, half, other_core):
    core = jnp.bitwise_xor(info_ref[2], other_core)
    rank = 2 * jnp.bitwise_xor(info_ref[1], step) + core
    pair = pair_ref[rank]
    return pair if half == 0 else 2 * ranks - 1 - pair


def fill_mask(bias_ref, pair_ref, info_ref, ranks, parts, block):
    rows = 2 * parts * block
    lanes = lax.broadcasted_iota(jnp.int32, (1, rows), 1)
    query_place = lanes % block
    for step in range(parts):
        for half in range(2):
            place = place_of_block(pair_ref, info_ref, ranks, step, half, 0)
            query_place = query_place + jnp.where(
                lanes // block == 2 * step + half, place * block, 0
            )
    ahead = lax.broadcasted_iota(jnp.int32, (block, rows), 0) - query_place
    for other in range(2):
        for step in range(parts):
            for half in range(2):
                place = place_of_block(pair_ref, info_ref, ranks, step, half, other)
                start = other * rows + (2 * step + half) * block
                bias_ref[start : start + block, :] = jnp.where(
                    ahead <= -place * block, 0.0, NEG_BIG
                )


def head_parallel(ranks, chips, seq_parts):
    parts = chips
    hw = HEADS // chips * HEAD_DIM

    def core_swap(member):
        return lax.ppermute(member, "ctx", [(i, i ^ 1) for i in range(ranks)])

    def chip_swap(member, step):
        return lax.ppermute(
            member, "ctx", [(i, 2 * ((i // 2) ^ step) + i % 2) for i in range(ranks)]
        )

    def seq_swap(member, step):
        return lax.ppermute(member, "dp", [(i, i ^ step) for i in range(seq_parts)])

    def per_device_heads(
        tokens,
        pair_of_rank,
        first_gain,
        first_shift,
        w_input,
        query_bias,
        value_bias,
        w_output,
        output_bias,
        second_gain,
        second_shift,
        w_expand,
        expand_bias,
        w_contract,
        contract_bias,
        cotangent,
    ):
        bf, f32 = jnp.bfloat16, jnp.float32
        rows, width = tokens.shape[1:]
        block = rows // 2
        own_width = width // seq_parts
        ff = expand_bias.shape[0]
        total = parts * rows
        half_width = width // 2
        half_ff = ff // 2
        sub = own_width // parts
        half_own = own_width // 2
        small_rows = 16
        others = range(1, parts)
        seq_id = lax.axis_index("dp")
        rank = lax.axis_index("ctx")
        chip = rank // 2
        core = rank % 2
        info = jnp.stack([seq_id, chip, core]).astype(jnp.int32)

        side = width - 3 * hw
        pack_rows = 2 * half_own

        def pack_kernel(info_ref, tok_ref, w_ref, wo_ref, *refs):
            vecs = refs[:8]
            packed_ref, tokens_ref, w_scr, wo_scr = refs[8:12]
            scrs, sems = refs[12:20], refs[20]
            mine = pl.ds(pl.multiple_of(info_ref[2] * half_own, half_own), half_own)
            pairs = [(w_ref.at[mine], w_scr), (wo_ref.at[mine], wo_scr), (tok_ref, tokens_ref)]
            pairs += list(zip(vecs, scrs))
            copies = [
                pltpu.make_async_copy(src, dst, sems.at[i]) for i, (src, dst) in enumerate(pairs)
            ]
            for copy in copies:
                copy.start()
            for copy in copies:
                copy.wait()
            at_w = slice(half_own, 2 * half_own)
            for at in range(chips):

                @pl.when(info_ref[1] == at)
                def _():
                    for base in range(3):
                        start = base * width + at * hw
                        packed_ref[at_w, base * hw : (base + 1) * hw] = w_scr[
                            :, start : start + hw
                        ]

            packed_ref[0:half_own, :] = wo_scr[...]
            small = jnp.concatenate(
                [v[...].astype(f32).reshape(1, own_width) for v in scrs], axis=0
            )
            small = jnp.concatenate([small, jnp.zeros_like(small)], axis=0)
            packed_ref[half_own : half_own + small_rows, 3 * hw :] = small.astype(bf)
            packed_ref[half_own + small_rows :, 3 * hw :] = jnp.zeros(
                (half_own - small_rows, side), bf
            )

        small_args = (
            first_gain,
            first_shift,
            query_bias,
            value_bias,
            output_bias,
            second_gain,
            second_shift,
            contract_bias,
        )
        packed, own_tokens = local_call(
            pack_kernel,
            "pack",
            [shape_of((pack_rows, width), bf), shape_of((rows, width), bf)],
            [info, tokens[0], w_input, w_output] + list(small_args),
            scalars=1,
            scratch=[pltpu.VMEM((half_own, 3 * width), bf), pltpu.VMEM((half_own, width), bf)]
            + [pltpu.VMEM((own_width,), bf)] * 8
            + [pltpu.SemaphoreType.DMA((11,))],
            space=pltpu.HBM,
            grant=60 * 1024 * 1024,
        )
        token_two = chip_swap(own_tokens, 2)
        token_parts = [own_tokens, chip_swap(own_tokens, 1), token_two, chip_swap(token_two, 1)]
        packed_near = [seq_swap(packed, j) for j in others]

        def stack_kernel(*refs):
            depth = refs[0].shape[0]
            for i, ref in enumerate(refs[:-1]):
                refs[-1][i * depth : (i + 1) * depth, :] = ref[...]

        (packed_all,) = local_call(
            stack_kernel,
            "pack_stack",
            [shape_of(((seq_parts - 1) * pack_rows, width), bf)],
            packed_near,
            after=token_parts[1:],
        )
        packed_far = core_swap(packed_all)
        own_cot = cotangent[0]

        def pack_more_kernel(info_ref, we_ref, cot_ref, *refs):
            for j in others:
                start = pl.multiple_of(info_ref[2] * half_own, half_own)
                refs[j - 1][0:half_own, :] = we_ref[
                    pl.ds(start, half_own), aligned(jnp.bitwise_xor(info_ref[0], j), ff)
                ]
                refs[j - 1][half_own:, :] = cot_ref[...]

        more = local_call(
            pack_more_kernel,
            "pack_more",
            [shape_of((half_own + rows, width), bf)] * (seq_parts - 1),
            [info, w_expand, own_cot],
            scalars=1,
            after=[packed],
        )
        more_parts = [seq_swap(more[j - 1], j) for j in others]

        def qkv_kernel(info_ref, w_own_ref, wo_own_ref, *refs):
            toks, own_pack, packs = refs[:parts], refs[parts], refs[parts + 1 : parts + 3]
            q_ref, kv_ref, normed_ref, w_ref, vec_ref, wo_ref, vec_scr = refs[parts + 3 :]
            for at in range(chips):

                @pl.when(info_ref[1] == at)
                def _():
                    for base in range(3):
                        start = base * width + at * hw
                        w_ref[aligned(info_ref[0], own_width), base * hw : (base + 1) * hw] = (
                            w_own_ref[:, start : start + hw]
                        )

            wo_ref[info_ref[0]] = wo_own_ref[...]
            at_small = slice(half_own, half_own + small_rows)
            vec_scr[info_ref[0]] = own_pack[at_small, 3 * hw :].astype(f32)
            for j in others:
                place = jnp.bitwise_xor(info_ref[0], j)
                base = (j - 1) * pack_rows
                vec_scr[place] = packs[0][
                    base + half_own : base + half_own + small_rows, 3 * hw :
                ].astype(f32)
                for flip in range(2):
                    member = packs[flip]
                    half = jnp.bitwise_xor(info_ref[2], flip)
                    down = pl.multiple_of(half * half_own, half_own)
                    wo_ref[place, pl.ds(down, half_own), :] = member[base : base + half_own, :]
                    start = pl.multiple_of(place * own_width + half * half_own, half_own)
                    w_ref[pl.ds(start, half_own), :] = member[
                        base + half_own : base + pack_rows, 0 : 3 * hw
                    ]
            vectors = jnp.concatenate([vec_scr[j] for j in range(parts)], axis=1)
            vec_ref[...] = vectors
            chosen = vec_scr[info_ref[1]]
            for k in range(parts):
                xhat, _ = norm_stats(toks[k][...].astype(f32))
                normed_ref[k * rows : (k + 1) * rows, :] = (
                    xhat * vectors[0:1] + vectors[1:2]
                ).astype(bf)
            mixed = mm(normed_ref[...], w_ref[...])
            q_ref[...] = (mixed[:, 0:hw] + chosen[2:3]).astype(bf)
            kv_ref[:, 0:hw] = mixed[:, hw : 2 * hw].astype(bf)
            kv_ref[:, hw : 2 * hw] = (mixed[:, 2 * hw :] + chosen[3:4]).astype(bf)

        query, own_kv, normed, w_heads_full, vectors, out_full = local_call(
            qkv_kernel,
            "project",
            [
                shape_of((total, hw), bf),
                shape_of((total, 2 * hw), bf),
                shape_of((total, width), bf),
                shape_of((width, 3 * hw), bf),
                shape_of((small_rows, width), f32),
                shape_of((parts, own_width, width), bf),
            ],
            [info, w_input, w_output] + token_parts + [packed, packed_all, packed_far],
            scalars=1,
            scratch=[pltpu.VMEM((parts, small_rows, own_width), f32)],
            flops=2 * total * width * 3 * hw,
        )
        far_kv = core_swap(own_kv)

        head_count = hw // HEAD_DIM
        scale = HEAD_DIM ** (-0.5)

        def head_columns(ref, base, head):
            start = base + head * HEAD_DIM
            return ref[:, start : start + HEAD_DIM]

        def attend_kernel(info_ref, pair_ref, q_ref, kv_ref, far_ref, *refs):
            outs = refs[:parts]
            flat_ref, lse_ref, bias_ref = refs[parts:]
            fill_mask(bias_ref, pair_ref, info_ref, ranks, parts, block)
            columns = []
            for head in range(head_count):
                keys = jnp.concatenate(
                    [head_columns(kv_ref, 0, head), head_columns(far_ref, 0, head)], axis=0
                )
                values = jnp.concatenate(
                    [head_columns(kv_ref, hw, head), head_columns(far_ref, hw, head)], axis=0
                )
                scores = mm_nt(keys, head_columns(q_ref, 0, head)) * scale + bias_ref[...]
                peak = jnp.max(scores, axis=0, keepdims=True)
                weights = jnp.exp(scores - peak)
                mass = jnp.sum(weights, axis=0, keepdims=True)
                lse_ref[head : head + 1, :] = peak + jnp.log(mass)
                mixed = mm_tn(values, weights.astype(bf)) / mass
                flat_ref[head * HEAD_DIM : (head + 1) * HEAD_DIM, :] = mixed
            attended = flat_ref[...].T.astype(bf)
            for k in range(parts):
                outs[k][...] = attended[k * rows : (k + 1) * rows]

        attend_out = local_call(
            attend_kernel,
            "attend",
            [shape_of((rows, hw), bf)] * parts
            + [shape_of((hw, total), f32), shape_of((8, total), f32)],
            [info, pair_of_rank, query, own_kv, far_kv],
            scalars=2,
            scratch=[pltpu.VMEM((2 * total, total), f32)],
            flops=2 * 2 * head_count * 2 * total * total * HEAD_DIM,
            grant=VMEM_LARGE,
        )
        flat_attended, row_lse = attend_out[parts:]
        att_parts = [attend_out[0]] + [chip_swap(attend_out[k], k) for k in others]

        def middle_kernel(info_ref, tok_ref, vec_ref, w_ref, *refs):
            atts = refs[:parts]
            mid_ref, normed_ref = refs[parts:]
            middle = tok_ref[...].astype(f32) + vec_ref[4:5]
            for k in range(parts):
                middle = middle + mm(atts[k][...], w_ref[jnp.bitwise_xor(info_ref[1], k)])
            mid_ref[...] = middle
            xhat, _ = norm_stats(middle)
            normed_ref[...] = (xhat * vec_ref[5:6] + vec_ref[6:7]).astype(bf)

        middle, own_normed_two = local_call(
            middle_kernel,
            "middle",
            [shape_of((rows, width), f32), shape_of((rows, width), bf)],
            [info, own_tokens, vectors, out_full] + att_parts,
            scalars=1,
            flops=2 * rows * width * width,
        )

        def expand_stack_kernel(*refs):
            for i, ref in enumerate(refs[:-1]):
                refs[-1][i * half_own : (i + 1) * half_own, :] = ref[0:half_own, :]

        (expand_all,) = local_call(
            expand_stack_kernel,
            "expand_stack",
            [shape_of(((seq_parts - 1) * half_own, ff), bf)],
            more_parts,
            after=[own_normed_two],
        )
        expand_far = core_swap(expand_all)
        n2_parts = [own_normed_two] + [seq_swap(own_normed_two, j) for j in others]

        span = ff // parts + own_width

        def ffn_kernel(info_ref, bias_ref, wc_ref, we_ref, own_cot_ref, far_we_ref, *refs):
            n2s = refs[:parts]
            mores = refs[parts : 2 * parts - 1]
            gns = refs[2 * parts - 1 : 3 * parts - 1]
            results = refs[3 * parts - 1 : 4 * parts - 1]
            keep_ref, send_ref, sum_ref = refs[4 * parts - 1 : 4 * parts + 2]
            active_ref, gh_ref, n2_ref, cot_ref, w_scr, scr = refs[4 * parts + 2 :]
            w_scr[aligned(info_ref[0], own_width), :] = we_ref[:, aligned(info_ref[0], ff)]
            for j in range(seq_parts):
                at = slice(j * rows, (j + 1) * rows)
                n2_ref[at, :] = n2s[j][...]
                if j == 0:
                    cot_ref[at, :] = own_cot_ref[...]
                    continue
                place = jnp.bitwise_xor(info_ref[0], j)
                for flip in range(2):
                    half = jnp.bitwise_xor(info_ref[2], flip)
                    start = pl.multiple_of(place * own_width + half * half_own, half_own)
                    w_scr[pl.ds(start, half_own), :] = (
                        far_we_ref[(j - 1) * half_own : j * half_own, :]
                        if flip
                        else mores[j - 1][0:half_own, :]
                    )
                cot_ref[at, :] = mores[j - 1][half_own:, :]
            hidden = mm(n2_ref[...], w_scr[...]) + bias_ref[...].astype(f32).reshape(1, ff)
            square = hidden * hidden
            curve = jnp.tanh(GELU_SCALE * hidden * (1.0 + GELU_CUBIC * square))
            active_ref[...] = (0.5 * hidden * (1.0 + curve)).astype(bf)
            slope = 0.5 * (1.0 + curve) + 0.5 * hidden * (1.0 - curve * curve) * GELU_SCALE * (
                1.0 + 3.0 * GELU_CUBIC * square
            )
            grad_hidden = mm_nt(cot_ref[...], wc_ref[...]) * slope
            gh_ref[...] = grad_hidden.astype(bf)
            sum_ref[...] = column_sums(gh_ref[...].astype(f32))
            grad = mm_nt(gh_ref[...], w_scr[...]).astype(bf)
            for j in range(parts):
                gns[j][...] = grad[j * rows : (j + 1) * rows]
            result = mm(active_ref[...], wc_ref[...]).astype(bf)
            for j in range(seq_parts):
                results[j][...] = result[j * rows : (j + 1) * rows]
            core_id = info_ref[2]
            for flip, out_ref in ((0, keep_ref), (1, send_ref)):
                half = jnp.bitwise_xor(core_id, flip)
                scr[...] = mm_tn(active_ref[...], cot_ref[:, aligned(half, half_width)]).astype(bf)
                for part in range(parts):
                    rows_to = ff // parts
                    out_ref[part, 0:rows_to, :] = scr[part * rows_to : (part + 1) * rows_to, :]
                scr[...] = mm_tn(n2_ref[...], gh_ref[:, aligned(half, half_ff)]).astype(bf)
                for part in range(parts):
                    for j in range(seq_parts):
                        at = ff // parts + j * sub
                        row = j * own_width + part * sub
                        out_ref[part, at : at + sub, :] = scr[row : row + sub, :]

        ffn_out = local_call(
            ffn_kernel,
            "feed",
            [shape_of((rows, width), bf)] * 2 * parts
            + [
                shape_of((parts, span, half_width), bf),
                shape_of((parts, span, half_width), bf),
                shape_of((1, ff), f32),
            ],
            [info, expand_bias, w_contract, w_expand, own_cot, expand_far] + n2_parts + more_parts,
            scalars=1,
            scratch=[
                pltpu.VMEM((total, ff), bf),
                pltpu.VMEM((total, ff), bf),
                pltpu.VMEM((total, width), bf),
                pltpu.VMEM((total, width), bf),
                pltpu.VMEM((width, ff), bf),
                pltpu.VMEM((width, half_ff), bf),
            ],
            flops=6 * 2 * total * width * ff,
            grant=VMEM_LARGE,
        )
        results = ffn_out[parts : 2 * parts]
        ffn_keep, ffn_send, grad_expand_row = ffn_out[2 * parts :]
        gn_parts = [ffn_out[0]] + [seq_swap(ffn_out[j], j) for j in others]
        ffn_far = core_swap(ffn_send)

        def halve_kernel(info_ref, keep_ref, far_ref, own_ref, out_ref):
            for k in range(parts):
                at = jnp.bitwise_xor(info_ref[1], k)
                piece = keep_ref[at].astype(f32) + far_ref[at].astype(f32)
                if k % 2:
                    out_ref[k // 2] = piece.astype(bf)
                else:
                    own_ref[k // 2] = piece

        rs_own, rs_send = local_call(
            halve_kernel,
            "feed_halves",
            [
                shape_of((parts // 2, span, half_width), f32),
                shape_of((parts // 2, span, half_width), bf),
            ],
            [info, ffn_keep, ffn_far],
            scalars=1,
        )
        rs_far = chip_swap(rs_send, 1)

        def back_kernel(info_ref, mid_ref, vec_ref, cot_ref, w_ref, *refs):
            gns = refs[:parts]
            douts = refs[parts : 2 * parts]
            gmid_ref, branch_ref, sums_ref = refs[2 * parts :]
            grad = gns[0][...].astype(f32)
            for j in others:
                grad = grad + gns[j][...].astype(f32)
            xhat, spread = norm_stats(mid_ref[...])
            cot = cot_ref[...].astype(f32)
            grad_middle = cot + norm_back(grad, vec_ref[5:6], xhat, spread)
            gmid_ref[...] = grad_middle
            branch = grad_middle.astype(bf)
            branch_ref[...] = branch
            for k in range(parts):
                douts[k][...] = mm_nt(branch, w_ref[jnp.bitwise_xor(info_ref[1], k)]).astype(bf)
            sums_ref[0:1, :] = column_sums(branch.astype(f32))
            sums_ref[1:2, :] = column_sums(grad * xhat)
            sums_ref[2:3, :] = column_sums(grad)
            sums_ref[3:4, :] = column_sums(cot)

        back_out = local_call(
            back_kernel,
            "middle_back",
            [shape_of((rows, hw), bf)] * parts
            + [
                shape_of((rows, width), f32),
                shape_of((rows, width), bf),
                shape_of((8, width), f32),
            ],
            [info, middle, vectors, own_cot, out_full] + gn_parts,
            scalars=1,
            after=[rs_send],
            flops=2 * rows * width * width,
        )
        grad_middle, grad_branch, late_sums = back_out[parts:]
        dout_parts = [back_out[0]] + [chip_swap(back_out[k], k) for k in others]

        def out_weights_kernel(info_ref, branch_ref, *refs):
            atts = refs[:parts]
            keep_ref, send_ref = refs[parts:]
            for flip, out_ref in ((0, keep_ref), (1, send_ref)):
                half = jnp.bitwise_xor(info_ref[2], flip)
                piece = branch_ref[:, aligned(half, half_width)]
                for k in range(parts):
                    out_ref[jnp.bitwise_xor(info_ref[1], k)] = mm_tn(atts[k][...], piece).astype(bf)

        out_keep, out_send = local_call(
            out_weights_kernel,
            "output_weights",
            [shape_of((parts, hw, half_width), bf)] * 2,
            [info, grad_branch] + att_parts,
            scalars=1,
            flops=2 * rows * width * width,
        )
        out_far = core_swap(out_send)

        fold = own_width // 2
        rider = -(-sub // 32) * 16
        pair_rows = fold // 2
        at_outs = slice(half_own, half_own + pair_rows)

        def fold_in(value):
            down = value.shape[0] // 2
            return jnp.concatenate([value[0:down], value[down:]], axis=1)

        def fold_out(value):
            across = value.shape[1] // 2
            return jnp.concatenate([value[:, 0:across], value[:, across:]], axis=0)

        def out_halves_kernel(info_ref, keep_ref, far_ref, own_ref, send_ref, scr):
            mine = info_ref[1] % 2
            for to in range(seq_parts):
                whole = fold_in(keep_ref[to].astype(f32) + far_ref[to].astype(f32))
                scr[0] = whole[0:pair_rows]
                scr[1] = whole[pair_rows:]
                own_ref[to] = scr[mine]
                send_ref[to] = scr[1 - mine].astype(bf)

        oh_own, oh_send = local_call(
            out_halves_kernel,
            "output_halves",
            [
                shape_of((seq_parts, pair_rows, width), f32),
                shape_of((seq_parts, pair_rows, width), bf),
            ],
            [info, out_keep, out_far],
            scalars=1,
            scratch=[pltpu.VMEM((2, pair_rows, width), f32)],
        )
        oh_far = chip_swap(oh_send, 1)

        def quarter_kernel(own_ref, far_ref, keep_ref, send_ref):
            keep_ref[...] = own_ref[0] + far_ref[0].astype(f32)
            send_ref[...] = (own_ref[1] + far_ref[1].astype(f32)).astype(bf)

        rs_own_two, rs_send_two = local_call(
            quarter_kernel,
            "feed_quarters",
            [shape_of((span, half_width), f32), shape_of((span, half_width), bf)],
            [rs_own, rs_far],
            after=[dout_parts[parts - 1]],
        )
        rs_far_two = chip_swap(rs_send_two, 2)

        def attend_back_kernel(info_ref, pair_ref, q_ref, kv_ref, far_ref, flat_ref, lse_ref, *refs):
            douts = refs[:parts]
            dq_ref, own_ref, send_ref, bias_ref, dout_ref = refs[parts:]
            fill_mask(bias_ref, pair_ref, info_ref, ranks, parts, block)
            for k in range(parts):
                dout_ref[k * rows : (k + 1) * rows, :] = douts[k][...].astype(f32)
            flat_dout = dout_ref[...].T
            for head in range(head_count):
                at = slice(head * HEAD_DIM, (head + 1) * HEAD_DIM)
                keys = jnp.concatenate(
                    [head_columns(kv_ref, 0, head), head_columns(far_ref, 0, head)], axis=0
                )
                values = jnp.concatenate(
                    [head_columns(kv_ref, hw, head), head_columns(far_ref, hw, head)], axis=0
                )
                queries = head_columns(q_ref, 0, head)
                dout = dout_ref[:, at].astype(bf)
                dout_turned = flat_dout[at, :]
                delta = column_sums(dout_turned * flat_ref[at, :])
                scores = mm_nt(keys, queries) * scale + bias_ref[...]
                probs = jnp.exp(scores - lse_ref[head : head + 1, :])
                grad_value = mm(probs.astype(bf), dout)
                grad_weights = mm(values, dout_turned.astype(bf))
                grad_scores = (probs * (grad_weights - delta)).astype(bf)
                grad_key = mm(grad_scores, queries) * scale
                dq_ref[at, :] = mm_tn(keys, grad_scores) * scale
                vat = slice(hw + head * HEAD_DIM, hw + (head + 1) * HEAD_DIM)
                own_ref[:, at] = grad_key[0:total]
                own_ref[:, vat] = grad_value[0:total]
                send_ref[:, at] = grad_key[total:].astype(bf)
                send_ref[:, vat] = grad_value[total:].astype(bf)

        flat_dq, dkv_own, dkv_send = local_call(
            attend_back_kernel,
            "attend_back",
            [
                shape_of((hw, total), f32),
                shape_of((total, 2 * hw), f32),
                shape_of((total, 2 * hw), bf),
            ],
            [info, pair_of_rank, query, own_kv, far_kv, flat_attended, row_lse] + dout_parts,
            scalars=2,
            after=[rs_send_two, out_send],
            scratch=[pltpu.VMEM((2 * total, total), f32), pltpu.VMEM((total, hw), f32)],
            flops=8 * 5 * 2 * head_count * 2 * total * total * HEAD_DIM,
            grant=VMEM_LARGE,
        )
        dkv_far = core_swap(dkv_send)

        def normed_back_kernel(dq_ref, own_ref, far_ref, w_ref, *refs):
            toks = refs[:parts]
            keep_ref, send_ref, mixed_ref, sums_ref, bias_ref = refs[parts:]
            mixed_ref[:, 0:hw] = dq_ref[...].T.astype(bf)
            mixed_ref[:, hw:] = (own_ref[...] + far_ref[...].astype(f32)).astype(bf)
            shift_sum = jnp.zeros((1, width), f32)
            gain_sum = jnp.zeros((1, width), f32)
            for k in range(parts):
                grad = mm_nt(mixed_ref[k * rows : (k + 1) * rows, :], w_ref[...])
                if k % 2:
                    send_ref[k // 2] = grad.astype(bf)
                else:
                    keep_ref[k // 2] = grad
                xhat, _ = norm_stats(toks[k][...].astype(f32))
                shift_sum = shift_sum + column_sums(grad)
                gain_sum = gain_sum + column_sums(grad * xhat)
            sums_ref[0:1, :] = gain_sum
            sums_ref[1:2, :] = shift_sum
            bias_ref[0:1, :] = column_sums(mixed_ref[...].astype(f32))

        nb_out = local_call(
            normed_back_kernel,
            "normed_back",
            [
                shape_of((parts // 2, rows, width), f32),
                shape_of((parts // 2, rows, width), bf),
                shape_of((total, 3 * hw), bf),
                shape_of((8, width), f32),
                shape_of((8, 3 * hw), f32),
            ],
            [flat_dq, dkv_own, dkv_far, w_heads_full] + token_parts,
            flops=0,
        )
        gt_keep, gt_send, grad_mixed, first_sums, mixed_sums = nb_out
        gt_far = chip_swap(gt_send, 1)


        def input_weights_kernel(
            info_ref, normed_ref, mixed_ref, first_ref, bias_ref, late_ref, row_ref, *refs
        ):
            keep_ref, *send_refs, grad_scr, small_scr = refs
            grad_scr[...] = mm_tn(normed_ref[...], mixed_ref[...])
            core_id, chip_id, seq = info_ref[2], info_ref[1], info_ref[0]
            small_scr[...] = jnp.zeros_like(small_scr)
            for j in range(seq_parts):
                at = slice(j * own_width, (j + 1) * own_width)
                small_scr[j, 0:2, :] = first_ref[0:2, at]
                small_scr[j, 4:8, :] = late_ref[0:4, at]
            small_scr[chip_id, 2:3, :] = bias_ref[0:1, 0:hw]
            small_scr[chip_id, 3:4, :] = bias_ref[0:1, 2 * hw : 3 * hw]
            for j in range(ff // own_width):
                small_scr[seq, 8 + j : 9 + j, :] = row_ref[:, j * own_width : (j + 1) * own_width]
            for flip in range(2):
                half = jnp.bitwise_xor(core_id, flip)
                for j in range(seq_parts):
                    out_ref = send_refs[j] if flip else keep_ref.at[j]
                    start = pl.multiple_of(j * own_width + half * half_own, 16)
                    out_ref[:, 0 : 3 * hw] = grad_scr[pl.ds(start, half_own), :].astype(bf)
                    out_ref[0:small_rows, 3 * hw :] = small_scr[j].astype(bf)
                    out_ref[small_rows:, 3 * hw :] = jnp.zeros(
                        (half_own - small_rows, side), bf
                    )

        in_keep, *in_send = local_call(
            input_weights_kernel,
            "input_weights",
            [shape_of((seq_parts, half_own, width), bf)]
            + [shape_of((half_own, width), bf)] * seq_parts,
            [info, normed, grad_mixed, first_sums, mixed_sums, late_sums, grad_expand_row],
            scalars=1,
            scratch=[
                pltpu.VMEM((width, 3 * hw), f32),
                pltpu.VMEM((seq_parts, small_rows, own_width), f32),
            ],
            flops=0,
        )
        in_far = [core_swap(member) for member in in_send]

        res_parts = [results[0]] + [seq_swap(results[j], j) for j in others]

        def result_kernel(mid_ref, vec_ref, *refs):
            result = mid_ref[...] + vec_ref[7:8]
            for j in range(seq_parts):
                result = result + refs[j][...].astype(f32)
            refs[seq_parts][0] = result.astype(bf)
            refs[seq_parts + 1][...] = jnp.zeros((8, 128), f32)

        block_out, block_done = local_call(
            result_kernel,
            "result",
            [shape_of((1, rows, width), bf), shape_of((8, 128), f32)],
            [middle, vectors] + res_parts,
            after=[in_keep],
        )

        def dp_pack_kernel(
            info_ref, own_ref, far_two_ref, keep_ref, ok_ref, of_ref, *refs
        ):
            fars, refs = refs[:seq_parts], refs[seq_parts:]
            con_ref, scr, far_scr = refs[seq_parts:]
            for j in range(seq_parts):
                far_scr[j] = fars[j][...]
            whole = own_ref[...] + far_two_ref[...].astype(f32)
            con_ref[...] = whole[0 : ff // parts].astype(bf)
            scr[...] = whole[ff // parts :]
            for j in range(seq_parts):
                at = jnp.bitwise_xor(info_ref[0], j)
                refs[j][0:half_own, :] = (
                    keep_ref[at].astype(f32) + far_scr[at].astype(f32)
                ).astype(bf)
                refs[j][at_outs, :] = (ok_ref[at] + of_ref[at].astype(f32)).astype(bf)
                piece = fold_in(scr[aligned(at, sub), :])
                piece = jnp.concatenate(
                    [piece, jnp.zeros((rider - sub // 2, width), f32)], axis=0
                )
                refs[j][half_own + pair_rows :, :] = piece.astype(bf)
        dp_out = local_call(
            dp_pack_kernel,
            "owners",
            [shape_of((half_own + pair_rows + rider, width), bf)] * seq_parts
            + [shape_of((ff // parts, half_width), bf)],
            [info, rs_own_two, rs_far_two, in_keep, oh_own, oh_far] + in_far,
            scalars=1,
            scratch=[
                pltpu.VMEM((own_width, half_ff), f32),
                pltpu.VMEM((seq_parts, half_own, width), bf),
            ],
            after=[block_done],
        )
        dp_parts = [dp_out[0]] + [seq_swap(dp_out[j], j) for j in others]
        con_one = dp_out[seq_parts]

        def half_sum_kernel(keep_ref, far_ref, own_ref, send_ref):
            own_ref[...] = keep_ref[0] + far_ref[0].astype(f32)
            send_ref[...] = (keep_ref[1] + far_ref[1].astype(f32)).astype(bf)

        gt_own, gt_send_two = local_call(
            half_sum_kernel,
            "tokens_halves",
            [shape_of((rows, width), f32), shape_of((rows, width), bf)],
            [gt_keep, gt_far],
            after=[con_one],
        )
        con_two = chip_swap(con_one, 2)
        gt_far_two = chip_swap(gt_send_two, 2)

        con_one_far = chip_swap(con_one, 1)
        con_two_far = chip_swap(con_two, 1)

        con_parts = [con_one, con_one_far, con_two, con_two_far]
        con_far = [core_swap(member) for member in con_parts]

        def contract_kernel(info_ref, *refs):
            con_ref, done_ref = refs[2 * parts :]
            done_ref[...] = jnp.zeros_like(done_ref)
            for flip in range(2):
                lanes = aligned(jnp.bitwise_xor(info_ref[2], flip), half_width)
                for k in range(parts):
                    at = jnp.bitwise_xor(info_ref[1], k)
                    con_ref[aligned(at, ff // parts), lanes] = refs[flip * parts + k][...].astype(
                        f32
                    )

        grad_contract, contract_done = local_call(
            contract_kernel,
            "contract_final",
            [shape_of((ff, width), f32), shape_of((8, 128), f32)],
            [info] + con_parts + con_far,
            scalars=1,
        )

        def dp_sum_kernel(info_ref, *refs):
            owned = refs[:seq_parts]
            last_ref, scr = refs[seq_parts:]
            top = half_own + pair_rows
            whole = owned[0][0:top, :].astype(f32)
            for j in others:
                whole = whole + owned[j][0:top, :].astype(f32)
            last_ref[0:top, :] = whole.astype(bf)
            for j in range(seq_parts):
                place = jnp.bitwise_xor(info_ref[0], j)
                piece = owned[j][top:, :].astype(f32)
                scr[aligned(place, sub), :] = fold_out(piece[0 : sub // 2])
            last_ref[top:, :] = fold_in(scr[...]).astype(bf)

        (last_one,) = local_call(
            dp_sum_kernel,
            "shares",
            [shape_of((half_own + pair_rows + fold, width), bf)],
            [info] + dp_parts,
            scalars=1,
            scratch=[pltpu.VMEM((own_width, half_ff), f32)],
            after=[con_one_far, con_two_far, gt_far_two],
        )
        last_two = chip_swap(last_one, 2)
        last_one_far = chip_swap(last_one, 1)
        def tokens_kernel(tok_ref, vec_ref, gmid_ref, own_ref, far_ref, out_ref, done_ref):
            done_ref[...] = jnp.zeros_like(done_ref)
            grad = own_ref[...] + far_ref[...].astype(f32)
            xhat, spread = norm_stats(tok_ref[...].astype(f32))
            out_ref[0] = gmid_ref[...] + norm_back(grad, vec_ref[0:1], xhat, spread)

        grad_tokens, tokens_done = local_call(
            tokens_kernel,
            "tokens_back",
            [shape_of((1, rows, width), f32), shape_of((8, 128), f32)],
            [own_tokens, vectors, grad_middle, gt_own, gt_far_two],
        )

        def pass_kernel(in_ref, out_ref):
            out_ref[...] = in_ref[...]

        (last_two_on,) = local_call(
            pass_kernel,
            "pass_on",
            [shape_of((half_own + pair_rows + fold, width), bf)],
            [last_two],
            after=[contract_done, tokens_done, last_one_far],
        )
        last_two_far = chip_swap(last_two_on, 1)
        last_parts = [last_one, last_one_far, last_two, last_two_far]
        last_far = [core_swap(member) for member in last_parts]

        def last_kernel(info_ref, *refs):
            gin_ref, gout_ref, exp_ref = refs[2 * parts : 2 * parts + 3]
            bias_ref, smalls, scr, out_scr = refs[2 * parts + 3], refs[2 * parts + 4 : -2], *refs[-2:]
            for flip in range(2):
                half = jnp.bitwise_xor(info_ref[2], flip)
                outs = [jnp.zeros((pair_rows, width), f32)] * 2
                for k in range(parts):
                    at = jnp.bitwise_xor(info_ref[1], k)
                    piece = refs[flip * parts + k][...].astype(f32)
                    scr[at, aligned(half, half_own), :] = piece[0:half_own, 0 : 3 * hw]
                    outs[k % 2] = outs[k % 2] + piece[at_outs]
                    turned = fold_out(piece[half_own + pair_rows :])
                    for j in range(seq_parts):
                        cols = pl.ds(pl.multiple_of(j * ff + half * half_ff, 128), half_ff)
                        exp_ref[aligned(at, sub), cols] = turned[j * sub : (j + 1) * sub]
                mine = info_ref[1] % 2
                out_scr[mine] = outs[0]
                out_scr[1 - mine] = outs[1]
                gout_ref[:, aligned(half, half_width)] = fold_out(
                    jnp.concatenate([out_scr[0], out_scr[1]], axis=0)
                )
            for at in range(parts):
                for base in range(3):
                    start = base * width + at * hw
                    gin_ref[:, start : start + hw] = scr[at, :, base * hw : (base + 1) * hw]
            small = refs[0][0:small_rows, 3 * hw :].astype(f32)
            for k in others:
                small = small + refs[k][0:small_rows, 3 * hw :].astype(f32)
            for i in range(8):
                smalls[i][...] = small[i : i + 1].reshape(own_width)
            bias_ref[...] = jnp.concatenate(
                [small[8 + i : 9 + i] for i in range(ff // own_width)], axis=1
            ).reshape(ff)

        last_out = local_call(
            last_kernel,
            "weights_final",
            [
                shape_of((own_width, 3 * width), f32),
                shape_of((own_width, width), f32),
                shape_of((own_width, seq_parts * ff), f32),
                shape_of((ff,), f32),
            ]
            + [shape_of((own_width,), f32)] * 8,
            [info] + last_parts + last_far,
            scalars=1,
            scratch=[
                pltpu.VMEM((parts, own_width, 3 * hw), f32),
                pltpu.VMEM((2, pair_rows, width), f32),
            ],
            grant=VMEM_LARGE,
        )
        grad_input, grad_output, grad_expand, grad_expand_bias = last_out[:4]
        small_of = last_out[4:]
        return (
            block_out,
            grad_tokens,
            small_of[0],
            small_of[1],
            grad_input,
            small_of[2],
            small_of[3],
            grad_output,
            small_of[4],
            small_of[5],
            small_of[6],
            grad_expand,
            grad_expand_bias,
            grad_contract,
            small_of[7],
        )

    return per_device_heads


def solution(mesh):
    ranks = mesh.shape["ctx"]
    chips = ranks // 2
    if chips == mesh.shape["dp"] and HEADS % chips == 0 and chips & (chips - 1) == 0:
        body = head_parallel(ranks, chips, mesh.shape["dp"])
    else:
        body = per_device
    return jax.shard_map(
        body,
        mesh=mesh,
        in_specs=(
            P("dp", "ctx", None),
            P(),
            P("dp"),
            P("dp"),
            P("dp", None),
            P("dp"),
            P("dp"),
            P("dp", None),
            P("dp"),
            P("dp"),
            P("dp"),
            P("dp", None),
            P("dp"),
            P("dp", None),
            P("dp"),
            P("dp", "ctx", None),
        ),
        out_specs=(
            P("dp", "ctx", None),
            P("dp", "ctx", None),
            P("dp"),
            P("dp"),
            P("dp", None),
            P("dp"),
            P("dp"),
            P("dp", None),
            P("dp"),
            P("dp"),
            P("dp"),
            P("dp", None),
            P("dp"),
            P("dp", None),
            P("dp"),
        ),
        check_vma=False,
    )
```

```python
import math

import jax
import jax.numpy as jnp
from jax import lax
from jax.experimental import pallas as pl
from jax.experimental.pallas import tpu as pltpu
from jax.sharding import PartitionSpec as P

HEADS = 12
HEAD_DIM = 64


NEG_BIG = -1e30
NORM_EPS = 1e-05
GELU_SCALE = 0.7978845608028654
GELU_CUBIC = 0.044715


def gelu_tanh(values):
    return (
        0.5
        * values
        * (1.0 + jnp.tanh(GELU_SCALE * (values + GELU_CUBIC * values * values * values)))
    )


def layer_norm(values, gain_row, shift_row):
    centre = values - jnp.mean(values, axis=-1, keepdims=True)
    spread = jnp.mean(centre * centre, axis=-1, keepdims=True)
    return centre * lax.rsqrt(spread + NORM_EPS) * gain_row + shift_row


def lookup_pair(pair_table, positions):
    ranks_all = jnp.arange(pair_table.shape[0], dtype=jnp.int32)
    return jnp.sum(jnp.where(positions[..., None] == ranks_all, pair_table, 0), axis=-1)


def group_count(blocks, sub_rows):
    chosen_count = 1
    for candidate in range(1, blocks + 1):
        if blocks % candidate == 0 and candidate * sub_rows <= max(512, sub_rows):
            chosen_count = candidate
    return chosen_count


def slot_mask(slot_ids, wanted, rank_count):
    return (slot_ids == wanted).reshape((-1,) + (1,) * (rank_count - 1))


def slot_add(values, slot_ids):
    early_sum = jnp.sum(jnp.where(slot_mask(slot_ids, 0, values.ndim), values, 0.0), axis=0)
    late_sum = jnp.sum(jnp.where(slot_mask(slot_ids, 1, values.ndim), values, 0.0), axis=0)
    return jnp.stack([early_sum, late_sum])


def slot_max(values, slot_ids):
    early_max = jnp.max(jnp.where(slot_mask(slot_ids, 0, values.ndim), values, NEG_BIG), axis=0)
    late_max = jnp.max(jnp.where(slot_mask(slot_ids, 1, values.ndim), values, NEG_BIG), axis=0)
    return jnp.stack([early_max, late_max])


def slot_pick(per_slot, slot_ids):
    return jnp.where(slot_mask(slot_ids, 0, per_slot.ndim), per_slot[0][None], per_slot[1][None])


def query_tiles(blocks, chosen):
    target = chosen.shape + blocks.shape[2:]
    chosen_view = chosen.reshape((-1,) + (1,) * (blocks.ndim - 2))
    late_part = jnp.broadcast_to(blocks[1], target)
    picked = jnp.where(chosen_view, blocks[0], blocks[1])
    return jnp.concatenate([late_part, picked], axis=0)


def key_tiles(blocks, chosen):
    target = chosen.shape + blocks.shape[2:]
    chosen_view = chosen.reshape((-1,) + (1,) * (blocks.ndim - 2))
    early_part = jnp.broadcast_to(blocks[0], target)
    picked = jnp.where(chosen_view, blocks[0], blocks[1])
    return jnp.concatenate([early_part, picked], axis=0)


def tile_slots(chosen):
    late_slot = jnp.where(chosen, 0, 1).astype(jnp.int32)
    query_slot = jnp.concatenate([jnp.ones_like(late_slot), late_slot])
    key_slot = jnp.concatenate([jnp.zeros_like(late_slot), late_slot])
    return (query_slot, key_slot)


def tile_mask(is_own, query_places, key_places):
    visible = key_places[:, None, :] <= query_places[:, :, None]
    visible = jnp.logical_or(visible, jnp.logical_not(is_own)[:, None, None])
    return jnp.concatenate([jnp.ones_like(visible), visible], axis=0)


def tile_scores(tile_query, tile_key, score_scale):
    return (
        jnp.einsum("tqhd,tkhd->thqk", tile_query, tile_key, preferred_element_type=jnp.float32)
        * score_scale
    )


def tile_probs(tile_query, tile_key, tile_visible, row_lse, score_scale):
    scores = tile_scores(tile_query, tile_key, score_scale)
    return jnp.where(tile_visible[:, None], jnp.exp(scores - row_lse[..., None]), 0.0)


def tile_dscore(probs, tile_dout, tile_value, row_delta):
    grad_probs = jnp.einsum(
        "tqhd,tkhd->thqk", tile_dout, tile_value, preferred_element_type=jnp.float32
    )
    return (probs * (grad_probs - row_delta[..., None])).astype(jnp.bfloat16)


def stats_update(running, tile_query, tile_key, query_slot, tile_visible, score_scale):
    run_peak, run_total = running
    visible = tile_visible[:, None]
    masked = jnp.where(visible, tile_scores(tile_query, tile_key, score_scale), NEG_BIG)
    new_peak = jnp.maximum(run_peak, slot_max(jnp.max(masked, axis=-1), query_slot))
    weights = jnp.where(visible, jnp.exp(masked - slot_pick(new_peak, query_slot)[..., None]), 0.0)
    run_total = run_total * jnp.exp(run_peak - new_peak) + slot_add(
        jnp.sum(weights, axis=-1), query_slot
    )
    return (new_peak, run_total)


def values_update(
    running, tile_query, tile_key, tile_value, query_slot, tile_visible, row_lse, score_scale
):
    probs = tile_probs(tile_query, tile_key, tile_visible, row_lse, score_scale)
    part_out = jnp.einsum(
        "thqk,tkhd->tqhd",
        probs.astype(jnp.bfloat16),
        tile_value,
        preferred_element_type=jnp.float32,
    )
    return running + slot_add(part_out, query_slot)


def sweep_piece(carried, pieces, block_rows, my_rank, pair_table, update):
    piece_rows = pieces[0].shape[1]
    sub_rows = math.gcd(piece_rows, block_rows)
    unit_count = piece_rows // sub_rows
    group_size = group_count(unit_count, sub_rows)

    def group_step(loop_index, running):
        offset = loop_index * (group_size * sub_rows)
        slices = tuple(
            (
                lax.dynamic_slice_in_dim(member, offset, group_size * sub_rows, 1).reshape(
                    (2, group_size, sub_rows) + member.shape[2:]
                )
                for member in pieces
            )
        )
        places = offset + jnp.arange(group_size * sub_rows, dtype=jnp.int32).reshape(
            group_size, sub_rows
        )
        far_ranks = places[:, 0] // block_rows
        far_pair = lookup_pair(pair_table, far_ranks)
        return update(running, slices, far_pair, far_ranks == my_rank, places % block_rows, offset)

    return lax.fori_loop(0, unit_count // group_size, group_step, carried)


def per_device(
    tokens,
    pair_of_rank,
    first_gain,
    first_shift,
    w_input,
    query_bias,
    value_bias,
    w_output,
    output_bias,
    second_gain,
    second_shift,
    w_expand,
    expand_bias,
    w_contract,
    contract_bias,
    cotangent,
):
    gathered = (
        lax.all_gather(first_gain, "dp", axis=0, tiled=True),
        lax.all_gather(first_shift, "dp", axis=0, tiled=True),
        lax.all_gather(w_input, "dp", axis=0, tiled=True),
        lax.all_gather(query_bias, "dp", axis=0, tiled=True),
        lax.all_gather(value_bias, "dp", axis=0, tiled=True),
        lax.all_gather(w_output, "dp", axis=0, tiled=True),
        lax.all_gather(output_bias, "dp", axis=0, tiled=True),
        lax.all_gather(second_gain, "dp", axis=0, tiled=True),
        lax.all_gather(second_shift, "dp", axis=0, tiled=True),
        lax.all_gather(w_expand, "dp", axis=0, tiled=True),
        lax.all_gather(expand_bias, "dp", axis=0, tiled=True),
        lax.all_gather(w_contract, "dp", axis=0, tiled=True),
        lax.all_gather(contract_bias, "dp", axis=0, tiled=True),
    )
    (
        full_first_gain,
        full_first_shift,
        full_input,
        full_query_bias,
        full_value_bias,
        full_output,
        full_output_bias,
        full_second_gain,
        full_second_shift,
        full_expand,
        full_expand_bias,
        full_contract,
        full_contract_bias,
    ) = gathered
    model_width = tokens.shape[2]
    block_rows = tokens.shape[1] // 2
    score_scale = HEAD_DIM ** (-0.5)
    slot_view = (2, block_rows, model_width)
    head_view = (2, block_rows, HEADS, HEAD_DIM)
    my_rank = lax.axis_index("ctx")
    my_pair = lookup_pair(pair_of_rank, my_rank)
    own_places = jnp.arange(block_rows, dtype=jnp.int32)[None, :]
    diag_mask = (own_places <= own_places.reshape(-1, 1))[None]
    zero_slot = jnp.zeros((1,), jnp.int32)

    def split_heads(member):
        return member.reshape(member.shape[:3] + (HEADS, HEAD_DIM))

    token_rows = tokens[0].astype(jnp.float32)
    normed_full, first_pullback = jax.vjp(
        layer_norm,
        token_rows,
        full_first_gain.astype(jnp.float32),
        full_first_shift.astype(jnp.float32),
    )
    normed = normed_full.astype(jnp.bfloat16)
    mixed_rows = jnp.dot(normed, full_input, preferred_element_type=jnp.float32)
    query_rows = (mixed_rows[:, :model_width] + full_query_bias.astype(jnp.float32)).astype(
        jnp.bfloat16
    )
    key_rows = mixed_rows[:, model_width : 2 * model_width].astype(jnp.bfloat16)
    value_rows = (mixed_rows[:, 2 * model_width :] + full_value_bias.astype(jnp.float32)).astype(
        jnp.bfloat16
    )
    own_query = query_rows.reshape(head_view)
    own_key = key_rows.reshape(head_view)
    own_value = value_rows.reshape(head_view)
    diag_query = own_query[0][None]
    diag_key = own_key[0][None]
    diag_value = own_value[0][None]
    key_slots = key_rows.reshape(slot_view)
    value_slots = value_rows.reshape(slot_view)
    query_slots = query_rows.reshape(slot_view)

    def stats_group(running, slices, far_pair, is_own, far_places, first_row):
        chosen = far_pair < my_pair
        query_slot, key_slot = tile_slots(chosen)
        return stats_update(
            running,
            query_tiles(own_query[:, None], chosen),
            key_tiles(split_heads(slices[0]), chosen),
            query_slot,
            tile_mask(is_own, own_places, far_places),
            score_scale,
        )

    stats_start = (
        jnp.full((2, HEADS, block_rows), NEG_BIG, jnp.float32),
        jnp.zeros((2, HEADS, block_rows), jnp.float32),
    )
    stats_start = stats_update(stats_start, diag_query, diag_key, zero_slot, diag_mask, score_scale)
    run_peak, run_total = sweep_piece(
        stats_start,
        (lax.all_gather(key_slots, "ctx", axis=1, tiled=True),),
        block_rows,
        my_rank,
        pair_of_rank,
        stats_group,
    )
    row_lse = run_peak + jnp.log(run_total)

    def values_group(running, slices, far_pair, is_own, far_places, first_row):
        chosen = far_pair < my_pair
        query_slot, key_slot = tile_slots(chosen)
        return values_update(
            running,
            query_tiles(own_query[:, None], chosen),
            key_tiles(split_heads(slices[0]), chosen),
            key_tiles(split_heads(slices[1]), chosen),
            query_slot,
            tile_mask(is_own, own_places, far_places),
            slot_pick(row_lse, query_slot),
            score_scale,
        )

    values_start = values_update(
        jnp.zeros(head_view, jnp.float32),
        diag_query,
        diag_key,
        diag_value,
        zero_slot,
        diag_mask,
        row_lse[0][None],
        score_scale,
    )
    attended = sweep_piece(
        values_start,
        (
            lax.all_gather(key_slots, "ctx", axis=1, tiled=True),
            lax.all_gather(value_slots, "ctx", axis=1, tiled=True),
        ),
        block_rows,
        my_rank,
        pair_of_rank,
        values_group,
    )
    attended_low = attended.reshape(2 * block_rows, model_width).astype(jnp.bfloat16)
    middle = (
        token_rows
        + jnp.dot(attended_low, full_output, preferred_element_type=jnp.float32)
        + full_output_bias.astype(jnp.float32)
    )
    normed_full_two, second_pullback = jax.vjp(
        layer_norm,
        middle,
        full_second_gain.astype(jnp.float32),
        full_second_shift.astype(jnp.float32),
    )
    normed_two = normed_full_two.astype(jnp.bfloat16)
    hidden = jnp.dot(
        normed_two, full_expand, preferred_element_type=jnp.float32
    ) + full_expand_bias.astype(jnp.float32)
    active_full, gelu_pullback = jax.vjp(gelu_tanh, hidden)
    active_low = active_full.astype(jnp.bfloat16)
    result = (
        middle
        + jnp.dot(active_low, full_contract, preferred_element_type=jnp.float32)
        + full_contract_bias.astype(jnp.float32)
    )
    block_out = result.astype(jnp.bfloat16)[None]
    back_input, back_output, back_expand, back_contract = (
        lax.all_gather(w_input, "dp", axis=0, tiled=True),
        lax.all_gather(w_output, "dp", axis=0, tiled=True),
        lax.all_gather(w_expand, "dp", axis=0, tiled=True),
        lax.all_gather(w_contract, "dp", axis=0, tiled=True),
    )
    grad_out_low = cotangent[0]
    grad_out = grad_out_low.astype(jnp.float32)
    grad_contract = jnp.einsum(
        "rf,rd->fd", active_low, grad_out_low, preferred_element_type=jnp.float32
    )
    grad_contract_bias = jnp.sum(grad_out, axis=0)
    grad_active = jnp.einsum(
        "rd,fd->rf", grad_out_low, back_contract, preferred_element_type=jnp.float32
    )
    grad_hidden = gelu_pullback(grad_active)[0].astype(jnp.bfloat16)
    grad_expand = jnp.einsum(
        "rd,rf->df", normed_two, grad_hidden, preferred_element_type=jnp.float32
    )
    grad_expand_bias = jnp.sum(grad_hidden.astype(jnp.float32), axis=0)
    grad_normed_two = jnp.einsum(
        "rf,df->rd", grad_hidden, back_expand, preferred_element_type=jnp.float32
    )
    grad_middle_part, grad_second_gain, grad_second_shift = second_pullback(grad_normed_two)
    grad_middle = grad_out + grad_middle_part
    grad_branch = grad_middle.astype(jnp.bfloat16)
    grad_output = jnp.einsum(
        "rd,re->de", attended_low, grad_branch, preferred_element_type=jnp.float32
    )
    grad_output_bias = jnp.sum(grad_branch.astype(jnp.float32), axis=0)
    grad_attended = jnp.einsum(
        "re,de->rd", grad_branch, back_output, preferred_element_type=jnp.float32
    ).astype(jnp.bfloat16)
    own_dout = grad_attended.reshape(head_view)
    dout_slots = grad_attended.reshape(slot_view)
    delta_rows = jnp.sum(own_dout.astype(jnp.float32) * attended, axis=-1)
    row_delta = jnp.transpose(delta_rows, (0, 2, 1))
    lse_rows = jnp.transpose(row_lse, (0, 2, 1))
    far_lse, far_delta = (
        lax.all_gather(lse_rows, "ctx", axis=1, tiled=True),
        lax.all_gather(delta_rows, "ctx", axis=1, tiled=True),
    )
    diag_probs = tile_probs(diag_query, diag_key, diag_mask, row_lse[0][None], score_scale)
    diag_dscore = tile_dscore(diag_probs, own_dout[0][None], diag_value, row_delta[0][None])
    query_start = slot_add(
        jnp.einsum("thqk,tkhd->tqhd", diag_dscore, diag_key, preferred_element_type=jnp.float32)
        * score_scale,
        zero_slot,
    )
    key_start = slot_add(
        jnp.einsum("thqk,tqhd->tkhd", diag_dscore, diag_query, preferred_element_type=jnp.float32)
        * score_scale,
        zero_slot,
    )
    value_start = slot_add(
        jnp.einsum(
            "thqk,tqhd->tkhd",
            diag_probs.astype(jnp.bfloat16),
            own_dout[0][None],
            preferred_element_type=jnp.float32,
        ),
        zero_slot,
    )

    def query_grad_group(running, slices, far_pair, is_own, far_places, first_row):
        chosen = far_pair < my_pair
        query_slot, key_slot = tile_slots(chosen)
        tile_key = key_tiles(split_heads(slices[0]), chosen)
        tile_value = key_tiles(split_heads(slices[1]), chosen)
        probs = tile_probs(
            query_tiles(own_query[:, None], chosen),
            tile_key,
            tile_mask(is_own, own_places, far_places),
            slot_pick(row_lse, query_slot),
            score_scale,
        )
        dscore = tile_dscore(
            probs,
            query_tiles(own_dout[:, None], chosen),
            tile_value,
            slot_pick(row_delta, query_slot),
        )
        part_grad = (
            jnp.einsum("thqk,tkhd->tqhd", dscore, tile_key, preferred_element_type=jnp.float32)
            * score_scale
        )
        return running + slot_add(part_grad, query_slot)

    def key_grad_group(running, slices, far_pair, is_own, far_places, first_row):
        chosen = my_pair < far_pair
        query_slot, key_slot = tile_slots(chosen)
        group_size = far_places.shape[0]
        sub_rows = far_places.shape[1]
        tile_query = query_tiles(split_heads(slices[0]), chosen)
        tile_dout = query_tiles(split_heads(slices[1]), chosen)
        lse_part = lax.dynamic_slice_in_dim(far_lse, first_row, group_size * sub_rows, 1).reshape(
            2, group_size, sub_rows, HEADS
        )
        delta_part = lax.dynamic_slice_in_dim(
            far_delta, first_row, group_size * sub_rows, 1
        ).reshape(2, group_size, sub_rows, HEADS)
        tile_lse = jnp.transpose(query_tiles(lse_part, chosen), (0, 2, 1))
        tile_delta = jnp.transpose(query_tiles(delta_part, chosen), (0, 2, 1))
        tile_key = key_tiles(own_key[:, None], chosen)
        tile_value = key_tiles(own_value[:, None], chosen)
        probs = tile_probs(
            tile_query, tile_key, tile_mask(is_own, far_places, own_places), tile_lse, score_scale
        )
        dscore = tile_dscore(probs, tile_dout, tile_value, tile_delta)
        key_part = (
            jnp.einsum("thqk,tqhd->tkhd", dscore, tile_query, preferred_element_type=jnp.float32)
            * score_scale
        )
        value_part = jnp.einsum(
            "thqk,tqhd->tkhd",
            probs.astype(jnp.bfloat16),
            tile_dout,
            preferred_element_type=jnp.float32,
        )
        return (
            running[0] + slot_add(key_part, key_slot),
            running[1] + slot_add(value_part, key_slot),
        )

    grad_query_sum = sweep_piece(
        query_start,
        (
            lax.all_gather(key_slots, "ctx", axis=1, tiled=True),
            lax.all_gather(value_slots, "ctx", axis=1, tiled=True),
        ),
        block_rows,
        my_rank,
        pair_of_rank,
        query_grad_group,
    )
    grad_key_sum, grad_value_sum = sweep_piece(
        (key_start, value_start),
        (
            lax.all_gather(query_slots, "ctx", axis=1, tiled=True),
            lax.all_gather(dout_slots, "ctx", axis=1, tiled=True),
        ),
        block_rows,
        my_rank,
        pair_of_rank,
        key_grad_group,
    )
    flat_rows = 2 * block_rows
    grad_query_low = grad_query_sum.reshape(flat_rows, model_width).astype(jnp.bfloat16)
    grad_key_low = grad_key_sum.reshape(flat_rows, model_width).astype(jnp.bfloat16)
    grad_value_low = grad_value_sum.reshape(flat_rows, model_width).astype(jnp.bfloat16)
    grad_mixed = jnp.concatenate([grad_query_low, grad_key_low, grad_value_low], axis=1)
    grad_input = jnp.einsum("rd,re->de", normed, grad_mixed, preferred_element_type=jnp.float32)
    grad_query_bias = jnp.sum(grad_query_low.astype(jnp.float32), axis=0)
    grad_value_bias = jnp.sum(grad_value_low.astype(jnp.float32), axis=0)
    grad_normed = jnp.einsum(
        "re,de->rd", grad_mixed, back_input, preferred_element_type=jnp.float32
    )
    grad_token_part, grad_first_gain, grad_first_shift = first_pullback(grad_normed)
    grad_tokens = (grad_middle + grad_token_part)[None]
    grad_local = (
        grad_first_gain,
        grad_first_shift,
        grad_input,
        grad_query_bias,
        grad_value_bias,
        grad_output,
        grad_output_bias,
        grad_second_gain,
        grad_second_shift,
        grad_expand,
        grad_expand_bias,
        grad_contract,
        grad_contract_bias,
    )
    grad_owned = (
        lax.psum_scatter(
            grad_local[0].astype(jnp.bfloat16), "dp", scatter_dimension=0, tiled=True
        ).astype(jnp.float32),
        lax.psum_scatter(
            grad_local[1].astype(jnp.bfloat16), "dp", scatter_dimension=0, tiled=True
        ).astype(jnp.float32),
        lax.psum_scatter(
            grad_local[2].astype(jnp.bfloat16), "dp", scatter_dimension=0, tiled=True
        ).astype(jnp.float32),
        lax.psum_scatter(
            grad_local[3].astype(jnp.bfloat16), "dp", scatter_dimension=0, tiled=True
        ).astype(jnp.float32),
        lax.psum_scatter(
            grad_local[4].astype(jnp.bfloat16), "dp", scatter_dimension=0, tiled=True
        ).astype(jnp.float32),
        lax.psum_scatter(
            grad_local[5].astype(jnp.bfloat16), "dp", scatter_dimension=0, tiled=True
        ).astype(jnp.float32),
        lax.psum_scatter(
            grad_local[6].astype(jnp.bfloat16), "dp", scatter_dimension=0, tiled=True
        ).astype(jnp.float32),
        lax.psum_scatter(
            grad_local[7].astype(jnp.bfloat16), "dp", scatter_dimension=0, tiled=True
        ).astype(jnp.float32),
        lax.psum_scatter(
            grad_local[8].astype(jnp.bfloat16), "dp", scatter_dimension=0, tiled=True
        ).astype(jnp.float32),
        lax.psum_scatter(
            grad_local[9].astype(jnp.bfloat16), "dp", scatter_dimension=0, tiled=True
        ).astype(jnp.float32),
        lax.psum_scatter(
            grad_local[10].astype(jnp.bfloat16), "dp", scatter_dimension=0, tiled=True
        ).astype(jnp.float32),
        lax.psum_scatter(
            grad_local[11].astype(jnp.bfloat16), "dp", scatter_dimension=0, tiled=True
        ).astype(jnp.float32),
        lax.psum_scatter(
            grad_local[12].astype(jnp.bfloat16), "dp", scatter_dimension=0, tiled=True
        ).astype(jnp.float32),
    )
    grad_final = tuple(
        lax.psum(
            (
                grad_owned[0],
                grad_owned[1],
                grad_owned[2],
                grad_owned[3],
                grad_owned[4],
                grad_owned[5],
                grad_owned[6],
                grad_owned[7],
                grad_owned[8],
                grad_owned[9],
                grad_owned[10],
                grad_owned[11],
                grad_owned[12],
            ),
            "ctx",
        )
    )
    return (block_out, grad_tokens) + tuple(grad_final)


VMEM_BYTES = 16 * 1024 * 1024
VMEM_LARGE = 28 * 1024 * 1024


def mm(left, right):
    return lax.dot_general(
        left, right, (((1,), (0,)), ((), ())), preferred_element_type=jnp.float32
    )


def mm_nt(left, right):
    return lax.dot_general(
        left, right, (((1,), (1,)), ((), ())), preferred_element_type=jnp.float32
    )


def mm_tn(left, right):
    return lax.dot_general(
        left, right, (((0,), (0,)), ((), ())), preferred_element_type=jnp.float32
    )


def aligned(index, size):
    return pl.ds(pl.multiple_of(index * size, size), size)


def norm_stats(values):
    centre = values - jnp.mean(values, axis=-1, keepdims=True)
    spread = jnp.mean(centre * centre, axis=-1, keepdims=True)
    scale = lax.rsqrt(spread + NORM_EPS)
    return centre * scale, scale


def norm_back(grad_normed, gain_row, xhat, scale):
    weighted = grad_normed * gain_row
    return scale * (
        weighted
        - jnp.mean(weighted, axis=-1, keepdims=True)
        - xhat * jnp.mean(weighted * xhat, axis=-1, keepdims=True)
    )


def column_sums(values):
    return jnp.sum(values, axis=0, keepdims=True)


def shape_of(dims, dtype):
    return jax.ShapeDtypeStruct(dims, dtype)


def local_call(
    kernel, name, outs, args, scalars=0, scratch=(), flops=0, after=(), space=pltpu.VMEM, grant=VMEM_BYTES
):
    moved = sum(math.prod(a.shape) * a.dtype.itemsize for a in tuple(args) + tuple(outs))

    def ordered(*refs):
        kernel(*refs[: len(args)], *refs[len(args) + len(after) :])

    return pl.pallas_call(
        ordered,
        out_shape=tuple(outs),
        in_specs=[pl.BlockSpec(memory_space=pltpu.SMEM)] * scalars
        + [pl.BlockSpec(memory_space=space)] * (len(args) - scalars)
        + [pl.BlockSpec(memory_space=pl.ANY)] * len(after),
        out_specs=tuple(pl.BlockSpec(memory_space=pltpu.VMEM) for _ in outs),
        scratch_shapes=list(scratch),
        compiler_params=pltpu.CompilerParams(vmem_limit_bytes=grant),
        cost_estimate=pl.CostEstimate(
            flops=flops, bytes_accessed=moved if flops else 0, transcendentals=0
        ),
        name=name,
    )(*args, *after)


def place_of_block(pair_ref, info_ref, ranks, step, half, other_core):
    core = jnp.bitwise_xor(info_ref[2], other_core)
    rank = 2 * jnp.bitwise_xor(info_ref[1], step) + core
    pair = pair_ref[rank]
    return pair if half == 0 else 2 * ranks - 1 - pair


def fill_mask(bias_ref, pair_ref, info_ref, ranks, parts, block):
    rows = 2 * parts * block
    lanes = lax.broadcasted_iota(jnp.int32, (1, rows), 1)
    query_place = lanes % block
    for step in range(parts):
        for half in range(2):
            place = place_of_block(pair_ref, info_ref, ranks, step, half, 0)
            query_place = query_place + jnp.where(
                lanes // block == 2 * step + half, place * block, 0
            )
    ahead = lax.broadcasted_iota(jnp.int32, (block, rows), 0) - query_place
    for other in range(2):
        for step in range(parts):
            for half in range(2):
                place = place_of_block(pair_ref, info_ref, ranks, step, half, other)
                start = other * rows + (2 * step + half) * block
                bias_ref[start : start + block, :] = jnp.where(
                    ahead <= -place * block, 0.0, NEG_BIG
                )


def head_parallel(ranks, chips, seq_parts):
    parts = chips
    hw = HEADS // chips * HEAD_DIM

    def core_swap(member):
        return lax.ppermute(member, "ctx", [(i, i ^ 1) for i in range(ranks)])

    def chip_swap(member, step):
        return lax.ppermute(
            member, "ctx", [(i, 2 * ((i // 2) ^ step) + i % 2) for i in range(ranks)]
        )

    def seq_swap(member, step):
        return lax.ppermute(member, "dp", [(i, i ^ step) for i in range(seq_parts)])

    def per_device_heads(
        tokens,
        pair_of_rank,
        first_gain,
        first_shift,
        w_input,
        query_bias,
        value_bias,
        w_output,
        output_bias,
        second_gain,
        second_shift,
        w_expand,
        expand_bias,
        w_contract,
        contract_bias,
        cotangent,
    ):
        bf, f32 = jnp.bfloat16, jnp.float32
        rows, width = tokens.shape[1:]
        block = rows // 2
        own_width = width // seq_parts
        ff = expand_bias.shape[0]
        total = parts * rows
        half_width = width // 2
        half_ff = ff // 2
        sub = own_width // parts
        half_own = own_width // 2
        small_rows = 16
        others = range(1, parts)
        seq_id = lax.axis_index("dp")
        rank = lax.axis_index("ctx")
        chip = rank // 2
        core = rank % 2
        info = jnp.stack([seq_id, chip, core]).astype(jnp.int32)

        side = width - 3 * hw
        pack_rows = 2 * half_own

        def pack_kernel(info_ref, tok_ref, w_ref, wo_ref, *refs):
            vecs = refs[:8]
            packed_ref, tokens_ref, w_scr, wo_scr = refs[8:12]
            scrs, sems = refs[12:20], refs[20]
            mine = pl.ds(pl.multiple_of(info_ref[2] * half_own, half_own), half_own)
            pairs = [(w_ref.at[mine], w_scr), (wo_ref.at[mine], wo_scr), (tok_ref, tokens_ref)]
            pairs += list(zip(vecs, scrs))
            copies = [
                pltpu.make_async_copy(src, dst, sems.at[i]) for i, (src, dst) in enumerate(pairs)
            ]
            for copy in copies:
                copy.start()
            for copy in copies:
                copy.wait()
            at_w = slice(half_own, 2 * half_own)
            for at in range(chips):

                @pl.when(info_ref[1] == at)
                def _():
                    for base in range(3):
                        start = base * width + at * hw
                        packed_ref[at_w, base * hw : (base + 1) * hw] = w_scr[
                            :, start : start + hw
                        ]

            packed_ref[0:half_own, :] = wo_scr[...]
            small = jnp.concatenate(
                [v[...].astype(f32).reshape(1, own_width) for v in scrs], axis=0
            )
            small = jnp.concatenate([small, jnp.zeros_like(small)], axis=0)
            packed_ref[half_own : half_own + small_rows, 3 * hw :] = small.astype(bf)
            packed_ref[half_own + small_rows :, 3 * hw :] = jnp.zeros(
                (half_own - small_rows, side), bf
            )

        small_args = (
            first_gain,
            first_shift,
            query_bias,
            value_bias,
            output_bias,
            second_gain,
            second_shift,
            contract_bias,
        )
        packed, own_tokens = local_call(
            pack_kernel,
            "pack",
            [shape_of((pack_rows, width), bf), shape_of((rows, width), bf)],
            [info, tokens[0], w_input, w_output] + list(small_args),
            scalars=1,
            scratch=[pltpu.VMEM((half_own, 3 * width), bf), pltpu.VMEM((half_own, width), bf)]
            + [pltpu.VMEM((own_width,), bf)] * 8
            + [pltpu.SemaphoreType.DMA((11,))],
            space=pltpu.HBM,
            grant=60 * 1024 * 1024,
        )
        token_two = chip_swap(own_tokens, 2)
        token_parts = [own_tokens, chip_swap(own_tokens, 1), token_two, chip_swap(token_two, 1)]
        packed_near = [seq_swap(packed, j) for j in others]

        def stack_kernel(*refs):
            depth = refs[0].shape[0]
            for i, ref in enumerate(refs[:-1]):
                refs[-1][i * depth : (i + 1) * depth, :] = ref[...]

        (packed_all,) = local_call(
            stack_kernel,
            "pack_stack",
            [shape_of(((seq_parts - 1) * pack_rows, width), bf)],
            packed_near,
            after=token_parts[1:],
        )
        packed_far = core_swap(packed_all)
        own_cot = cotangent[0]

        def pack_more_kernel(info_ref, we_ref, cot_ref, *refs):
            for j in others:
                start = pl.multiple_of(info_ref[2] * half_own, half_own)
                refs[j - 1][0:half_own, :] = we_ref[
                    pl.ds(start, half_own), aligned(jnp.bitwise_xor(info_ref[0], j), ff)
                ]
                refs[j - 1][half_own:, :] = cot_ref[...]

        more = local_call(
            pack_more_kernel,
            "pack_more",
            [shape_of((half_own + rows, width), bf)] * (seq_parts - 1),
            [info, w_expand, own_cot],
            scalars=1,
            after=[packed],
        )
        more_parts = [seq_swap(more[j - 1], j) for j in others]

        def qkv_kernel(info_ref, w_own_ref, wo_own_ref, *refs):
            toks, own_pack, packs = refs[:parts], refs[parts], refs[parts + 1 : parts + 3]
            q_ref, kv_ref, normed_ref, w_ref, vec_ref, wo_ref, vec_scr = refs[parts + 3 :]
            for at in range(chips):

                @pl.when(info_ref[1] == at)
                def _():
                    for base in range(3):
                        start = base * width + at * hw
                        w_ref[aligned(info_ref[0], own_width), base * hw : (base + 1) * hw] = (
                            w_own_ref[:, start : start + hw]
                        )

            wo_ref[info_ref[0]] = wo_own_ref[...]
            at_small = slice(half_own, half_own + small_rows)
            vec_scr[info_ref[0]] = own_pack[at_small, 3 * hw :].astype(f32)
            for j in others:
                place = jnp.bitwise_xor(info_ref[0], j)
                base = (j - 1) * pack_rows
                vec_scr[place] = packs[0][
                    base + half_own : base + half_own + small_rows, 3 * hw :
                ].astype(f32)
                for flip in range(2):
                    member = packs[flip]
                    half = jnp.bitwise_xor(info_ref[2], flip)
                    down = pl.multiple_of(half * half_own, half_own)
                    wo_ref[place, pl.ds(down, half_own), :] = member[base : base + half_own, :]
                    start = pl.multiple_of(place * own_width + half * half_own, half_own)
                    w_ref[pl.ds(start, half_own), :] = member[
                        base + half_own : base + pack_rows, 0 : 3 * hw
                    ]
            vectors = jnp.concatenate([vec_scr[j] for j in range(parts)], axis=1)
            vec_ref[...] = vectors
            chosen = vec_scr[info_ref[1]]
            for k in range(parts):
                xhat, _ = norm_stats(toks[k][...].astype(f32))
                normed_ref[k * rows : (k + 1) * rows, :] = (
                    xhat * vectors[0:1] + vectors[1:2]
                ).astype(bf)
            mixed = mm(normed_ref[...], w_ref[...])
            q_ref[...] = (mixed[:, 0:hw] + chosen[2:3]).astype(bf)
            kv_ref[:, 0:hw] = mixed[:, hw : 2 * hw].astype(bf)
            kv_ref[:, hw : 2 * hw] = (mixed[:, 2 * hw :] + chosen[3:4]).astype(bf)

        query, own_kv, normed, w_heads_full, vectors, out_full = local_call(
            qkv_kernel,
            "project",
            [
                shape_of((total, hw), bf),
                shape_of((total, 2 * hw), bf),
                shape_of((total, width), bf),
                shape_of((width, 3 * hw), bf),
                shape_of((small_rows, width), f32),
                shape_of((parts, own_width, width), bf),
            ],
            [info, w_input, w_output] + token_parts + [packed, packed_all, packed_far],
            scalars=1,
            scratch=[pltpu.VMEM((parts, small_rows, own_width), f32)],
            flops=2 * total * width * 3 * hw,
        )
        far_kv = core_swap(own_kv)

        head_count = hw // HEAD_DIM
        scale = HEAD_DIM ** (-0.5)

        def head_columns(ref, base, head):
            start = base + head * HEAD_DIM
            return ref[:, start : start + HEAD_DIM]

        def attend_kernel(info_ref, pair_ref, q_ref, kv_ref, far_ref, *refs):
            outs = refs[:parts]
            flat_ref, lse_ref, bias_ref = refs[parts:]
            fill_mask(bias_ref, pair_ref, info_ref, ranks, parts, block)
            columns = []
            for head in range(head_count):
                keys = jnp.concatenate(
                    [head_columns(kv_ref, 0, head), head_columns(far_ref, 0, head)], axis=0
                )
                values = jnp.concatenate(
                    [head_columns(kv_ref, hw, head), head_columns(far_ref, hw, head)], axis=0
                )
                scores = mm_nt(keys, head_columns(q_ref, 0, head)) * scale + bias_ref[...]
                peak = jnp.max(scores, axis=0, keepdims=True)
                weights = jnp.exp(scores - peak)
                mass = jnp.sum(weights, axis=0, keepdims=True)
                lse_ref[head : head + 1, :] = peak + jnp.log(mass)
                mixed = mm_tn(values, weights.astype(bf)) / mass
                flat_ref[head * HEAD_DIM : (head + 1) * HEAD_DIM, :] = mixed
            attended = flat_ref[...].T.astype(bf)
            for k in range(parts):
                outs[k][...] = attended[k * rows : (k + 1) * rows]

        attend_out = local_call(
            attend_kernel,
            "attend",
            [shape_of((rows, hw), bf)] * parts
            + [shape_of((hw, total), f32), shape_of((8, total), f32)],
            [info, pair_of_rank, query, own_kv, far_kv],
            scalars=2,
            scratch=[pltpu.VMEM((2 * total, total), f32)],
            flops=2 * 2 * head_count * 2 * total * total * HEAD_DIM,
            grant=VMEM_LARGE,
        )
        flat_attended, row_lse = attend_out[parts:]
        att_parts = [attend_out[0]] + [chip_swap(attend_out[k], k) for k in others]

        def middle_kernel(info_ref, tok_ref, vec_ref, w_ref, *refs):
            atts = refs[:parts]
            mid_ref, normed_ref = refs[parts:]
            middle = tok_ref[...].astype(f32) + vec_ref[4:5]
            for k in range(parts):
                middle = middle + mm(atts[k][...], w_ref[jnp.bitwise_xor(info_ref[1], k)])
            mid_ref[...] = middle
            xhat, _ = norm_stats(middle)
            normed_ref[...] = (xhat * vec_ref[5:6] + vec_ref[6:7]).astype(bf)

        middle, own_normed_two = local_call(
            middle_kernel,
            "middle",
            [shape_of((rows, width), f32), shape_of((rows, width), bf)],
            [info, own_tokens, vectors, out_full] + att_parts,
            scalars=1,
            flops=2 * rows * width * width,
        )

        def expand_stack_kernel(*refs):
            for i, ref in enumerate(refs[:-1]):
                refs[-1][i * half_own : (i + 1) * half_own, :] = ref[0:half_own, :]

        (expand_all,) = local_call(
            expand_stack_kernel,
            "expand_stack",
            [shape_of(((seq_parts - 1) * half_own, ff), bf)],
            more_parts,
            after=[own_normed_two],
        )
        expand_far = core_swap(expand_all)
        n2_parts = [own_normed_two] + [seq_swap(own_normed_two, j) for j in others]

        span = ff // parts + own_width

        def ffn_kernel(info_ref, bias_ref, wc_ref, we_ref, own_cot_ref, far_we_ref, *refs):
            n2s = refs[:parts]
            mores = refs[parts : 2 * parts - 1]
            gns = refs[2 * parts - 1 : 3 * parts - 1]
            results = refs[3 * parts - 1 : 4 * parts - 1]
            keep_ref, send_ref, sum_ref = refs[4 * parts - 1 : 4 * parts + 2]
            active_ref, gh_ref, n2_ref, cot_ref, w_scr, scr = refs[4 * parts + 2 :]
            w_scr[aligned(info_ref[0], own_width), :] = we_ref[:, aligned(info_ref[0], ff)]
            for j in range(seq_parts):
                at = slice(j * rows, (j + 1) * rows)
                n2_ref[at, :] = n2s[j][...]
                if j == 0:
                    cot_ref[at, :] = own_cot_ref[...]
                    continue
                place = jnp.bitwise_xor(info_ref[0], j)
                for flip in range(2):
                    half = jnp.bitwise_xor(info_ref[2], flip)
                    start = pl.multiple_of(place * own_width + half * half_own, half_own)
                    w_scr[pl.ds(start, half_own), :] = (
                        far_we_ref[(j - 1) * half_own : j * half_own, :]
                        if flip
                        else mores[j - 1][0:half_own, :]
                    )
                cot_ref[at, :] = mores[j - 1][half_own:, :]
            hidden = mm(n2_ref[...], w_scr[...]) + bias_ref[...].astype(f32).reshape(1, ff)
            square = hidden * hidden
            curve = jnp.tanh(GELU_SCALE * hidden * (1.0 + GELU_CUBIC * square))
            active_ref[...] = (0.5 * hidden * (1.0 + curve)).astype(bf)
            slope = 0.5 * (1.0 + curve) + 0.5 * hidden * (1.0 - curve * curve) * GELU_SCALE * (
                1.0 + 3.0 * GELU_CUBIC * square
            )
            grad_hidden = mm_nt(cot_ref[...], wc_ref[...]) * slope
            gh_ref[...] = grad_hidden.astype(bf)
            sum_ref[...] = column_sums(gh_ref[...].astype(f32))
            grad = mm_nt(gh_ref[...], w_scr[...]).astype(bf)
            for j in range(parts):
                gns[j][...] = grad[j * rows : (j + 1) * rows]
            result = mm(active_ref[...], wc_ref[...]).astype(bf)
            for j in range(seq_parts):
                results[j][...] = result[j * rows : (j + 1) * rows]
            core_id = info_ref[2]
            for flip, out_ref in ((0, keep_ref), (1, send_ref)):
                half = jnp.bitwise_xor(core_id, flip)
                scr[...] = mm_tn(active_ref[...], cot_ref[:, aligned(half, half_width)]).astype(bf)
                for part in range(parts):
                    rows_to = ff // parts
                    out_ref[part, 0:rows_to, :] = scr[part * rows_to : (part + 1) * rows_to, :]
                scr[...] = mm_tn(n2_ref[...], gh_ref[:, aligned(half, half_ff)]).astype(bf)
                for part in range(parts):
                    for j in range(seq_parts):
                        at = ff // parts + j * sub
                        row = j * own_width + part * sub
                        out_ref[part, at : at + sub, :] = scr[row : row + sub, :]

        ffn_out = local_call(
            ffn_kernel,
            "feed",
            [shape_of((rows, width), bf)] * 2 * parts
            + [
                shape_of((parts, span, half_width), bf),
                shape_of((parts, span, half_width), bf),
                shape_of((1, ff), f32),
            ],
            [info, expand_bias, w_contract, w_expand, own_cot, expand_far] + n2_parts + more_parts,
            scalars=1,
            scratch=[
                pltpu.VMEM((total, ff), bf),
                pltpu.VMEM((total, ff), bf),
                pltpu.VMEM((total, width), bf),
                pltpu.VMEM((total, width), bf),
                pltpu.VMEM((width, ff), bf),
                pltpu.VMEM((width, half_ff), bf),
            ],
            flops=6 * 2 * total * width * ff,
            grant=VMEM_LARGE,
        )
        results = ffn_out[parts : 2 * parts]
        ffn_keep, ffn_send, grad_expand_row = ffn_out[2 * parts :]
        gn_parts = [ffn_out[0]] + [seq_swap(ffn_out[j], j) for j in others]
        ffn_far = core_swap(ffn_send)

        def halve_kernel(info_ref, keep_ref, far_ref, own_ref, out_ref):
            for k in range(parts):
                at = jnp.bitwise_xor(info_ref[1], k)
                piece = keep_ref[at].astype(f32) + far_ref[at].astype(f32)
                if k % 2:
                    out_ref[k // 2] = piece.astype(bf)
                else:
                    own_ref[k // 2] = piece

        rs_own, rs_send = local_call(
            halve_kernel,
            "feed_halves",
            [
                shape_of((parts // 2, span, half_width), f32),
                shape_of((parts // 2, span, half_width), bf),
            ],
            [info, ffn_keep, ffn_far],
            scalars=1,
        )
        rs_far = chip_swap(rs_send, 1)

        def back_kernel(info_ref, mid_ref, vec_ref, cot_ref, w_ref, *refs):
            gns = refs[:parts]
            douts = refs[parts : 2 * parts]
            gmid_ref, branch_ref, sums_ref = refs[2 * parts :]
            grad = gns[0][...].astype(f32)
            for j in others:
                grad = grad + gns[j][...].astype(f32)
            xhat, spread = norm_stats(mid_ref[...])
            cot = cot_ref[...].astype(f32)
            grad_middle = cot + norm_back(grad, vec_ref[5:6], xhat, spread)
            gmid_ref[...] = grad_middle
            branch = grad_middle.astype(bf)
            branch_ref[...] = branch
            for k in range(parts):
                douts[k][...] = mm_nt(branch, w_ref[jnp.bitwise_xor(info_ref[1], k)]).astype(bf)
            sums_ref[0:1, :] = column_sums(branch.astype(f32))
            sums_ref[1:2, :] = column_sums(grad * xhat)
            sums_ref[2:3, :] = column_sums(grad)
            sums_ref[3:4, :] = column_sums(cot)

        back_out = local_call(
            back_kernel,
            "middle_back",
            [shape_of((rows, hw), bf)] * parts
            + [
                shape_of((rows, width), f32),
                shape_of((rows, width), bf),
                shape_of((8, width), f32),
            ],
            [info, middle, vectors, own_cot, out_full] + gn_parts,
            scalars=1,
            after=[rs_send],
            flops=2 * rows * width * width,
        )
        grad_middle, grad_branch, late_sums = back_out[parts:]
        dout_parts = [back_out[0]] + [chip_swap(back_out[k], k) for k in others]

        def out_weights_kernel(info_ref, branch_ref, *refs):
            atts = refs[:parts]
            keep_ref, send_ref = refs[parts:]
            for flip, out_ref in ((0, keep_ref), (1, send_ref)):
                half = jnp.bitwise_xor(info_ref[2], flip)
                piece = branch_ref[:, aligned(half, half_width)]
                for k in range(parts):
                    out_ref[jnp.bitwise_xor(info_ref[1], k)] = mm_tn(atts[k][...], piece).astype(bf)

        out_keep, out_send = local_call(
            out_weights_kernel,
            "output_weights",
            [shape_of((parts, hw, half_width), bf)] * 2,
            [info, grad_branch] + att_parts,
            scalars=1,
            flops=2 * rows * width * width,
        )
        out_far = core_swap(out_send)

        fold = own_width // 2
        rider = -(-sub // 32) * 16
        pair_rows = fold // 2
        at_outs = slice(half_own, half_own + pair_rows)

        def fold_in(value):
            down = value.shape[0] // 2
            return jnp.concatenate([value[0:down], value[down:]], axis=1)

        def fold_out(value):
            across = value.shape[1] // 2
            return jnp.concatenate([value[:, 0:across], value[:, across:]], axis=0)

        def out_halves_kernel(info_ref, keep_ref, far_ref, own_ref, send_ref, scr):
            mine = info_ref[1] % 2
            for to in range(seq_parts):
                whole = fold_in(keep_ref[to].astype(f32) + far_ref[to].astype(f32))
                scr[0] = whole[0:pair_rows]
                scr[1] = whole[pair_rows:]
                own_ref[to] = scr[mine]
                send_ref[to] = scr[1 - mine].astype(bf)

        oh_own, oh_send = local_call(
            out_halves_kernel,
            "output_halves",
            [
                shape_of((seq_parts, pair_rows, width), f32),
                shape_of((seq_parts, pair_rows, width), bf),
            ],
            [info, out_keep, out_far],
            scalars=1,
            scratch=[pltpu.VMEM((2, pair_rows, width), f32)],
        )
        oh_far = chip_swap(oh_send, 1)

        def quarter_kernel(own_ref, far_ref, keep_ref, send_ref):
            keep_ref[...] = own_ref[0] + far_ref[0].astype(f32)
            send_ref[...] = (own_ref[1] + far_ref[1].astype(f32)).astype(bf)

        rs_own_two, rs_send_two = local_call(
            quarter_kernel,
            "feed_quarters",
            [shape_of((span, half_width), f32), shape_of((span, half_width), bf)],
            [rs_own, rs_far],
            after=[dout_parts[parts - 1]],
        )
        rs_far_two = chip_swap(rs_send_two, 2)

        def attend_back_kernel(info_ref, pair_ref, q_ref, kv_ref, far_ref, flat_ref, lse_ref, *refs):
            douts = refs[:parts]
            dq_ref, own_ref, send_ref, bias_ref, dout_ref = refs[parts:]
            fill_mask(bias_ref, pair_ref, info_ref, ranks, parts, block)
            for k in range(parts):
                dout_ref[k * rows : (k + 1) * rows, :] = douts[k][...].astype(f32)
            flat_dout = dout_ref[...].T
            for head in range(head_count):
                at = slice(head * HEAD_DIM, (head + 1) * HEAD_DIM)
                keys = jnp.concatenate(
                    [head_columns(kv_ref, 0, head), head_columns(far_ref, 0, head)], axis=0
                )
                values = jnp.concatenate(
                    [head_columns(kv_ref, hw, head), head_columns(far_ref, hw, head)], axis=0
                )
                queries = head_columns(q_ref, 0, head)
                dout = dout_ref[:, at].astype(bf)
                dout_turned = flat_dout[at, :]
                delta = column_sums(dout_turned * flat_ref[at, :])
                scores = mm_nt(keys, queries) * scale + bias_ref[...]
                probs = jnp.exp(scores - lse_ref[head : head + 1, :])
                grad_value = mm(probs.astype(bf), dout)
                grad_weights = mm(values, dout_turned.astype(bf))
                grad_scores = (probs * (grad_weights - delta)).astype(bf)
                grad_key = mm(grad_scores, queries) * scale
                dq_ref[at, :] = mm_tn(keys, grad_scores) * scale
                vat = slice(hw + head * HEAD_DIM, hw + (head + 1) * HEAD_DIM)
                own_ref[:, at] = grad_key[0:total]
                own_ref[:, vat] = grad_value[0:total]
                send_ref[:, at] = grad_key[total:].astype(bf)
                send_ref[:, vat] = grad_value[total:].astype(bf)

        flat_dq, dkv_own, dkv_send = local_call(
            attend_back_kernel,
            "attend_back",
            [
                shape_of((hw, total), f32),
                shape_of((total, 2 * hw), f32),
                shape_of((total, 2 * hw), bf),
            ],
            [info, pair_of_rank, query, own_kv, far_kv, flat_attended, row_lse] + dout_parts,
            scalars=2,
            after=[rs_send_two, out_send],
            scratch=[pltpu.VMEM((2 * total, total), f32), pltpu.VMEM((total, hw), f32)],
            flops=8 * 5 * 2 * head_count * 2 * total * total * HEAD_DIM,
            grant=VMEM_LARGE,
        )
        dkv_far = core_swap(dkv_send)

        def normed_back_kernel(dq_ref, own_ref, far_ref, w_ref, *refs):
            toks = refs[:parts]
            keep_ref, send_ref, mixed_ref, sums_ref, bias_ref = refs[parts:]
            mixed_ref[:, 0:hw] = dq_ref[...].T.astype(bf)
            mixed_ref[:, hw:] = (own_ref[...] + far_ref[...].astype(f32)).astype(bf)
            shift_sum = jnp.zeros((1, width), f32)
            gain_sum = jnp.zeros((1, width), f32)
            for k in range(parts):
                grad = mm_nt(mixed_ref[k * rows : (k + 1) * rows, :], w_ref[...])
                if k % 2:
                    send_ref[k // 2] = grad.astype(bf)
                else:
                    keep_ref[k // 2] = grad
                xhat, _ = norm_stats(toks[k][...].astype(f32))
                shift_sum = shift_sum + column_sums(grad)
                gain_sum = gain_sum + column_sums(grad * xhat)
            sums_ref[0:1, :] = gain_sum
            sums_ref[1:2, :] = shift_sum
            bias_ref[0:1, :] = column_sums(mixed_ref[...].astype(f32))

        nb_out = local_call(
            normed_back_kernel,
            "normed_back",
            [
                shape_of((parts // 2, rows, width), f32),
                shape_of((parts // 2, rows, width), bf),
                shape_of((total, 3 * hw), bf),
                shape_of((8, width), f32),
                shape_of((8, 3 * hw), f32),
            ],
            [flat_dq, dkv_own, dkv_far, w_heads_full] + token_parts,
            flops=0,
        )
        gt_keep, gt_send, grad_mixed, first_sums, mixed_sums = nb_out
        gt_far = chip_swap(gt_send, 1)


        def input_weights_kernel(
            info_ref, normed_ref, mixed_ref, first_ref, bias_ref, late_ref, row_ref, *refs
        ):
            keep_ref, *send_refs, grad_scr, small_scr = refs
            grad_scr[...] = mm_tn(normed_ref[...], mixed_ref[...])
            core_id, chip_id, seq = info_ref[2], info_ref[1], info_ref[0]
            small_scr[...] = jnp.zeros_like(small_scr)
            for j in range(seq_parts):
                at = slice(j * own_width, (j + 1) * own_width)
                small_scr[j, 0:2, :] = first_ref[0:2, at]
                small_scr[j, 4:8, :] = late_ref[0:4, at]
            small_scr[chip_id, 2:3, :] = bias_ref[0:1, 0:hw]
            small_scr[chip_id, 3:4, :] = bias_ref[0:1, 2 * hw : 3 * hw]
            for j in range(ff // own_width):
                small_scr[seq, 8 + j : 9 + j, :] = row_ref[:, j * own_width : (j + 1) * own_width]
            for flip in range(2):
                half = jnp.bitwise_xor(core_id, flip)
                for j in range(seq_parts):
                    out_ref = send_refs[j] if flip else keep_ref.at[j]
                    start = pl.multiple_of(j * own_width + half * half_own, 16)
                    out_ref[:, 0 : 3 * hw] = grad_scr[pl.ds(start, half_own), :].astype(bf)
                    out_ref[0:small_rows, 3 * hw :] = small_scr[j].astype(bf)
                    out_ref[small_rows:, 3 * hw :] = jnp.zeros(
                        (half_own - small_rows, side), bf
                    )

        in_keep, *in_send = local_call(
            input_weights_kernel,
            "input_weights",
            [shape_of((seq_parts, half_own, width), bf)]
            + [shape_of((half_own, width), bf)] * seq_parts,
            [info, normed, grad_mixed, first_sums, mixed_sums, late_sums, grad_expand_row],
            scalars=1,
            scratch=[
                pltpu.VMEM((width, 3 * hw), f32),
                pltpu.VMEM((seq_parts, small_rows, own_width), f32),
            ],
            flops=0,
        )
        in_far = [core_swap(member) for member in in_send]

        res_parts = [results[0]] + [seq_swap(results[j], j) for j in others]

        def result_kernel(mid_ref, vec_ref, *refs):
            result = mid_ref[...] + vec_ref[7:8]
            for j in range(seq_parts):
                result = result + refs[j][...].astype(f32)
            refs[seq_parts][0] = result.astype(bf)
            refs[seq_parts + 1][...] = jnp.zeros((8, 128), f32)

        block_out, block_done = local_call(
            result_kernel,
            "result",
            [shape_of((1, rows, width), bf), shape_of((8, 128), f32)],
            [middle, vectors] + res_parts,
            after=[in_keep],
        )

        def dp_pack_kernel(
            info_ref, own_ref, far_two_ref, keep_ref, ok_ref, of_ref, *refs
        ):
            fars, refs = refs[:seq_parts], refs[seq_parts:]
            con_ref, scr, far_scr = refs[seq_parts:]
            for j in range(seq_parts):
                far_scr[j] = fars[j][...]
            whole = own_ref[...] + far_two_ref[...].astype(f32)
            con_ref[...] = whole[0 : ff // parts].astype(bf)
            scr[...] = whole[ff // parts :]
            for j in range(seq_parts):
                at = jnp.bitwise_xor(info_ref[0], j)
                refs[j][0:half_own, :] = (
                    keep_ref[at].astype(f32) + far_scr[at].astype(f32)
                ).astype(bf)
                refs[j][at_outs, :] = (ok_ref[at] + of_ref[at].astype(f32)).astype(bf)
                piece = fold_in(scr[aligned(at, sub), :])
                piece = jnp.concatenate(
                    [piece, jnp.zeros((rider - sub // 2, width), f32)], axis=0
                )
                refs[j][half_own + pair_rows :, :] = piece.astype(bf)
        dp_out = local_call(
            dp_pack_kernel,
            "owners",
            [shape_of((half_own + pair_rows + rider, width), bf)] * seq_parts
            + [shape_of((ff // parts, half_width), bf)],
            [info, rs_own_two, rs_far_two, in_keep, oh_own, oh_far] + in_far,
            scalars=1,
            scratch=[
                pltpu.VMEM((own_width, half_ff), f32),
                pltpu.VMEM((seq_parts, half_own, width), bf),
            ],
        )
        dp_parts = [dp_out[0]] + [seq_swap(dp_out[j], j) for j in others]
        con_one = dp_out[seq_parts]

        def half_sum_kernel(keep_ref, far_ref, own_ref, send_ref):
            own_ref[...] = keep_ref[0] + far_ref[0].astype(f32)
            send_ref[...] = (keep_ref[1] + far_ref[1].astype(f32)).astype(bf)

        gt_own, gt_send_two = local_call(
            half_sum_kernel,
            "tokens_halves",
            [shape_of((rows, width), f32), shape_of((rows, width), bf)],
            [gt_keep, gt_far],
            after=[con_one],
        )
        con_two = chip_swap(con_one, 2)
        gt_far_two = chip_swap(gt_send_two, 2)

        con_one_far = chip_swap(con_one, 1)
        con_two_far = chip_swap(con_two, 1)

        con_parts = [con_one, con_one_far, con_two, con_two_far]
        con_far = [core_swap(member) for member in con_parts]

        def contract_kernel(info_ref, *refs):
            con_ref, done_ref = refs[2 * parts :]
            done_ref[...] = jnp.zeros_like(done_ref)
            for flip in range(2):
                lanes = aligned(jnp.bitwise_xor(info_ref[2], flip), half_width)
                for k in range(parts):
                    at = jnp.bitwise_xor(info_ref[1], k)
                    con_ref[aligned(at, ff // parts), lanes] = refs[flip * parts + k][...].astype(
                        f32
                    )

        grad_contract, contract_done = local_call(
            contract_kernel,
            "contract_final",
            [shape_of((ff, width), f32), shape_of((8, 128), f32)],
            [info] + con_parts + con_far,
            scalars=1,
        )

        def dp_sum_kernel(info_ref, *refs):
            owned = refs[:seq_parts]
            last_ref, scr = refs[seq_parts:]
            top = half_own + pair_rows
            whole = owned[0][0:top, :].astype(f32)
            for j in others:
                whole = whole + owned[j][0:top, :].astype(f32)
            last_ref[0:top, :] = whole.astype(bf)
            for j in range(seq_parts):
                place = jnp.bitwise_xor(info_ref[0], j)
                piece = owned[j][top:, :].astype(f32)
                scr[aligned(place, sub), :] = fold_out(piece[0 : sub // 2])
            last_ref[top:, :] = fold_in(scr[...]).astype(bf)

        (last_one,) = local_call(
            dp_sum_kernel,
            "shares",
            [shape_of((half_own + pair_rows + fold, width), bf)],
            [info] + dp_parts,
            scalars=1,
            scratch=[pltpu.VMEM((own_width, half_ff), f32)],
            after=[con_one_far, con_two_far, gt_far_two, block_done],
        )
        last_two = chip_swap(last_one, 2)
        last_one_far = chip_swap(last_one, 1)
        def tokens_kernel(tok_ref, vec_ref, gmid_ref, own_ref, far_ref, out_ref, done_ref):
            done_ref[...] = jnp.zeros_like(done_ref)
            grad = own_ref[...] + far_ref[...].astype(f32)
            xhat, spread = norm_stats(tok_ref[...].astype(f32))
            out_ref[0] = gmid_ref[...] + norm_back(grad, vec_ref[0:1], xhat, spread)

        grad_tokens, tokens_done = local_call(
            tokens_kernel,
            "tokens_back",
            [shape_of((1, rows, width), f32), shape_of((8, 128), f32)],
            [own_tokens, vectors, grad_middle, gt_own, gt_far_two],
        )

        def pass_kernel(in_ref, out_ref):
            out_ref[...] = in_ref[...]

        (last_two_on,) = local_call(
            pass_kernel,
            "pass_on",
            [shape_of((half_own + pair_rows + fold, width), bf)],
            [last_two],
            after=[contract_done, tokens_done, last_one_far],
        )
        last_two_far = chip_swap(last_two_on, 1)
        last_parts = [last_one, last_one_far, last_two, last_two_far]
        last_far = [core_swap(member) for member in last_parts]

        def last_kernel(info_ref, *refs):
            gin_ref, gout_ref, exp_ref = refs[2 * parts : 2 * parts + 3]
            bias_ref, smalls, scr, out_scr = refs[2 * parts + 3], refs[2 * parts + 4 : -2], *refs[-2:]
            for flip in range(2):
                half = jnp.bitwise_xor(info_ref[2], flip)
                outs = [jnp.zeros((pair_rows, width), f32)] * 2
                for k in range(parts):
                    at = jnp.bitwise_xor(info_ref[1], k)
                    piece = refs[flip * parts + k][...].astype(f32)
                    scr[at, aligned(half, half_own), :] = piece[0:half_own, 0 : 3 * hw]
                    outs[k % 2] = outs[k % 2] + piece[at_outs]
                    turned = fold_out(piece[half_own + pair_rows :])
                    for j in range(seq_parts):
                        cols = pl.ds(pl.multiple_of(j * ff + half * half_ff, 128), half_ff)
                        exp_ref[aligned(at, sub), cols] = turned[j * sub : (j + 1) * sub]
                mine = info_ref[1] % 2
                out_scr[mine] = outs[0]
                out_scr[1 - mine] = outs[1]
                gout_ref[:, aligned(half, half_width)] = fold_out(
                    jnp.concatenate([out_scr[0], out_scr[1]], axis=0)
                )
            for at in range(parts):
                for base in range(3):
                    start = base * width + at * hw
                    gin_ref[:, start : start + hw] = scr[at, :, base * hw : (base + 1) * hw]
            small = refs[0][0:small_rows, 3 * hw :].astype(f32)
            for k in others:
                small = small + refs[k][0:small_rows, 3 * hw :].astype(f32)
            for i in range(8):
                smalls[i][...] = small[i : i + 1].reshape(own_width)
            bias_ref[...] = jnp.concatenate(
                [small[8 + i : 9 + i] for i in range(ff // own_width)], axis=1
            ).reshape(ff)

        last_out = local_call(
            last_kernel,
            "weights_final",
            [
                shape_of((own_width, 3 * width), f32),
                shape_of((own_width, width), f32),
                shape_of((own_width, seq_parts * ff), f32),
                shape_of((ff,), f32),
            ]
            + [shape_of((own_width,), f32)] * 8,
            [info] + last_parts + last_far,
            scalars=1,
            scratch=[
                pltpu.VMEM((parts, own_width, 3 * hw), f32),
                pltpu.VMEM((2, pair_rows, width), f32),
            ],
            grant=VMEM_LARGE,
        )
        grad_input, grad_output, grad_expand, grad_expand_bias = last_out[:4]
        small_of = last_out[4:]
        return (
            block_out,
            grad_tokens,
            small_of[0],
            small_of[1],
            grad_input,
            small_of[2],
            small_of[3],
            grad_output,
            small_of[4],
            small_of[5],
            small_of[6],
            grad_expand,
            grad_expand_bias,
            grad_contract,
            small_of[7],
        )

    return per_device_heads


def solution(mesh):
    ranks = mesh.shape["ctx"]
    chips = ranks // 2
    if chips == mesh.shape["dp"] and HEADS % chips == 0 and chips & (chips - 1) == 0:
        body = head_parallel(ranks, chips, mesh.shape["dp"])
    else:
        body = per_device
    return jax.shard_map(
        body,
        mesh=mesh,
        in_specs=(
            P("dp", "ctx", None),
            P(),
            P("dp"),
            P("dp"),
            P("dp", None),
            P("dp"),
            P("dp"),
            P("dp", None),
            P("dp"),
            P("dp"),
            P("dp"),
            P("dp", None),
            P("dp"),
            P("dp", None),
            P("dp"),
            P("dp", "ctx", None),
        ),
        out_specs=(
            P("dp", "ctx", None),
            P("dp", "ctx", None),
            P("dp"),
            P("dp"),
            P("dp", None),
            P("dp"),
            P("dp"),
            P("dp", None),
            P("dp"),
            P("dp"),
            P("dp"),
            P("dp", None),
            P("dp"),
            P("dp", None),
            P("dp"),
        ),
        check_vma=False,
    )
```
